32 devices in a mesh: gx: 4 (over y, x), gz: 8 (over z, core).
Axes of the slice: x: 2, y: 2, z: 4, core: 2. Of those that a mesh axis runs over, the one named last changes fastest.
Arguments:
- source: float32 [64, 16, 1024], P('gx', None, 'gz'), may hold values from -14 to 14
- previous: float32 [64, 16, 1024], P('gx', None, 'gz'), may hold values from -6 to 6
- coefficients: float32 [3, 8, 2, 128], P(None, 'gx', None, 'gz'), may hold values from 0.3 to 3
- stiffness: float32 [8, 8], replicated, may hold values from -0.2 to 2.5, as said below
- fdm_vectors: float32 [8, 8], replicated, may hold values from -0.1 to 1.2
- fdm_values: float32 [8], replicated, may hold values from 0.1 to 10
- coarse_inverse: float32 [64, 64], P(('gx', 'gz')), may hold values from -0.004 to 0.008, as said below
- vertex_map: int32 [8, 8, 2, 128], P(None, 'gx', None, 'gz'), may hold values from 0 to 63, as said below
Outputs:
- new_solution: float32 [64, 16, 1024], P('gx', None, 'gz')
- new_residual: float32 [64, 16, 1024], P('gx', None, 'gz')
The draws below stay inside these ranges and needn't reach their ends.
Inputs may be any that keep to these rules, and one draw needn't show every extreme that they name: stiffness is symmetric. coarse_inverse is symmetric. `vertex_map`: corners of elements that meet at one grid vertex carry the same number; each number labels the vertices of one aligned block of 2 x 3 x 8 grid vertices along the three dimensions; every number occurs.
All inputs are finite; a program needn't handle non-finite values.
Results may differ from the reference program's by a relative error of at most 0.00012.
Values sent between devices are 32-bit elements; how exact they have to be, the bound alone decides.
No kernel may reach another device: no remote copies, remote signals or barrier semaphores. Data moves between devices by JAX's collectives and lax.ppermute only.
A program may use at most 64 MiB of HBM per device.

```python
import math
import jax
import jax.numpy as jnp
from jax import lax

NODES = 8
WALL_LAYERS = 2
STREAM_ELEMENTS = 8
SPAN_ELEMENTS = 128
NXN = 64
NYN = 16
NZN = 1024
NV = 64


def draw_source(key, part):
    key_values = jax.random.fold_in(key, 0)
    along_x = 0.5 + jnp.arange(NXN, dtype=jnp.float32) / NXN
    along_z = 0.5 + jnp.arange(NZN, dtype=jnp.float32) / NZN
    ramp = along_x[:, None, None] * along_z[None, None, :]
    rough = jnp.clip(jax.random.normal(key_values, (NXN, NYN, NZN), jnp.float32), -6.0, 6.0)
    return ramp * rough


def draw_stiffness(key, part):
    key_diag, key_off = jax.random.split(key)
    offdiag = jax.random.uniform(key_off, (NODES, NODES), jnp.float32, -0.2, 0.2)
    offdiag = (offdiag + offdiag.T) / 2.0
    diagonal = jax.random.uniform(key_diag, (NODES,), jnp.float32, 1.5, 2.5)
    return jnp.where(jnp.eye(NODES, dtype=bool), jnp.diag(diagonal), offdiag)


def draw_fdm_vectors(key, part):
    key_diag, key_off = jax.random.split(key)
    offdiag = jax.random.uniform(key_off, (NODES, NODES), jnp.float32, -0.1, 0.1)
    diagonal = jax.random.uniform(key_diag, (NODES,), jnp.float32, 0.8, 1.2)
    return jnp.where(jnp.eye(NODES, dtype=bool), jnp.diag(diagonal), offdiag)


def draw_coarse_inverse(key, part):
    key_diag, key_off = jax.random.split(key)
    offdiag = jax.random.uniform(key_off, (NV, NV), jnp.float32, -1.0, 1.0)
    offdiag = (offdiag + offdiag.T) * (0.45 / NV)
    diagonal = jax.random.uniform(key_diag, (NV,), jnp.float32, 1.0, 2.0)
    return 0.004 * jnp.where(jnp.eye(NV, dtype=bool), jnp.diag(diagonal), offdiag)


def draw_vertex_map(key, part):
    groups_y = (WALL_LAYERS + 1) // 3
    spanwise_groups = SPAN_ELEMENTS // 8
    labels = jax.random.permutation(key, NV).astype(jnp.int32)
    corner_point = jnp.arange(8, dtype=jnp.int32).reshape(8, 1, 1, 1)
    vertex_x = (jnp.arange(STREAM_ELEMENTS, dtype=jnp.int32).reshape(1, STREAM_ELEMENTS, 1, 1) + corner_point // 4) % STREAM_ELEMENTS
    vertex_y = jnp.arange(WALL_LAYERS, dtype=jnp.int32).reshape(1, 1, WALL_LAYERS, 1) + corner_point // 2 % 2
    spanwise_vertex = (jnp.arange(SPAN_ELEMENTS, dtype=jnp.int32).reshape(1, 1, 1, SPAN_ELEMENTS) + corner_point % 2) % SPAN_ELEMENTS
    group = vertex_x // 2 * (groups_y * spanwise_groups) + vertex_y // 3 * spanwise_groups + spanwise_vertex // 8
    return labels[group].astype(jnp.int32)


def block_scale(stream_key, extent, pieces, least, top_value):
    level, own = 1.0, jax.random.fold_in(stream_key, 6)
    for dim, parts in pieces:
        steps = jnp.exp(jax.random.uniform(jax.random.fold_in(own, dim), (parts,), jnp.float32, least / len(pieces), top_value / len(pieces)))
        level = level * jnp.repeat(steps, extent[dim] // parts).reshape([-1 if axis == dim else 1 for axis in range(len(extent))])
    return level


def normal_values(rng, shape, scale, bound, pieces=(), kind=jnp.bfloat16):
    loudness = block_scale(rng, shape, pieces, -0.22, 0.18) if pieces else 1.0
    values = jax.random.normal(rng, shape, jnp.float32) * scale * loudness
    return jnp.minimum(jnp.maximum(values, -bound), bound).astype(kind)


def setup_inputs(seed: int = 0) -> dict:
    splits = jax.random.split(jax.random.key(seed), 9)
    return {
        "source": draw_source(jax.random.fold_in(splits[8], 71), 0),
        "previous": normal_values(splits[1], (NXN, NYN, NZN), 1.0, 6.0, ((0, 4), (2, 8)), jnp.float32),
        "coefficients": jnp.clip(jnp.exp(math.log(3.0) - 2.3025851 * jax.random.uniform(splits[2], (3, STREAM_ELEMENTS, WALL_LAYERS, SPAN_ELEMENTS), jnp.float32) ** block_scale(splits[2], (3, STREAM_ELEMENTS, WALL_LAYERS, SPAN_ELEMENTS), ((1, 4), (3, 8)), -0.2, 0.2)), 0.3, 3.0),
        "stiffness": draw_stiffness(jax.random.fold_in(splits[8], 71), 0),
        "fdm_vectors": draw_fdm_vectors(jax.random.fold_in(splits[8], 71), 0),
        "fdm_values": jnp.clip(jnp.exp(jax.random.uniform(splits[5], (NODES,), jnp.float32, math.log(0.1), math.log(10.0))), 0.1, 10.0),
        "coarse_inverse": draw_coarse_inverse(jax.random.fold_in(splits[8], 71), 0),
        "vertex_map": draw_vertex_map(jax.random.fold_in(splits[8], 71), 0),
    }


GLL_POINTS = [-1.0, -0.8717401485096066, -0.5917001814331423, -0.2092992179024789, 0.2092992179024789, 0.5917001814331423, 0.8717401485096066, 1.0]
GLL_WEIGHTS = [0.03571428571428571, 0.21070422714350603, 0.34112269248350436, 0.4124587946587038, 0.4124587946587038, 0.34112269248350436, 0.21070422714350603, 0.03571428571428571]


def node_weights(length):
    return jnp.tile(jnp.array(GLL_WEIGHTS, dtype=jnp.float32), length // 8)


def contract_axis(values, matrix, axis_number):
    layout = values.shape
    length = layout[axis_number]
    split = values.reshape(layout[:axis_number] + (length // 8, 8) + layout[axis_number + 1:])
    moved = jnp.moveaxis(split, axis_number + 1, -1)
    result = jnp.einsum('...p,ip->...i', moved, matrix, precision=lax.Precision.HIGHEST)
    return jnp.moveaxis(result, -1, axis_number + 1).reshape(layout)


def pair_sum(values, axis_number, periodic):
    length = values.shape[axis_number]
    if periodic:
        upper = jnp.roll(values, -1, axis=axis_number)
        lower = jnp.roll(values, 1, axis=axis_number)
    else:
        widths = [(0, 0), (0, 0), (0, 0)]
        widths[axis_number] = (1, 1)
        padded = jnp.pad(values, widths)
        upper = lax.slice_in_dim(padded, 2, length + 2, axis=axis_number)
        lower = lax.slice_in_dim(padded, 0, length, axis=axis_number)
    layout = [1, 1, 1]
    layout[axis_number] = length
    position = (jnp.arange(length) % 8).reshape(layout)
    return values + jnp.where(position == 7, upper, 0.0) + jnp.where(position == 0, lower, 0.0)


def assemble(values):
    values = pair_sum(values, 0, True)
    values = pair_sum(values, 1, False)
    return pair_sum(values, 2, True)


def spread(layer):
    return jnp.repeat(jnp.repeat(jnp.repeat(layer, 8, axis=0), 8, axis=1), 8, axis=2)


def apply_operator(values, spreads, stiffness):
    weight_x = node_weights(values.shape[0])[:, None, None]
    weight_y = node_weights(values.shape[1])[None, :, None]
    weight_z = node_weights(values.shape[2])[None, None, :]
    result = spreads[0] * contract_axis(values, stiffness, 0) * weight_y * weight_z
    result = result + spreads[1] * contract_axis(values, stiffness, 1) * weight_x * weight_z
    return result + spreads[2] * contract_axis(values, stiffness, 2) * weight_x * weight_y


def local_solve(values, spreads, vectors, eigen):
    moved = contract_axis(values, vectors.T, 0)
    moved = contract_axis(moved, vectors.T, 1)
    moved = contract_axis(moved, vectors.T, 2)
    lam_x = jnp.tile(eigen, values.shape[0] // 8)[:, None, None]
    lam_y = jnp.tile(eigen, values.shape[1] // 8)[None, :, None]
    lam_z = jnp.tile(eigen, values.shape[2] // 8)[None, None, :]
    moved = moved / (spreads[0] * lam_x + spreads[1] * lam_y + spreads[2] * lam_z)
    moved = contract_axis(moved, vectors, 0)
    moved = contract_axis(moved, vectors, 1)
    return contract_axis(moved, vectors, 2)


def reference(source, previous, coefficients, stiffness, fdm_vectors, fdm_values, coarse_inverse, vertex_map):
    rows_x, rows_y, spanwise_rows = source.shape
    elements_x, elements_y, elements_z = rows_x // 8, rows_y // 8, spanwise_rows // 8
    count_coarse = coarse_inverse.shape[0]
    copies = assemble(jnp.ones_like(source))
    keep = (jnp.arange(rows_y) < rows_y - 1).astype(source.dtype).reshape(1, rows_y, 1)
    spreads = [spread(coefficients[component]) for component in range(3)]
    start = keep * assemble(previous) / copies
    residual = keep * assemble(source - apply_operator(start, spreads, stiffness))
    local_part = local_solve(residual, spreads, fdm_vectors, fdm_values)
    points = jnp.array(GLL_POINTS, dtype=jnp.float32)
    basis = jnp.stack([(1.0 - points) / 2.0, (1.0 + points) / 2.0])
    weighted = (residual / copies).reshape(elements_x, 8, elements_y, 8, elements_z, 8)
    corner_sums = jnp.einsum('xi,yj,zk,aibjek->axbyez', basis, basis, basis, weighted, precision=lax.Precision.HIGHEST)
    corner_sums = corner_sums.transpose(1, 3, 5, 0, 2, 4).reshape(8, elements_x, elements_y, elements_z)
    coarse_rhs = jax.ops.segment_sum(corner_sums.reshape(-1), vertex_map.reshape(-1).astype(jnp.int32), num_segments=count_coarse)
    coarse_values = jnp.dot(coarse_inverse, coarse_rhs, precision=lax.Precision.HIGHEST)
    picked = coarse_values[vertex_map.astype(jnp.int32)].reshape(2, 2, 2, elements_x, elements_y, elements_z)
    picked = picked.transpose(3, 0, 4, 1, 5, 2)
    coarse_part = jnp.einsum('axbyez,xi,yj,zk->aibjek', picked, basis, basis, basis, precision=lax.Precision.HIGHEST)
    coarse_part = coarse_part.reshape(rows_x, rows_y, spanwise_rows)
    precond = keep * (assemble(local_part) + coarse_part)
    numerator = jnp.sum(residual * precond / copies)
    image = keep * assemble(apply_operator(precond, spreads, stiffness))
    denominator = jnp.sum(precond * image / copies)
    alpha = numerator / denominator
    return start + alpha * precond, residual - alpha * image
```

```python
import functools

import jax
import jax.numpy as jnp
import numpy as np
from jax import lax
from jax.experimental import pallas as pl
from jax.experimental.pallas import tpu as pltpu
from jax.sharding import PartitionSpec as P

POINTS = [
    -1.0,
    -0.8717401485096066,
    -0.5917001814331423,
    -0.2092992179024789,
    0.2092992179024789,
    0.5917001814331423,
    0.8717401485096066,
    1.0,
]
WEIGHTS = [
    0.03571428571428571,
    0.21070422714350603,
    0.34112269248350435,
    0.4124587946587038,
    0.4124587946587038,
    0.34112269248350435,
    0.21070422714350603,
    0.03571428571428571,
]
LOW = [(1.0 - s) / 2.0 for s in POINTS]
HIGH = [(1.0 + s) / 2.0 for s in POINTS]
EXACT = lax.Precision.HIGHEST

ROWS = 16
LANES = 128
WIDE = 256
HALO = 32
PAIRS = ((0, 0), (0, 1), (1, 1))
GROUP_X = ([1.0] * 8 + LOW, [0.0] * 8 + HIGH)
INVERSE_X = [0.5] + [1.0] * 6 + [0.5] + [0.5] + [1.0] * 6 + [0.5]


def iota(shape, dim):
    return lax.broadcasted_iota(jnp.int32, shape, dim)


def pick(index, values):
    result = jnp.full(index.shape, values[0], jnp.float32)
    for i in range(1, 8):
        result = jnp.where(index == i, values[i], result)
    return result


def even_index(axis):
    return lax.rem(lax.axis_index(axis), 2) == 0


class Geometry:
    def __init__(self, lanes):
        shape = (2, 8, lanes)
        self.element_y, self.row, lane = iota(shape, 0), iota(shape, 1), iota(shape, 2)
        self.position = lane & 7
        self.first = self.position == 0
        self.last = self.position == 7
        self.edge = self.first | self.last
        self.weight_y = pick(self.row, WEIGHTS)
        self.weight_z = pick(self.position, WEIGHTS)
        self.inverse_z = jnp.where(self.edge, 0.5, 1.0)
        self.wall = (self.element_y == 1) & (self.row == 7)
        inner = ((self.element_y == 0) & (self.row == 7)) | ((self.element_y == 1) & (self.row == 0))
        self.inverse_y = jnp.where(inner, 0.5, 1.0)
        self.keep = jnp.where(self.wall, 0.0, 1.0)
        self.lanes = lanes

    def pair_y(self, v):
        lower, upper = v[0], v[1]
        row = self.row[0]
        up = jnp.where(row == 7, pltpu.roll(upper, 7, 0), 0.0)
        down = jnp.where(row == 0, pltpu.roll(lower, 1, 0), 0.0)
        return jnp.stack([lower + up, upper + down])

    def pair_z(self, v):
        flat = v.reshape(16, self.lanes)
        after = pltpu.roll(flat, self.lanes - 1, 1).reshape(v.shape)
        before = pltpu.roll(flat, 1, 1).reshape(v.shape)
        return v + jnp.where(self.edge, jnp.where(self.last, after, before), 0.0)

    def pair(self, v):
        return self.pair_z(self.pair_y(v))


def contract_x(rows, matrix, i, transpose=False):
    total = None
    for p in range(8):
        factor = matrix[p, i] if transpose else matrix[i, p]
        term = factor * rows[p]
        total = term if total is None else total + term
    return total


def contract_y(v, diagonals):
    total = diagonals[0] * v
    for d in range(1, 8):
        rolled = jnp.stack([pltpu.roll(v[e], 8 - d, 0) for e in range(2)])
        total = total + diagonals[d] * rolled
    return total


def contract_z(flat, block):
    pieces = [
        jnp.dot(
            flat[:, at : at + LANES], block, precision=EXACT, preferred_element_type=jnp.float32
        )
        for at in range(0, flat.shape[1], LANES)
    ]
    return pieces[0] if len(pieces) == 1 else jnp.concatenate(pieces, axis=1)


def wide_diagonals(ref, which, lanes):
    one = [ref[which, d] for d in range(8)]
    return [jnp.concatenate([c] * (lanes // LANES), axis=1)[None] for c in one]


def metric(ref, component, element, lanes):
    at = (component * 2 + element) * 2
    return jnp.stack([jnp.broadcast_to(ref[at + e : at + e + 1, :lanes], (8, lanes)) for e in range(2)])


def apply_rows(geo, source_ref, along_z, metrics, stiffness, diagonals):
    lanes = geo.lanes
    rows = [source_ref[x].reshape(2, 8, lanes) for x in range(ROWS)]
    result = []
    for element in range(2):
        cx, cy, cz = metrics[element]
        factor_x = cx * geo.weight_y * geo.weight_z
        factor_y = cy * geo.weight_z
        factor_z = cz * geo.weight_y
        own = rows[element * 8 : element * 8 + 8]
        for i in range(8):
            x = element * 8 + i
            term_y = factor_y * contract_y(own[i], diagonals)
            term_z = factor_z * along_z[x * 16 : x * 16 + 16].reshape(2, 8, lanes)
            result.append(factor_x * contract_x(own, stiffness, i) + WEIGHTS[i] * (term_y + term_z))
    return result


def join_middle(rows):
    middle = rows[7] + rows[8]
    return rows[:7] + [middle, middle] + rows[9:]


def prepare_kernel(stiffness, vectors, blocks, diagonals):
    spread_rows = (iota((LANES, 8), 0) & 7 == iota((LANES, 8), 1)).astype(jnp.float32)
    same = (iota((LANES, LANES), 0) >> 3) == (iota((LANES, LANES), 1) >> 3)
    unit = (iota((8, 8), 0) == iota((8, 8), 1)).astype(jnp.float32)

    def dot(a, b, dims):
        return lax.dot_general(a, b, ((dims), ((), ())), precision=EXACT, preferred_element_type=jnp.float32)

    def block(matrix):
        half = dot(spread_rows, matrix, ((1,), (0,)))
        return jnp.where(same, dot(half, spread_rows, ((1,), (1,))), 0.0)

    def put_diagonals(at, matrix):
        row, column = iota((8, 8), 0), iota((8, 8), 1)
        for d in range(8):
            chosen = jnp.where(column == ((row + d) & 7), matrix, 0.0)
            diagonals[at, d] = jnp.broadcast_to(jnp.sum(chosen, axis=1, keepdims=True), (8, LANES))

    k, s = stiffness[...], vectors[...]
    k_turned, s_turned = dot(k, unit, ((0,), (0,))), dot(s, unit, ((0,), (0,)))
    blocks[0] = block(k_turned)
    blocks[1] = block(s)
    blocks[2] = block(s_turned)
    put_diagonals(0, k)
    put_diagonals(1, s_turned)
    put_diagonals(2, s)


def pack_kernel(source, previous, coefficients, first, second, metrics, scratch):
    even = even_index("gz")
    scratch[...] = jnp.zeros_like(scratch)
    for c in range(3):
        for element in range(2):
            at = (c * 2 + element) * 2
            scratch[at : at + 2, :] = coefficients[c, element]
    widen = (iota((16, LANES), 0) == (iota((16, LANES), 1) >> 3)).astype(jnp.float32)
    spread = jnp.dot(scratch[...], widen, precision=EXACT, preferred_element_type=jnp.float32)
    metrics[...] = spread
    group = iota((8 * ROWS, LANES), 1) // HALO
    parts = [
        ref[lo : lo + 8].reshape(8 * ROWS, LANES) for ref in (previous, source) for lo in (0, 8)
    ]
    for to_right, out in ((even, first), (jnp.logical_not(even), second)):
        base = jnp.where(to_right, HALO, 0)
        packed = None
        for k, part in enumerate(parts):
            moved = pltpu.roll(part, lax.rem(base + HALO * k, LANES), 1)
            packed = moved if packed is None else jnp.where(group == k, moved, packed)
        out[0:8] = packed.reshape(8, ROWS, LANES)
        out[8] = spread


def start_kernel(
    source, previous, own_metrics, first, second, stiffness, blocks, diagonals,
    start, rest, metrics, message_a, message_b, field,
):
    even = even_index("gz")
    lane = iota((ROWS, LANES), 1)

    def beyond(plane, right_shift, left_shift, fill):
        a, b = first[plane], second[plane]
        right, left = jnp.where(even, a, b), jnp.where(even, b, a)
        if right_shift:
            right = pltpu.roll(right, right_shift, 1)
        if left_shift:
            left = pltpu.roll(left, left_shift, 1)
        return jnp.where(lane < HALO, right, jnp.where(lane >= LANES - HALO, left, fill))

    def wide(ref, x, kind):
        slot = 2 * kind + x // 8
        right_shift = (LANES - HALO * slot) % LANES
        left_shift = (LANES - HALO - HALO * slot) % LANES
        return jnp.concatenate([ref[x], beyond(x % 8, right_shift, left_shift, 0.0)], axis=1).reshape(2, 8, WIDE)

    geo = Geometry(WIDE)
    metrics[:, :LANES] = own_metrics[...]
    metrics[:, LANES:] = beyond(8, 0, 0, 1.0)
    factor = geo.keep * geo.inverse_y * geo.inverse_z
    rows = [geo.pair(wide(previous, x, 0)) * (factor * INVERSE_X[x]) for x in range(ROWS)]
    rows = join_middle(rows)
    faces = (rows[0], rows[15])
    rows[0] = rows[15] = jnp.zeros_like(rows[0])
    for x in range(ROWS):
        field[x] = rows[x].reshape(ROWS, WIDE)
        start[x] = rows[x].reshape(ROWS, WIDE)[:, :LANES]
    along_z = contract_z(field[...].reshape(ROWS * ROWS, WIDE), blocks[0])
    factors = [[metric(metrics, c, e, WIDE) for c in range(3)] for e in range(2)]
    applied = apply_rows(geo, field, along_z, factors, stiffness, wide_diagonals(diagonals, 0, WIDE))
    for x in range(ROWS):
        rest[x] = (wide(source, x, 1) - applied[x]).reshape(ROWS, WIDE)
    even_x = even_index("gx")

    def choose(right, left):
        return jnp.where(even_x, right, left), jnp.where(even_x, left, right)

    for at, right, left in (
        (0, faces[1].reshape(ROWS, WIDE), faces[0].reshape(ROWS, WIDE)),
        (16, rest[15], rest[0]),
    ):
        message_a[at : at + 16], message_b[at : at + 16] = choose(right, left)
    for c in range(3):
        at = 32 + 2 * c
        right, left = metrics[(c * 2 + 1) * 2 : (c * 2 + 1) * 2 + 2], metrics[c * 4 : c * 4 + 2]
        message_a[at : at + 2], message_b[at : at + 2] = choose(right, left)
    message_a[38:40] = jnp.zeros((2, WIDE), jnp.float32)
    message_b[38:40] = jnp.zeros((2, WIDE), jnp.float32)


def face_metric(ref_right, ref_left, c, even, right):
    def rows(ref):
        return jnp.stack([jnp.broadcast_to(ref[32 + 2 * c + e : 33 + 2 * c + e], (8, WIDE)) for e in range(2)])

    a, b = rows(ref_right), rows(ref_left)
    return jnp.where(even, a, b) if right else jnp.where(even, b, a)


def solve_kernel(
    start, rest, metrics, own_a, own_b, got_a, got_b, stiffness, vectors, eigen, blocks, diagonals,
    new_start, residual, local, message_a, message_b, sums, field,
):
    even = even_index("gx")
    geo = Geometry(WIDE)
    factors = [[metric(metrics, c, e, WIDE) for c in range(3)] for e in range(2)]

    def sided(a, b, at):
        one, two = a[at : at + 16].reshape(2, 8, WIDE), b[at : at + 16].reshape(2, 8, WIDE)
        return jnp.where(even, one, two), jnp.where(even, two, one)

    mine, theirs = sided(own_a, own_b, 0), sided(got_a, got_b, 0)
    right, left = mine[0] + theirs[0], mine[1] + theirs[1]
    other_rest = sided(got_a, got_b, 16)
    for x in range(1, 15):
        new_start[x] = start[x]
    new_start[0] = left.reshape(ROWS, WIDE)[:, :LANES]
    new_start[15] = right.reshape(ROWS, WIDE)[:, :LANES]

    stiff = wide_diagonals(diagonals, 0, WIDE)
    rows = [rest[x].reshape(2, 8, WIDE) for x in range(ROWS)]
    for element, near, face, across, far, side in ((0, 0, left, 7, 1, False), (1, 7, right, 0, 0, True)):
        cx, cy, cz = factors[element]
        other = [face_metric(got_a, got_b, c, even, side) for c in range(3)]
        weights = geo.weight_y * geo.weight_z
        scaled = cx * weights * face
        for i in range(8):
            if i != near:
                rows[element * 8 + i] = rows[element * 8 + i] - stiffness[i, near] * scaled
        along_z = contract_z(face.reshape(ROWS, WIDE), blocks[0]).reshape(2, 8, WIDE)
        taken = stiffness[near, near] * scaled + stiffness[across, across] * (other[0] * weights * face)
        taken = taken + WEIGHTS[0] * (
            (cy + other[1]) * geo.weight_z * contract_y(face, stiff) + (cz + other[2]) * geo.weight_y * along_z
        )
        x = element * 8 + near
        rows[x] = rows[x] + other_rest[far] - taken
    rows = [geo.pair(v) * geo.keep for v in join_middle(rows)]
    weight = geo.inverse_y * geo.inverse_z
    parts = [None, None]
    for x in range(ROWS):
        field[x] = rows[x].reshape(ROWS, WIDE)
        residual[x] = rows[x].reshape(ROWS, WIDE)[:, :LANES]
        for a in range(2):
            if GROUP_X[a][x] * INVERSE_X[x] != 0.0:
                term = (GROUP_X[a][x] * INVERSE_X[x]) * rows[x][:, :, :LANES]
                parts[a] = term if parts[a] is None else parts[a] + term

    def down(v):
        return jnp.sum(v.reshape(ROWS, LANES), axis=0, keepdims=True)

    for a in range(2):
        sums[a : a + 1] = down(parts[a] * weight[:, :, :LANES])

    forward, backward = wide_diagonals(diagonals, 1, WIDE), wide_diagonals(diagonals, 2, WIDE)
    moved = []
    for element in range(2):
        own = [field[element * 8 + p].reshape(2, 8, WIDE) for p in range(8)]
        for i in range(8):
            moved.append(contract_y(contract_x(own, vectors, i, True), forward).reshape(ROWS, WIDE))
    spectral = contract_z(jnp.concatenate(moved, axis=0), blocks[1])
    lam = [eigen[i] for i in range(8)]
    lam_y, lam_z = pick(geo.row, lam), pick(geo.position, lam)
    divided = []
    for element in range(2):
        cx, cy, cz = factors[element]
        base = cy * lam_y + cz * lam_z
        for i in range(8):
            x = element * 8 + i
            value = spectral[x * 16 : x * 16 + 16].reshape(2, 8, WIDE)
            divided.append((value / (cx * lam[i] + base)).reshape(ROWS, WIDE))
    back = contract_z(jnp.concatenate(divided, axis=0), blocks[2])
    solved = []
    for element in range(2):
        own = [
            contract_y(back[x * 16 : x * 16 + 16].reshape(2, 8, WIDE), backward)
            for x in range(element * 8, element * 8 + 8)
        ]
        solved += [contract_x(own, vectors, i) for i in range(8)]
    total = None
    for x in range(ROWS):
        term = solved[x][:, :, :LANES] * residual[x].reshape(2, 8, LANES)
        total = term if total is None else total + term
    sums[2:3] = down(total)
    sums[3:8] = jnp.zeros((5, LANES), jnp.float32)
    solved = [(geo.pair(v) * geo.keep).reshape(ROWS, WIDE) for v in join_middle(solved)]
    for x in range(ROWS):
        local[x] = solved[x]
    message_a[...] = jnp.where(even, solved[15], solved[0])
    message_b[...] = jnp.where(even, solved[0], solved[15])


def group_lanes(lanes, group):
    lane = iota((1, lanes), 1)
    signed = jnp.where(lane < lanes // 2 + lanes // 4, lane, lane - lanes) if lanes > LANES else lane
    element, position = signed >> 3, lane & 7
    low, high = pick(position, LOW), pick(position, HIGH)
    here = jnp.where((element >> 3) == group, low, 0.0)
    return here + jnp.where(((element + 1) >> 3) == group, high, 0.0)


def image_kernel(
    local, metrics, got_a, got_b, stiffness, labels, coarse, sums, blocks, diagonals,
    local_own, image, message_a, message_b, payload, field,
):
    even = even_index("gx")
    geo = Geometry(WIDE)
    one, two = got_a[...], got_b[...]
    for x in range(ROWS):
        value = local[x]
        if x == 0:
            value = value + jnp.where(even, two, one)
        if x == 15:
            value = value + jnp.where(even, one, two)
        field[x] = value
        local_own[x] = value[:, :LANES]
    along_z = contract_z(field[...].reshape(ROWS * ROWS, WIDE), blocks[0])
    factors = [[metric(metrics, c, e, WIDE) for c in range(3)] for e in range(2)]
    applied = apply_rows(geo, field, along_z, factors, stiffness, wide_diagonals(diagonals, 0, WIDE))

    total, parts = None, [None, None]
    for x in range(ROWS):
        own = applied[x][:, :, :LANES]
        term = own * local_own[x].reshape(2, 8, LANES)
        total = term if total is None else total + term
        for a in range(2):
            if GROUP_X[a][x] != 0.0:
                term = GROUP_X[a][x] * own
                parts[a] = term if parts[a] is None else parts[a] + term
    keep = geo.keep[:, :, :LANES]

    def down(v):
        return jnp.sum(v.reshape(ROWS, LANES), axis=0, keepdims=True)

    applied = [(geo.pair(v) * geo.keep).reshape(ROWS, WIDE)[:, :LANES] for v in join_middle(applied)]
    for x in range(ROWS):
        image[x] = applied[x]
    message_a[...] = jnp.where(even, applied[15], applied[0])
    message_b[...] = jnp.where(even, applied[0], applied[15])

    groups = [group_lanes(LANES, b) for b in range(3)]
    stacked = jnp.concatenate(groups + [jnp.zeros((5, LANES), jnp.float32)], axis=0)
    stiff_z = contract_z(stacked, blocks[0])
    weight_z = pick(iota((1, LANES), 1) & 7, WEIGHTS)
    kept = [[1.0] * 8, [1.0] * 7 + [0.0]]
    mass_y = [sum(w * k for w, k in zip(WEIGHTS, line)) for line in kept]
    inner = None
    for i in range(7):
        for j in range(7):
            inner = stiffness[i, j] if inner is None else inner + stiffness[i, j]
    border = stiffness[7, 7]
    for i in range(7):
        border = border + stiffness[i, 7] + stiffness[7, i]
    stiff_y = [inner + border, inner]
    matrix_rows = []
    for a, b in PAIRS:
        across, along = jnp.zeros((1, LANES), jnp.float32), jnp.zeros((1, LANES), jnp.float32)
        for element in range(2):
            fa = GROUP_X[a][element * 8 : element * 8 + 8]
            fb = GROUP_X[b][element * 8 : element * 8 + 8]
            if not (any(fa) and any(fb)):
                continue
            mass_x = sum(w * p * q for w, p, q in zip(WEIGHTS, fa, fb))
            stiff_x = None
            for i in range(8):
                for j in range(8):
                    if fa[i] * fb[j] != 0.0:
                        term = (fa[i] * fb[j]) * stiffness[i, j]
                        stiff_x = term if stiff_x is None else stiff_x + term
            for e in range(2):
                cx, cy, cz = (metrics[(c * 2 + element) * 2 + e, :LANES].reshape(1, LANES) for c in range(3))
                across = across + cx * (stiff_x * mass_y[e]) + cy * (stiff_y[e] * mass_x)
                along = along + cz * (mass_x * mass_y[e])
        across = across * weight_z
        for k in range(3):
            matrix_rows.append(across * groups[k] + along * stiff_z[k : k + 1])
    zero = jnp.zeros((1, LANES), jnp.float32)
    lines = [sums[0:1], sums[1:2]] + [down(part * keep) for part in parts] + matrix_rows
    lines = jnp.concatenate(lines + [sums[2:3], down(total), zero], axis=0)
    lane = iota((LANES, LANES), 1) & 7
    node = iota((LANES, LANES), 0)
    element, position = node >> 3, node & 7
    low, high = pick(position, LOW), pick(position, HIGH)
    columns = jnp.where(lane == (element >> 3), low, 0.0) + jnp.where(lane == ((element + 1) >> 3), high, 0.0)
    columns = jnp.where(lane == 3, 1.0, jnp.where(lane < 3, columns, 0.0))
    reduced = jnp.dot(lines, columns, precision=EXACT, preferred_element_type=jnp.float32)
    mine = (iota((16, LANES), 1) >> 3) == iota((16, LANES), 0)
    row = jnp.sum(jnp.where(mine, reduced, 0.0), axis=0, keepdims=True)
    place = iota((1, LANES), 1)
    for a in range(2):
        for b in range(3):
            corner, x, z = 4 * a + (b == 2), a, (0, 8, 15)[b]
            number = labels[corner, x, 0, z].astype(jnp.float32)
            row = jnp.where(place == 8 * (3 * a + b) + 4, number, row)
    if coarse is None:
        below = zero
    else:
        per, count = coarse.shape
        below = [coarse[i : i + 1, :] for i in range(per)]
        if per * count < LANES:
            below.append(jnp.zeros((1, LANES - per * count), jnp.float32))
        below = jnp.concatenate(below, axis=1)
    block = jnp.concatenate([row, below] * 4, axis=0)
    copies = payload.shape[0] // 8
    payload[...] = jnp.broadcast_to(block[None], (copies, 8, LANES)).reshape(copies * 8, LANES)


def lane_tables():
    one = np.zeros((8, LANES), np.float32)
    two = np.zeros((8, LANES), np.float32)
    top = np.zeros((8, LANES), np.float32)
    for a in range(2):
        for b in range(3):
            one[6, 8 * a + b], two[3 * a + b, 8 * a + b], top[0, 8 * a + b] = 1.0, 1.0, 1.0
            one[6, 8 * (2 + a) + b], two[3 * a + b, 8 * (2 + a) + b] = 2.0, 1.0
            top[1, 8 * (2 + a) + b] = 1.0
    for p, (a, other) in enumerate(PAIRS):
        for b in range(3):
            for c in range(3):
                at = 8 * (4 + 3 * p + b) + c
                one[3 * a + b, at] = 1.0 if a == other else 2.0
                two[3 * other + c, at] = 1.0
                top[1, at] = 1.0
    one[6, 8 * 13 + 3], two[6, 8 * 13 + 3], top[0, 8 * 13 + 3] = 1.0, 1.0, 1.0
    one[6, 8 * 14 + 3], two[6, 8 * 14 + 3], top[1, 8 * 14 + 3] = 1.0, 1.0, 1.0
    return np.stack([one, two, top])


def final_kernel(
    devices, spans, count, per,
    start, residual, local, image, got_a, got_b, far_a, far_b, metrics, stiffness, blocks, diagonals, tables,
    gathered, given, new_solution, new_residual, values,
):
    even = even_index("gx")
    geo = Geometry(WIDE)
    rows = gathered[pl.ds(0, devices, stride=2), :]
    place = iota((1, LANES), 1)
    if given is None:
        spot = iota((devices, count), 1)
        hits = []
        rhs = [jnp.zeros((1, devices), jnp.float32) for _ in range(per)]
        owner = iota((devices, devices), 1)
        for k in range(6):
            label = rows[:, 8 * k + 4 : 8 * k + 5].astype(jnp.int32)
            at = 8 * (k // 3) + k % 3
            value = rows[:, at : at + 1]
            hits.append(spot == label)
            for q in range(per):
                chosen = jnp.where(owner * per + q == label, value, 0.0)
                rhs[q] = rhs[q] + jnp.sum(chosen, axis=0, keepdims=True)
        inverse = gathered[pl.ds(1, devices, stride=2), :]
        coarse = None
        for q in range(per):
            term = jnp.dot(
                rhs[q], inverse[:, q * count : q * count + count], precision=EXACT,
                preferred_element_type=jnp.float32,
            )
            coarse = term if coarse is None else coarse + term
        columns = [jnp.sum(jnp.where(hit, coarse, 0.0), axis=1, keepdims=True) for hit in hits]
        kept = jnp.zeros((devices, LANES), jnp.float32)
        for k in range(6):
            kept = jnp.where(iota((devices, LANES), 1) == k, columns[k], kept)
        values[...] = kept
    else:
        columns = [given[:, k : k + 1] for k in range(6)]
        values[...] = given[...]
    one, two = tables[0, 6:7, :], tables[1, 6:7, :]
    for k in range(6):
        one = one + columns[k] * tables[0, k : k + 1, :]
        two = two + columns[k] * tables[1, k : k + 1, :]
    product = jnp.sum(rows * one * two, axis=0, keepdims=True)
    numerator = jnp.sum(product * tables[2, 0:1, :], axis=1, keepdims=True)
    denominator = jnp.sum(product * tables[2, 1:2, :], axis=1, keepdims=True)
    alpha = numerator / denominator

    gx, gz = lax.axis_index("gx"), lax.axis_index("gz")
    before_x = lax.rem(gx + devices // spans - 1, devices // spans)
    before_z = lax.rem(gz + spans - 1, spans)
    here = values[pl.ds(gx * spans + gz, 1), :]
    behind = values[pl.ds(gx * spans + before_z, 1), :]
    aside = values[pl.ds(before_x * spans + gz, 1), :]
    corner = values[pl.ds(before_x * spans + before_z, 1), :]
    functions = [group_lanes(WIDE, b) for b in (-1, 0, 1, 2)]

    def along(line, back, a):
        total = back[:, 3 * a + 1 : 3 * a + 2] * functions[0]
        for b in range(3):
            total = total + line[:, 3 * a + b : 3 * a + b + 1] * functions[1 + b]
        return total

    lines = [along(here, behind, 0), along(here, behind, 1), along(aside, corner, 0)]
    flat = jnp.concatenate(lines + [jnp.zeros((5, WIDE), jnp.float32)], axis=0)
    stiff_lines = contract_z(flat, blocks[0])
    wide = [jnp.broadcast_to(line, (8, WIDE))[None] for line in lines]
    stiff_wide = [jnp.broadcast_to(stiff_lines[a : a + 1], (8, WIDE))[None] for a in range(3)]
    stiff_keep = contract_y(geo.keep, wide_diagonals(diagonals, 0, WIDE))

    def spread(c, weights_x, stiff_x, weight, side):
        cx, cy, cz = c
        plain = flat_x = turned = None
        for a, w, s in zip(side, weights_x, stiff_x):
            if s is not None:
                flat_x = s * wide[a] if flat_x is None else flat_x + s * wide[a]
            if w != 0.0:
                plain = w * wide[a] if plain is None else plain + w * wide[a]
                turned = w * stiff_wide[a] if turned is None else turned + w * stiff_wide[a]
        return cx * flat_x + weight * (cy * plain + cz * turned)

    def folded(c):
        return (
            c[0] * (geo.weight_y * geo.weight_z * geo.keep),
            c[1] * (geo.weight_z * stiff_keep),
            c[2] * (geo.weight_y * geo.keep),
        )

    def stiff_of(i, line):
        total = None
        for p in range(8):
            if line[p] != 0.0:
                term = stiffness[i, p] * line[p] if line[p] != 1.0 else stiffness[i, p]
                total = term if total is None else total + term
        return total

    applied = []
    for element in range(2):
        c = folded([metric(metrics, k, element, WIDE) for k in range(3)])
        for i in range(8):
            x = element * 8 + i
            parts = [GROUP_X[a][element * 8 : element * 8 + 8] for a in range(2)]
            stiff_x = [stiff_of(i, line) for line in parts]
            applied.append(spread(c, [GROUP_X[a][x] for a in range(2)], stiff_x, WEIGHTS[i], (0, 1)))
    other = folded([face_metric(far_a, far_b, k, even, False) for k in range(3)])
    applied[0] = applied[0] + spread(other, [1.0, 0.0], [stiff_of(7, HIGH), stiff_of(7, LOW)], WEIGHTS[7], (0, 2))
    other = folded([face_metric(far_a, far_b, k, even, True) for k in range(3)])
    applied[15] = applied[15] + spread(other, [1.0], [stiff_of(0, [1.0] * 8)], WEIGHTS[0], (1,))

    applied = join_middle(applied)
    first, second = got_a[...], got_b[...]
    keep = geo.keep[:, :, :LANES].reshape(ROWS, LANES)
    for x in range(ROWS):
        value = (geo.pair(applied[x]) * geo.keep).reshape(ROWS, WIDE)[:, :LANES] + image[x]
        if x == 0:
            value = value + jnp.where(even, second, first)
        if x == 15:
            value = value + jnp.where(even, first, second)
        new_residual[x] = residual[x] - alpha * value
        coarse_line = None
        for a in range(2):
            if GROUP_X[a][x] != 0.0:
                term = GROUP_X[a][x] * lines[a][:, :LANES]
                coarse_line = term if coarse_line is None else coarse_line + term
        new_solution[x] = start[x] + alpha * (local[x] + keep * coarse_line)


VMEM = pl.BlockSpec(memory_space=pltpu.VMEM)
SMEM = pl.BlockSpec(memory_space=pltpu.SMEM)


def call(kernel, shapes, specs, scratch, name):
    return pl.pallas_call(
        kernel,
        out_shape=[jax.ShapeDtypeStruct(shape, jnp.float32) for shape in shapes],
        in_specs=specs,
        out_specs=[VMEM] * len(shapes),
        scratch_shapes=[pltpu.VMEM(shape, jnp.float32) for shape in scratch],
        compiler_params=pltpu.CompilerParams(vmem_limit_bytes=16 * 1024 * 1024),
        name=name,
    )


def swap(first, second, axis):
    size = lax.axis_size(axis)
    odd = [(i, (i + 1) % size) for i in range(1, size, 2)]
    one = lax.ppermute(first, axis, [(i, i ^ 1) for i in range(size)])
    two = lax.ppermute(second, axis, odd + [(b, a) for a, b in odd])
    return one, two


def body(
    source, previous, coefficients, stiffness, fdm_vectors, fdm_values, coarse_inverse, vertex_map
):
    assert source.shape == (ROWS, ROWS, LANES)
    spans = lax.axis_size("gz")
    devices = lax.axis_size("gx") * spans
    per, count = coarse_inverse.shape
    block, wide = (ROWS, ROWS, LANES), (ROWS, ROWS, WIDE)
    halo = (9, ROWS, LANES)

    first, second, own_metrics = call(
        pack_kernel, [halo, halo, (16, LANES)], [VMEM] * 3, [(16, 16)], "pack"
    )(source, previous, coefficients)
    first, second = swap(first, second, "gz")
    blocks, diagonals = call(
        prepare_kernel, [(3, LANES, LANES), (3, 8, 8, LANES)], [VMEM] * 2, [], "prepare"
    )(stiffness, fdm_vectors)

    message = (40, WIDE)
    start, rest, metrics, own_a, own_b = call(
        start_kernel,
        [block, wide, (16, WIDE), message, message],
        [VMEM] * 5 + [SMEM, VMEM, VMEM],
        [wide],
        "start",
    )(source, previous, own_metrics, first, second, stiffness, blocks, diagonals)
    far_a, far_b = swap(own_a, own_b, "gx")

    start, residual, local, face_a, face_b, sums = call(
        solve_kernel,
        [block, block, wide, (ROWS, WIDE), (ROWS, WIDE), (8, LANES)],
        [VMEM] * 7 + [SMEM] * 3 + [VMEM] * 2,
        [wide],
        "solve",
    )(
        start, rest, metrics, own_a, own_b, far_a, far_b,
        stiffness, fdm_vectors, fdm_values, blocks, diagonals,
    )
    face_a, face_b = swap(face_a, face_b, "gx")

    small = per * count <= LANES
    kernel = image_kernel
    operands = [local, metrics, face_a, face_b, stiffness, vertex_map, coarse_inverse, sums, blocks, diagonals]
    specs = [VMEM] * 4 + [SMEM, SMEM] + [VMEM] * 4
    if not small:
        del operands[6], specs[6]

        def kernel(*refs):
            image_kernel(*refs[:6], None, *refs[6:])

    local, image, side_a, side_b, payload = call(
        kernel,
        [block, block, (ROWS, LANES), (ROWS, LANES), (2 * devices, LANES)],
        specs,
        [wide],
        "image",
    )(*operands)
    side_a, side_b = swap(side_a, side_b, "gx")
    gathered = lax.all_to_all(payload.reshape(devices, 2, LANES), ("gx", "gz"), 0, 0)
    gathered = gathered.reshape(2 * devices, LANES)

    tables = jnp.asarray(lane_tables())
    operands = [
        start, residual, local, image, side_a, side_b, far_a, far_b, metrics, stiffness, blocks, diagonals,
        tables, gathered,
    ]
    specs = [VMEM] * 9 + [SMEM] + [VMEM] * 4
    finish = functools.partial(final_kernel, devices, spans, count, per)
    if small:

        def kernel(*refs):
            finish(*refs[:14], None, *refs[14:])

    else:
        kernel = finish
        rows = gathered[0::2]
        keys = [8 * k + 4 for k in range(6)]
        labels = rows[:, jnp.array(keys)].astype(jnp.int32)
        parts = rows[:, jnp.array([8 * (k // 3) + k % 3 for k in range(6)])]
        rhs = jnp.zeros((count,), jnp.float32).at[labels.reshape(-1)].add(parts.reshape(-1))
        own = jnp.dot(coarse_inverse, rhs, precision=EXACT)
        coarse = lax.all_gather(own, ("gx", "gz"), axis=0, tiled=True)
        operands.append(jnp.pad(coarse[labels], ((0, 0), (0, LANES - 6))))
        specs.append(VMEM)
    return tuple(call(kernel, [block, block], specs, [(devices, LANES)], "finish")(*operands))


def solution(mesh):
    placed = (
        P("gx", None, "gz"),
        P("gx", None, "gz"),
        P(None, "gx", None, "gz"),
        P(),
        P(),
        P(),
        P(("gx", "gz"), None),
        P(None, "gx", None, "gz"),
    )
    return jax.shard_map(
        body,
        mesh=mesh,
        in_specs=placed,
        out_specs=(P("gx", None, "gz"), P("gx", None, "gz")),
        check_vma=False,
    )
```

```python
import functools

import jax
import jax.numpy as jnp
import numpy as np
from jax import lax
from jax.experimental import pallas as pl
from jax.experimental.pallas import tpu as pltpu
from jax.sharding import PartitionSpec as P

POINTS = [
    -1.0,
    -0.8717401485096066,
    -0.5917001814331423,
    -0.2092992179024789,
    0.2092992179024789,
    0.5917001814331423,
    0.8717401485096066,
    1.0,
]
WEIGHTS = [
    0.03571428571428571,
    0.21070422714350603,
    0.34112269248350435,
    0.4124587946587038,
    0.4124587946587038,
    0.34112269248350435,
    0.21070422714350603,
    0.03571428571428571,
]
ONES = [1.0] * 8
LOW = [(1.0 - s) / 2.0 for s in POINTS]
HIGH = [(1.0 + s) / 2.0 for s in POINTS]
EXACT = lax.Precision.HIGHEST

ROWS = 16
LANES = 128
WIDE = 256
HALO = 32
PAIRS = ((0, 0), (0, 1), (1, 1))
GROUP_X = (ONES + LOW, [0.0] * 8 + HIGH)
INVERSE_X = [0.5] + [1.0] * 6 + [0.5] + [0.5] + [1.0] * 6 + [0.5]


def iota(shape, dim):
    return lax.broadcasted_iota(jnp.int32, shape, dim)


def pick(index, values):
    result = jnp.full(index.shape, values[0], jnp.float32)
    for i in range(1, 8):
        result = jnp.where(index == i, values[i], result)
    return result


def even_index(axis):
    return lax.rem(lax.axis_index(axis), 2) == 0


class Geometry:
    def __init__(self, lanes):
        shape = (2, 8, lanes)
        self.element_y, self.row, lane = iota(shape, 0), iota(shape, 1), iota(shape, 2)
        self.position = lane & 7
        self.first = self.position == 0
        self.last = self.position == 7
        self.edge = self.first | self.last
        self.weight_y = pick(self.row, WEIGHTS)
        self.weight_z = pick(self.position, WEIGHTS)
        self.inverse_z = jnp.where(self.edge, 0.5, 1.0)
        self.wall = (self.element_y == 1) & (self.row == 7)
        inner = ((self.element_y == 0) & (self.row == 7)) | ((self.element_y == 1) & (self.row == 0))
        self.inverse_y = jnp.where(inner, 0.5, 1.0)
        self.keep = jnp.where(self.wall, 0.0, 1.0)
        self.lanes = lanes

    def pair_y(self, v):
        lower, upper = v[0], v[1]
        row = self.row[0]
        up = jnp.where(row == 7, pltpu.roll(upper, 7, 0), 0.0)
        down = jnp.where(row == 0, pltpu.roll(lower, 1, 0), 0.0)
        return jnp.stack([lower + up, upper + down])

    def pair_z(self, v):
        flat = v.reshape(16, self.lanes)
        after = pltpu.roll(flat, self.lanes - 1, 1).reshape(v.shape)
        before = pltpu.roll(flat, 1, 1).reshape(v.shape)
        return v + jnp.where(self.edge, jnp.where(self.last, after, before), 0.0)

    def pair(self, v):
        return self.pair_z(self.pair_y(v))

    def assemble(self, v):
        return self.pair(v) * self.keep


def solid(v):
    return v.reshape(ROWS, v.shape[-1])


def split(v):
    return v.reshape(2, 8, v.shape[-1])


def own(v):
    return v[..., :LANES]


def down(v):
    return jnp.sum(v.reshape(ROWS, LANES), axis=0, keepdims=True)


def line_of(ref, at, lanes):
    row = ref[at : at + 1, :]
    return jnp.concatenate([row] * (lanes // LANES), axis=1)[None]


def contract_x(rows, table, i, transpose=False):
    total = None
    for p in range(8):
        factor = line_of(table, p * 8 + i if transpose else i * 8 + p, WIDE)
        term = factor * rows[p]
        total = term if total is None else total + term
    return total


def contract_y(v, diagonals):
    total = diagonals[0] * v
    for d in range(1, 8):
        rolled = jnp.stack([pltpu.roll(v[e], 8 - d, 0) for e in range(2)])
        total = total + diagonals[d] * rolled
    return total


def thirds(v):
    high = v.astype(jnp.bfloat16)
    rest = v - high.astype(jnp.float32)
    middle = rest.astype(jnp.bfloat16)
    return high, middle, (rest - middle.astype(jnp.float32)).astype(jnp.bfloat16)


def contract_z(flat, upper, lower, which):
    pieces = []
    for at in range(0, flat.shape[1], LANES):
        high, middle, low = thirds(flat[:, at : at + LANES])
        one = jnp.dot(
            jnp.concatenate([high, middle], axis=1), upper[which], preferred_element_type=jnp.float32
        )
        two = jnp.dot(jnp.concatenate([low, high], axis=1), lower[which], preferred_element_type=jnp.float32)
        pieces.append(one[:, :LANES] + (one[:, LANES:] + two))
    return pieces[0] if len(pieces) == 1 else jnp.concatenate(pieces, axis=1)


def wide_diagonals(ref, which):
    return [jnp.concatenate([ref[which, d]] * (WIDE // LANES), axis=1)[None] for d in range(8)]


def metric(ref, component, element):
    at = (component * 2 + element) * 2
    return jnp.stack([jnp.broadcast_to(ref[at + e : at + e + 1, :], (8, WIDE)) for e in range(2)])


def scaled_metrics(geo, c):
    return c[0] * geo.weight_y * geo.weight_z, c[1] * geo.weight_z, c[2] * geo.weight_y


def stored_factors(ref, element):
    return [split(ref[c, element]) for c in range(3)]


def apply_rows(rows, along_z, factors, stiffness, diagonals):
    result = []
    for element in range(2):
        factor_x, factor_y, factor_z = factors[element]
        inside = rows[element * 8 : element * 8 + 8]
        for i in range(8):
            x = element * 8 + i
            term_y = factor_y * contract_y(inside[i], diagonals)
            term_z = factor_z * split(along_z[x * 16 : x * 16 + 16])
            result.append(factor_x * contract_x(inside, stiffness, i) + WEIGHTS[i] * (term_y + term_z))
    return result


def join_middle(rows):
    middle = rows[7] + rows[8]
    return rows[:7] + [middle, middle] + rows[9:]


def group_lanes(lanes, group):
    lane = iota((1, lanes), 1)
    signed = jnp.where(lane < lanes // 2 + lanes // 4, lane, lane - lanes) if lanes > LANES else lane
    element, position = signed >> 3, lane & 7
    low, high = pick(position, LOW), pick(position, HIGH)
    here = jnp.where((element >> 3) == group, low, 0.0)
    return here + jnp.where(((element + 1) >> 3) == group, high, 0.0)


def pack_kernel(source, previous, coefficients, first, second, metrics, near_source, near_previous, raw, scratch, ready):
    copies = [
        pltpu.make_async_copy(source, near_source, ready.at[0]),
        pltpu.make_async_copy(previous, near_previous, ready.at[1]),
        pltpu.make_async_copy(coefficients, raw, ready.at[2]),
    ]
    for copy in copies:
        copy.start()
    even = even_index("gz")
    scratch[...] = jnp.zeros_like(scratch)
    widen = (iota((16, LANES), 0) == (iota((16, LANES), 1) >> 3)).astype(jnp.float32)
    for copy in copies:
        copy.wait()
    for c in range(3):
        for element in range(2):
            at = (c * 2 + element) * 2
            scratch[at : at + 2, :] = raw[c, element]
    spread = jnp.dot(scratch[...], widen, precision=EXACT, preferred_element_type=jnp.float32)
    metrics[...] = spread
    group = iota((8 * ROWS, LANES), 1) // HALO
    parts = [
        ref[lo : lo + 8].reshape(8 * ROWS, LANES) for ref in (near_previous, near_source) for lo in (0, 8)
    ]
    for to_right, out in ((even, first), (jnp.logical_not(even), second)):
        base = jnp.where(to_right, HALO, 0)
        packed = None
        for k, part in enumerate(parts):
            moved = pltpu.roll(part, lax.rem(base + HALO * k, LANES), 1)
            packed = moved if packed is None else jnp.where(group == k, moved, packed)
        out[0:8] = packed.reshape(8, ROWS, LANES)
        out[8] = spread


def prepare_kernel(
    with_coarse, metrics, stiffness, vectors, eigen, labels, coarse, tables,
    upper, lower, diagonals, stiff_table, vector_table, lam, lines, fixed, near_tables,
):
    near_tables[...] = tables[...]
    repeat = (iota((LANES, 8), 0) & 7 == iota((LANES, 8), 1)).astype(jnp.float32)
    same = (iota((LANES, LANES), 0) >> 3) == (iota((LANES, LANES), 1) >> 3)
    unit = (iota((8, 8), 0) == iota((8, 8), 1)).astype(jnp.float32)
    row, column = iota((8, 8), 0), iota((8, 8), 1)

    def dot(a, b, dims):
        return lax.dot_general(a, b, (dims, ((), ())), precision=EXACT, preferred_element_type=jnp.float32)

    def put_block(at, matrix):
        half = dot(repeat, matrix, ((1,), (0,)))
        block = jnp.where(same, dot(half, repeat, ((1,), (1,))), 0.0)
        high, middle, low = thirds(block)
        both = jnp.concatenate([high, middle], axis=1)
        upper[at] = jnp.concatenate([both, both], axis=0)
        lower[at] = jnp.concatenate([high, low], axis=0)

    def put_diagonals(at, matrix):
        for d in range(8):
            chosen = jnp.where(column == ((row + d) & 7), matrix, 0.0)
            diagonals[at, d] = jnp.broadcast_to(jnp.sum(chosen, axis=1, keepdims=True), (8, LANES))

    def put_table(out, matrix):
        tall = (iota((64, 8), 0) >> 3 == iota((64, 8), 1)).astype(jnp.float32)
        chosen = jnp.where(iota((64, 8), 0) & 7 == iota((64, 8), 1), dot(tall, matrix, ((1,), (0,))), 0.0)
        out[...] = jnp.broadcast_to(jnp.sum(chosen, axis=1, keepdims=True), (64, LANES))

    k, s = stiffness[...], vectors[...]
    k_turned, s_turned = dot(k, unit, ((0,), (0,))), dot(s, unit, ((0,), (0,)))
    for at, matrix in enumerate((k_turned, s, s_turned)):
        put_block(at, matrix)
    for at, matrix in enumerate((k, s_turned, s)):
        put_diagonals(at, matrix)
    put_table(stiff_table, k)
    put_table(vector_table, s)
    values = [eigen[i] for i in range(8)]
    lam[0] = pick(iota((8, LANES), 0), values)
    lam[1] = pick(iota((8, LANES), 1) & 7, values)
    stiff_lines = []
    for at, line in enumerate((ONES, LOW, HIGH)):
        total = jnp.sum(k * pick(column, line), axis=1, keepdims=True)
        stiff_lines.append(jnp.broadcast_to(total, (8, LANES)))
        lines[at] = stiff_lines[at]

    groups = [group_lanes(LANES, b) for b in range(3)]
    stacked = jnp.concatenate(groups + [jnp.zeros((13, LANES), jnp.float32)], axis=0)
    stiff_z = contract_z(stacked, upper, lower, 0)
    weight_z = pick(iota((1, LANES), 1) & 7, WEIGHTS)
    node = iota((8, LANES), 0)
    mass_y = [sum(WEIGHTS), sum(WEIGHTS[:7])]
    last = jnp.broadcast_to(k[:, 7:8], (8, LANES))
    inner = jnp.where(node == 7, 0.0, stiff_lines[0] - last)
    stiff_y = [jnp.sum(v, axis=0, keepdims=True) for v in (stiff_lines[0], inner)]
    at = 0
    for a, b in PAIRS:
        across, along = jnp.zeros((1, LANES), jnp.float32), jnp.zeros((1, LANES), jnp.float32)
        for element in range(2):
            fa = GROUP_X[a][element * 8 : element * 8 + 8]
            fb = GROUP_X[b][element * 8 : element * 8 + 8]
            if not (any(fa) and any(fb)):
                continue
            mass_x = sum(w * p * q for w, p, q in zip(WEIGHTS, fa, fb))
            applied = stiff_lines[0 if fb == ONES else 1 + b]
            stiff_x = jnp.sum(applied * pick(node, fa), axis=0, keepdims=True)
            for e in range(2):
                cx, cy, cz = (metrics[(c * 2 + element) * 2 + e, :].reshape(1, LANES) for c in range(3))
                across = across + cx * (stiff_x * mass_y[e]) + cy * (stiff_y[e] * mass_x)
                along = along + cz * (mass_x * mass_y[e])
        across = across * weight_z
        for b in range(3):
            fixed[at : at + 1] = across * groups[b] + along * stiff_z[b : b + 1]
            at += 1
    fixed[9:16] = jnp.zeros((7, LANES), jnp.float32)
    place = iota((1, LANES), 1)
    numbers = jnp.zeros((1, LANES), jnp.float32)
    for a in range(2):
        for b in range(3):
            corner, x, z = 4 * a + (b == 2), a, (0, 8, 15)[b]
            number = labels[corner, x, 0, z].astype(jnp.float32)
            numbers = jnp.where(place == 8 * (3 * a + b) + 4, number, numbers)
    fixed[16:17] = numbers
    below = jnp.zeros((1, LANES), jnp.float32)
    if with_coarse:
        per, count = coarse.shape
        below = [coarse[i : i + 1, :] for i in range(per)]
        if per * count < LANES:
            below.append(jnp.zeros((1, LANES - per * count), jnp.float32))
        below = jnp.concatenate(below, axis=1)
    fixed[17:18] = below
    fixed[18:24] = jnp.zeros((6, LANES), jnp.float32)


def start_kernel(
    source, previous, own_metrics, first, second, stiffness, upper, lower, diagonals,
    start, rest, metrics, factors, message_a, message_b,
):
    even = even_index("gz")
    lane = iota((ROWS, LANES), 1)

    def beyond(plane, right_shift, left_shift, fill):
        a, b = first[plane], second[plane]
        right, left = jnp.where(even, a, b), jnp.where(even, b, a)
        if right_shift:
            right = pltpu.roll(right, right_shift, 1)
        if left_shift:
            left = pltpu.roll(left, left_shift, 1)
        return jnp.where(lane < HALO, right, jnp.where(lane >= LANES - HALO, left, fill))

    def wide(ref, x, kind):
        slot = 2 * kind + x // 8
        right_shift = (LANES - HALO * slot) % LANES
        left_shift = (LANES - HALO - HALO * slot) % LANES
        return split(jnp.concatenate([ref[x], beyond(x % 8, right_shift, left_shift, 0.0)], axis=1))

    geo = Geometry(WIDE)
    metrics[:, :LANES] = own_metrics[...]
    metrics[:, LANES:] = beyond(8, 0, 0, 1.0)
    factor = geo.keep * geo.inverse_y * geo.inverse_z
    rows = [geo.pair(wide(previous, x, 0)) * (factor * INVERSE_X[x]) for x in range(ROWS)]
    rows = join_middle(rows)
    faces = (rows[0], rows[15])
    rows[0] = rows[15] = jnp.zeros_like(rows[0])
    for x in range(ROWS):
        start[x] = solid(own(rows[x]))
    along_z = contract_z(jnp.concatenate([solid(v) for v in rows], axis=0), upper, lower, 0)
    scaled = [scaled_metrics(geo, [metric(metrics, c, e) for c in range(3)]) for e in range(2)]
    for e in range(2):
        for c in range(3):
            factors[c, e] = solid(scaled[e][c])
    applied = apply_rows(rows, along_z, scaled, stiffness, wide_diagonals(diagonals, 0))
    for x in range(ROWS):
        rest[x] = solid(wide(source, x, 1) - applied[x])
    even_x = even_index("gx")

    def choose(right, left):
        return jnp.where(even_x, right, left), jnp.where(even_x, left, right)

    for at, right, left in ((0, solid(faces[1]), solid(faces[0])), (16, rest[15], rest[0])):
        message_a[at : at + 16], message_b[at : at + 16] = choose(right, left)
    for c in range(3):
        at = 32 + 2 * c
        right, left = metrics[(c * 2 + 1) * 2 : (c * 2 + 1) * 2 + 2], metrics[c * 4 : c * 4 + 2]
        message_a[at : at + 2], message_b[at : at + 2] = choose(right, left)
    message_a[38:40] = jnp.zeros((2, WIDE), jnp.float32)
    message_b[38:40] = jnp.zeros((2, WIDE), jnp.float32)


def sided(even, a, b, at, size=16):
    one, two = a[at : at + size], b[at : at + size]
    return jnp.where(even, one, two), jnp.where(even, two, one)


def face_metrics(even, a, b):
    sides = [[], []]
    for c in range(3):
        for side, pair in enumerate(sided(even, a, b, 32 + 2 * c, 2)):
            sides[side].append(jnp.stack([jnp.broadcast_to(pair[e : e + 1], (8, WIDE)) for e in range(2)]))
    return sides


def coarse_pieces(geo, factors, stiff_keep, functions, stiff_functions):
    factor_x, factor_y, factor_z = factors
    kept_x, kept_y, kept_z = factor_x * geo.keep, factor_y * stiff_keep, factor_z * geo.keep
    result = []
    for plain, turned in zip(functions, stiff_functions):
        result.append(
            (geo.assemble(kept_x * plain[None]), geo.assemble(kept_y * plain[None] + kept_z * turned[None]))
        )
    return result


def wide_functions(upper, lower):
    functions = [group_lanes(WIDE, b) for b in (-1, 0, 1, 2)]
    stacked = jnp.concatenate(functions + [jnp.zeros((12, WIDE), jnp.float32)], axis=0)
    turned = contract_z(stacked, upper, lower, 0)
    return functions, [turned[b : b + 1] for b in range(4)]


def kept_stiffness(geo, lines, stiffness):
    row = iota((8, LANES), 0)
    last = jnp.zeros((8, LANES), jnp.float32)
    for j in range(8):
        last = jnp.where(row == j, stiffness[j * 8 + 7 : j * 8 + 8, :], last)
    both = jnp.stack([lines[0], lines[0] - last])
    return jnp.concatenate([both] * (WIDE // LANES), axis=2)


def ready_kernel(rest, metrics, factors, lam, stiffness, lines, upper, lower, known, inverse, pieces):
    geo = Geometry(WIDE)
    rows = join_middle([split(rest[x]) for x in range(ROWS)])
    for x in range(1, ROWS - 1):
        known[x] = solid(geo.assemble(rows[x]))
    known[0] = known[15] = jnp.zeros((ROWS, WIDE), jnp.float32)
    lam_y = jnp.concatenate([lam[0]] * (WIDE // LANES), axis=1)[None]
    lam_z = jnp.concatenate([lam[1]] * (WIDE // LANES), axis=1)[None]
    for element in range(2):
        cx, cy, cz = (metric(metrics, c, element) for c in range(3))
        base = cy * lam_y + cz * lam_z
        for i in range(8):
            inverse[element * 8 + i] = solid(1.0 / (cx * line_of(lam.at[0], i, WIDE) + base))
    functions, turned = wide_functions(upper, lower)
    stiff_keep = kept_stiffness(geo, lines, stiffness)
    for element in range(2):
        made = coarse_pieces(geo, stored_factors(factors, element), stiff_keep, functions, turned)
        for b in range(4):
            for k in range(2):
                pieces[element, k, b] = solid(own(made[b][k]))


def solve_kernel(
    rest, known, factors, inverse, own_a, own_b, got_a, got_b,
    stiffness, vectors, upper, lower, diagonals,
    start_faces, residual, local, message_a, message_b, sums,
):
    even = even_index("gx")
    geo = Geometry(WIDE)
    mine, theirs = sided(even, own_a, own_b, 0), sided(even, got_a, got_b, 0)
    right, left = split(mine[0] + theirs[0]), split(mine[1] + theirs[1])
    start_faces[0], start_faces[1] = solid(own(left)), solid(own(right))
    other_right, other_left = (split(v) for v in sided(even, got_a, got_b, 16))
    metrics_right, metrics_left = face_metrics(even, got_a, got_b)
    stiff = wide_diagonals(diagonals, 0)
    along_z = contract_z(jnp.concatenate([solid(left), solid(right)], axis=0), upper, lower, 0)
    rows = [split(known[x]) for x in range(ROWS)]
    for element, near, face, across, arrived, other, turned in (
        (0, 0, left, 7, other_left, metrics_left, along_z[:16]),
        (1, 7, right, 0, other_right, metrics_right, along_z[16:]),
    ):
        mine = stored_factors(factors, element)
        theirs = scaled_metrics(geo, other)
        scaled = mine[0] * face
        beside = line_of(stiffness, near * 9, WIDE) * scaled
        beside = beside + line_of(stiffness, across * 9, WIDE) * (theirs[0] * face)
        beside = beside + WEIGHTS[0] * (
            (mine[1] + theirs[1]) * contract_y(face, stiff) + (mine[2] + theirs[2]) * split(turned)
        )
        x = element * 8 + near
        rows[x] = geo.assemble(split(rest[x]) + arrived - beside)
        moved = geo.assemble(scaled)
        for i in range(8):
            if i != near:
                change = line_of(stiffness, i * 8 + near, WIDE) * moved
                x = element * 8 + i
                rows[x] = rows[x] - change
                if x in (7, 8):
                    rows[15 - x] = rows[15 - x] - change
    parts = [None, None]
    for x in range(ROWS):
        residual[x] = solid(own(rows[x]))
        for a in range(2):
            if GROUP_X[a][x] * INVERSE_X[x] != 0.0:
                term = (GROUP_X[a][x] * INVERSE_X[x]) * own(rows[x])
                parts[a] = term if parts[a] is None else parts[a] + term
    weight = own(geo.inverse_y * geo.inverse_z)
    for a in range(2):
        sums[a : a + 1] = down(parts[a] * weight)

    forward, backward = wide_diagonals(diagonals, 1), wide_diagonals(diagonals, 2)
    moved = []
    for element in range(2):
        inside = rows[element * 8 : element * 8 + 8]
        moved += [solid(contract_y(contract_x(inside, vectors, i, True), forward)) for i in range(8)]
    spectral = contract_z(jnp.concatenate(moved, axis=0), upper, lower, 1)
    divided = [spectral[x * 16 : x * 16 + 16] * inverse[x] for x in range(ROWS)]
    back = contract_z(jnp.concatenate(divided, axis=0), upper, lower, 2)
    solved = []
    for element in range(2):
        inside = [
            contract_y(split(back[x * 16 : x * 16 + 16]), backward) for x in range(element * 8, element * 8 + 8)
        ]
        solved += [contract_x(inside, vectors, i) for i in range(8)]
    total = None
    for x in range(ROWS):
        term = own(solved[x]) * own(rows[x])
        total = term if total is None else total + term
    sums[2:3] = down(total)
    sums[3:8] = jnp.zeros((5, LANES), jnp.float32)
    solved = [geo.assemble(v) for v in join_middle(solved)]
    for x in range(ROWS):
        local[x] = solid(solved[x])
    beside = []
    for element, near in ((0, 0), (1, 7)):
        total = None
        for p in range(8):
            if p != near:
                term = line_of(stiffness, near * 8 + p, WIDE) * solved[element * 8 + p]
                total = term if total is None else total + term
        beside.append(solid(total))
    for at, left_row, right_row in ((0, solid(solved[0]), solid(solved[15])), (16, beside[0], beside[1])):
        message_a[at : at + 16] = jnp.where(even, right_row, left_row)
        message_b[at : at + 16] = jnp.where(even, left_row, right_row)


def ahead_kernel(
    local, factors, far_a, far_b, stiffness, lines, upper, lower, diagonals,
    image, sums, face_factors, face_pieces,
):
    even = even_index("gx")
    geo = Geometry(WIDE)
    rows = [split(local[x]) for x in range(ROWS)]
    rows[0] = rows[15] = jnp.zeros_like(rows[0])
    along_z = contract_z(jnp.concatenate([solid(v) for v in rows], axis=0), upper, lower, 0)
    scaled = [stored_factors(factors, e) for e in range(2)]
    applied = apply_rows(rows, along_z, scaled, stiffness, wide_diagonals(diagonals, 0))
    total, parts = None, [None, None]
    for x in range(1, ROWS - 1):
        term = own(applied[x]) * own(rows[x])
        total = term if total is None else total + term
        for a in range(2):
            if GROUP_X[a][x] != 0.0:
                term = GROUP_X[a][x] * own(applied[x])
                parts[a] = term if parts[a] is None else parts[a] + term
    for at, value in enumerate(parts + [total]):
        sums[at : at + 1] = down(value * own(geo.keep))
    sums[3:8] = jnp.zeros((5, LANES), jnp.float32)
    joined = join_middle(applied)
    for x in range(1, ROWS - 1):
        image[x] = solid(own(geo.assemble(joined[x])))
    image[0] = image[15] = jnp.zeros((ROWS, LANES), jnp.float32)
    functions, turned = wide_functions(upper, lower)
    stiff_keep = kept_stiffness(geo, lines, stiffness)
    for side, raw in enumerate(face_metrics(even, far_a, far_b)):
        theirs = scaled_metrics(geo, raw)
        for c in range(3):
            face_factors[side, c] = solid(theirs[c])
        made = coarse_pieces(geo, theirs, stiff_keep, functions, turned)
        for b in range(4):
            for k in range(2):
                face_pieces[side, k, b] = solid(own(made[b][k]))


def image_kernel(
    known, factors, face_factors, own_a, own_b, got_a, got_b, first_sums, second_sums, fixed,
    stiffness, lines, upper, lower, diagonals,
    image, faces, payload,
):
    even = even_index("gx")
    geo = Geometry(WIDE)
    stiff = wide_diagonals(diagonals, 0)
    mine, theirs = sided(even, own_a, own_b, 0), sided(even, got_a, got_b, 0)
    mine_beside, theirs_beside = sided(even, own_a, own_b, 16), sided(even, got_a, got_b, 16)
    values = [mine[side] + theirs[side] for side in range(2)]
    along_z = contract_z(jnp.concatenate(values, axis=0), upper, lower, 0)
    extra = [second_sums[a : a + 1] for a in range(3)]
    rows = [known[x] for x in range(ROWS)]
    for side, element, near, across in ((0, 1, 7, 0), (1, 0, 0, 7)):
        value, arrived = split(values[side]), split(theirs[side])
        faces[1 - side] = solid(own(value))
        here, there = stored_factors(factors, element), [split(face_factors[side, c]) for c in range(3)]
        along_y, turned = contract_y(value, stiff), split(along_z[side * 16 : side * 16 + 16])
        beside = split(mine_beside[side])
        ours = here[0] * (beside + line_of(stiffness, near * 9, WIDE) * value)
        ours = ours + WEIGHTS[0] * (here[1] * along_y + here[2] * turned)
        other = there[0] * (split(theirs_beside[side]) + line_of(stiffness, across * 9, WIDE) * value)
        other = other + WEIGHTS[0] * (there[1] * along_y + there[2] * turned)
        rows[element * 8 + near] = solid(own(geo.assemble(ours + other)))
        spread = here[0] * value
        moved = solid(own(geo.assemble(spread)))
        for i in range(8):
            if i != near:
                change = stiffness[i * 8 + near : i * 8 + near + 1, :] * moved
                x = element * 8 + i
                rows[x] = rows[x] + change
                if x in (7, 8):
                    rows[15 - x] = rows[15 - x] + change
        near_only = own(spread * geo.keep)
        kept = own(ours * geo.keep)
        for a in range(2):
            line = GROUP_X[a][element * 8 : element * 8 + 8]
            if any(line):
                at = 0 if line == ONES else 1 + a
                factor = lines[at, near : near + 1, :]
                if line[near] != 0.0:
                    factor = factor - line[near] * stiffness[near * 9 : near * 9 + 1, :]
                    extra[a] = extra[a] + down(line[near] * kept)
                extra[a] = extra[a] + factor * down(near_only)
        extra[2] = extra[2] + down(own(beside) * near_only + own(value) * kept)
    for x in range(ROWS):
        image[x] = rows[x]
    zero = jnp.zeros((1, LANES), jnp.float32)
    table = jnp.concatenate(
        [first_sums[0:2], extra[0], extra[1], fixed[0:9], first_sums[2:3], extra[2], zero], axis=0
    )
    lane = iota((LANES, LANES), 1) & 7
    node = iota((LANES, LANES), 0)
    element, position = node >> 3, node & 7
    low, high = pick(position, LOW), pick(position, HIGH)
    columns = jnp.where(lane == (element >> 3), low, 0.0) + jnp.where(lane == ((element + 1) >> 3), high, 0.0)
    columns = jnp.where(lane == 3, 1.0, jnp.where(lane < 3, columns, 0.0))
    reduced = jnp.dot(table, columns, precision=EXACT, preferred_element_type=jnp.float32)
    mine = (iota((16, LANES), 1) >> 3) == iota((16, LANES), 0)
    row = jnp.sum(jnp.where(mine, reduced, 0.0), axis=0, keepdims=True) + fixed[16:17]
    block = jnp.concatenate([row, fixed[17:18]] * 4, axis=0)
    copies = payload.shape[0] // 8
    payload[...] = jnp.broadcast_to(block[None], (copies, 8, LANES)).reshape(copies * 8, LANES)


def lane_tables():
    one = np.zeros((8, LANES), np.float32)
    two = np.zeros((8, LANES), np.float32)
    top = np.zeros((8, LANES), np.float32)
    for a in range(2):
        for b in range(3):
            one[6, 8 * a + b], two[3 * a + b, 8 * a + b], top[0, 8 * a + b] = 1.0, 1.0, 1.0
            one[6, 8 * (2 + a) + b], two[3 * a + b, 8 * (2 + a) + b] = 2.0, 1.0
            top[1, 8 * (2 + a) + b] = 1.0
    for p, (a, other) in enumerate(PAIRS):
        for b in range(3):
            for c in range(3):
                at = 8 * (4 + 3 * p + b) + c
                one[3 * a + b, at] = 1.0 if a == other else 2.0
                two[3 * other + c, at] = 1.0
                top[1, at] = 1.0
    one[6, 8 * 13 + 3], two[6, 8 * 13 + 3], top[0, 8 * 13 + 3] = 1.0, 1.0, 1.0
    one[6, 8 * 14 + 3], two[6, 8 * 14 + 3], top[1, 8 * 14 + 3] = 1.0, 1.0, 1.0
    return np.stack([one, two, top])


def final_kernel(
    devices, spans, count, per,
    start, start_faces, residual, local, faces, image, pieces, face_pieces, lines, tables,
    gathered, given, new_solution, new_residual, values,
):
    rows = gathered[pl.ds(0, devices, stride=2), :]
    if given is None:
        spot = iota((devices, count), 1)
        hits = []
        rhs = [jnp.zeros((1, devices), jnp.float32) for _ in range(per)]
        owner = iota((devices, devices), 1)
        for k in range(6):
            label = rows[:, 8 * k + 4 : 8 * k + 5].astype(jnp.int32)
            at = 8 * (k // 3) + k % 3
            value = rows[:, at : at + 1]
            hits.append(spot == label)
            for q in range(per):
                chosen = jnp.where(owner * per + q == label, value, 0.0)
                rhs[q] = rhs[q] + jnp.sum(chosen, axis=0, keepdims=True)
        inverse = gathered[pl.ds(1, devices, stride=2), :]
        coarse = None
        for q in range(per):
            term = jnp.dot(
                rhs[q], inverse[:, q * count : q * count + count], precision=EXACT,
                preferred_element_type=jnp.float32,
            )
            coarse = term if coarse is None else coarse + term
        columns = [jnp.sum(jnp.where(hit, coarse, 0.0), axis=1, keepdims=True) for hit in hits]
        kept = jnp.zeros((devices, LANES), jnp.float32)
        for k in range(6):
            kept = jnp.where(iota((devices, LANES), 1) == k, columns[k], kept)
        values[...] = kept
    else:
        columns = [given[:, k : k + 1] for k in range(6)]
        values[...] = given[...]
    one, two = tables[0, 6:7, :], tables[1, 6:7, :]
    for k in range(6):
        one = one + columns[k] * tables[0, k : k + 1, :]
        two = two + columns[k] * tables[1, k : k + 1, :]
    product = jnp.sum(rows * one * two, axis=0, keepdims=True)
    numerator = jnp.sum(product * tables[2, 0:1, :], axis=1, keepdims=True)
    denominator = jnp.sum(product * tables[2, 1:2, :], axis=1, keepdims=True)
    alpha = numerator / denominator

    gx, gz = lax.axis_index("gx"), lax.axis_index("gz")
    before_x = lax.rem(gx + devices // spans - 1, devices // spans)
    before_z = lax.rem(gz + spans - 1, spans)
    here = values[pl.ds(gx * spans + gz, 1), :]
    behind = values[pl.ds(gx * spans + before_z, 1), :]
    aside = values[pl.ds(before_x * spans + gz, 1), :]
    corner = values[pl.ds(before_x * spans + before_z, 1), :]
    functions = [group_lanes(LANES, b) for b in range(3)]

    def four(line, back, a):
        return [back[:, 3 * a + 1 : 3 * a + 2]] + [line[:, 3 * a + b : 3 * a + b + 1] for b in range(3)]

    def mix(numbers, ref):
        total = numbers[0] * ref[0]
        for b in range(1, 4):
            total = total + numbers[b] * ref[b]
        return total

    near, right, left = four(here, behind, 0), four(here, behind, 1), four(aside, corner, 0)
    line_near = sum(near[1 + b] * functions[b] for b in range(3))
    line_right = sum(right[1 + b] * functions[b] for b in range(3))
    whole = [mix(near, pieces.at[0, k]) for k in range(2)]
    low = [mix(near, pieces.at[1, k]) for k in range(2)]
    high = [mix(right, pieces.at[1, k]) for k in range(2)]

    def stiff(line, i):
        return lines[line, i : i + 1, :]

    extra = [stiff(0, i) * whole[0] + WEIGHTS[i] * whole[1] for i in range(8)]
    for i in range(8):
        extra.append(
            stiff(1, i) * low[0] + stiff(2, i) * high[0] + WEIGHTS[i] * (LOW[i] * low[1] + HIGH[i] * high[1])
        )
    extra = join_middle(extra)
    beyond_x, beyond_w = face_pieces.at[1, 0], face_pieces.at[1, 1]
    extra[0] = extra[0] + (
        stiff(1, 7) * mix(left, beyond_x) + stiff(2, 7) * mix(near, beyond_x) + WEIGHTS[7] * mix(near, beyond_w)
    )
    extra[15] = extra[15] + stiff(0, 0) * mix(right, face_pieces.at[0, 0]) + WEIGHTS[0] * mix(right, face_pieces.at[0, 1])
    keep = solid(Geometry(LANES).keep)
    for x in range(ROWS):
        begin = start_faces[x // 15] if x in (0, 15) else start[x]
        mine = faces[x // 15] if x in (0, 15) else local[x, :, :LANES]
        new_residual[x] = residual[x] - alpha * (image[x] + extra[x])
        coarse_line = GROUP_X[0][x] * line_near
        if GROUP_X[1][x] != 0.0:
            coarse_line = coarse_line + GROUP_X[1][x] * line_right
        new_solution[x] = begin + alpha * (mine + keep * coarse_line)


VMEM = pl.BlockSpec(memory_space=pltpu.VMEM)
SMEM = pl.BlockSpec(memory_space=pltpu.SMEM)
FAR = pl.BlockSpec(memory_space=pltpu.HBM)


def call(kernel, shapes, specs, name, scratch=()):
    def leaf(shape):
        kind = jnp.float32
        if shape[0] == "half":
            shape, kind = shape[1:], jnp.bfloat16
        return jax.ShapeDtypeStruct(shape, kind)

    return pl.pallas_call(
        kernel,
        out_shape=[leaf(shape) for shape in shapes],
        in_specs=specs,
        out_specs=[VMEM] * len(shapes),
        scratch_shapes=list(scratch),
        compiler_params=pltpu.CompilerParams(vmem_limit_bytes=16 * 1024 * 1024),
        name=name,
    )


def swap(first, second, axis):
    size = lax.axis_size(axis)
    odd = [(i, (i + 1) % size) for i in range(1, size, 2)]
    one = lax.ppermute(first, axis, [(i, i ^ 1) for i in range(size)])
    two = lax.ppermute(second, axis, odd + [(b, a) for a, b in odd])
    return one, two


def body(
    source, previous, coefficients, stiffness, fdm_vectors, fdm_values, coarse_inverse, vertex_map
):
    assert source.shape == (ROWS, ROWS, LANES)
    spans = lax.axis_size("gz")
    devices = lax.axis_size("gx") * spans
    per, count = coarse_inverse.shape
    small = per * count <= LANES
    block, wide, face = (ROWS, ROWS, LANES), (ROWS, ROWS, WIDE), (ROWS, LANES)
    halo = (9, ROWS, LANES)

    first, second, own_metrics, source, previous = call(
        pack_kernel,
        [halo, halo, face, block, block],
        [FAR] * 3,
        "pack",
        [pltpu.VMEM(coefficients.shape, jnp.float32), pltpu.VMEM((16, 16), jnp.float32), pltpu.SemaphoreType.DMA((3,))],
    )(*(pltpu.with_memory_space_constraint(v, pltpu.HBM) for v in (source, previous, coefficients)))
    first, second = swap(first, second, "gz")
    upper, lower, diagonals, stiff, vectors, lam, lines, fixed, tables = call(
        functools.partial(prepare_kernel, small),
        [
            ("half", 3, WIDE, WIDE), ("half", 3, WIDE, LANES), (3, 8, 8, LANES),
            (64, LANES), (64, LANES), (2, 8, LANES), (3, 8, LANES), (24, LANES), (3, 8, LANES),
        ],
        [VMEM] * 3 + [SMEM] * 2 + [VMEM if small else FAR, VMEM],
        "prepare",
    )(own_metrics, stiffness, fdm_vectors, fdm_values, vertex_map, coarse_inverse, jnp.asarray(lane_tables()))

    message = (40, WIDE)
    start, rest, metrics, factors, own_a, own_b = call(
        start_kernel,
        [block, wide, (16, WIDE), (3, 2, ROWS, WIDE), message, message],
        [VMEM] * 9,
        "start",
    )(source, previous, own_metrics, first, second, stiff, upper, lower, diagonals)
    far_a, far_b = swap(own_a, own_b, "gx")
    known, inverse, pieces = call(
        ready_kernel, [wide, wide, (2, 2, 4, ROWS, LANES)], [VMEM] * 8, "ready"
    )(rest, metrics, factors, lam, stiff, lines, upper, lower)

    message = (32, WIDE)
    start_faces, residual, local, side_a, side_b, sums = call(
        solve_kernel,
        [(2, ROWS, LANES), block, wide, message, message, (8, LANES)],
        [VMEM] * 13,
        "solve",
    )(rest, known, factors, inverse, own_a, own_b, far_a, far_b, stiff, vectors, upper, lower, diagonals)
    got_a, got_b = swap(side_a, side_b, "gx")
    image, more_sums, face_factors, face_pieces = call(
        ahead_kernel,
        [block, (8, LANES), (2, 3, ROWS, WIDE), (2, 2, 4, ROWS, LANES)],
        [VMEM] * 9,
        "ahead",
    )(local, factors, far_a, far_b, stiff, lines, upper, lower, diagonals)

    image, faces, payload = call(
        image_kernel, [block, (2, ROWS, LANES), (2 * devices, LANES)], [VMEM] * 15, "image"
    )(
        image, factors, face_factors, side_a, side_b, got_a, got_b, sums, more_sums, fixed,
        stiff, lines, upper, lower, diagonals,
    )
    gathered = lax.all_to_all(payload.reshape(devices, 2, LANES), ("gx", "gz"), 0, 0)
    gathered = gathered.reshape(2 * devices, LANES)

    operands = [
        start, start_faces, residual, local, faces, image, pieces, face_pieces, lines,
        tables, gathered,
    ]
    finish = functools.partial(final_kernel, devices, spans, count, per)
    if small:

        def kernel(*refs):
            finish(*refs[:11], None, *refs[11:])

    else:
        kernel = finish
        rows = gathered[0::2]
        labels = rows[:, jnp.array([8 * k + 4 for k in range(6)])].astype(jnp.int32)
        parts = rows[:, jnp.array([8 * (k // 3) + k % 3 for k in range(6)])]
        rhs = jnp.zeros((count,), jnp.float32).at[labels.reshape(-1)].add(parts.reshape(-1))
        mine = jnp.dot(coarse_inverse, rhs, precision=EXACT)
        coarse = lax.all_gather(mine, ("gx", "gz"), axis=0, tiled=True)
        operands.append(jnp.pad(coarse[labels], ((0, 0), (0, LANES - 6))))
    return tuple(
        call(kernel, [block, block], [VMEM] * len(operands), "finish", [pltpu.VMEM((devices, LANES), jnp.float32)])(
            *operands
        )
    )


def solution(mesh):
    placed = (
        P("gx", None, "gz"),
        P("gx", None, "gz"),
        P(None, "gx", None, "gz"),
        P(),
        P(),
        P(),
        P(("gx", "gz"), None),
        P(None, "gx", None, "gz"),
    )
    return jax.shard_map(
        body,
        mesh=mesh,
        in_specs=placed,
        out_specs=(P("gx", None, "gz"), P("gx", None, "gz")),
        check_vma=False,
    )
```

```python
import functools

import jax
import jax.numpy as jnp
import numpy as np
from jax import lax
from jax.experimental import pallas as pl
from jax.experimental.pallas import tpu as pltpu
from jax.sharding import PartitionSpec as P

POINTS = [
    -1.0,
    -0.8717401485096066,
    -0.5917001814331423,
    -0.2092992179024789,
    0.2092992179024789,
    0.5917001814331423,
    0.8717401485096066,
    1.0,
]
WEIGHTS = [
    0.03571428571428571,
    0.21070422714350603,
    0.34112269248350435,
    0.4124587946587038,
    0.4124587946587038,
    0.34112269248350435,
    0.21070422714350603,
    0.03571428571428571,
]
ONES = [1.0] * 8
LOW = [(1.0 - s) / 2.0 for s in POINTS]
HIGH = [(1.0 + s) / 2.0 for s in POINTS]
EXACT = lax.Precision.HIGHEST

ROWS = 16
LANES = 128
WIDE = 256
HALO = 32
DEEP, SHALLOW = 25, 17
SLOT = DEEP + SHALLOW
FIRST_FIELDS = ((0, 24), (41, 17), (75, 17))
SECOND_FIELDS = ((0, 8), (16, 8), (32, 8), (48, 8))
FIRST_ROWS, SECOND_ROWS = 56, 40
PAIRS = ((0, 0), (0, 1), (1, 1))
GROUP_X = (ONES + LOW, [0.0] * 8 + HIGH)
INVERSE_X = [0.5] + [1.0] * 6 + [0.5] + [0.5] + [1.0] * 6 + [0.5]


def iota(shape, dim):
    return lax.broadcasted_iota(jnp.int32, shape, dim)


def pick(index, values):
    result = jnp.full(index.shape, values[0], jnp.float32)
    for i in range(1, 8):
        result = jnp.where(index == i, values[i], result)
    return result


def even_index(axis):
    return lax.rem(lax.axis_index(axis), 2) == 0


class Geometry:
    def __init__(self, lanes):
        shape = (2, 8, lanes)
        self.element_y, self.row, lane = iota(shape, 0), iota(shape, 1), iota(shape, 2)
        self.position = lane & 7
        self.first = self.position == 0
        self.last = self.position == 7
        self.edge = self.first | self.last
        self.weight_y = pick(self.row, WEIGHTS)
        self.weight_z = pick(self.position, WEIGHTS)
        self.inverse_z = jnp.where(self.edge, 0.5, 1.0)
        self.wall = (self.element_y == 1) & (self.row == 7)
        inner = ((self.element_y == 0) & (self.row == 7)) | ((self.element_y == 1) & (self.row == 0))
        self.inverse_y = jnp.where(inner, 0.5, 1.0)
        self.keep = jnp.where(self.wall, 0.0, 1.0)
        self.lanes = lanes

    def pair_y(self, v):
        lower, upper = v[0], v[1]
        row = self.row[0]
        up = jnp.where(row == 7, pltpu.roll(upper, 7, 0), 0.0)
        down = jnp.where(row == 0, pltpu.roll(lower, 1, 0), 0.0)
        return jnp.stack([lower + up, upper + down])

    def pair_z(self, v):
        flat = v.reshape(16, self.lanes)
        after = pltpu.roll(flat, self.lanes - 1, 1).reshape(v.shape)
        before = pltpu.roll(flat, 1, 1).reshape(v.shape)
        return v + jnp.where(self.edge, jnp.where(self.last, after, before), 0.0)

    def pair(self, v):
        return self.pair_z(self.pair_y(v))

    def assemble(self, v):
        return self.pair(v) * self.keep


def solid(v):
    return v.reshape(ROWS, v.shape[-1])


def split(v):
    return v.reshape(2, 8, v.shape[-1])


def own(v):
    return v[..., :LANES]


def down(v):
    return jnp.sum(v.reshape(ROWS, LANES), axis=0, keepdims=True)


def line_of(ref, at, lanes):
    row = ref[at : at + 1, :]
    return jnp.concatenate([row] * (lanes // LANES), axis=1)[None]


def contract_x(rows, table, i, transpose=False):
    total = None
    for p in range(8):
        factor = line_of(table, p * 8 + i if transpose else i * 8 + p, WIDE)
        term = factor * rows[p]
        total = term if total is None else total + term
    return total


def contract_y(v, diagonals):
    total = diagonals[0] * v
    for d in range(1, 8):
        rolled = jnp.stack([pltpu.roll(v[e], 8 - d, 0) for e in range(2)])
        total = total + diagonals[d] * rolled
    return total


def thirds(v):
    high = v.astype(jnp.bfloat16)
    rest = v - high.astype(jnp.float32)
    middle = rest.astype(jnp.bfloat16)
    return high, middle, (rest - middle.astype(jnp.float32)).astype(jnp.bfloat16)


def contract_z(flat, upper, lower, which):
    pieces = []
    for at in range(0, flat.shape[1], LANES):
        high, middle, low = thirds(flat[:, at : at + LANES])
        one = jnp.dot(
            jnp.concatenate([high, middle], axis=1), upper[which], preferred_element_type=jnp.float32
        )
        two = jnp.dot(jnp.concatenate([low, high], axis=1), lower[which], preferred_element_type=jnp.float32)
        pieces.append(one[:, :LANES] + (one[:, LANES:] + two))
    return pieces[0] if len(pieces) == 1 else jnp.concatenate(pieces, axis=1)


def wide_diagonals(ref, which):
    return [jnp.concatenate([ref[which, d]] * (WIDE // LANES), axis=1)[None] for d in range(8)]


def metric(ref, component, element):
    at = (component * 2 + element) * 2
    return jnp.stack([jnp.broadcast_to(ref[at + e : at + e + 1, :], (8, WIDE)) for e in range(2)])


def scaled_metrics(geo, c):
    return c[0] * geo.weight_y * geo.weight_z, c[1] * geo.weight_z, c[2] * geo.weight_y


def stored_factors(ref, element):
    return [split(ref[c, element]) for c in range(3)]


def apply_rows(rows, along_z, factors, stiffness, diagonals):
    result = []
    for element in range(2):
        factor_x, factor_y, factor_z = factors[element]
        inside = rows[element * 8 : element * 8 + 8]
        for i in range(8):
            x = element * 8 + i
            term_y = factor_y * contract_y(inside[i], diagonals)
            term_z = factor_z * split(along_z[x * 16 : x * 16 + 16])
            result.append(factor_x * contract_x(inside, stiffness, i) + WEIGHTS[i] * (term_y + term_z))
    return result


def join_middle(rows):
    middle = rows[7] + rows[8]
    return rows[:7] + [middle, middle] + rows[9:]


def fold(parts, fields):
    lane = iota((8, LANES), 1)
    result = parts[0]
    for part, (offset, half) in list(zip(parts, fields))[1:]:
        taken = ((lane - offset + half) & (LANES - 1)) < 2 * half
        result = jnp.where(taken, pltpu.roll(part, offset, 1), result)
    return result


def unfold(packed, field, fill=0.0):
    offset, half = field
    lane = iota((8, LANES), 1)
    moved = pltpu.roll(packed, LANES - offset, 1) if offset else packed
    return jnp.where(((lane + half) & (LANES - 1)) < 2 * half, moved, fill)


def widen(tile, pieces):
    return jnp.concatenate([tile, jnp.concatenate(pieces, axis=0)], axis=1)


def group_lanes(lanes, group):
    lane = iota((1, lanes), 1)
    signed = jnp.where(lane < lanes // 2 + lanes // 4, lane, lane - lanes) if lanes > LANES else lane
    element, position = signed >> 3, lane & 7
    low, high = pick(position, LOW), pick(position, HIGH)
    here = jnp.where((element >> 3) == group, low, 0.0)
    return here + jnp.where(((element + 1) >> 3) == group, high, 0.0)


def pack_kernel(source, previous, coefficients, first, second, metrics, near_source, near_previous, raw, scratch, ready):
    copies = [
        pltpu.make_async_copy(source, near_source, ready.at[0]),
        pltpu.make_async_copy(previous, near_previous, ready.at[1]),
        pltpu.make_async_copy(coefficients, raw, ready.at[2]),
    ]
    for copy in copies:
        copy.start()
    even = even_index("gz")
    scratch[...] = jnp.zeros_like(scratch)
    widen = (iota((16, LANES), 0) == (iota((16, LANES), 1) >> 3)).astype(jnp.float32)
    for copy in copies:
        copy.wait()
    for c in range(3):
        for element in range(2):
            at = (c * 2 + element) * 2
            scratch[at : at + 2, :] = raw[c, element]
    spread = jnp.dot(scratch[...], widen, precision=EXACT, preferred_element_type=jnp.float32)
    metrics[...] = spread
    slot = iota((8, LANES), 1)
    for to_right, out in ((even, first), (jnp.logical_not(even), second)):
        for tile in range(11):
            packed = None
            for k in range(3):
                n = 3 * tile + k
                if n >= 2 * ROWS:
                    break
                for ref, width, at in ((near_previous, DEEP, SLOT * k), (near_source, SHALLOW, SLOT * k + DEEP)):
                    shift = jnp.where(to_right, (at + width) % LANES, at)
                    moved = pltpu.roll(ref[n // 2, 8 * (n % 2) : 8 * (n % 2) + 8], shift, 1)
                    packed = moved if packed is None else jnp.where(slot >= at, moved, packed)
            out[tile] = packed
        out[11] = spread[:8]
        out[12] = spread[8:]


def prepare_kernel(
    with_coarse, metrics, stiffness, vectors, eigen, labels, coarse, tables,
    upper, lower, diagonals, stiff_table, vector_table, lam, lines, fixed, near_tables,
):
    near_tables[...] = tables[...]
    repeat = (iota((LANES, 8), 0) & 7 == iota((LANES, 8), 1)).astype(jnp.float32)
    same = (iota((LANES, LANES), 0) >> 3) == (iota((LANES, LANES), 1) >> 3)
    unit = (iota((8, 8), 0) == iota((8, 8), 1)).astype(jnp.float32)
    row, column = iota((8, 8), 0), iota((8, 8), 1)

    def dot(a, b, dims):
        return lax.dot_general(a, b, (dims, ((), ())), precision=EXACT, preferred_element_type=jnp.float32)

    def put_block(at, matrix):
        half = dot(repeat, matrix, ((1,), (0,)))
        block = jnp.where(same, dot(half, repeat, ((1,), (1,))), 0.0)
        high, middle, low = thirds(block)
        both = jnp.concatenate([high, middle], axis=1)
        upper[at] = jnp.concatenate([both, both], axis=0)
        lower[at] = jnp.concatenate([high, low], axis=0)

    def put_diagonals(at, matrix):
        for d in range(8):
            chosen = jnp.where(column == ((row + d) & 7), matrix, 0.0)
            diagonals[at, d] = jnp.broadcast_to(jnp.sum(chosen, axis=1, keepdims=True), (8, LANES))

    def put_table(out, matrix):
        tall = (iota((64, 8), 0) >> 3 == iota((64, 8), 1)).astype(jnp.float32)
        chosen = jnp.where(iota((64, 8), 0) & 7 == iota((64, 8), 1), dot(tall, matrix, ((1,), (0,))), 0.0)
        out[...] = jnp.broadcast_to(jnp.sum(chosen, axis=1, keepdims=True), (64, LANES))

    k, s = stiffness[...], vectors[...]
    k_turned, s_turned = dot(k, unit, ((0,), (0,))), dot(s, unit, ((0,), (0,)))
    for at, matrix in enumerate((k_turned, s, s_turned)):
        put_block(at, matrix)
    for at, matrix in enumerate((k, s_turned, s)):
        put_diagonals(at, matrix)
    put_table(stiff_table, k)
    put_table(vector_table, s)
    values = [eigen[i] for i in range(8)]
    lam[0] = pick(iota((8, LANES), 0), values)
    lam[1] = pick(iota((8, LANES), 1) & 7, values)
    stiff_lines = []
    for at, line in enumerate((ONES, LOW, HIGH)):
        total = jnp.sum(k * pick(column, line), axis=1, keepdims=True)
        stiff_lines.append(jnp.broadcast_to(total, (8, LANES)))
        lines[at] = stiff_lines[at]

    groups = [group_lanes(LANES, b) for b in range(3)]
    stacked = jnp.concatenate(groups + [jnp.zeros((13, LANES), jnp.float32)], axis=0)
    stiff_z = contract_z(stacked, upper, lower, 0)
    weight_z = pick(iota((1, LANES), 1) & 7, WEIGHTS)
    node = iota((8, LANES), 0)
    mass_y = [sum(WEIGHTS), sum(WEIGHTS[:7])]
    last = jnp.broadcast_to(k[:, 7:8], (8, LANES))
    inner = jnp.where(node == 7, 0.0, stiff_lines[0] - last)
    stiff_y = [jnp.sum(v, axis=0, keepdims=True) for v in (stiff_lines[0], inner)]
    at = 0
    for a, b in PAIRS:
        across, along = jnp.zeros((1, LANES), jnp.float32), jnp.zeros((1, LANES), jnp.float32)
        for element in range(2):
            fa = GROUP_X[a][element * 8 : element * 8 + 8]
            fb = GROUP_X[b][element * 8 : element * 8 + 8]
            if not (any(fa) and any(fb)):
                continue
            mass_x = sum(w * p * q for w, p, q in zip(WEIGHTS, fa, fb))
            applied = stiff_lines[0 if fb == ONES else 1 + b]
            stiff_x = jnp.sum(applied * pick(node, fa), axis=0, keepdims=True)
            for e in range(2):
                cx, cy, cz = (metrics[(c * 2 + element) * 2 + e, :].reshape(1, LANES) for c in range(3))
                across = across + cx * (stiff_x * mass_y[e]) + cy * (stiff_y[e] * mass_x)
                along = along + cz * (mass_x * mass_y[e])
        across = across * weight_z
        for b in range(3):
            fixed[at : at + 1] = across * groups[b] + along * stiff_z[b : b + 1]
            at += 1
    fixed[9:16] = jnp.zeros((7, LANES), jnp.float32)
    place = iota((1, LANES), 1)
    numbers = jnp.zeros((1, LANES), jnp.float32)
    for a in range(2):
        for b in range(3):
            corner, x, z = 4 * a + (b == 2), a, (0, 8, 15)[b]
            number = labels[corner, x, 0, z].astype(jnp.float32)
            numbers = jnp.where(place == 8 * (3 * a + b) + 4, number, numbers)
    fixed[16:17] = numbers
    below = jnp.zeros((1, LANES), jnp.float32)
    if with_coarse:
        per, count = coarse.shape
        below = [coarse[i : i + 1, :] for i in range(per)]
        if per * count < LANES:
            below.append(jnp.zeros((1, LANES - per * count), jnp.float32))
        below = jnp.concatenate(below, axis=1)
    fixed[17:18] = below
    fixed[18:24] = jnp.zeros((6, LANES), jnp.float32)


def start_kernel(
    source, previous, own_metrics, first, second, stiffness, upper, lower, diagonals,
    start, rest, metrics, factors, halves, message_a, message_b,
):
    even = even_index("gz")
    lane = iota((8, LANES), 1)
    one, two = first[...], second[...]
    from_right, from_left = jnp.where(even, one, two), jnp.where(even, two, one)

    def beyond(n, at, width):
        at = at + SLOT * (n % 3)
        right, left = from_right[n // 3], from_left[n // 3]
        if at:
            right = pltpu.roll(right, LANES - at, 1)
        left = pltpu.roll(left, (LANES - width - at) % LANES, 1)
        return jnp.where(lane < width, right, jnp.where(lane >= LANES - width, left, 0.0))

    def wide(ref, x, at, width):
        return split(widen(ref[x], [beyond(2 * x + e, at, width) for e in range(2)]))

    geo = Geometry(WIDE)
    metrics[:, :LANES] = own_metrics[...]
    for e in range(2):
        right, left = from_right[11 + e], from_left[11 + e]
        metrics[8 * e : 8 * e + 8, LANES:] = jnp.where(
            lane < HALO, right, jnp.where(lane >= LANES - HALO, left, 1.0)
        )
    factor = geo.keep * geo.inverse_y * geo.inverse_z
    rows = [geo.pair(wide(previous, x, 0, DEEP)) * (factor * INVERSE_X[x]) for x in range(ROWS)]
    rows = join_middle(rows)
    faces = (rows[0], rows[15])
    rows[0] = rows[15] = jnp.zeros_like(rows[0])
    for x in range(ROWS):
        start[x] = solid(own(rows[x]))
    along_z = contract_z(jnp.concatenate([solid(v) for v in rows], axis=0), upper, lower, 0)
    scaled = [scaled_metrics(geo, [metric(metrics, c, e) for c in range(3)]) for e in range(2)]
    for e in range(2):
        for c in range(3):
            factors[c, e] = solid(scaled[e][c])
    applied = apply_rows(rows, along_z, scaled, stiffness, wide_diagonals(diagonals, 0))
    for x in range(ROWS):
        rest[x] = solid(wide(source, x, DEEP, SHALLOW) - applied[x])
    halves[0], halves[1] = solid(faces[0]), solid(faces[1])
    messages = []
    for side, x in ((0, 0), (1, 15)):
        half, value = halves[side], rest[x]
        rows = [metrics[(c * 2 + side) * 2 : (c * 2 + side) * 2 + 2] for c in range(3)]
        rows = jnp.concatenate(rows + [jnp.ones((2, WIDE), jnp.float32)], axis=0)
        lower_fold = fold([half[:8, LANES:], value[:8, LANES:], rows[:, LANES:]], FIRST_FIELDS)
        upper_fold = fold([half[8:, LANES:], value[8:, LANES:]], FIRST_FIELDS[:2])
        messages.append(
            jnp.concatenate([half[:, :LANES], value[:, :LANES], lower_fold, upper_fold, rows[:, :LANES]], axis=0)
        )
    even_x = even_index("gx")
    message_a[...] = jnp.where(even_x, messages[1], messages[0])
    message_b[...] = jnp.where(even_x, messages[0], messages[1])


def both_sides(even, a, b):
    one, two = a[...], b[...]
    return jnp.where(even, two, one), jnp.where(even, one, two)


def read_first(message):
    lower_fold, upper_fold = message[32:40], message[40:48]
    half, value = (
        widen(message[16 * k : 16 * k + 16], [unfold(lower_fold, FIRST_FIELDS[k]), unfold(upper_fold, FIRST_FIELDS[k])])
        for k in range(2)
    )
    rows = widen(message[48:56], [unfold(lower_fold, FIRST_FIELDS[2], 1.0)])
    metrics = [
        jnp.stack([jnp.broadcast_to(rows[2 * c + e : 2 * c + e + 1], (8, WIDE)) for e in range(2)]) for c in range(3)
    ]
    return split(half), split(value), metrics


def read_second(message):
    pieces = [unfold(message[32:40], field) for field in SECOND_FIELDS]
    return widen(message[0:16], pieces[:2]), widen(message[16:32], pieces[2:])


def coarse_pieces(geo, factors, stiff_keep, functions, stiff_functions):
    factor_x, factor_y, factor_z = factors
    kept_x, kept_y, kept_z = factor_x * geo.keep, factor_y * stiff_keep, factor_z * geo.keep
    result = []
    for plain, turned in zip(functions, stiff_functions):
        result.append(
            (geo.assemble(kept_x * plain[None]), geo.assemble(kept_y * plain[None] + kept_z * turned[None]))
        )
    return result


def wide_functions(upper, lower):
    functions = [group_lanes(WIDE, b) for b in (-1, 0, 1, 2)]
    stacked = jnp.concatenate(functions + [jnp.zeros((12, WIDE), jnp.float32)], axis=0)
    turned = contract_z(stacked, upper, lower, 0)
    return functions, [turned[b : b + 1] for b in range(4)]


def kept_stiffness(geo, lines, stiffness):
    row = iota((8, LANES), 0)
    last = jnp.zeros((8, LANES), jnp.float32)
    for j in range(8):
        last = jnp.where(row == j, stiffness[j * 8 + 7 : j * 8 + 8, :], last)
    both = jnp.stack([lines[0], lines[0] - last])
    return jnp.concatenate([both] * (WIDE // LANES), axis=2)


def ready_kernel(rest, metrics, factors, lam, stiffness, lines, upper, lower, known, inverse, pieces):
    geo = Geometry(WIDE)
    rows = join_middle([split(rest[x]) for x in range(ROWS)])
    for x in range(1, ROWS - 1):
        known[x] = solid(geo.assemble(rows[x]))
    known[0] = known[15] = jnp.zeros((ROWS, WIDE), jnp.float32)
    lam_y = jnp.concatenate([lam[0]] * (WIDE // LANES), axis=1)[None]
    lam_z = jnp.concatenate([lam[1]] * (WIDE // LANES), axis=1)[None]
    for element in range(2):
        cx, cy, cz = (metric(metrics, c, element) for c in range(3))
        base = cy * lam_y + cz * lam_z
        for i in range(8):
            inverse[element * 8 + i] = solid(1.0 / (cx * line_of(lam.at[0], i, WIDE) + base))
    functions, turned = wide_functions(upper, lower)
    stiff_keep = kept_stiffness(geo, lines, stiffness)
    for element in range(2):
        made = coarse_pieces(geo, stored_factors(factors, element), stiff_keep, functions, turned)
        for b in range(4):
            for k in range(2):
                pieces[element, k, b] = solid(own(made[b][k]))


def solve_kernel(
    rest, known, factors, inverse, halves, got_a, got_b,
    stiffness, vectors, upper, lower, diagonals,
    start_faces, residual, local, face_values, face_factors, message_a, message_b, sums,
):
    even = even_index("gx")
    geo = Geometry(WIDE)
    arrived = [read_first(message) for message in both_sides(even, got_a, got_b)]
    values = [split(halves[side]) + arrived[side][0] for side in range(2)]
    stiff = wide_diagonals(diagonals, 0)
    along_z = contract_z(jnp.concatenate([solid(v) for v in values], axis=0), upper, lower, 0)
    rows = [split(known[x]) for x in range(ROWS)]
    for side, near, across in ((0, 0, 7), (1, 7, 0)):
        face, element = values[side], side
        start_faces[side] = solid(own(face))
        mine = stored_factors(factors, element)
        theirs = scaled_metrics(geo, arrived[side][2])
        for c in range(3):
            face_factors[side, c] = solid(theirs[c])
        scaled = mine[0] * face
        beside = line_of(stiffness, near * 9, WIDE) * scaled
        beside = beside + line_of(stiffness, across * 9, WIDE) * (theirs[0] * face)
        beside = beside + WEIGHTS[0] * (
            (mine[1] + theirs[1]) * contract_y(face, stiff)
            + (mine[2] + theirs[2]) * split(along_z[side * 16 : side * 16 + 16])
        )
        x = element * 8 + near
        rows[x] = geo.assemble(split(rest[x]) + arrived[side][1] - beside)
        moved = geo.assemble(scaled)
        for i in range(8):
            if i != near:
                change = line_of(stiffness, i * 8 + near, WIDE) * moved
                x = element * 8 + i
                rows[x] = rows[x] - change
                if x in (7, 8):
                    rows[15 - x] = rows[15 - x] - change
    parts = [None, None]
    for x in range(ROWS):
        residual[x] = solid(own(rows[x]))
        for a in range(2):
            if GROUP_X[a][x] * INVERSE_X[x] != 0.0:
                term = (GROUP_X[a][x] * INVERSE_X[x]) * own(rows[x])
                parts[a] = term if parts[a] is None else parts[a] + term
    weight = own(geo.inverse_y * geo.inverse_z)
    for a in range(2):
        sums[a : a + 1] = down(parts[a] * weight)

    forward, backward = wide_diagonals(diagonals, 1), wide_diagonals(diagonals, 2)
    moved = []
    for element in range(2):
        inside = rows[element * 8 : element * 8 + 8]
        moved += [solid(contract_y(contract_x(inside, vectors, i, True), forward)) for i in range(8)]
    spectral = contract_z(jnp.concatenate(moved, axis=0), upper, lower, 1)
    divided = [spectral[x * 16 : x * 16 + 16] * inverse[x] for x in range(ROWS)]
    back = contract_z(jnp.concatenate(divided, axis=0), upper, lower, 2)
    solved = []
    for element in range(2):
        inside = [
            contract_y(split(back[x * 16 : x * 16 + 16]), backward) for x in range(element * 8, element * 8 + 8)
        ]
        solved += [contract_x(inside, vectors, i) for i in range(8)]
    total = None
    for x in range(ROWS):
        term = own(solved[x]) * own(rows[x])
        total = term if total is None else total + term
    sums[2:3] = down(total)
    sums[3:8] = jnp.zeros((5, LANES), jnp.float32)
    solved = [geo.assemble(v) for v in join_middle(solved)]
    for x in range(ROWS):
        local[x] = solid(solved[x])
    messages = []
    for side, near in ((0, 0), (1, 7)):
        total = None
        for p in range(8):
            if p != near:
                term = line_of(stiffness, near * 8 + p, WIDE) * solved[side * 8 + p]
                total = term if total is None else total + term
        value, beside = solid(solved[side * 8 + near]), solid(total)
        face_values[side, 0], face_values[side, 1] = value, beside
        folded = fold([v[at : at + 8, LANES:] for v in (value, beside) for at in (0, 8)], SECOND_FIELDS)
        messages.append(jnp.concatenate([value[:, :LANES], beside[:, :LANES], folded], axis=0))
    message_a[...] = jnp.where(even, messages[1], messages[0])
    message_b[...] = jnp.where(even, messages[0], messages[1])


def ahead_kernel(
    local, factors, face_factors, stiffness, lines, upper, lower, diagonals,
    image, sums, face_pieces,
):
    geo = Geometry(WIDE)
    rows = [split(local[x]) for x in range(ROWS)]
    rows[0] = rows[15] = jnp.zeros_like(rows[0])
    along_z = contract_z(jnp.concatenate([solid(v) for v in rows], axis=0), upper, lower, 0)
    scaled = [stored_factors(factors, e) for e in range(2)]
    applied = apply_rows(rows, along_z, scaled, stiffness, wide_diagonals(diagonals, 0))
    total, parts = None, [None, None]
    for x in range(1, ROWS - 1):
        term = own(applied[x]) * own(rows[x])
        total = term if total is None else total + term
        for a in range(2):
            if GROUP_X[a][x] != 0.0:
                term = GROUP_X[a][x] * own(applied[x])
                parts[a] = term if parts[a] is None else parts[a] + term
    for at, value in enumerate(parts + [total]):
        sums[at : at + 1] = down(value * own(geo.keep))
    sums[3:8] = jnp.zeros((5, LANES), jnp.float32)
    joined = join_middle(applied)
    for x in range(1, ROWS - 1):
        image[x] = solid(own(geo.assemble(joined[x])))
    image[0] = image[15] = jnp.zeros((ROWS, LANES), jnp.float32)
    functions, turned = wide_functions(upper, lower)
    stiff_keep = kept_stiffness(geo, lines, stiffness)
    for side in range(2):
        theirs = [split(face_factors[side, c]) for c in range(3)]
        made = coarse_pieces(geo, theirs, stiff_keep, functions, turned)
        for b in range(4):
            for k in range(2):
                face_pieces[side, k, b] = solid(own(made[b][k]))


def image_kernel(
    known, factors, face_factors, face_values, got_a, got_b, first_sums, second_sums, fixed,
    stiffness, lines, upper, lower, diagonals,
    image, faces, payload,
):
    even = even_index("gx")
    geo = Geometry(WIDE)
    stiff = wide_diagonals(diagonals, 0)
    arrived = [read_second(message) for message in both_sides(even, got_a, got_b)]
    values = [face_values[side, 0] + arrived[side][0] for side in range(2)]
    along_z = contract_z(jnp.concatenate(values, axis=0), upper, lower, 0)
    extra = [second_sums[a : a + 1] for a in range(3)]
    rows = [known[x] for x in range(ROWS)]
    for side, near, across in ((0, 0, 7), (1, 7, 0)):
        element, value = side, split(values[side])
        faces[side] = solid(own(value))
        here, there = stored_factors(factors, element), [split(face_factors[side, c]) for c in range(3)]
        along_y, turned = contract_y(value, stiff), split(along_z[side * 16 : side * 16 + 16])
        beside = split(face_values[side, 1])
        ours = here[0] * (beside + line_of(stiffness, near * 9, WIDE) * value)
        ours = ours + WEIGHTS[0] * (here[1] * along_y + here[2] * turned)
        other = there[0] * (split(arrived[side][1]) + line_of(stiffness, across * 9, WIDE) * value)
        other = other + WEIGHTS[0] * (there[1] * along_y + there[2] * turned)
        rows[element * 8 + near] = solid(own(geo.assemble(ours + other)))
        spread = here[0] * value
        moved = solid(own(geo.assemble(spread)))
        for i in range(8):
            if i != near:
                change = stiffness[i * 8 + near : i * 8 + near + 1, :] * moved
                x = element * 8 + i
                rows[x] = rows[x] + change
                if x in (7, 8):
                    rows[15 - x] = rows[15 - x] + change
        near_only = own(spread * geo.keep)
        kept = own(ours * geo.keep)
        for a in range(2):
            line = GROUP_X[a][element * 8 : element * 8 + 8]
            if any(line):
                at = 0 if line == ONES else 1 + a
                factor = lines[at, near : near + 1, :]
                if line[near] != 0.0:
                    factor = factor - line[near] * stiffness[near * 9 : near * 9 + 1, :]
                    extra[a] = extra[a] + down(line[near] * kept)
                extra[a] = extra[a] + factor * down(near_only)
        extra[2] = extra[2] + down(own(beside) * near_only + own(value) * kept)
    for x in range(ROWS):
        image[x] = rows[x]
    zero = jnp.zeros((1, LANES), jnp.float32)
    table = jnp.concatenate(
        [first_sums[0:2], extra[0], extra[1], fixed[0:9], first_sums[2:3], extra[2], zero], axis=0
    )
    lane = iota((LANES, LANES), 1) & 7
    node = iota((LANES, LANES), 0)
    element, position = node >> 3, node & 7
    low, high = pick(position, LOW), pick(position, HIGH)
    columns = jnp.where(lane == (element >> 3), low, 0.0) + jnp.where(lane == ((element + 1) >> 3), high, 0.0)
    columns = jnp.where(lane == 3, 1.0, jnp.where(lane < 3, columns, 0.0))
    reduced = jnp.dot(table, columns, precision=EXACT, preferred_element_type=jnp.float32)
    mine = (iota((16, LANES), 1) >> 3) == iota((16, LANES), 0)
    row = jnp.sum(jnp.where(mine, reduced, 0.0), axis=0, keepdims=True) + fixed[16:17]
    block = jnp.concatenate([row, fixed[17:18]] * 4, axis=0)
    copies = payload.shape[0] // 8
    payload[...] = jnp.broadcast_to(block[None], (copies, 8, LANES)).reshape(copies * 8, LANES)


def lane_tables():
    one = np.zeros((8, LANES), np.float32)
    two = np.zeros((8, LANES), np.float32)
    top = np.zeros((8, LANES), np.float32)
    for a in range(2):
        for b in range(3):
            one[6, 8 * a + b], two[3 * a + b, 8 * a + b], top[0, 8 * a + b] = 1.0, 1.0, 1.0
            one[6, 8 * (2 + a) + b], two[3 * a + b, 8 * (2 + a) + b] = 2.0, 1.0
            top[1, 8 * (2 + a) + b] = 1.0
    for p, (a, other) in enumerate(PAIRS):
        for b in range(3):
            for c in range(3):
                at = 8 * (4 + 3 * p + b) + c
                one[3 * a + b, at] = 1.0 if a == other else 2.0
                two[3 * other + c, at] = 1.0
                top[1, at] = 1.0
    one[6, 8 * 13 + 3], two[6, 8 * 13 + 3], top[0, 8 * 13 + 3] = 1.0, 1.0, 1.0
    one[6, 8 * 14 + 3], two[6, 8 * 14 + 3], top[1, 8 * 14 + 3] = 1.0, 1.0, 1.0
    return np.stack([one, two, top])


def final_kernel(
    devices, spans, count, per,
    start, start_faces, residual, local, faces, image, pieces, face_pieces, lines, tables,
    gathered, given, new_solution, new_residual, values,
):
    rows = gathered[pl.ds(0, devices, stride=2), :]
    if given is None:
        spot = iota((devices, count), 1)
        hits = []
        rhs = [jnp.zeros((1, devices), jnp.float32) for _ in range(per)]
        owner = iota((devices, devices), 1)
        for k in range(6):
            label = rows[:, 8 * k + 4 : 8 * k + 5].astype(jnp.int32)
            at = 8 * (k // 3) + k % 3
            value = rows[:, at : at + 1]
            hits.append(spot == label)
            for q in range(per):
                chosen = jnp.where(owner * per + q == label, value, 0.0)
                rhs[q] = rhs[q] + jnp.sum(chosen, axis=0, keepdims=True)
        inverse = gathered[pl.ds(1, devices, stride=2), :]
        coarse = None
        for q in range(per):
            term = jnp.dot(
                rhs[q], inverse[:, q * count : q * count + count], precision=EXACT,
                preferred_element_type=jnp.float32,
            )
            coarse = term if coarse is None else coarse + term
        columns = [jnp.sum(jnp.where(hit, coarse, 0.0), axis=1, keepdims=True) for hit in hits]
        kept = jnp.zeros((devices, LANES), jnp.float32)
        for k in range(6):
            kept = jnp.where(iota((devices, LANES), 1) == k, columns[k], kept)
        values[...] = kept
    else:
        columns = [given[:, k : k + 1] for k in range(6)]
        values[...] = given[...]
    one, two = tables[0, 6:7, :], tables[1, 6:7, :]
    for k in range(6):
        one = one + columns[k] * tables[0, k : k + 1, :]
        two = two + columns[k] * tables[1, k : k + 1, :]
    product = jnp.sum(rows * one * two, axis=0, keepdims=True)
    numerator = jnp.sum(product * tables[2, 0:1, :], axis=1, keepdims=True)
    denominator = jnp.sum(product * tables[2, 1:2, :], axis=1, keepdims=True)
    alpha = numerator / denominator

    gx, gz = lax.axis_index("gx"), lax.axis_index("gz")
    before_x = lax.rem(gx + devices // spans - 1, devices // spans)
    before_z = lax.rem(gz + spans - 1, spans)
    here = values[pl.ds(gx * spans + gz, 1), :]
    behind = values[pl.ds(gx * spans + before_z, 1), :]
    aside = values[pl.ds(before_x * spans + gz, 1), :]
    corner = values[pl.ds(before_x * spans + before_z, 1), :]
    functions = [group_lanes(LANES, b) for b in range(3)]

    def four(line, back, a):
        return [back[:, 3 * a + 1 : 3 * a + 2]] + [line[:, 3 * a + b : 3 * a + b + 1] for b in range(3)]

    def mix(numbers, ref):
        total = numbers[0] * ref[0]
        for b in range(1, 4):
            total = total + numbers[b] * ref[b]
        return total

    near, right, left = four(here, behind, 0), four(here, behind, 1), four(aside, corner, 0)
    line_near = sum(near[1 + b] * functions[b] for b in range(3))
    line_right = sum(right[1 + b] * functions[b] for b in range(3))
    whole = [mix(near, pieces.at[0, k]) for k in range(2)]
    low = [mix(near, pieces.at[1, k]) for k in range(2)]
    high = [mix(right, pieces.at[1, k]) for k in range(2)]

    def stiff(line, i):
        return lines[line, i : i + 1, :]

    extra = [stiff(0, i) * whole[0] + WEIGHTS[i] * whole[1] for i in range(8)]
    for i in range(8):
        extra.append(
            stiff(1, i) * low[0] + stiff(2, i) * high[0] + WEIGHTS[i] * (LOW[i] * low[1] + HIGH[i] * high[1])
        )
    extra = join_middle(extra)
    beyond_x, beyond_w = face_pieces.at[0, 0], face_pieces.at[0, 1]
    extra[0] = extra[0] + (
        stiff(1, 7) * mix(left, beyond_x) + stiff(2, 7) * mix(near, beyond_x) + WEIGHTS[7] * mix(near, beyond_w)
    )
    extra[15] = extra[15] + stiff(0, 0) * mix(right, face_pieces.at[1, 0]) + WEIGHTS[0] * mix(right, face_pieces.at[1, 1])
    keep = solid(Geometry(LANES).keep)
    for x in range(ROWS):
        begin = start_faces[x // 15] if x in (0, 15) else start[x]
        mine = faces[x // 15] if x in (0, 15) else local[x, :, :LANES]
        new_residual[x] = residual[x] - alpha * (image[x] + extra[x])
        coarse_line = GROUP_X[0][x] * line_near
        if GROUP_X[1][x] != 0.0:
            coarse_line = coarse_line + GROUP_X[1][x] * line_right
        new_solution[x] = begin + alpha * (mine + keep * coarse_line)


VMEM = pl.BlockSpec(memory_space=pltpu.VMEM)
SMEM = pl.BlockSpec(memory_space=pltpu.SMEM)
FAR = pl.BlockSpec(memory_space=pltpu.HBM)


def call(kernel, shapes, specs, name, scratch=()):
    def leaf(shape):
        kind = jnp.float32
        if shape[0] == "half":
            shape, kind = shape[1:], jnp.bfloat16
        return jax.ShapeDtypeStruct(shape, kind)

    return pl.pallas_call(
        kernel,
        out_shape=[leaf(shape) for shape in shapes],
        in_specs=specs,
        out_specs=[VMEM] * len(shapes),
        scratch_shapes=list(scratch),
        compiler_params=pltpu.CompilerParams(vmem_limit_bytes=16 * 1024 * 1024),
        name=name,
    )


def swap(first, second, axis):
    size = lax.axis_size(axis)
    odd = [(i, (i + 1) % size) for i in range(1, size, 2)]
    one = lax.ppermute(first, axis, [(i, i ^ 1) for i in range(size)])
    two = lax.ppermute(second, axis, odd + [(b, a) for a, b in odd])
    return one, two


def body(
    source, previous, coefficients, stiffness, fdm_vectors, fdm_values, coarse_inverse, vertex_map
):
    assert source.shape == (ROWS, ROWS, LANES)
    spans = lax.axis_size("gz")
    devices = lax.axis_size("gx") * spans
    per, count = coarse_inverse.shape
    small = per * count <= LANES
    block, wide, face = (ROWS, ROWS, LANES), (ROWS, ROWS, WIDE), (ROWS, LANES)
    halo = (13, 8, LANES)

    first, second, own_metrics, source, previous = call(
        pack_kernel,
        [halo, halo, face, block, block],
        [FAR] * 3,
        "pack",
        [pltpu.VMEM(coefficients.shape, jnp.float32), pltpu.VMEM((16, 16), jnp.float32), pltpu.SemaphoreType.DMA((3,))],
    )(*(pltpu.with_memory_space_constraint(v, pltpu.HBM) for v in (source, previous, coefficients)))
    first, second = swap(first, second, "gz")
    upper, lower, diagonals, stiff, vectors, lam, lines, fixed, tables = call(
        functools.partial(prepare_kernel, small),
        [
            ("half", 3, WIDE, WIDE), ("half", 3, WIDE, LANES), (3, 8, 8, LANES),
            (64, LANES), (64, LANES), (2, 8, LANES), (3, 8, LANES), (24, LANES), (3, 8, LANES),
        ],
        [VMEM] * 3 + [SMEM] * 2 + [VMEM if small else FAR, VMEM],
        "prepare",
    )(own_metrics, stiffness, fdm_vectors, fdm_values, vertex_map, coarse_inverse, jnp.asarray(lane_tables()))

    message = (FIRST_ROWS, LANES)
    start, rest, metrics, factors, halves, own_a, own_b = call(
        start_kernel,
        [block, wide, (16, WIDE), (3, 2, ROWS, WIDE), (2, ROWS, WIDE), message, message],
        [VMEM] * 9,
        "start",
    )(source, previous, own_metrics, first, second, stiff, upper, lower, diagonals)
    far_a, far_b = swap(own_a, own_b, "gx")
    known, inverse, pieces = call(
        ready_kernel, [wide, wide, (2, 2, 4, ROWS, LANES)], [VMEM] * 8, "ready"
    )(rest, metrics, factors, lam, stiff, lines, upper, lower)

    message = (SECOND_ROWS, LANES)
    start_faces, residual, local, face_values, face_factors, side_a, side_b, sums = call(
        solve_kernel,
        [(2, ROWS, LANES), block, wide, (2, 2, ROWS, WIDE), (2, 3, ROWS, WIDE), message, message, (8, LANES)],
        [VMEM] * 12,
        "solve",
    )(rest, known, factors, inverse, halves, far_a, far_b, stiff, vectors, upper, lower, diagonals)
    got_a, got_b = swap(side_a, side_b, "gx")
    image, more_sums, face_pieces = call(
        ahead_kernel,
        [block, (8, LANES), (2, 2, 4, ROWS, LANES)],
        [VMEM] * 8,
        "ahead",
    )(local, factors, face_factors, stiff, lines, upper, lower, diagonals)

    image, faces, payload = call(
        image_kernel, [block, (2, ROWS, LANES), (2 * devices, LANES)], [VMEM] * 14, "image"
    )(
        image, factors, face_factors, face_values, got_a, got_b, sums, more_sums, fixed,
        stiff, lines, upper, lower, diagonals,
    )
    gathered = lax.all_to_all(payload.reshape(devices, 2, LANES), ("gx", "gz"), 0, 0)
    gathered = gathered.reshape(2 * devices, LANES)

    operands = [
        start, start_faces, residual, local, faces, image, pieces, face_pieces, lines,
        tables, gathered,
    ]
    finish = functools.partial(final_kernel, devices, spans, count, per)
    if small:

        def kernel(*refs):
            finish(*refs[:11], None, *refs[11:])

    else:
        kernel = finish
        rows = gathered[0::2]
        labels = rows[:, jnp.array([8 * k + 4 for k in range(6)])].astype(jnp.int32)
        parts = rows[:, jnp.array([8 * (k // 3) + k % 3 for k in range(6)])]
        rhs = jnp.zeros((count,), jnp.float32).at[labels.reshape(-1)].add(parts.reshape(-1))
        mine = jnp.dot(coarse_inverse, rhs, precision=EXACT)
        coarse = lax.all_gather(mine, ("gx", "gz"), axis=0, tiled=True)
        operands.append(jnp.pad(coarse[labels], ((0, 0), (0, LANES - 6))))
    return tuple(
        call(kernel, [block, block], [VMEM] * len(operands), "finish", [pltpu.VMEM((devices, LANES), jnp.float32)])(
            *operands
        )
    )


def solution(mesh):
    placed = (
        P("gx", None, "gz"),
        P("gx", None, "gz"),
        P(None, "gx", None, "gz"),
        P(),
        P(),
        P(),
        P(("gx", "gz"), None),
        P(None, "gx", None, "gz"),
    )
    return jax.shard_map(
        body,
        mesh=mesh,
        in_specs=placed,
        out_specs=(P("gx", None, "gz"), P("gx", None, "gz")),
        check_vma=False,
    )
```

```python
import functools

import jax
import jax.numpy as jnp
import numpy as np
from jax import lax
from jax.experimental import pallas as pl
from jax.experimental.pallas import tpu as pltpu
from jax.sharding import PartitionSpec as P

POINTS = [
    -1.0,
    -0.8717401485096066,
    -0.5917001814331423,
    -0.2092992179024789,
    0.2092992179024789,
    0.5917001814331423,
    0.8717401485096066,
    1.0,
]
WEIGHTS = [
    0.03571428571428571,
    0.21070422714350603,
    0.34112269248350435,
    0.4124587946587038,
    0.4124587946587038,
    0.34112269248350435,
    0.21070422714350603,
    0.03571428571428571,
]
ONES = [1.0] * 8
LOW = [(1.0 - s) / 2.0 for s in POINTS]
HIGH = [(1.0 + s) / 2.0 for s in POINTS]
EXACT = lax.Precision.HIGHEST

ROWS = 16
LANES = 128
WIDE = 256
HALO = 32
DEEP, SHALLOW = 25, 17
SLOT = DEEP + SHALLOW
FIRST_FIELDS = ((0, 24), (41, 17), (75, 17))
SECOND_FIELDS = ((0, 16), (32, 16), (64, 16), (96, 16))
FIRST_ROWS, SECOND_ROWS = 56, 40
PAIRS = ((0, 0), (0, 1), (1, 1))
GROUP_X = (ONES + LOW, [0.0] * 8 + HIGH)
INVERSE_X = [0.5] + [1.0] * 6 + [0.5] + [0.5] + [1.0] * 6 + [0.5]


def iota(shape, dim):
    return lax.broadcasted_iota(jnp.int32, shape, dim)


def pick(index, values):
    result = jnp.full(index.shape, values[0], jnp.float32)
    for i in range(1, 8):
        result = jnp.where(index == i, values[i], result)
    return result


def even_index(axis):
    return lax.rem(lax.axis_index(axis), 2) == 0


class Geometry:
    def __init__(self, lanes):
        shape = (2, 8, lanes)
        self.element_y, self.row, lane = iota(shape, 0), iota(shape, 1), iota(shape, 2)
        self.position = lane & 7
        self.first = self.position == 0
        self.last = self.position == 7
        self.edge = self.first | self.last
        self.weight_y = pick(self.row, WEIGHTS)
        self.weight_z = pick(self.position, WEIGHTS)
        self.inverse_z = jnp.where(self.edge, 0.5, 1.0)
        self.wall = (self.element_y == 1) & (self.row == 7)
        inner = ((self.element_y == 0) & (self.row == 7)) | ((self.element_y == 1) & (self.row == 0))
        self.inverse_y = jnp.where(inner, 0.5, 1.0)
        self.keep = jnp.where(self.wall, 0.0, 1.0)
        self.lanes = lanes

    def pair_y(self, v):
        lower, upper = v[0], v[1]
        row = self.row[0]
        up = jnp.where(row == 7, pltpu.roll(upper, 7, 0), 0.0)
        down = jnp.where(row == 0, pltpu.roll(lower, 1, 0), 0.0)
        return jnp.stack([lower + up, upper + down])

    def pair_z(self, v):
        flat = v.reshape(16, self.lanes)
        after = pltpu.roll(flat, self.lanes - 1, 1).reshape(v.shape)
        before = pltpu.roll(flat, 1, 1).reshape(v.shape)
        return v + jnp.where(self.edge, jnp.where(self.last, after, before), 0.0)

    def pair(self, v):
        return self.pair_z(self.pair_y(v))

    def assemble(self, v):
        return self.pair(v) * self.keep


def solid(v):
    return v.reshape(ROWS, v.shape[-1])


def split(v):
    return v.reshape(2, 8, v.shape[-1])


def own(v):
    return v[..., :LANES]


def down(v):
    return jnp.sum(v.reshape(ROWS, LANES), axis=0, keepdims=True)


def line_of(ref, at, lanes):
    row = ref[at : at + 1, :]
    return jnp.concatenate([row] * (lanes // LANES), axis=1)[None]


def weighted(factors, rows):
    total = None
    for factor, row in zip(factors, rows):
        total = factor * row if total is None else total + factor * row
    return total


def divisors_of(geo, c, lam):
    lam_y = jnp.concatenate([lam[0]] * (WIDE // LANES), axis=1)[None]
    lam_z = jnp.concatenate([lam[1]] * (WIDE // LANES), axis=1)[None]
    base = c[1] * lam_y + c[2] * lam_z
    return [1.0 / (c[0] * line_of(lam.at[0], i, WIDE) + base) for i in range(8)]


def contract_x(rows, table, i, transpose=False, without=None):
    total = None
    for p in range(8):
        if p == without:
            continue
        factor = line_of(table, p * 8 + i if transpose else i * 8 + p, WIDE)
        term = factor * rows[p]
        total = term if total is None else total + term
    return total


def contract_y(v, diagonals):
    total = diagonals[0] * v
    for d in range(1, 8):
        rolled = jnp.stack([pltpu.roll(v[e], 8 - d, 0) for e in range(2)])
        total = total + diagonals[d] * rolled
    return total


def thirds(v):
    high = v.astype(jnp.bfloat16)
    rest = v - high.astype(jnp.float32)
    middle = rest.astype(jnp.bfloat16)
    return high, middle, (rest - middle.astype(jnp.float32)).astype(jnp.bfloat16)


def contract_z(flat, upper, lower, which):
    pieces = []
    for at in range(0, flat.shape[1], LANES):
        high, middle, low = thirds(flat[:, at : at + LANES])
        one = jnp.dot(
            jnp.concatenate([high, middle], axis=1), upper[which], preferred_element_type=jnp.float32
        )
        two = jnp.dot(jnp.concatenate([low, high], axis=1), lower[which], preferred_element_type=jnp.float32)
        pieces.append(one[:, :LANES] + (one[:, LANES:] + two))
    return pieces[0] if len(pieces) == 1 else jnp.concatenate(pieces, axis=1)


def wide_diagonals(ref, which):
    return [jnp.concatenate([ref[which, d]] * (WIDE // LANES), axis=1)[None] for d in range(8)]


def metric(ref, component, element):
    at = (component * 2 + element) * 2
    return jnp.stack([jnp.broadcast_to(ref[at + e : at + e + 1, :], (8, WIDE)) for e in range(2)])


def scaled_metrics(geo, c):
    return c[0] * geo.weight_y * geo.weight_z, c[1] * geo.weight_z, c[2] * geo.weight_y


def stored_factors(ref, element):
    return [split(ref[c, element]) for c in range(3)]


def apply_rows(rows, along_z, factors, stiffness, diagonals):
    result = []
    for element in range(2):
        factor_x, factor_y, factor_z = factors[element]
        inside = rows[element * 8 : element * 8 + 8]
        for i in range(8):
            x = element * 8 + i
            term_y = factor_y * contract_y(inside[i], diagonals)
            term_z = factor_z * split(along_z[x * 16 : x * 16 + 16])
            result.append(factor_x * contract_x(inside, stiffness, i) + WEIGHTS[i] * (term_y + term_z))
    return result


def join_middle(rows):
    middle = rows[7] + rows[8]
    return rows[:7] + [middle, middle] + rows[9:]


def fold(parts, fields):
    lane = iota((8, LANES), 1)
    result = parts[0]
    for part, (offset, half) in list(zip(parts, fields))[1:]:
        taken = ((lane - offset + half) & (LANES - 1)) < 2 * half
        result = jnp.where(taken, pltpu.roll(part, offset, 1), result)
    return result


def unfold(packed, field, fill=0.0):
    offset, half = field
    lane = iota((8, LANES), 1)
    moved = pltpu.roll(packed, LANES - offset, 1) if offset else packed
    return jnp.where(((lane + half) & (LANES - 1)) < 2 * half, moved, fill)


def widen(tile, pieces):
    return jnp.concatenate([tile, jnp.concatenate(pieces, axis=0)], axis=1)


def group_lanes(lanes, group):
    lane = iota((1, lanes), 1)
    signed = jnp.where(lane < lanes // 2 + lanes // 4, lane, lane - lanes) if lanes > LANES else lane
    element, position = signed >> 3, lane & 7
    low, high = pick(position, LOW), pick(position, HIGH)
    here = jnp.where((element >> 3) == group, low, 0.0)
    return here + jnp.where(((element + 1) >> 3) == group, high, 0.0)


def pack_kernel(source, previous, coefficients, first, second, metrics, near_source, near_previous, raw, scratch, ready):
    copies = [
        pltpu.make_async_copy(source, near_source, ready.at[0]),
        pltpu.make_async_copy(previous, near_previous, ready.at[1]),
        pltpu.make_async_copy(coefficients, raw, ready.at[2]),
    ]
    for copy in copies:
        copy.start()
    even = even_index("gz")
    scratch[...] = jnp.zeros_like(scratch)
    widen = (iota((16, LANES), 0) == (iota((16, LANES), 1) >> 3)).astype(jnp.float32)
    for copy in copies:
        copy.wait()
    for c in range(3):
        for element in range(2):
            at = (c * 2 + element) * 2
            scratch[at : at + 2, :] = raw[c, element]
    spread = jnp.dot(scratch[...], widen, precision=EXACT, preferred_element_type=jnp.float32)
    metrics[...] = spread
    slot = iota((8, LANES), 1)
    for to_right, out in ((even, first), (jnp.logical_not(even), second)):
        for tile in range(11):
            packed = None
            for k in range(3):
                n = 3 * tile + k
                if n >= 2 * ROWS:
                    break
                for ref, width, at in ((near_previous, DEEP, SLOT * k), (near_source, SHALLOW, SLOT * k + DEEP)):
                    shift = jnp.where(to_right, (at + width) % LANES, at)
                    moved = pltpu.roll(ref[n // 2, 8 * (n % 2) : 8 * (n % 2) + 8], shift, 1)
                    packed = moved if packed is None else jnp.where(slot >= at, moved, packed)
            out[tile] = packed
        out[11] = spread[:8]
        out[12] = spread[8:]


def prepare_kernel(
    with_coarse, metrics, stiffness, vectors, eigen, labels, coarse, tables,
    upper, lower, diagonals, stiff_table, vector_table, bend, lam, lines, fixed, near_tables,
):
    near_tables[...] = tables[...]
    repeat = (iota((LANES, 8), 0) & 7 == iota((LANES, 8), 1)).astype(jnp.float32)
    same = (iota((LANES, LANES), 0) >> 3) == (iota((LANES, LANES), 1) >> 3)
    unit = (iota((8, 8), 0) == iota((8, 8), 1)).astype(jnp.float32)
    row, column = iota((8, 8), 0), iota((8, 8), 1)

    def dot(a, b, dims):
        return lax.dot_general(a, b, (dims, ((), ())), precision=EXACT, preferred_element_type=jnp.float32)

    def put_block(at, matrix):
        half = dot(repeat, matrix, ((1,), (0,)))
        block = jnp.where(same, dot(half, repeat, ((1,), (1,))), 0.0)
        high, middle, low = thirds(block)
        both = jnp.concatenate([high, middle], axis=1)
        upper[at] = jnp.concatenate([both, both], axis=0)
        lower[at] = jnp.concatenate([high, low], axis=0)

    def put_diagonals(at, matrix):
        for d in range(8):
            chosen = jnp.where(column == ((row + d) & 7), matrix, 0.0)
            diagonals[at, d] = jnp.broadcast_to(jnp.sum(chosen, axis=1, keepdims=True), (8, LANES))

    def put_table(out, matrix):
        tall = (iota((64, 8), 0) >> 3 == iota((64, 8), 1)).astype(jnp.float32)
        chosen = jnp.where(iota((64, 8), 0) & 7 == iota((64, 8), 1), dot(tall, matrix, ((1,), (0,))), 0.0)
        out[...] = jnp.broadcast_to(jnp.sum(chosen, axis=1, keepdims=True), (64, LANES))

    k, s = stiffness[...], vectors[...]
    k_turned, s_turned = dot(k, unit, ((0,), (0,))), dot(s, unit, ((0,), (0,)))
    for at, matrix in enumerate((k_turned, s, s_turned)):
        put_block(at, matrix)
    for at, matrix in enumerate((k, s_turned, s)):
        put_diagonals(at, matrix)
    put_table(stiff_table, k)
    put_table(vector_table, s)
    for side, near in ((0, 0), (1, 7)):
        chosen = jnp.where(column == near, 0.0, s_turned * k[near : near + 1, :])
        total = jnp.sum(chosen, axis=1, keepdims=True)
        bend[8 * side : 8 * side + 8] = jnp.broadcast_to(total, (8, LANES))
    values = [eigen[i] for i in range(8)]
    lam[0] = pick(iota((8, LANES), 0), values)
    lam[1] = pick(iota((8, LANES), 1) & 7, values)
    stiff_lines = []
    for at, line in enumerate((ONES, LOW, HIGH)):
        total = jnp.sum(k * pick(column, line), axis=1, keepdims=True)
        stiff_lines.append(jnp.broadcast_to(total, (8, LANES)))
        lines[at] = stiff_lines[at]

    groups = [group_lanes(LANES, b) for b in range(3)]
    stacked = jnp.concatenate(groups + [jnp.zeros((13, LANES), jnp.float32)], axis=0)
    stiff_z = contract_z(stacked, upper, lower, 0)
    weight_z = pick(iota((1, LANES), 1) & 7, WEIGHTS)
    node = iota((8, LANES), 0)
    mass_y = [sum(WEIGHTS), sum(WEIGHTS[:7])]
    last = jnp.broadcast_to(k[:, 7:8], (8, LANES))
    inner = jnp.where(node == 7, 0.0, stiff_lines[0] - last)
    stiff_y = [jnp.sum(v, axis=0, keepdims=True) for v in (stiff_lines[0], inner)]
    at = 0
    for a, b in PAIRS:
        across, along = jnp.zeros((1, LANES), jnp.float32), jnp.zeros((1, LANES), jnp.float32)
        for element in range(2):
            fa = GROUP_X[a][element * 8 : element * 8 + 8]
            fb = GROUP_X[b][element * 8 : element * 8 + 8]
            if not (any(fa) and any(fb)):
                continue
            mass_x = sum(w * p * q for w, p, q in zip(WEIGHTS, fa, fb))
            applied = stiff_lines[0 if fb == ONES else 1 + b]
            stiff_x = jnp.sum(applied * pick(node, fa), axis=0, keepdims=True)
            for e in range(2):
                cx, cy, cz = (metrics[(c * 2 + element) * 2 + e, :].reshape(1, LANES) for c in range(3))
                across = across + cx * (stiff_x * mass_y[e]) + cy * (stiff_y[e] * mass_x)
                along = along + cz * (mass_x * mass_y[e])
        across = across * weight_z
        for b in range(3):
            fixed[at : at + 1] = across * groups[b] + along * stiff_z[b : b + 1]
            at += 1
    fixed[9:16] = jnp.zeros((7, LANES), jnp.float32)
    place = iota((1, LANES), 1)
    numbers = jnp.zeros((1, LANES), jnp.float32)
    for a in range(2):
        for b in range(3):
            corner, x, z = 4 * a + (b == 2), a, (0, 8, 15)[b]
            number = labels[corner, x, 0, z].astype(jnp.float32)
            numbers = jnp.where(place == 8 * (3 * a + b) + 4, number, numbers)
    fixed[16:17] = numbers
    below = jnp.zeros((1, LANES), jnp.float32)
    if with_coarse:
        per, count = coarse.shape
        below = [coarse[i : i + 1, :] for i in range(per)]
        if per * count < LANES:
            below.append(jnp.zeros((1, LANES - per * count), jnp.float32))
        below = jnp.concatenate(below, axis=1)
    fixed[17:18] = below
    fixed[18:24] = jnp.zeros((6, LANES), jnp.float32)


def start_kernel(
    source, previous, own_metrics, first, second, stiffness, vectors, bend, lam, upper, lower, diagonals,
    start, known, factors, halves, remainders, spectrum, inverse, message_a, message_b, common, metrics,
):
    even = even_index("gz")
    lane = iota((8, LANES), 1)
    one, two = first[...], second[...]
    from_right, from_left = jnp.where(even, one, two), jnp.where(even, two, one)

    def beyond(n, at, width):
        at = at + SLOT * (n % 3)
        right, left = from_right[n // 3], from_left[n // 3]
        if at:
            right = pltpu.roll(right, LANES - at, 1)
        left = pltpu.roll(left, (LANES - width - at) % LANES, 1)
        return jnp.where(lane < width, right, jnp.where(lane >= LANES - width, left, 0.0))

    def wide(ref, x, at, width):
        return split(widen(ref[x], [beyond(2 * x + e, at, width) for e in range(2)]))

    geo = Geometry(WIDE)
    metrics[:, :LANES] = own_metrics[...]
    for e in range(2):
        right, left = from_right[11 + e], from_left[11 + e]
        metrics[8 * e : 8 * e + 8, LANES:] = jnp.where(
            lane < HALO, right, jnp.where(lane >= LANES - HALO, left, 1.0)
        )
    factor = geo.keep * geo.inverse_y * geo.inverse_z
    rows = [geo.pair(wide(previous, x, 0, DEEP)) * (factor * INVERSE_X[x]) for x in range(ROWS)]
    rows = join_middle(rows)
    faces = (rows[0], rows[15])
    rows[0] = rows[15] = jnp.zeros_like(rows[0])
    for x in range(ROWS):
        start[x] = solid(own(rows[x]))
    along_z = contract_z(jnp.concatenate([solid(v) for v in rows], axis=0), upper, lower, 0)
    scaled = [scaled_metrics(geo, [metric(metrics, c, e) for c in range(3)]) for e in range(2)]
    for e in range(2):
        for c in range(3):
            factors[c, e] = solid(scaled[e][c])
    applied = apply_rows(rows, along_z, scaled, stiffness, wide_diagonals(diagonals, 0))
    rest = [wide(source, x, DEEP, SHALLOW) - applied[x] for x in range(ROWS)]
    halves[0], halves[1] = solid(faces[0]), solid(faces[1])
    remainders[0], remainders[1] = solid(rest[0]), solid(rest[15])
    messages = []
    for side, x in ((0, 0), (1, 15)):
        half, value = solid(faces[side]), solid(rest[x])
        rows = [metrics[(c * 2 + side) * 2 : (c * 2 + side) * 2 + 2] for c in range(3)]
        rows = jnp.concatenate(rows + [jnp.ones((2, WIDE), jnp.float32)], axis=0)
        lower_fold = fold([half[:8, LANES:], value[:8, LANES:], rows[:, LANES:]], FIRST_FIELDS)
        upper_fold = fold([half[8:, LANES:], value[8:, LANES:]], FIRST_FIELDS[:2])
        messages += [half[:, :LANES], value[:, :LANES], lower_fold, upper_fold, rows[:, :LANES]]
    messages = jnp.concatenate(messages, axis=0)
    common[...] = messages
    message_a[: 2 * FIRST_ROWS], message_b[: 2 * FIRST_ROWS] = messages, messages

    rest = join_middle(rest)
    zero = jnp.zeros((2, 8, WIDE), jnp.float32)
    rest = [zero] + [geo.assemble(v) for v in rest[1:15]] + [zero]
    forward = wide_diagonals(diagonals, 1)
    moved = []
    for element in range(2):
        inside = rest[element * 8 : element * 8 + 8]
        moved += [solid(contract_y(contract_x(inside, vectors, i, True, 7 * element), forward)) for i in range(8)]
    for x in range(ROWS):
        known[x] = solid(rest[x])
    transformed = contract_z(jnp.concatenate(moved, axis=0), upper, lower, 1)
    damped = []
    for element in range(2):
        divisors = divisors_of(geo, [metric(metrics, c, element) for c in range(3)], lam)
        for i in range(8):
            x = element * 8 + i
            value = split(transformed[x * 16 : x * 16 + 16])
            spectrum[x], inverse[x] = solid(value), solid(divisors[i])
            damped.append(value * divisors[i])
    messages = []
    for side, near in ((0, 0), (1, 7)):
        inside, across = damped[side * 8 : side * 8 + 8], damped[8 - side * 8 : 16 - side * 8]
        value = contract_x(inside, vectors, near)
        beside = weighted([line_of(bend, side * 8 + i, WIDE) for i in range(8)], inside)
        beside = beside + line_of(stiffness, near * 8 + 7 - near, WIDE) * contract_x(across, vectors, near)
        value, beside = solid(value), solid(beside)
        folded = fold([v[at : at + 8, LANES:] for v in (value, beside) for at in (0, 8)], SECOND_FIELDS)
        messages.append(jnp.concatenate([value[:, :LANES], beside[:, :LANES], folded], axis=0))
    even_x = even_index("gx")
    message_a[2 * FIRST_ROWS :] = jnp.where(even_x, messages[1], messages[0])
    message_b[2 * FIRST_ROWS :] = jnp.where(even_x, messages[0], messages[1])


def both_sides(even, a, b):
    one, two = a[...], b[...]
    return jnp.where(even, two, one), jnp.where(even, one, two)


def read_first(message):
    lower_fold, upper_fold = message[32:40], message[40:48]
    half, value = (
        widen(message[16 * k : 16 * k + 16], [unfold(lower_fold, FIRST_FIELDS[k]), unfold(upper_fold, FIRST_FIELDS[k])])
        for k in range(2)
    )
    rows = widen(message[48:56], [unfold(lower_fold, FIRST_FIELDS[2], 1.0)])
    metrics = [
        jnp.stack([jnp.broadcast_to(rows[2 * c + e : 2 * c + e + 1], (8, WIDE)) for e in range(2)]) for c in range(3)
    ]
    return split(half), split(value), metrics


def read_second(message):
    pieces = [unfold(message[32:40], field) for field in SECOND_FIELDS]
    return widen(message[0:16], pieces[:2]), widen(message[16:32], pieces[2:])


def coarse_pieces(geo, factors, stiff_keep, functions, stiff_functions):
    factor_x, factor_y, factor_z = factors
    kept_x, kept_y, kept_z = factor_x * geo.keep, factor_y * stiff_keep, factor_z * geo.keep
    result = []
    for plain, turned in zip(functions, stiff_functions):
        result.append(
            (geo.assemble(kept_x * plain[None]), geo.assemble(kept_y * plain[None] + kept_z * turned[None]))
        )
    return result


def wide_functions(upper, lower):
    functions = [group_lanes(WIDE, b) for b in (-1, 0, 1, 2)]
    stacked = jnp.concatenate(functions + [jnp.zeros((12, WIDE), jnp.float32)], axis=0)
    turned = contract_z(stacked, upper, lower, 0)
    return functions, [turned[b : b + 1] for b in range(4)]


def kept_stiffness(geo, lines, stiffness):
    row = iota((8, LANES), 0)
    last = jnp.zeros((8, LANES), jnp.float32)
    for j in range(8):
        last = jnp.where(row == j, stiffness[j * 8 + 7 : j * 8 + 8, :], last)
    both = jnp.stack([lines[0], lines[0] - last])
    return jnp.concatenate([both] * (WIDE // LANES), axis=2)


def ready_kernel(factors, stiffness, lines, upper, lower, pieces, waves, stiff_keep):
    geo = Geometry(WIDE)
    functions, turned = wide_functions(upper, lower)
    for b in range(4):
        waves[b : b + 1], waves[4 + b : 5 + b] = functions[b], turned[b]
    along_y = kept_stiffness(geo, lines, stiffness)
    stiff_keep[...] = solid(along_y)
    for element in range(2):
        made = coarse_pieces(geo, stored_factors(factors, element), along_y, functions, turned)
        for b in range(4):
            for k in range(2):
                pieces[element, k, b] = solid(own(made[b][k]))


def solve_kernel(
    known, factors, halves, remainders, spectrum, inverse, got_a, got_b, got_c, _,
    stiffness, vectors, bend, lam, upper, lower, diagonals,
    start_faces, residual, local, beside, face_factors, sums,
):
    even = even_index("gx")
    geo = Geometry(WIDE)
    sides = both_sides(even, got_a, got_b)
    beyond = got_c[...]
    at = [side[: 2 * FIRST_ROWS] for side in sides]
    near = [read_first(at[0][FIRST_ROWS:]), read_first(at[1][:FIRST_ROWS])]
    far = [read_first(at[0][:FIRST_ROWS]), read_first(at[1][FIRST_ROWS:])]
    last = [read_first(beyond[FIRST_ROWS:]), read_first(beyond[:FIRST_ROWS])]
    mine = [stored_factors(factors, e) for e in range(2)]
    near_factors, far_factors, last_factors = ([scaled_metrics(geo, v[2]) for v in group] for group in (near, far, last))
    for side in range(2):
        for c in range(3):
            face_factors[side, c] = solid(near_factors[side][c])
    values = [split(halves[side]) + near[side][0] for side in range(2)]
    values += [far[side][0] + last[side][0] for side in range(2)]
    remains = [split(remainders[side]) + near[side][1] for side in range(2)]
    remains += [far[side][1] + last[side][1] for side in range(2)]
    beside_left = [near_factors[0], mine[1], last_factors[0], far_factors[1]]
    beside_right = [mine[0], near_factors[1], far_factors[0], last_factors[1]]
    stiff = wide_diagonals(diagonals, 0)
    along_z = contract_z(jnp.concatenate([solid(v) for v in values], axis=0), upper, lower, 0)
    first, last_corner = line_of(stiffness, 0, WIDE), line_of(stiffness, 63, WIDE)
    cross = line_of(stiffness, 7, WIDE)
    totals, into_left, into_right = [], [], []
    for k in range(4):
        one, two, value = beside_left[k], beside_right[k], values[k]
        left, right = one[0] * value, two[0] * value
        taken = last_corner * left + first * right + WEIGHTS[0] * (
            (one[1] + two[1]) * contract_y(value, stiff) + (one[2] + two[2]) * split(along_z[k * 16 : k * 16 + 16])
        )
        totals.append(geo.assemble(remains[k] - taken))
        into_left.append(geo.assemble(left) if k != 2 else None)
        into_right.append(geo.assemble(right) if k != 3 else None)
    for side in range(2):
        start_faces[side] = solid(own(values[side]))

    moved = [into_right[0], into_left[1]]
    rows = [own(split(known[x])) for x in range(ROWS)]
    rows[0], rows[15] = own(totals[0]), own(totals[1])
    for side, face in ((0, 0), (1, 7)):
        for i in range(8):
            if i != face:
                change = line_of(stiffness, i * 8 + face, LANES) * own(moved[side])
                x = side * 8 + i
                rows[x] = rows[x] - change
                if x in (7, 8):
                    rows[15 - x] = rows[15 - x] - change
    parts = [None, None]
    for x in range(ROWS):
        residual[x] = solid(rows[x])
        for a in range(2):
            if GROUP_X[a][x] * INVERSE_X[x] != 0.0:
                term = (GROUP_X[a][x] * INVERSE_X[x]) * rows[x]
                parts[a] = term if parts[a] is None else parts[a] + term
    weight = own(geo.inverse_y * geo.inverse_z)
    for a in range(2):
        sums[a : a + 1] = down(parts[a] * weight)

    forward, backward = wide_diagonals(diagonals, 1), wide_diagonals(diagonals, 2)
    fields = totals + [into_left[0], into_left[1], into_left[3], into_right[0], into_right[1], into_right[2]]
    flat = jnp.concatenate([solid(contract_y(v, forward)) for v in fields], axis=0)
    flat = contract_z(flat, upper, lower, 1)
    flat = [split(flat[k * 16 : k * 16 + 16]) for k in range(len(fields))]
    totals, into_left = flat[:4], {0: flat[4], 1: flat[5], 3: flat[6]}
    into_right = {0: flat[7], 1: flat[8], 2: flat[9]}

    def vector(p, i):
        return line_of(vectors, p * 8 + i, WIDE)

    def changes(element, total, close, distant):
        face, other = 7 * element, 7 - 7 * element
        crossed = cross * distant
        return [
            vector(face, i) * total - line_of(bend, element * 8 + i, WIDE) * close - vector(other, i) * crossed
            for i in range(8)
        ]

    moved = []
    for element, change in enumerate(
        (changes(0, totals[0], into_right[0], into_left[1]), changes(1, totals[1], into_left[1], into_right[0]))
    ):
        moved += [solid((split(spectrum[element * 8 + i]) + change[i]) * split(inverse[element * 8 + i])) for i in range(8)]
    for side in range(2):
        value, partial = (split(v) for v in read_second(sides[side][2 * FIRST_ROWS :]))
        near_element, far_element = 1 - side, side
        if side == 0:
            close = changes(1, totals[0], into_left[0], into_right[2])
            distant = changes(0, totals[2], into_right[2], into_left[0])
        else:
            close = changes(0, totals[1], into_right[1], into_left[3])
            distant = changes(1, totals[3], into_left[3], into_right[1])
        face = 7 * near_element
        close = [a * b for a, b in zip(close, divisors_of(geo, near[side][2], lam))]
        distant = [a * b for a, b in zip(distant, divisors_of(geo, far[side][2], lam))]
        value = value + weighted([vector(face, i) for i in range(8)], close)
        partial = partial + weighted([line_of(bend, near_element * 8 + i, WIDE) for i in range(8)], close)
        partial = partial + cross * weighted([vector(face, i) for i in range(8)], distant)
        moved += [solid(value), solid(partial)]

    back = contract_z(jnp.concatenate(moved, axis=0), upper, lower, 2)
    back = [contract_y(split(back[k * 16 : k * 16 + 16]), backward) for k in range(ROWS + 4)]
    solved = []
    for element in range(2):
        inside = back[element * 8 : element * 8 + 8]
        solved += [contract_x(inside, vectors, i) for i in range(8)]
    total = None
    for x in range(ROWS):
        term = own(solved[x]) * rows[x]
        total = term if total is None else total + term
    sums[2:3] = down(total)
    sums[3:8] = jnp.zeros((5, LANES), jnp.float32)
    solved = join_middle(solved)
    solved[0], solved[15] = solved[0] + back[16], solved[15] + back[18]
    for x in range(ROWS):
        local[x] = solid(geo.assemble(solved[x]))
    for side in range(2):
        beside[side] = solid(geo.assemble(back[17 + 2 * side]))


def image_kernel(
    local, factors, face_factors, beside, sums, fixed, stiffness, lines, upper, lower, diagonals,
    image, payload,
):
    geo = Geometry(WIDE)
    rows = [split(local[x]) for x in range(ROWS)]
    along_z = contract_z(jnp.concatenate([solid(v) for v in rows], axis=0), upper, lower, 0)
    scaled = [stored_factors(factors, e) for e in range(2)]
    stiff = wide_diagonals(diagonals, 0)
    applied = apply_rows(rows, along_z, scaled, stiffness, stiff)
    total, parts = None, [None, None]
    for x in range(ROWS):
        term = own(applied[x]) * own(rows[x])
        total = term if total is None else total + term
        for a in range(2):
            if GROUP_X[a][x] != 0.0:
                term = GROUP_X[a][x] * own(applied[x])
                parts[a] = term if parts[a] is None else parts[a] + term
    extra = [down(value * own(geo.keep)) for value in parts + [total]]
    for side, x, across in ((0, 0, 63), (1, 15, 0)):
        there = [split(face_factors[side, c]) for c in range(3)]
        other = there[0] * (split(beside[side]) + line_of(stiffness, across, WIDE) * rows[x])
        turned = split(along_z[x * 16 : x * 16 + 16])
        other = other + WEIGHTS[0] * (there[1] * contract_y(rows[x], stiff) + there[2] * turned)
        applied[x] = applied[x] + other
    applied = join_middle(applied)
    for x in range(ROWS):
        image[x] = solid(own(geo.assemble(applied[x])))
    zero = jnp.zeros((1, LANES), jnp.float32)
    table = jnp.concatenate(
        [sums[0:2], extra[0], extra[1], fixed[0:9], sums[2:3], extra[2], zero], axis=0
    )
    lane = iota((LANES, LANES), 1) & 7
    node = iota((LANES, LANES), 0)
    element, position = node >> 3, node & 7
    low, high = pick(position, LOW), pick(position, HIGH)
    columns = jnp.where(lane == (element >> 3), low, 0.0) + jnp.where(lane == ((element + 1) >> 3), high, 0.0)
    columns = jnp.where(lane == 3, 1.0, jnp.where(lane < 3, columns, 0.0))
    reduced = jnp.dot(table, columns, precision=EXACT, preferred_element_type=jnp.float32)
    mine = (iota((16, LANES), 1) >> 3) == iota((16, LANES), 0)
    row = jnp.sum(jnp.where(mine, reduced, 0.0), axis=0, keepdims=True) + fixed[16:17]
    block = jnp.concatenate([row, fixed[17:18]] * 4, axis=0)
    copies = payload.shape[0] // 8
    payload[...] = jnp.broadcast_to(block[None], (copies, 8, LANES)).reshape(copies * 8, LANES)


def lane_tables():
    one = np.zeros((8, LANES), np.float32)
    two = np.zeros((8, LANES), np.float32)
    top = np.zeros((8, LANES), np.float32)
    for a in range(2):
        for b in range(3):
            one[6, 8 * a + b], two[3 * a + b, 8 * a + b], top[0, 8 * a + b] = 1.0, 1.0, 1.0
            one[6, 8 * (2 + a) + b], two[3 * a + b, 8 * (2 + a) + b] = 2.0, 1.0
            top[1, 8 * (2 + a) + b] = 1.0
    for p, (a, other) in enumerate(PAIRS):
        for b in range(3):
            for c in range(3):
                at = 8 * (4 + 3 * p + b) + c
                one[3 * a + b, at] = 1.0 if a == other else 2.0
                two[3 * other + c, at] = 1.0
                top[1, at] = 1.0
    one[6, 8 * 13 + 3], two[6, 8 * 13 + 3], top[0, 8 * 13 + 3] = 1.0, 1.0, 1.0
    one[6, 8 * 14 + 3], two[6, 8 * 14 + 3], top[1, 8 * 14 + 3] = 1.0, 1.0, 1.0
    return np.stack([one, two, top])


def final_kernel(
    devices, spans, count, per,
    start, start_faces, residual, local, image, pieces, face_factors, waves, stiff_keep, lines, tables,
    gathered, given, new_solution, new_residual, values,
):
    rows = gathered[pl.ds(0, devices, stride=2), :]
    if given is None:
        spot = iota((devices, count), 1)
        hits = []
        rhs = [jnp.zeros((1, devices), jnp.float32) for _ in range(per)]
        owner = iota((devices, devices), 1)
        for k in range(6):
            label = rows[:, 8 * k + 4 : 8 * k + 5].astype(jnp.int32)
            at = 8 * (k // 3) + k % 3
            value = rows[:, at : at + 1]
            hits.append(spot == label)
            for q in range(per):
                chosen = jnp.where(owner * per + q == label, value, 0.0)
                rhs[q] = rhs[q] + jnp.sum(chosen, axis=0, keepdims=True)
        inverse = gathered[pl.ds(1, devices, stride=2), :]
        coarse = None
        for q in range(per):
            term = jnp.dot(
                rhs[q], inverse[:, q * count : q * count + count], precision=EXACT,
                preferred_element_type=jnp.float32,
            )
            coarse = term if coarse is None else coarse + term
        columns = [jnp.sum(jnp.where(hit, coarse, 0.0), axis=1, keepdims=True) for hit in hits]
        kept = jnp.zeros((devices, LANES), jnp.float32)
        for k in range(6):
            kept = jnp.where(iota((devices, LANES), 1) == k, columns[k], kept)
        values[...] = kept
    else:
        columns = [given[:, k : k + 1] for k in range(6)]
        values[...] = given[...]
    one, two = tables[0, 6:7, :], tables[1, 6:7, :]
    for k in range(6):
        one = one + columns[k] * tables[0, k : k + 1, :]
        two = two + columns[k] * tables[1, k : k + 1, :]
    product = jnp.sum(rows * one * two, axis=0, keepdims=True)
    numerator = jnp.sum(product * tables[2, 0:1, :], axis=1, keepdims=True)
    denominator = jnp.sum(product * tables[2, 1:2, :], axis=1, keepdims=True)
    alpha = numerator / denominator

    gx, gz = lax.axis_index("gx"), lax.axis_index("gz")
    before_x = lax.rem(gx + devices // spans - 1, devices // spans)
    before_z = lax.rem(gz + spans - 1, spans)
    here = values[pl.ds(gx * spans + gz, 1), :]
    behind = values[pl.ds(gx * spans + before_z, 1), :]
    aside = values[pl.ds(before_x * spans + gz, 1), :]
    corner = values[pl.ds(before_x * spans + before_z, 1), :]

    def four(line, back, a):
        return [back[:, 3 * a + 1 : 3 * a + 2]] + [line[:, 3 * a + b : 3 * a + b + 1] for b in range(3)]

    def mix(numbers, ref):
        total = numbers[0] * ref[0]
        for b in range(1, 4):
            total = total + numbers[b] * ref[b]
        return total

    near, right, left = four(here, behind, 0), four(here, behind, 1), four(aside, corner, 0)
    whole = [mix(near, pieces.at[0, k]) for k in range(2)]
    low = [mix(near, pieces.at[1, k]) for k in range(2)]
    high = [mix(right, pieces.at[1, k]) for k in range(2)]

    def stiff(line, i):
        return lines[line, i : i + 1, :]

    extra = [stiff(0, i) * whole[0] + WEIGHTS[i] * whole[1] for i in range(8)]
    for i in range(8):
        extra.append(
            stiff(1, i) * low[0] + stiff(2, i) * high[0] + WEIGHTS[i] * (LOW[i] * low[1] + HIGH[i] * high[1])
        )
    extra = join_middle(extra)
    geo = Geometry(WIDE)

    def line(numbers, at):
        total = numbers[0] * waves[at : at + 1, :]
        for b in range(1, 4):
            total = total + numbers[b] * waves[at + b : at + b + 1, :]
        return total

    def wide_stiff(k, i):
        return jnp.concatenate([stiff(k, i)] * (WIDE // LANES), axis=1)

    def beyond(side, stiff_x, plain, turned):
        fx, fy, fz = (split(face_factors[side, c]) for c in range(3))
        value = fx * geo.keep * stiff_x[None]
        value = value + WEIGHTS[0] * (fy * split(stiff_keep[...]) * plain[None] + fz * geo.keep * turned[None])
        return solid(own(geo.assemble(value)))

    wave_near, wave_right = line(near, 0), line(right, 0)
    across = wide_stiff(1, 7) * line(left, 0) + wide_stiff(2, 7) * wave_near
    extra[0] = extra[0] + beyond(0, across, wave_near, line(near, 4))
    extra[15] = extra[15] + beyond(1, wide_stiff(0, 0) * wave_right, wave_right, line(right, 4))
    keep = solid(own(geo.keep))
    line_near, line_right = wave_near[:, :LANES], wave_right[:, :LANES]
    for x in range(ROWS):
        begin = start_faces[x // 15] if x in (0, 15) else start[x]
        mine = local[x, :, :LANES]
        new_residual[x] = residual[x] - alpha * (image[x] + extra[x])
        coarse_line = GROUP_X[0][x] * line_near
        if GROUP_X[1][x] != 0.0:
            coarse_line = coarse_line + GROUP_X[1][x] * line_right
        new_solution[x] = begin + alpha * (mine + keep * coarse_line)


VMEM = pl.BlockSpec(memory_space=pltpu.VMEM)
SMEM = pl.BlockSpec(memory_space=pltpu.SMEM)
FAR = pl.BlockSpec(memory_space=pltpu.HBM)


def call(kernel, shapes, specs, name, scratch=()):
    def leaf(shape):
        kind = jnp.float32
        if shape[0] == "half":
            shape, kind = shape[1:], jnp.bfloat16
        return jax.ShapeDtypeStruct(shape, kind)

    return pl.pallas_call(
        kernel,
        out_shape=[leaf(shape) for shape in shapes],
        in_specs=specs,
        out_specs=[VMEM] * len(shapes),
        scratch_shapes=list(scratch),
        compiler_params=pltpu.CompilerParams(vmem_limit_bytes=16 * 1024 * 1024),
        name=name,
    )


def swap(first, second, axis):
    size = lax.axis_size(axis)
    odd = [(i, (i + 1) % size) for i in range(1, size, 2)]
    one = lax.ppermute(first, axis, [(i, i ^ 1) for i in range(size)])
    two = lax.ppermute(second, axis, odd + [(b, a) for a, b in odd])
    return one, two


def second_neighbours(common, axis):
    size = lax.axis_size(axis)
    if size == 4:
        return lax.ppermute(common, axis, [(i, i ^ 2) for i in range(size)])
    left = lax.ppermute(common[:FIRST_ROWS], axis, [(i, (i - 2) % size) for i in range(size)])
    right = lax.ppermute(common[FIRST_ROWS:], axis, [(i, (i + 2) % size) for i in range(size)])
    return jnp.concatenate([left, right], axis=0)


def body(
    source, previous, coefficients, stiffness, fdm_vectors, fdm_values, coarse_inverse, vertex_map
):
    assert source.shape == (ROWS, ROWS, LANES)
    spans = lax.axis_size("gz")
    devices = lax.axis_size("gx") * spans
    per, count = coarse_inverse.shape
    small = per * count <= LANES
    block, wide, face = (ROWS, ROWS, LANES), (ROWS, ROWS, WIDE), (ROWS, LANES)
    halo = (13, 8, LANES)

    first, second, own_metrics, source, previous = call(
        pack_kernel,
        [halo, halo, face, block, block],
        [FAR] * 3,
        "pack",
        [pltpu.VMEM(coefficients.shape, jnp.float32), pltpu.VMEM((16, 16), jnp.float32), pltpu.SemaphoreType.DMA((3,))],
    )(*(pltpu.with_memory_space_constraint(v, pltpu.HBM) for v in (source, previous, coefficients)))
    first, second = swap(first, second, "gz")
    upper, lower, diagonals, stiff, vectors, bend, lam, lines, fixed, tables = call(
        functools.partial(prepare_kernel, small),
        [
            ("half", 3, WIDE, WIDE), ("half", 3, WIDE, LANES), (3, 8, 8, LANES),
            (64, LANES), (64, LANES), (16, LANES), (2, 8, LANES), (3, 8, LANES), (24, LANES), (3, 8, LANES),
        ],
        [VMEM] * 3 + [SMEM] * 2 + [VMEM if small else FAR, VMEM],
        "prepare",
    )(own_metrics, stiffness, fdm_vectors, fdm_values, vertex_map, coarse_inverse, jnp.asarray(lane_tables()))

    message = (2 * FIRST_ROWS + SECOND_ROWS, LANES)
    start, known, factors, halves, remainders, spectrum, inverse, side_a, side_b, common = call(
        start_kernel,
        [
            block, wide, (3, 2, ROWS, WIDE), (2, ROWS, WIDE), (2, ROWS, WIDE), wide, wide,
            message, message, (2 * FIRST_ROWS, LANES),
        ],
        [VMEM] * 12,
        "start",
        [pltpu.VMEM((16, WIDE), jnp.float32)],
    )(source, previous, own_metrics, first, second, stiff, vectors, bend, lam, upper, lower, diagonals)
    beyond = second_neighbours(common, "gx")
    side_a, side_b = swap(side_a, side_b, "gx")
    pieces, waves, stiff_keep = call(
        ready_kernel, [(2, 2, 4, ROWS, LANES), (8, WIDE), (ROWS, WIDE)], [VMEM] * 5, "ready"
    )(factors, stiff, lines, upper, lower)

    start_faces, residual, local, beside, face_factors, sums = call(
        solve_kernel,
        [(2, ROWS, LANES), block, wide, (2, ROWS, WIDE), (2, 3, ROWS, WIDE), (8, LANES)],
        [VMEM] * 17,
        "solve",
    )(
        known, factors, halves, remainders, spectrum, inverse, side_a, side_b, beyond, waves,
        stiff, vectors, bend, lam, upper, lower, diagonals,
    )
    image, payload = call(image_kernel, [block, (2 * devices, LANES)], [VMEM] * 11, "image")(
        local, factors, face_factors, beside, sums, fixed, stiff, lines, upper, lower, diagonals
    )
    gathered = lax.all_to_all(payload.reshape(devices, 2, LANES), ("gx", "gz"), 0, 0)
    gathered = gathered.reshape(2 * devices, LANES)

    operands = [
        start, start_faces, residual, local, image, pieces, face_factors, waves, stiff_keep, lines,
        tables, gathered,
    ]
    finish = functools.partial(final_kernel, devices, spans, count, per)
    if small:

        def kernel(*refs):
            finish(*refs[:12], None, *refs[12:])

    else:
        kernel = finish
        rows = gathered[0::2]
        labels = rows[:, jnp.array([8 * k + 4 for k in range(6)])].astype(jnp.int32)
        parts = rows[:, jnp.array([8 * (k // 3) + k % 3 for k in range(6)])]
        rhs = jnp.zeros((count,), jnp.float32).at[labels.reshape(-1)].add(parts.reshape(-1))
        mine = jnp.dot(coarse_inverse, rhs, precision=EXACT)
        coarse = lax.all_gather(mine, ("gx", "gz"), axis=0, tiled=True)
        operands.append(jnp.pad(coarse[labels], ((0, 0), (0, LANES - 6))))
    return tuple(
        call(kernel, [block, block], [VMEM] * len(operands), "finish", [pltpu.VMEM((devices, LANES), jnp.float32)])(
            *operands
        )
    )


def solution(mesh):
    placed = (
        P("gx", None, "gz"),
        P("gx", None, "gz"),
        P(None, "gx", None, "gz"),
        P(),
        P(),
        P(),
        P(("gx", "gz"), None),
        P(None, "gx", None, "gz"),
    )
    return jax.shard_map(
        body,
        mesh=mesh,
        in_specs=placed,
        out_specs=(P("gx", None, "gz"), P("gx", None, "gz")),
        check_vma=False,
    )
```

```python
import functools

import jax
import jax.numpy as jnp
import numpy as np
from jax import lax
from jax.experimental import pallas as pl
from jax.experimental.pallas import tpu as pltpu
from jax.sharding import PartitionSpec as P

POINTS = [
    -1.0,
    -0.8717401485096066,
    -0.5917001814331423,
    -0.2092992179024789,
    0.2092992179024789,
    0.5917001814331423,
    0.8717401485096066,
    1.0,
]
WEIGHTS = [
    0.03571428571428571,
    0.21070422714350603,
    0.34112269248350435,
    0.4124587946587038,
    0.4124587946587038,
    0.34112269248350435,
    0.21070422714350603,
    0.03571428571428571,
]
ONES = [1.0] * 8
LOW = [(1.0 - s) / 2.0 for s in POINTS]
HIGH = [(1.0 + s) / 2.0 for s in POINTS]
EXACT = lax.Precision.HIGHEST

ROWS = 16
LANES = 128
WIDE = 256
HALO = 32
DEEP, SHALLOW = 25, 17
SLOT = DEEP + SHALLOW
FIRST_FIELDS = ((0, 24), (41, 17), (75, 17))
SECOND_FIELDS = ((0, 16), (32, 16), (64, 16), (96, 16))
FAR_FIELDS = ((0, 24), (48, 24))
FIRST_ROWS, FAR_ROWS, SECOND_ROWS = 56, 32, 40
PAIRS = ((0, 0), (0, 1), (1, 1))
GROUP_X = (ONES + LOW, [0.0] * 8 + HIGH)
INVERSE_X = [0.5] + [1.0] * 6 + [0.5] + [0.5] + [1.0] * 6 + [0.5]


def iota(shape, dim):
    return lax.broadcasted_iota(jnp.int32, shape, dim)


def pick(index, values):
    result = jnp.full(index.shape, values[0], jnp.float32)
    for i in range(1, 8):
        result = jnp.where(index == i, values[i], result)
    return result


def even_index(axis):
    return lax.rem(lax.axis_index(axis), 2) == 0


class Geometry:
    def __init__(self, lanes):
        shape = (2, 8, lanes)
        self.element_y, self.row, lane = iota(shape, 0), iota(shape, 1), iota(shape, 2)
        self.position = lane & 7
        self.first = self.position == 0
        self.last = self.position == 7
        self.edge = self.first | self.last
        self.weight_y = pick(self.row, WEIGHTS)
        self.weight_z = pick(self.position, WEIGHTS)
        self.inverse_z = jnp.where(self.edge, 0.5, 1.0)
        self.wall = (self.element_y == 1) & (self.row == 7)
        inner = ((self.element_y == 0) & (self.row == 7)) | ((self.element_y == 1) & (self.row == 0))
        self.inverse_y = jnp.where(inner, 0.5, 1.0)
        self.keep = jnp.where(self.wall, 0.0, 1.0)
        self.lanes = lanes

    def pair_y(self, v):
        lower, upper = v[0], v[1]
        row = self.row[0]
        up = jnp.where(row == 7, pltpu.roll(upper, 7, 0), 0.0)
        down = jnp.where(row == 0, pltpu.roll(lower, 1, 0), 0.0)
        return jnp.stack([lower + up, upper + down])

    def pair_z(self, v):
        flat = v.reshape(16, self.lanes)
        after = pltpu.roll(flat, self.lanes - 1, 1).reshape(v.shape)
        before = pltpu.roll(flat, 1, 1).reshape(v.shape)
        return v + jnp.where(self.edge, jnp.where(self.last, after, before), 0.0)

    def pair(self, v):
        return self.pair_z(self.pair_y(v))

    def assemble(self, v):
        return self.pair(v) * self.keep


def solid(v):
    return v.reshape(ROWS, v.shape[-1])


def split(v):
    return v.reshape(2, 8, v.shape[-1])


def own(v):
    return v[..., :LANES]


def down(v):
    return jnp.sum(v.reshape(ROWS, LANES), axis=0, keepdims=True)


def line_of(ref, at, lanes):
    row = ref[at : at + 1, :]
    return jnp.concatenate([row] * (lanes // LANES), axis=1)[None]


def weighted(factors, rows):
    total = None
    for factor, row in zip(factors, rows):
        total = factor * row if total is None else total + factor * row
    return total


def divisors_of(geo, c, lam):
    lam_y = jnp.concatenate([lam[0]] * (WIDE // LANES), axis=1)[None]
    lam_z = jnp.concatenate([lam[1]] * (WIDE // LANES), axis=1)[None]
    base = c[1] * lam_y + c[2] * lam_z
    return [1.0 / (c[0] * line_of(lam.at[0], i, WIDE) + base) for i in range(8)]


def contract_x(rows, table, i, transpose=False):
    total = None
    for p in range(8):
        factor = line_of(table, p * 8 + i if transpose else i * 8 + p, WIDE)
        term = factor * rows[p]
        total = term if total is None else total + term
    return total


def contract_y(v, diagonals):
    def moved(value, rows):
        return jnp.stack([pltpu.roll(value[e], 8 - rows, 0) for e in range(2)])

    shifted = [v] + [moved(v, d) for d in range(1, 4)]
    return weighted(diagonals[:4], shifted) + moved(weighted(diagonals[4:], shifted), 4)


def thirds(v):
    high = v.astype(jnp.bfloat16)
    rest = v - high.astype(jnp.float32)
    middle = rest.astype(jnp.bfloat16)
    return high, middle, (rest - middle.astype(jnp.float32)).astype(jnp.bfloat16)


def contract_z(flat, upper, lower, which):
    pieces = []
    for at in range(0, flat.shape[1], LANES):
        high, middle, low = thirds(flat[:, at : at + LANES])
        one = jnp.dot(
            jnp.concatenate([high, middle], axis=1), upper[which], preferred_element_type=jnp.float32
        )
        two = jnp.dot(jnp.concatenate([low, high], axis=1), lower[which], preferred_element_type=jnp.float32)
        pieces.append(one[:, :LANES] + (one[:, LANES:] + two))
    return pieces[0] if len(pieces) == 1 else jnp.concatenate(pieces, axis=1)


def wide_diagonals(ref, which):
    return [jnp.concatenate([ref[which, d]] * (WIDE // LANES), axis=1)[None] for d in range(8)]


def metric(ref, component, element):
    at = (component * 2 + element) * 2
    return jnp.stack([jnp.broadcast_to(ref[at + e : at + e + 1, :], (8, WIDE)) for e in range(2)])


def scaled_metrics(geo, c):
    return c[0] * geo.weight_y * geo.weight_z, c[1] * geo.weight_z, c[2] * geo.weight_y


def stored_factors(ref, element):
    return [split(ref[c, element]) for c in range(3)]


def apply_rows(rows, along_z, factors, stiffness, diagonals):
    result = []
    for element in range(2):
        factor_x, factor_y, factor_z = factors[element]
        inside = rows[element * 8 : element * 8 + 8]
        for i in range(8):
            x = element * 8 + i
            term_y = factor_y * contract_y(inside[i], diagonals)
            term_z = factor_z * split(along_z[x * 16 : x * 16 + 16])
            result.append(factor_x * contract_x(inside, stiffness, i) + WEIGHTS[i] * (term_y + term_z))
    return result


def join_middle(rows):
    middle = rows[7] + rows[8]
    return rows[:7] + [middle, middle] + rows[9:]


def fold(parts, fields):
    lane = iota((8, LANES), 1)
    result = parts[0]
    for part, (offset, half) in list(zip(parts, fields))[1:]:
        taken = ((lane - offset + half) & (LANES - 1)) < 2 * half
        result = jnp.where(taken, pltpu.roll(part, offset, 1), result)
    return result


def unfold(packed, field, fill=0.0):
    offset, half = field
    lane = iota((8, LANES), 1)
    moved = pltpu.roll(packed, LANES - offset, 1) if offset else packed
    return jnp.where(((lane + half) & (LANES - 1)) < 2 * half, moved, fill)


def widen(tile, pieces):
    return jnp.concatenate([tile, jnp.concatenate(pieces, axis=0)], axis=1)


def group_lanes(lanes, group):
    lane = iota((1, lanes), 1)
    signed = jnp.where(lane < lanes // 2 + lanes // 4, lane, lane - lanes) if lanes > LANES else lane
    element, position = signed >> 3, lane & 7
    low, high = pick(position, LOW), pick(position, HIGH)
    here = jnp.where((element >> 3) == group, low, 0.0)
    return here + jnp.where(((element + 1) >> 3) == group, high, 0.0)


def pack_kernel(source, previous, coefficients, first, second, elements, near_source, near_previous, raw, ready):
    copies = [
        pltpu.make_async_copy(source, near_source, ready.at[0]),
        pltpu.make_async_copy(previous, near_previous, ready.at[1]),
        pltpu.make_async_copy(coefficients, raw, ready.at[2]),
    ]
    for copy in copies:
        copy.start()
    even = even_index("gz")
    elements[...] = jnp.zeros_like(elements)
    for copy in copies:
        copy.wait()
    for c in range(3):
        for element in range(2):
            at = (c * 2 + element) * 2
            elements[at : at + 2, 0:16] = raw[c, element]
    slot = iota((8, LANES), 1)
    for to_right, out in ((even, first), (jnp.logical_not(even), second)):
        for tile in range(11):
            packed = None
            for k in range(3):
                n = 3 * tile + k
                if n >= 2 * ROWS:
                    break
                for ref, width, at in ((near_previous, DEEP, SLOT * k), (near_source, SHALLOW, SLOT * k + DEEP)):
                    shift = jnp.where(to_right, (at + width) % LANES, at)
                    moved = pltpu.roll(ref[n // 2, 8 * (n % 2) : 8 * (n % 2) + 8], shift, 1)
                    packed = moved if packed is None else jnp.where(slot >= at, moved, packed)
            out[tile] = packed
        out[11] = elements[:8]
        out[12] = elements[8:]


def lanes_of(elements):
    widen = (iota((16, LANES), 0) == (iota((16, LANES), 1) >> 3)).astype(jnp.float32)
    return jnp.dot(elements[:, 0:16], widen, precision=EXACT, preferred_element_type=jnp.float32)


def prepare_kernel(
    with_coarse, elements, stiffness, vectors, eigen, labels, coarse, tables,
    metrics, upper, lower, diagonals, stiff_table, vector_table, bend, lam, lines, fixed, near_tables,
):
    near_tables[...] = tables[...]
    metrics[...] = lanes_of(elements[...])
    repeat = (iota((LANES, 8), 0) & 7 == iota((LANES, 8), 1)).astype(jnp.float32)
    same = (iota((LANES, LANES), 0) >> 3) == (iota((LANES, LANES), 1) >> 3)
    unit = (iota((8, 8), 0) == iota((8, 8), 1)).astype(jnp.float32)
    row, column = iota((8, 8), 0), iota((8, 8), 1)

    def dot(a, b, dims):
        return lax.dot_general(a, b, (dims, ((), ())), precision=EXACT, preferred_element_type=jnp.float32)

    def put_block(at, matrix):
        half = dot(repeat, matrix, ((1,), (0,)))
        put_thirds(at, jnp.where(same, dot(half, repeat, ((1,), (1,))), 0.0))

    def put_thirds(at, block):
        high, middle, low = thirds(block)
        both = jnp.concatenate([high, middle], axis=1)
        upper[at] = jnp.concatenate([both, both], axis=0)
        lower[at] = jnp.concatenate([high, low], axis=0)

    def put_diagonals(at, matrix):
        turned = jnp.concatenate([matrix[4:], matrix[:4]], axis=0)
        for d in range(8):
            chosen = jnp.where(column == ((row + d % 4) & 7), matrix if d < 4 else turned, 0.0)
            diagonals[at, d] = jnp.broadcast_to(jnp.sum(chosen, axis=1, keepdims=True), (8, LANES))

    def put_table(out, matrix):
        tall = (iota((64, 8), 0) >> 3 == iota((64, 8), 1)).astype(jnp.float32)
        chosen = jnp.where(iota((64, 8), 0) & 7 == iota((64, 8), 1), dot(tall, matrix, ((1,), (0,))), 0.0)
        out[...] = jnp.broadcast_to(jnp.sum(chosen, axis=1, keepdims=True), (64, LANES))

    lane = iota((LANES, LANES), 1) & 7
    node = iota((LANES, LANES), 0)
    element, position = node >> 3, node & 7
    low, high = pick(position, LOW), pick(position, HIGH)
    columns = jnp.where(lane == (element >> 3), low, 0.0) + jnp.where(lane == ((element + 1) >> 3), high, 0.0)
    columns = jnp.where(lane == 3, 1.0, jnp.where(lane < 3, columns, 0.0))
    put_thirds(3, columns)
    k, s = stiffness[...], vectors[...]
    k_turned, s_turned = dot(k, unit, ((0,), (0,))), dot(s, unit, ((0,), (0,)))
    for at, matrix in enumerate((k_turned, s, s_turned)):
        put_block(at, matrix)
    for at, matrix in enumerate((k, s_turned, s)):
        put_diagonals(at, matrix)
    put_table(stiff_table, k)
    put_table(vector_table, s)
    for side, near in ((0, 0), (1, 7)):
        chosen = jnp.where(column == near, 0.0, s_turned * k[near : near + 1, :])
        total = jnp.sum(chosen, axis=1, keepdims=True)
        bend[8 * side : 8 * side + 8] = jnp.broadcast_to(total, (8, LANES))
    values = [eigen[i] for i in range(8)]
    lam[0] = pick(iota((8, LANES), 0), values)
    lam[1] = pick(iota((8, LANES), 1) & 7, values)
    stiff_lines = []
    for at, line in enumerate((ONES, LOW, HIGH)):
        total = jnp.sum(k * pick(column, line), axis=1, keepdims=True)
        stiff_lines.append(jnp.broadcast_to(total, (8, LANES)))
        lines[at] = stiff_lines[at]

    groups = [group_lanes(LANES, b) for b in range(3)]
    stacked = jnp.concatenate(groups + [jnp.zeros((13, LANES), jnp.float32)], axis=0)
    stiff_z = contract_z(stacked, upper, lower, 0)
    weight_z = pick(iota((1, LANES), 1) & 7, WEIGHTS)
    node = iota((8, LANES), 0)
    mass_y = [sum(WEIGHTS), sum(WEIGHTS[:7])]
    last = jnp.broadcast_to(k[:, 7:8], (8, LANES))
    inner = jnp.where(node == 7, 0.0, stiff_lines[0] - last)
    stiff_y = [jnp.sum(v, axis=0, keepdims=True) for v in (stiff_lines[0], inner)]
    at = 0
    for a, b in PAIRS:
        across, along = jnp.zeros((1, LANES), jnp.float32), jnp.zeros((1, LANES), jnp.float32)
        for element in range(2):
            fa = GROUP_X[a][element * 8 : element * 8 + 8]
            fb = GROUP_X[b][element * 8 : element * 8 + 8]
            if not (any(fa) and any(fb)):
                continue
            mass_x = sum(w * p * q for w, p, q in zip(WEIGHTS, fa, fb))
            applied = stiff_lines[0 if fb == ONES else 1 + b]
            stiff_x = jnp.sum(applied * pick(node, fa), axis=0, keepdims=True)
            for e in range(2):
                cx, cy, cz = (metrics[(c * 2 + element) * 2 + e, :].reshape(1, LANES) for c in range(3))
                across = across + cx * (stiff_x * mass_y[e]) + cy * (stiff_y[e] * mass_x)
                along = along + cz * (mass_x * mass_y[e])
        across = across * weight_z
        for b in range(3):
            fixed[at : at + 1] = across * groups[b] + along * stiff_z[b : b + 1]
            at += 1
    fixed[9:16] = jnp.zeros((7, LANES), jnp.float32)
    place = iota((1, LANES), 1)
    numbers = jnp.zeros((1, LANES), jnp.float32)
    for a in range(2):
        for b in range(3):
            corner, x, z = 4 * a + (b == 2), a, (0, 8, 15)[b]
            number = labels[corner, x, 0, z].astype(jnp.float32)
            numbers = jnp.where(place == 8 * (3 * a + b) + 4, number, numbers)
    fixed[16:17] = numbers
    below = jnp.zeros((1, LANES), jnp.float32)
    if with_coarse:
        per, count = coarse.shape
        below = [coarse[i : i + 1, :] for i in range(per)]
        if per * count < LANES:
            below.append(jnp.zeros((1, LANES - per * count), jnp.float32))
        below = jnp.concatenate(below, axis=1)
    fixed[17:18] = below
    fixed[18:24] = jnp.zeros((6, LANES), jnp.float32)


def start_kernel(
    source, previous, own_metrics, first, second, stiffness, vectors, bend, lam, upper, lower, diagonals,
    start, known, factors, halves, remainders, spectrum, inverse, message_a, message_b, common, metrics,
):
    even = even_index("gz")
    lane = iota((8, LANES), 1)
    one, two = first[...], second[...]
    from_right, from_left = jnp.where(even, one, two), jnp.where(even, two, one)

    def beyond(n, at, width):
        at = at + SLOT * (n % 3)
        right, left = from_right[n // 3], from_left[n // 3]
        if at:
            right = pltpu.roll(right, LANES - at, 1)
        left = pltpu.roll(left, (LANES - width - at) % LANES, 1)
        return jnp.where(lane < width, right, jnp.where(lane >= LANES - width, left, 0.0))

    def wide(ref, x, at, width):
        return split(widen(ref[x], [beyond(2 * x + e, at, width) for e in range(2)]))

    geo = Geometry(WIDE)
    metrics[:, :LANES] = own_metrics[...]
    around = lanes_of(jnp.concatenate([from_right[11], from_right[12], from_left[11], from_left[12]], axis=0))
    wide_lane = iota((16, LANES), 1)
    metrics[:, LANES:] = jnp.where(
        wide_lane < HALO, around[:16], jnp.where(wide_lane >= LANES - HALO, around[16:], 1.0)
    )
    factor = geo.keep * geo.inverse_y * geo.inverse_z
    rows = [geo.pair(wide(previous, x, 0, DEEP)) * (factor * INVERSE_X[x]) for x in range(ROWS)]
    rows = join_middle(rows)
    faces = (rows[0], rows[15])
    for x in range(ROWS):
        start[x] = solid(own(rows[x]))
    along_z = contract_z(jnp.concatenate([solid(v) for v in rows], axis=0), upper, lower, 0)
    scaled = [scaled_metrics(geo, [metric(metrics, c, e) for c in range(3)]) for e in range(2)]
    for e in range(2):
        for c in range(3):
            factors[c, e] = solid(scaled[e][c])
    applied = apply_rows(rows, along_z, scaled, stiffness, wide_diagonals(diagonals, 0))
    rest = [wide(source, x, DEEP, SHALLOW) - applied[x] for x in range(ROWS)]
    halves[0], halves[1] = solid(faces[0]), solid(faces[1])
    remainders[0], remainders[1] = solid(rest[0]), solid(rest[15])
    coefficients = [
        jnp.concatenate(
            [metrics[(c * 2 + side) * 2 : (c * 2 + side) * 2 + 2] for c in range(3)] + [jnp.ones((2, WIDE), jnp.float32)],
            axis=0,
        )
        for side in range(2)
    ]
    messages, distant = [], []
    for side, x in ((0, 0), (1, 15)):
        half, value = solid(faces[side]), solid(rest[x])
        rows, others = coefficients[side], coefficients[1 - side]
        lower_fold = fold([half[:8, LANES:], value[:8, LANES:], rows[:, LANES:]], FIRST_FIELDS)
        upper_fold = fold([half[8:, LANES:], value[8:, LANES:], others[:, LANES:]], FIRST_FIELDS)
        parts = [half[:, :LANES], value[:, :LANES], lower_fold, upper_fold, rows[:, :LANES]]
        messages.append(jnp.concatenate(parts, axis=0))
        folded = fold([half[:8, LANES:], half[8:, LANES:]], FAR_FIELDS)
        distant.append(jnp.concatenate([half[:, :LANES], folded, rows[:, :LANES]], axis=0))
    common[...] = jnp.concatenate(messages, axis=0)
    both = [jnp.concatenate([messages[side], distant[1 - side]], axis=0) for side in range(2)]

    rest = [geo.assemble(v) for v in join_middle(rest)]
    forward = wide_diagonals(diagonals, 1)
    moved = []
    for element in range(2):
        inside = rest[element * 8 : element * 8 + 8]
        moved += [solid(contract_y(contract_x(inside, vectors, i, True), forward)) for i in range(8)]
    for x in range(ROWS):
        known[x] = solid(rest[x])
    transformed = contract_z(jnp.concatenate(moved, axis=0), upper, lower, 1)
    damped = []
    for element in range(2):
        divisors = divisors_of(geo, [metric(metrics, c, element) for c in range(3)], lam)
        for i in range(8):
            x = element * 8 + i
            value = split(transformed[x * 16 : x * 16 + 16])
            spectrum[x], inverse[x] = solid(value), solid(divisors[i])
            damped.append(value * divisors[i])
    messages = []
    for side, near in ((0, 0), (1, 7)):
        inside, across = damped[side * 8 : side * 8 + 8], damped[8 - side * 8 : 16 - side * 8]
        value = contract_x(inside, vectors, near)
        beside = weighted([line_of(bend, side * 8 + i, WIDE) for i in range(8)], inside)
        beside = beside + line_of(stiffness, near * 8 + 7 - near, WIDE) * contract_x(across, vectors, near)
        value, beside = solid(value), solid(beside)
        folded = fold([v[at : at + 8, LANES:] for v in (value, beside) for at in (0, 8)], SECOND_FIELDS)
        messages.append(jnp.concatenate([value[:, :LANES], beside[:, :LANES], folded], axis=0))
    even_x = even_index("gx")
    both = [jnp.concatenate([both[side], messages[side]], axis=0) for side in range(2)]
    message_a[...] = jnp.where(even_x, both[1], both[0])
    message_b[...] = jnp.where(even_x, both[0], both[1])


def both_sides(even, a, b):
    one, two = a[...], b[...]
    return jnp.where(even, two, one), jnp.where(even, one, two)


def read_first(message):
    lower_fold, upper_fold = message[32:40], message[40:48]
    half, value = (
        widen(message[16 * k : 16 * k + 16], [unfold(lower_fold, FIRST_FIELDS[k]), unfold(upper_fold, FIRST_FIELDS[k])])
        for k in range(2)
    )
    return split(half), split(value), spread_metrics(message[48:56], lower_fold)


def spread_metrics(tile, folded):
    rows = widen(tile, [unfold(folded, FIRST_FIELDS[2], 1.0)])
    return [
        jnp.stack([jnp.broadcast_to(rows[2 * c + e : 2 * c + e + 1], (8, WIDE)) for e in range(2)]) for c in range(3)
    ]


def read_far(message):
    far = message[FIRST_ROWS : FIRST_ROWS + FAR_ROWS]
    half = widen(far[0:16], [unfold(far[16:24], field) for field in FAR_FIELDS])
    return split(half), spread_metrics(far[24:32], message[40:48])


def read_second(message):
    pieces = [unfold(message[32:40], field) for field in SECOND_FIELDS]
    return widen(message[0:16], pieces[:2]), widen(message[16:32], pieces[2:])


def coarse_pieces(geo, factors, stiff_keep, functions, stiff_functions):
    factor_x, factor_y, factor_z = factors
    kept_x, kept_y, kept_z = factor_x * geo.keep, factor_y * stiff_keep, factor_z * geo.keep
    result = []
    for plain, turned in zip(functions, stiff_functions):
        result.append(
            (geo.assemble(kept_x * plain[None]), geo.assemble(kept_y * plain[None] + kept_z * turned[None]))
        )
    return result


def wide_functions(upper, lower):
    functions = [group_lanes(WIDE, b) for b in (-1, 0, 1, 2)]
    stacked = jnp.concatenate(functions + [jnp.zeros((12, WIDE), jnp.float32)], axis=0)
    turned = contract_z(stacked, upper, lower, 0)
    return functions, [turned[b : b + 1] for b in range(4)]


def kept_stiffness(geo, lines, stiffness):
    row = iota((8, LANES), 0)
    last = jnp.zeros((8, LANES), jnp.float32)
    for j in range(8):
        last = jnp.where(row == j, stiffness[j * 8 + 7 : j * 8 + 8, :], last)
    both = jnp.stack([lines[0], lines[0] - last])
    return jnp.concatenate([both] * (WIDE // LANES), axis=2)


def ready_kernel(factors, stiffness, lines, upper, lower, pieces, waves, stiff_keep):
    geo = Geometry(WIDE)
    functions, turned = wide_functions(upper, lower)
    for b in range(4):
        waves[b : b + 1], waves[4 + b : 5 + b] = functions[b], turned[b]
    along_y = kept_stiffness(geo, lines, stiffness)
    stiff_keep[...] = solid(along_y)
    for element in range(2):
        made = coarse_pieces(geo, stored_factors(factors, element), along_y, functions, turned)
        for b in range(4):
            for k in range(2):
                pieces[element, k, b] = solid(own(made[b][k]))


def solve_kernel(
    known, factors, halves, remainders, spectrum, inverse, got_a, got_b, got_c, _,
    stiffness, vectors, bend, lam, upper, lower, diagonals,
    start_faces, residual, local, beside, face_factors, sums,
):
    even = even_index("gx")
    geo = Geometry(WIDE)
    sides = both_sides(even, got_a, got_b)
    beyond = got_c[...]
    near = [read_first(side) for side in sides]
    far = [read_far(side) for side in sides]
    last = [read_first(beyond[FIRST_ROWS:]), read_first(beyond[:FIRST_ROWS])]
    mine = [stored_factors(factors, e) for e in range(2)]
    near_factors, far_factors, last_factors = (
        [scaled_metrics(geo, v[-1]) for v in group] for group in (near, far, last)
    )
    for side in range(2):
        for c in range(3):
            face_factors[side, c] = solid(near_factors[side][c])
    half = [split(halves[side]) for side in range(2)]
    remain = [split(remainders[side]) for side in range(2)]
    left_half = [near[0][0], half[1], last[0][0], far[1][0]]
    right_half = [half[0], near[1][0], far[0][0], last[1][0]]
    left_factors = [near_factors[0], mine[1], last_factors[0], far_factors[1]]
    right_factors = [mine[0], near_factors[1], far_factors[0], last_factors[1]]
    stiff = wide_diagonals(diagonals, 0)
    along_z = contract_z(jnp.concatenate([solid(v) for v in left_half + right_half], axis=0), upper, lower, 0)
    first, last_corner = line_of(stiffness, 0, WIDE), line_of(stiffness, 63, WIDE)
    cross = line_of(stiffness, 7, WIDE)
    taken, into_left, into_right = [], [], []
    for k in range(4):
        left, right = left_factors[k][0] * right_half[k], right_factors[k][0] * left_half[k]
        from_left, from_right = split(along_z[k * 16 : k * 16 + 16]), split(along_z[k * 16 + 64 : k * 16 + 80])
        rest = left_factors[k][1] * contract_y(right_half[k], stiff) + right_factors[k][1] * contract_y(left_half[k], stiff)
        rest = rest + left_factors[k][2] * from_right + right_factors[k][2] * from_left
        taken.append(last_corner * left + first * right + WEIGHTS[0] * rest)
        into_left.append(geo.assemble(left) if k != 2 else None)
        into_right.append(geo.assemble(right) if k != 3 else None)
    to_right = [geo.assemble(v - t) for v, t in zip((near[0][1], remain[1], last[0][1]), taken[:3])]
    to_left = [geo.assemble(v - taken[k]) for k, v in ((0, remain[0]), (1, near[1][1]), (3, last[1][1]))]
    for side in range(2):
        start_faces[side] = solid(own(left_half[side] + right_half[side]))

    moved = [into_right[0], into_left[1]]
    rows = [own(split(known[x])) for x in range(ROWS)]
    rows[0], rows[15] = rows[0] + own(to_right[0]), rows[15] + own(to_left[1])
    for side, face in ((0, 0), (1, 7)):
        for i in range(8):
            if i != face:
                change = line_of(stiffness, i * 8 + face, LANES) * own(moved[side])
                x = side * 8 + i
                rows[x] = rows[x] - change
                if x in (7, 8):
                    rows[15 - x] = rows[15 - x] - change
    parts = [None, None]
    for x in range(ROWS):
        residual[x] = solid(rows[x])
        for a in range(2):
            if GROUP_X[a][x] * INVERSE_X[x] != 0.0:
                term = (GROUP_X[a][x] * INVERSE_X[x]) * rows[x]
                parts[a] = term if parts[a] is None else parts[a] + term
    weight = own(geo.inverse_y * geo.inverse_z)
    for a in range(2):
        sums[a : a + 1] = down(parts[a] * weight)

    forward, backward = wide_diagonals(diagonals, 1), wide_diagonals(diagonals, 2)
    fields = to_right + to_left + [into_left[0], into_left[1], into_left[3], into_right[0], into_right[1], into_right[2]]
    flat = jnp.concatenate([solid(contract_y(v, forward)) for v in fields], axis=0)
    flat = contract_z(flat, upper, lower, 1)
    flat = [split(flat[k * 16 : k * 16 + 16]) for k in range(len(fields))]
    to_right, to_left = flat[:3], flat[3:6]
    into_left, into_right = {0: flat[6], 1: flat[7], 3: flat[8]}, {0: flat[9], 1: flat[10], 2: flat[11]}

    def vector(p, i):
        return line_of(vectors, p * 8 + i, WIDE)

    def changes(element, total, close, distant):
        face, other = 7 * element, 7 - 7 * element
        crossed = cross * distant
        return [
            vector(face, i) * total - line_of(bend, element * 8 + i, WIDE) * close - vector(other, i) * crossed
            for i in range(8)
        ]

    moved = []
    for element, change in enumerate(
        (changes(0, to_right[0], into_right[0], into_left[1]), changes(1, to_left[1], into_left[1], into_right[0]))
    ):
        moved += [solid((split(spectrum[element * 8 + i]) + change[i]) * split(inverse[element * 8 + i])) for i in range(8)]
    for side in range(2):
        value, partial = (split(v) for v in read_second(sides[side][FIRST_ROWS + FAR_ROWS :]))
        near_element, far_element = 1 - side, side
        if side == 0:
            close = changes(1, to_left[0], into_left[0], into_right[2])
            distant = changes(0, to_right[2], into_right[2], into_left[0])
        else:
            close = changes(0, to_right[1], into_right[1], into_left[3])
            distant = changes(1, to_left[2], into_left[3], into_right[1])
        face = 7 * near_element
        close = [a * b for a, b in zip(close, divisors_of(geo, near[side][2], lam))]
        distant = [a * b for a, b in zip(distant, divisors_of(geo, far[side][1], lam))]
        value = value + weighted([vector(face, i) for i in range(8)], close)
        partial = partial + weighted([line_of(bend, near_element * 8 + i, WIDE) for i in range(8)], close)
        partial = partial + cross * weighted([vector(face, i) for i in range(8)], distant)
        moved += [solid(value), solid(partial)]

    back = contract_z(jnp.concatenate(moved, axis=0), upper, lower, 2)
    back = [contract_y(split(back[k * 16 : k * 16 + 16]), backward) for k in range(ROWS + 4)]
    solved = []
    for element in range(2):
        inside = back[element * 8 : element * 8 + 8]
        solved += [contract_x(inside, vectors, i) for i in range(8)]
    total = None
    for x in range(ROWS):
        term = own(solved[x]) * rows[x]
        total = term if total is None else total + term
    sums[2:3] = down(total)
    sums[3:8] = jnp.zeros((5, LANES), jnp.float32)
    solved = join_middle(solved)
    solved[0], solved[15] = solved[0] + back[16], solved[15] + back[18]
    for x in range(ROWS):
        local[x] = solid(geo.assemble(solved[x]))
    for side in range(2):
        beside[side] = solid(geo.assemble(back[17 + 2 * side]))


def image_kernel(
    local, factors, face_factors, beside, sums, fixed, stiffness, lines, upper, lower, diagonals,
    image, payload,
):
    geo = Geometry(WIDE)
    rows = [split(local[x]) for x in range(ROWS)]
    along_z = contract_z(jnp.concatenate([solid(v) for v in rows], axis=0), upper, lower, 0)
    scaled = [stored_factors(factors, e) for e in range(2)]
    stiff = wide_diagonals(diagonals, 0)
    applied = apply_rows(rows, along_z, scaled, stiffness, stiff)
    total, parts = None, [None, None]
    for x in range(ROWS):
        term = own(applied[x]) * own(rows[x])
        total = term if total is None else total + term
        for a in range(2):
            if GROUP_X[a][x] != 0.0:
                term = GROUP_X[a][x] * own(applied[x])
                parts[a] = term if parts[a] is None else parts[a] + term
    extra = [down(value * own(geo.keep)) for value in parts + [total]]
    for side, x, across in ((0, 0, 63), (1, 15, 0)):
        there = [split(face_factors[side, c]) for c in range(3)]
        other = there[0] * (split(beside[side]) + line_of(stiffness, across, WIDE) * rows[x])
        turned = split(along_z[x * 16 : x * 16 + 16])
        other = other + WEIGHTS[0] * (there[1] * contract_y(rows[x], stiff) + there[2] * turned)
        applied[x] = applied[x] + other
    applied = join_middle(applied)
    for x in range(ROWS):
        image[x] = solid(own(geo.assemble(applied[x])))
    zero = jnp.zeros((1, LANES), jnp.float32)
    table = jnp.concatenate(
        [sums[0:2], extra[0], extra[1], fixed[0:9], sums[2:3], extra[2], zero], axis=0
    )
    reduced = contract_z(table, upper, lower, 3)
    mine = (iota((16, LANES), 1) >> 3) == iota((16, LANES), 0)
    row = jnp.sum(jnp.where(mine, reduced, 0.0), axis=0, keepdims=True) + fixed[16:17]
    block = jnp.concatenate([row, fixed[17:18]] * 4, axis=0)
    copies = payload.shape[0] // 8
    payload[...] = jnp.broadcast_to(block[None], (copies, 8, LANES)).reshape(copies * 8, LANES)


def middle_kernel(
    known, factors, halves, remainders, spectrum, inverse, got_a, got_b, got_c, waves,
    stiffness, vectors, bend, lam, upper, lower, diagonals, fixed, lines,
    start_faces, residual, local, face_factors, image, payload, beside, sums,
):
    solve_kernel(
        known, factors, halves, remainders, spectrum, inverse, got_a, got_b, got_c, waves,
        stiffness, vectors, bend, lam, upper, lower, diagonals,
        start_faces, residual, local, beside, face_factors, sums,
    )
    image_kernel(
        local, factors, face_factors, beside, sums, fixed, stiffness, lines, upper, lower, diagonals, image, payload
    )


def lane_tables():
    one = np.zeros((8, LANES), np.float32)
    two = np.zeros((8, LANES), np.float32)
    top = np.zeros((8, LANES), np.float32)
    for a in range(2):
        for b in range(3):
            one[6, 8 * a + b], two[3 * a + b, 8 * a + b], top[0, 8 * a + b] = 1.0, 1.0, 1.0
            one[6, 8 * (2 + a) + b], two[3 * a + b, 8 * (2 + a) + b] = 2.0, 1.0
            top[1, 8 * (2 + a) + b] = 1.0
    for p, (a, other) in enumerate(PAIRS):
        for b in range(3):
            for c in range(3):
                at = 8 * (4 + 3 * p + b) + c
                one[3 * a + b, at] = 1.0 if a == other else 2.0
                two[3 * other + c, at] = 1.0
                top[1, at] = 1.0
    one[6, 8 * 13 + 3], two[6, 8 * 13 + 3], top[0, 8 * 13 + 3] = 1.0, 1.0, 1.0
    one[6, 8 * 14 + 3], two[6, 8 * 14 + 3], top[1, 8 * 14 + 3] = 1.0, 1.0, 1.0
    return np.stack([one, two, top])


def final_kernel(
    devices, spans, count, per,
    start, start_faces, residual, local, image, pieces, face_factors, waves, stiff_keep, lines, tables,
    gathered, given, new_solution, new_residual, values,
):
    rows = gathered[pl.ds(0, devices, stride=2), :]
    if given is None:
        spot = iota((devices, count), 1)
        hits = []
        rhs = [jnp.zeros((1, devices), jnp.float32) for _ in range(per)]
        owner = iota((devices, devices), 1)
        for k in range(6):
            label = rows[:, 8 * k + 4 : 8 * k + 5].astype(jnp.int32)
            at = 8 * (k // 3) + k % 3
            value = rows[:, at : at + 1]
            hits.append(spot == label)
            for q in range(per):
                chosen = jnp.where(owner * per + q == label, value, 0.0)
                rhs[q] = rhs[q] + jnp.sum(chosen, axis=0, keepdims=True)
        inverse = gathered[pl.ds(1, devices, stride=2), :]
        coarse = None
        for q in range(per):
            term = jnp.dot(
                rhs[q], inverse[:, q * count : q * count + count], precision=EXACT,
                preferred_element_type=jnp.float32,
            )
            coarse = term if coarse is None else coarse + term
        columns = [jnp.sum(jnp.where(hit, coarse, 0.0), axis=1, keepdims=True) for hit in hits]
        kept = jnp.zeros((devices, LANES), jnp.float32)
        for k in range(6):
            kept = jnp.where(iota((devices, LANES), 1) == k, columns[k], kept)
        values[...] = kept
    else:
        columns = [given[:, k : k + 1] for k in range(6)]
        values[...] = given[...]
    one, two = tables[0, 6:7, :], tables[1, 6:7, :]
    for k in range(6):
        one = one + columns[k] * tables[0, k : k + 1, :]
        two = two + columns[k] * tables[1, k : k + 1, :]
    product = jnp.sum(rows * one * two, axis=0, keepdims=True)
    numerator = jnp.sum(product * tables[2, 0:1, :], axis=1, keepdims=True)
    denominator = jnp.sum(product * tables[2, 1:2, :], axis=1, keepdims=True)
    alpha = numerator / denominator

    gx, gz = lax.axis_index("gx"), lax.axis_index("gz")
    before_x = lax.rem(gx + devices // spans - 1, devices // spans)
    before_z = lax.rem(gz + spans - 1, spans)
    here = values[pl.ds(gx * spans + gz, 1), :]
    behind = values[pl.ds(gx * spans + before_z, 1), :]
    aside = values[pl.ds(before_x * spans + gz, 1), :]
    corner = values[pl.ds(before_x * spans + before_z, 1), :]

    def four(line, back, a):
        return [back[:, 3 * a + 1 : 3 * a + 2]] + [line[:, 3 * a + b : 3 * a + b + 1] for b in range(3)]

    def mix(numbers, ref):
        total = numbers[0] * ref[0]
        for b in range(1, 4):
            total = total + numbers[b] * ref[b]
        return total

    near, right, left = four(here, behind, 0), four(here, behind, 1), four(aside, corner, 0)
    whole = [mix(near, pieces.at[0, k]) for k in range(2)]
    low = [mix(near, pieces.at[1, k]) for k in range(2)]
    high = [mix(right, pieces.at[1, k]) for k in range(2)]

    def stiff(line, i):
        return lines[line, i : i + 1, :]

    extra = [stiff(0, i) * whole[0] + WEIGHTS[i] * whole[1] for i in range(8)]
    for i in range(8):
        extra.append(
            stiff(1, i) * low[0] + stiff(2, i) * high[0] + WEIGHTS[i] * (LOW[i] * low[1] + HIGH[i] * high[1])
        )
    extra = join_middle(extra)
    geo = Geometry(WIDE)

    def line(numbers, at):
        total = numbers[0] * waves[at : at + 1, :]
        for b in range(1, 4):
            total = total + numbers[b] * waves[at + b : at + b + 1, :]
        return total

    def wide_stiff(k, i):
        return jnp.concatenate([stiff(k, i)] * (WIDE // LANES), axis=1)

    def beyond(side, stiff_x, plain, turned):
        fx, fy, fz = (split(face_factors[side, c]) for c in range(3))
        value = fx * geo.keep * stiff_x[None]
        value = value + WEIGHTS[0] * (fy * split(stiff_keep[...]) * plain[None] + fz * geo.keep * turned[None])
        return solid(own(geo.assemble(value)))

    wave_near, wave_right = line(near, 0), line(right, 0)
    across = wide_stiff(1, 7) * line(left, 0) + wide_stiff(2, 7) * wave_near
    extra[0] = extra[0] + beyond(0, across, wave_near, line(near, 4))
    extra[15] = extra[15] + beyond(1, wide_stiff(0, 0) * wave_right, wave_right, line(right, 4))
    keep = solid(own(geo.keep))
    line_near, line_right = wave_near[:, :LANES], wave_right[:, :LANES]
    for x in range(ROWS):
        begin = start_faces[x // 15] if x in (0, 15) else start[x]
        mine = local[x, :, :LANES]
        new_residual[x] = residual[x] - alpha * (image[x] + extra[x])
        coarse_line = GROUP_X[0][x] * line_near
        if GROUP_X[1][x] != 0.0:
            coarse_line = coarse_line + GROUP_X[1][x] * line_right
        new_solution[x] = begin + alpha * (mine + keep * coarse_line)


VMEM = pl.BlockSpec(memory_space=pltpu.VMEM)
SMEM = pl.BlockSpec(memory_space=pltpu.SMEM)
FAR = pl.BlockSpec(memory_space=pltpu.HBM)


def call(kernel, shapes, specs, name, scratch=()):
    def leaf(shape):
        kind = jnp.float32
        if shape[0] == "half":
            shape, kind = shape[1:], jnp.bfloat16
        return jax.ShapeDtypeStruct(shape, kind)

    return pl.pallas_call(
        kernel,
        out_shape=[leaf(shape) for shape in shapes],
        in_specs=specs,
        out_specs=[VMEM] * len(shapes),
        scratch_shapes=list(scratch),
        compiler_params=pltpu.CompilerParams(vmem_limit_bytes=16 * 1024 * 1024),
        name=name,
    )


def swap(first, second, axis):
    size = lax.axis_size(axis)
    odd = [(i, (i + 1) % size) for i in range(1, size, 2)]
    one = lax.ppermute(first, axis, [(i, i ^ 1) for i in range(size)])
    two = lax.ppermute(second, axis, odd + [(b, a) for a, b in odd])
    return one, two


def second_neighbours(common, axis):
    size = lax.axis_size(axis)
    if size == 4:
        return lax.ppermute(common, axis, [(i, i ^ 2) for i in range(size)])
    left = lax.ppermute(common[:FIRST_ROWS], axis, [(i, (i - 2) % size) for i in range(size)])
    right = lax.ppermute(common[FIRST_ROWS:], axis, [(i, (i + 2) % size) for i in range(size)])
    return jnp.concatenate([left, right], axis=0)


def body(
    source, previous, coefficients, stiffness, fdm_vectors, fdm_values, coarse_inverse, vertex_map
):
    assert source.shape == (ROWS, ROWS, LANES)
    spans = lax.axis_size("gz")
    devices = lax.axis_size("gx") * spans
    per, count = coarse_inverse.shape
    small = per * count <= LANES
    block, wide, face = (ROWS, ROWS, LANES), (ROWS, ROWS, WIDE), (ROWS, LANES)
    halo = (13, 8, LANES)

    first, second, elements, source, previous = call(
        pack_kernel,
        [halo, halo, face, block, block],
        [FAR] * 3,
        "pack",
        [pltpu.VMEM(coefficients.shape, jnp.float32), pltpu.SemaphoreType.DMA((3,))],
    )(*(pltpu.with_memory_space_constraint(v, pltpu.HBM) for v in (source, previous, coefficients)))
    first, second = swap(first, second, "gz")
    own_metrics, upper, lower, diagonals, stiff, vectors, bend, lam, lines, fixed, tables = call(
        functools.partial(prepare_kernel, small),
        [
            face, ("half", 4, WIDE, WIDE), ("half", 4, WIDE, LANES), (3, 8, 8, LANES),
            (64, LANES), (64, LANES), (16, LANES), (2, 8, LANES), (3, 8, LANES), (24, LANES), (3, 8, LANES),
        ],
        [VMEM] * 3 + [SMEM] * 2 + [VMEM if small else FAR, VMEM],
        "prepare",
    )(elements, stiffness, fdm_vectors, fdm_values, vertex_map, coarse_inverse, jnp.asarray(lane_tables()))

    message = (FIRST_ROWS + FAR_ROWS + SECOND_ROWS, LANES)
    start, known, factors, halves, remainders, spectrum, inverse, side_a, side_b, common = call(
        start_kernel,
        [
            block, wide, (3, 2, ROWS, WIDE), (2, ROWS, WIDE), (2, ROWS, WIDE), wide, wide,
            message, message, (2 * FIRST_ROWS, LANES),
        ],
        [VMEM] * 12,
        "start",
        [pltpu.VMEM((16, WIDE), jnp.float32)],
    )(source, previous, own_metrics, first, second, stiff, vectors, bend, lam, upper, lower, diagonals)
    beyond = second_neighbours(common, "gx")
    side_a, side_b = swap(side_a, side_b, "gx")
    pieces, waves, stiff_keep = call(
        ready_kernel, [(2, 2, 4, ROWS, LANES), (8, WIDE), (ROWS, WIDE)], [VMEM] * 5, "ready"
    )(factors, stiff, lines, upper, lower)

    start_faces, residual, local, face_factors, image, payload = call(
        middle_kernel,
        [(2, ROWS, LANES), block, wide, (2, 3, ROWS, WIDE), block, (2 * devices, LANES)],
        [VMEM] * 19,
        "middle",
        [pltpu.VMEM((2, ROWS, WIDE), jnp.float32), pltpu.VMEM((8, LANES), jnp.float32)],
    )(
        known, factors, halves, remainders, spectrum, inverse, side_a, side_b, beyond, waves,
        stiff, vectors, bend, lam, upper, lower, diagonals, fixed, lines,
    )
    gathered = lax.all_to_all(payload.reshape(devices, 2, LANES), ("gx", "gz"), 0, 0)
    gathered = gathered.reshape(2 * devices, LANES)

    operands = [
        start, start_faces, residual, local, image, pieces, face_factors, waves, stiff_keep, lines,
        tables, gathered,
    ]
    finish = functools.partial(final_kernel, devices, spans, count, per)
    if small:

        def kernel(*refs):
            finish(*refs[:12], None, *refs[12:])

    else:
        kernel = finish
        rows = gathered[0::2]
        labels = rows[:, jnp.array([8 * k + 4 for k in range(6)])].astype(jnp.int32)
        parts = rows[:, jnp.array([8 * (k // 3) + k % 3 for k in range(6)])]
        rhs = jnp.zeros((count,), jnp.float32).at[labels.reshape(-1)].add(parts.reshape(-1))
        mine = jnp.dot(coarse_inverse, rhs, precision=EXACT)
        coarse = lax.all_gather(mine, ("gx", "gz"), axis=0, tiled=True)
        operands.append(jnp.pad(coarse[labels], ((0, 0), (0, LANES - 6))))
    return tuple(
        call(kernel, [block, block], [VMEM] * len(operands), "finish", [pltpu.VMEM((devices, LANES), jnp.float32)])(
            *operands
        )
    )


def solution(mesh):
    placed = (
        P("gx", None, "gz"),
        P("gx", None, "gz"),
        P(None, "gx", None, "gz"),
        P(),
        P(),
        P(),
        P(("gx", "gz"), None),
        P(None, "gx", None, "gz"),
    )
    return jax.shard_map(
        body,
        mesh=mesh,
        in_specs=placed,
        out_specs=(P("gx", None, "gz"), P("gx", None, "gz")),
        check_vma=False,
    )
```

```python
import functools

import jax
import jax.numpy as jnp
import numpy as np
from jax import lax
from jax.experimental import pallas as pl
from jax.experimental.pallas import tpu as pltpu
from jax.sharding import PartitionSpec as P

POINTS = [
    -1.0,
    -0.8717401485096066,
    -0.5917001814331423,
    -0.2092992179024789,
    0.2092992179024789,
    0.5917001814331423,
    0.8717401485096066,
    1.0,
]
WEIGHTS = [
    0.03571428571428571,
    0.21070422714350603,
    0.34112269248350435,
    0.4124587946587038,
    0.4124587946587038,
    0.34112269248350435,
    0.21070422714350603,
    0.03571428571428571,
]
ONES = [1.0] * 8
LOW = [(1.0 - s) / 2.0 for s in POINTS]
HIGH = [(1.0 + s) / 2.0 for s in POINTS]
EXACT = lax.Precision.HIGHEST

ROWS = 16
LANES = 128
WIDE = 256
HALO = 32
DEEP, SHALLOW = 25, 17
SLOT = DEEP + SHALLOW
FIRST_FIELDS = ((0, 24), (41, 17), (75, 17))
SECOND_FIELDS = ((0, 16), (32, 16), (64, 16), (96, 16))
FAR_FIELDS = ((0, 24), (48, 24))
FIRST_ROWS, FAR_ROWS, SECOND_ROWS = 56, 32, 40
PAIRS = ((0, 0), (0, 1), (1, 1))
GROUP_X = (ONES + LOW, [0.0] * 8 + HIGH)
INVERSE_X = [0.5] + [1.0] * 6 + [0.5] + [0.5] + [1.0] * 6 + [0.5]


def iota(shape, dim):
    return lax.broadcasted_iota(jnp.int32, shape, dim)


def pick(index, values):
    result = jnp.full(index.shape, values[0], jnp.float32)
    for i in range(1, 8):
        result = jnp.where(index == i, values[i], result)
    return result


def even_index(axis):
    return lax.rem(lax.axis_index(axis), 2) == 0


class Geometry:
    def __init__(self, lanes):
        shape = (2, 8, lanes)
        self.element_y, self.row, lane = iota(shape, 0), iota(shape, 1), iota(shape, 2)
        self.position = lane & 7
        self.first = self.position == 0
        self.last = self.position == 7
        self.edge = self.first | self.last
        self.weight_y = pick(self.row, WEIGHTS)
        self.weight_z = pick(self.position, WEIGHTS)
        self.inverse_z = jnp.where(self.edge, 0.5, 1.0)
        self.wall = (self.element_y == 1) & (self.row == 7)
        inner = ((self.element_y == 0) & (self.row == 7)) | ((self.element_y == 1) & (self.row == 0))
        self.inverse_y = jnp.where(inner, 0.5, 1.0)
        self.keep = jnp.where(self.wall, 0.0, 1.0)
        self.lanes = lanes

    def pair_y(self, v):
        lower, upper = v[0], v[1]
        row = self.row[0]
        up = jnp.where(row == 7, pltpu.roll(upper, 7, 0), 0.0)
        down = jnp.where(row == 0, pltpu.roll(lower, 1, 0), 0.0)
        return jnp.stack([lower + up, upper + down])

    def pair_z(self, v):
        flat = v.reshape(16, self.lanes)
        after = pltpu.roll(flat, self.lanes - 1, 1).reshape(v.shape)
        before = pltpu.roll(flat, 1, 1).reshape(v.shape)
        return v + jnp.where(self.edge, jnp.where(self.last, after, before), 0.0)

    def pair(self, v):
        return self.pair_z(self.pair_y(v))

    def assemble(self, v):
        return self.pair(v) * self.keep


def solid(v):
    return v.reshape(ROWS, v.shape[-1])


def split(v):
    return v.reshape(2, 8, v.shape[-1])


def own(v):
    return v[..., :LANES]


def down(v):
    return jnp.sum(v.reshape(ROWS, LANES), axis=0, keepdims=True)


def line_of(ref, at, lanes):
    row = ref[at : at + 1, :]
    return jnp.concatenate([row] * (lanes // LANES), axis=1)[None]


def weighted(factors, rows):
    total = None
    for factor, row in zip(factors, rows):
        total = factor * row if total is None else total + factor * row
    return total


def divisors_of(geo, c, lam):
    lam_y = jnp.concatenate([lam[0]] * (WIDE // LANES), axis=1)[None]
    lam_z = jnp.concatenate([lam[1]] * (WIDE // LANES), axis=1)[None]
    base = c[1] * lam_y + c[2] * lam_z
    return [1.0 / (c[0] * line_of(lam.at[0], i, WIDE) + base) for i in range(8)]


def contract_x(rows, table, i, transpose=False):
    total = None
    for p in range(8):
        factor = line_of(table, p * 8 + i if transpose else i * 8 + p, WIDE)
        term = factor * rows[p]
        total = term if total is None else total + term
    return total


def contract_y(v, diagonals):
    def moved(value, rows):
        return jnp.stack([pltpu.roll(value[e], 8 - rows, 0) for e in range(2)])

    shifted = [v] + [moved(v, d) for d in range(1, 4)]
    return weighted(diagonals[:4], shifted) + moved(weighted(diagonals[4:], shifted), 4)


def thirds(v):
    high = v.astype(jnp.bfloat16)
    rest = v - high.astype(jnp.float32)
    middle = rest.astype(jnp.bfloat16)
    return high, middle, (rest - middle.astype(jnp.float32)).astype(jnp.bfloat16)


def contract_z(flat, upper, lower, which):
    pieces = []
    for at in range(0, flat.shape[1], LANES):
        high, middle, low = thirds(flat[:, at : at + LANES])
        one = jnp.dot(
            jnp.concatenate([high, middle], axis=1), upper[which], preferred_element_type=jnp.float32
        )
        two = jnp.dot(jnp.concatenate([low, high], axis=1), lower[which], preferred_element_type=jnp.float32)
        pieces.append(one[:, :LANES] + (one[:, LANES:] + two))
    return pieces[0] if len(pieces) == 1 else jnp.concatenate(pieces, axis=1)


def wide_diagonals(ref, which):
    return [jnp.concatenate([ref[which, d]] * (WIDE // LANES), axis=1)[None] for d in range(8)]


def metric(ref, component, element):
    at = (component * 2 + element) * 2
    return jnp.stack([jnp.broadcast_to(ref[at + e : at + e + 1, :], (8, WIDE)) for e in range(2)])


def scaled_metrics(geo, c):
    return c[0] * geo.weight_y * geo.weight_z, c[1] * geo.weight_z, c[2] * geo.weight_y


def stored_factors(ref, element):
    return [split(ref[c, element]) for c in range(3)]


def apply_rows(rows, along_z, factors, stiffness, diagonals):
    result = []
    for element in range(2):
        factor_x, factor_y, factor_z = factors[element]
        inside = rows[element * 8 : element * 8 + 8]
        for i in range(8):
            x = element * 8 + i
            term_y = factor_y * contract_y(inside[i], diagonals)
            term_z = factor_z * split(along_z[x * 16 : x * 16 + 16])
            result.append(factor_x * contract_x(inside, stiffness, i) + WEIGHTS[i] * (term_y + term_z))
    return result


def join_middle(rows):
    middle = rows[7] + rows[8]
    return rows[:7] + [middle, middle] + rows[9:]


def fold(parts, fields):
    lane = iota((8, LANES), 1)
    result = parts[0]
    for part, (offset, half) in list(zip(parts, fields))[1:]:
        taken = ((lane - offset + half) & (LANES - 1)) < 2 * half
        result = jnp.where(taken, pltpu.roll(part, offset, 1), result)
    return result


def unfold(packed, field, fill=0.0):
    offset, half = field
    lane = iota((8, LANES), 1)
    moved = pltpu.roll(packed, LANES - offset, 1) if offset else packed
    return jnp.where(((lane + half) & (LANES - 1)) < 2 * half, moved, fill)


def widen(tile, pieces):
    return jnp.concatenate([tile, jnp.concatenate(pieces, axis=0)], axis=1)


def group_lanes(lanes, group):
    lane = iota((1, lanes), 1)
    signed = jnp.where(lane < lanes // 2 + lanes // 4, lane, lane - lanes) if lanes > LANES else lane
    element, position = signed >> 3, lane & 7
    low, high = pick(position, LOW), pick(position, HIGH)
    here = jnp.where((element >> 3) == group, low, 0.0)
    return here + jnp.where(((element + 1) >> 3) == group, high, 0.0)


def pack_kernel(source, previous, coefficients, first, second, elements, near_source, near_previous, raw, ready):
    copies = [
        pltpu.make_async_copy(source, near_source, ready.at[0]),
        pltpu.make_async_copy(previous, near_previous, ready.at[1]),
        pltpu.make_async_copy(coefficients, raw, ready.at[2]),
    ]
    for copy in copies:
        copy.start()
    even = even_index("gz")
    elements[...] = jnp.zeros_like(elements)
    for copy in copies:
        copy.wait()
    for c in range(3):
        for element in range(2):
            at = (c * 2 + element) * 2
            elements[at : at + 2, 0:16] = raw[c, element]
    slot = iota((8, LANES), 1)
    for to_right, out in ((even, first), (jnp.logical_not(even), second)):
        for tile in range(11):
            packed = None
            for k in range(3):
                n = 3 * tile + k
                if n >= 2 * ROWS:
                    break
                for ref, width, at in ((near_previous, DEEP, SLOT * k), (near_source, SHALLOW, SLOT * k + DEEP)):
                    shift = jnp.where(to_right, (at + width) % LANES, at)
                    moved = pltpu.roll(ref[n // 2, 8 * (n % 2) : 8 * (n % 2) + 8], shift, 1)
                    packed = moved if packed is None else jnp.where(slot >= at, moved, packed)
            out[tile] = packed
        out[11] = elements[:8]
        out[12] = elements[8:]


def lanes_of(elements):
    widen = (iota((16, LANES), 0) == (iota((16, LANES), 1) >> 3)).astype(jnp.float32)
    return jnp.dot(elements[:, 0:16], widen, precision=EXACT, preferred_element_type=jnp.float32)


def prepare_kernel(
    with_coarse, elements, stiffness, vectors, eigen, labels, coarse, tables,
    metrics, upper, lower, diagonals, stiff_table, vector_table, bend, lam, lines, fixed, near_tables,
):
    near_tables[...] = tables[...]
    metrics[...] = lanes_of(elements[...])
    repeat = (iota((LANES, 8), 0) & 7 == iota((LANES, 8), 1)).astype(jnp.float32)
    same = (iota((LANES, LANES), 0) >> 3) == (iota((LANES, LANES), 1) >> 3)
    unit = (iota((8, 8), 0) == iota((8, 8), 1)).astype(jnp.float32)
    row, column = iota((8, 8), 0), iota((8, 8), 1)

    def dot(a, b, dims):
        return lax.dot_general(a, b, (dims, ((), ())), precision=EXACT, preferred_element_type=jnp.float32)

    def put_block(at, matrix):
        half = dot(repeat, matrix, ((1,), (0,)))
        put_thirds(at, jnp.where(same, dot(half, repeat, ((1,), (1,))), 0.0))

    def put_thirds(at, block):
        high, middle, low = thirds(block)
        both = jnp.concatenate([high, middle], axis=1)
        upper[at] = jnp.concatenate([both, both], axis=0)
        lower[at] = jnp.concatenate([high, low], axis=0)

    def put_diagonals(at, matrix):
        turned = jnp.concatenate([matrix[4:], matrix[:4]], axis=0)
        for d in range(8):
            chosen = jnp.where(column == ((row + d % 4) & 7), matrix if d < 4 else turned, 0.0)
            diagonals[at, d] = jnp.broadcast_to(jnp.sum(chosen, axis=1, keepdims=True), (8, LANES))

    def put_table(out, matrix):
        tall = (iota((64, 8), 0) >> 3 == iota((64, 8), 1)).astype(jnp.float32)
        chosen = jnp.where(iota((64, 8), 0) & 7 == iota((64, 8), 1), dot(tall, matrix, ((1,), (0,))), 0.0)
        out[...] = jnp.broadcast_to(jnp.sum(chosen, axis=1, keepdims=True), (64, LANES))

    lane = iota((LANES, LANES), 1) & 7
    node = iota((LANES, LANES), 0)
    element, position = node >> 3, node & 7
    low, high = pick(position, LOW), pick(position, HIGH)
    columns = jnp.where(lane == (element >> 3), low, 0.0) + jnp.where(lane == ((element + 1) >> 3), high, 0.0)
    columns = jnp.where(lane == 3, 1.0, jnp.where(lane < 3, columns, 0.0))
    put_thirds(3, columns)
    k, s = stiffness[...], vectors[...]
    k_turned, s_turned = dot(k, unit, ((0,), (0,))), dot(s, unit, ((0,), (0,)))
    for at, matrix in enumerate((k_turned, s, s_turned)):
        put_block(at, matrix)
    for at, matrix in enumerate((k, s_turned, s)):
        put_diagonals(at, matrix)
    put_table(stiff_table, k)
    put_table(vector_table, s)
    for side, near in ((0, 0), (1, 7)):
        chosen = jnp.where(column == near, 0.0, s_turned * k[near : near + 1, :])
        total = jnp.sum(chosen, axis=1, keepdims=True)
        bend[8 * side : 8 * side + 8] = jnp.broadcast_to(total, (8, LANES))
    values = [eigen[i] for i in range(8)]
    lam[0] = pick(iota((8, LANES), 0), values)
    lam[1] = pick(iota((8, LANES), 1) & 7, values)
    stiff_lines = []
    for at, line in enumerate((ONES, LOW, HIGH)):
        total = jnp.sum(k * pick(column, line), axis=1, keepdims=True)
        stiff_lines.append(jnp.broadcast_to(total, (8, LANES)))
        lines[at] = stiff_lines[at]

    groups = [group_lanes(LANES, b) for b in range(3)]
    stacked = jnp.concatenate(groups + [jnp.zeros((13, LANES), jnp.float32)], axis=0)
    stiff_z = contract_z(stacked, upper, lower, 0)
    weight_z = pick(iota((1, LANES), 1) & 7, WEIGHTS)
    node = iota((8, LANES), 0)
    mass_y = [sum(WEIGHTS), sum(WEIGHTS[:7])]
    last = jnp.broadcast_to(k[:, 7:8], (8, LANES))
    inner = jnp.where(node == 7, 0.0, stiff_lines[0] - last)
    stiff_y = [jnp.sum(v, axis=0, keepdims=True) for v in (stiff_lines[0], inner)]
    at = 0
    for a, b in PAIRS:
        across, along = jnp.zeros((1, LANES), jnp.float32), jnp.zeros((1, LANES), jnp.float32)
        for element in range(2):
            fa = GROUP_X[a][element * 8 : element * 8 + 8]
            fb = GROUP_X[b][element * 8 : element * 8 + 8]
            if not (any(fa) and any(fb)):
                continue
            mass_x = sum(w * p * q for w, p, q in zip(WEIGHTS, fa, fb))
            applied = stiff_lines[0 if fb == ONES else 1 + b]
            stiff_x = jnp.sum(applied * pick(node, fa), axis=0, keepdims=True)
            for e in range(2):
                cx, cy, cz = (metrics[(c * 2 + element) * 2 + e, :].reshape(1, LANES) for c in range(3))
                across = across + cx * (stiff_x * mass_y[e]) + cy * (stiff_y[e] * mass_x)
                along = along + cz * (mass_x * mass_y[e])
        across = across * weight_z
        for b in range(3):
            fixed[at : at + 1] = across * groups[b] + along * stiff_z[b : b + 1]
            at += 1
    fixed[9:16] = jnp.zeros((7, LANES), jnp.float32)
    place = iota((1, LANES), 1)
    numbers = jnp.zeros((1, LANES), jnp.float32)
    for a in range(2):
        for b in range(3):
            corner, x, z = 4 * a + (b == 2), a, (0, 8, 15)[b]
            number = labels[corner, x, 0, z].astype(jnp.float32)
            numbers = jnp.where(place == 8 * (3 * a + b) + 4, number, numbers)
    fixed[16:17] = numbers
    below = jnp.zeros((1, LANES), jnp.float32)
    if with_coarse:
        per, count = coarse.shape
        below = [coarse[i : i + 1, :] for i in range(per)]
        if per * count < LANES:
            below.append(jnp.zeros((1, LANES - per * count), jnp.float32))
        below = jnp.concatenate(below, axis=1)
    fixed[17:18] = below
    fixed[18:24] = jnp.zeros((6, LANES), jnp.float32)


def start_kernel(
    source, previous, own_metrics, first, second, stiffness, upper, lower, diagonals,
    start, remainder, factors, halves, common, part, metrics,
):
    even = even_index("gz")
    lane = iota((8, LANES), 1)
    one, two = first[...], second[...]
    from_right, from_left = jnp.where(even, one, two), jnp.where(even, two, one)

    def beyond(n, at, width):
        at = at + SLOT * (n % 3)
        right, left = from_right[n // 3], from_left[n // 3]
        if at:
            right = pltpu.roll(right, LANES - at, 1)
        left = pltpu.roll(left, (LANES - width - at) % LANES, 1)
        return jnp.where(lane < width, right, jnp.where(lane >= LANES - width, left, 0.0))

    def wide(ref, x, at, width):
        return split(widen(ref[x], [beyond(2 * x + e, at, width) for e in range(2)]))

    geo = Geometry(WIDE)
    metrics[:, :LANES] = own_metrics[...]
    around = lanes_of(jnp.concatenate([from_right[11], from_right[12], from_left[11], from_left[12]], axis=0))
    wide_lane = iota((16, LANES), 1)
    metrics[:, LANES:] = jnp.where(
        wide_lane < HALO, around[:16], jnp.where(wide_lane >= LANES - HALO, around[16:], 1.0)
    )
    factor = geo.keep * geo.inverse_y * geo.inverse_z
    rows = [geo.pair(wide(previous, x, 0, DEEP)) * (factor * INVERSE_X[x]) for x in range(ROWS)]
    rows = join_middle(rows)
    faces = (rows[0], rows[15])
    for x in range(ROWS):
        start[x] = solid(own(rows[x]))
    along_z = contract_z(jnp.concatenate([solid(v) for v in rows], axis=0), upper, lower, 0)
    scaled = [scaled_metrics(geo, [metric(metrics, c, e) for c in range(3)]) for e in range(2)]
    for e in range(2):
        for c in range(3):
            factors[c, e] = solid(scaled[e][c])
    applied = apply_rows(rows, along_z, scaled, stiffness, wide_diagonals(diagonals, 0))
    rest = [wide(source, x, DEEP, SHALLOW) - applied[x] for x in range(ROWS)]
    halves[0], halves[1] = solid(faces[0]), solid(faces[1])
    for x in range(ROWS):
        remainder[x] = solid(rest[x])
    coefficients = [
        jnp.concatenate(
            [metrics[(c * 2 + side) * 2 : (c * 2 + side) * 2 + 2] for c in range(3)] + [jnp.ones((2, WIDE), jnp.float32)],
            axis=0,
        )
        for side in range(2)
    ]
    messages, distant = [], []
    for side, x in ((0, 0), (1, 15)):
        half, value = solid(faces[side]), solid(rest[x])
        rows, others = coefficients[side], coefficients[1 - side]
        lower_fold = fold([half[:8, LANES:], value[:8, LANES:], rows[:, LANES:]], FIRST_FIELDS)
        upper_fold = fold([half[8:, LANES:], value[8:, LANES:], others[:, LANES:]], FIRST_FIELDS)
        parts = [half[:, :LANES], value[:, :LANES], lower_fold, upper_fold, rows[:, :LANES]]
        messages.append(jnp.concatenate(parts, axis=0))
        folded = fold([half[:8, LANES:], half[8:, LANES:]], FAR_FIELDS)
        distant.append(jnp.concatenate([half[:, :LANES], folded, rows[:, :LANES]], axis=0))
    common[: 2 * FIRST_ROWS] = jnp.concatenate(messages, axis=0)
    common[2 * FIRST_ROWS :] = jnp.zeros((16, LANES), jnp.float32)
    for side in range(2):
        part[side] = jnp.concatenate([messages[side], distant[1 - side]], axis=0)


def guess_kernel(
    remainder, metrics, part, stiffness, vectors, bend, lam, upper, lower, diagonals,
    known, spectrum, inverse, message_a, message_b,
):
    geo = Geometry(WIDE)
    rest = [split(remainder[x]) for x in range(ROWS)]
    rest = [geo.assemble(v) for v in join_middle(rest)]
    forward = wide_diagonals(diagonals, 1)
    moved = []
    for element in range(2):
        inside = rest[element * 8 : element * 8 + 8]
        moved += [solid(contract_y(contract_x(inside, vectors, i, True), forward)) for i in range(8)]
    for x in range(ROWS):
        known[x] = solid(rest[x])
    transformed = contract_z(jnp.concatenate(moved, axis=0), upper, lower, 1)
    damped = []
    for element in range(2):
        divisors = divisors_of(geo, [metric(metrics, c, element) for c in range(3)], lam)
        for i in range(8):
            x = element * 8 + i
            value = split(transformed[x * 16 : x * 16 + 16])
            spectrum[x], inverse[x] = solid(value), solid(divisors[i])
            damped.append(value * divisors[i])
    messages = []
    for side, near in ((0, 0), (1, 7)):
        inside, across = damped[side * 8 : side * 8 + 8], damped[8 - side * 8 : 16 - side * 8]
        value = contract_x(inside, vectors, near)
        beside = weighted([line_of(bend, side * 8 + i, WIDE) for i in range(8)], inside)
        beside = beside + line_of(stiffness, near * 8 + 7 - near, WIDE) * contract_x(across, vectors, near)
        value, beside = solid(value), solid(beside)
        folded = fold([v[at : at + 8, LANES:] for v in (value, beside) for at in (0, 8)], SECOND_FIELDS)
        messages.append(jnp.concatenate([value[:, :LANES], beside[:, :LANES], folded], axis=0))
    even_x = even_index("gx")
    both = [jnp.concatenate([part[side], messages[side]], axis=0) for side in range(2)]
    message_a[...] = jnp.where(even_x, both[1], both[0])
    message_b[...] = jnp.where(even_x, both[0], both[1])


def both_sides(even, a, b):
    one, two = a[...], b[...]
    return jnp.where(even, two, one), jnp.where(even, one, two)


def read_first(message):
    lower_fold, upper_fold = message[32:40], message[40:48]
    half, value = (
        widen(message[16 * k : 16 * k + 16], [unfold(lower_fold, FIRST_FIELDS[k]), unfold(upper_fold, FIRST_FIELDS[k])])
        for k in range(2)
    )
    return split(half), split(value), spread_metrics(message[48:56], lower_fold)


def spread_metrics(tile, folded):
    rows = widen(tile, [unfold(folded, FIRST_FIELDS[2], 1.0)])
    return [
        jnp.stack([jnp.broadcast_to(rows[2 * c + e : 2 * c + e + 1], (8, WIDE)) for e in range(2)]) for c in range(3)
    ]


def read_far(message):
    far = message[FIRST_ROWS : FIRST_ROWS + FAR_ROWS]
    half = widen(far[0:16], [unfold(far[16:24], field) for field in FAR_FIELDS])
    return split(half), spread_metrics(far[24:32], message[40:48])


def read_second(message):
    pieces = [unfold(message[32:40], field) for field in SECOND_FIELDS]
    return widen(message[0:16], pieces[:2]), widen(message[16:32], pieces[2:])


def coarse_pieces(geo, factors, stiff_keep, functions, stiff_functions):
    factor_x, factor_y, factor_z = factors
    kept_x, kept_y, kept_z = factor_x * geo.keep, factor_y * stiff_keep, factor_z * geo.keep
    result = []
    for plain, turned in zip(functions, stiff_functions):
        result.append(
            (geo.assemble(kept_x * plain[None]), geo.assemble(kept_y * plain[None] + kept_z * turned[None]))
        )
    return result


def wide_functions(upper, lower):
    functions = [group_lanes(WIDE, b) for b in (-1, 0, 1, 2)]
    stacked = jnp.concatenate(functions + [jnp.zeros((12, WIDE), jnp.float32)], axis=0)
    turned = contract_z(stacked, upper, lower, 0)
    return functions, [turned[b : b + 1] for b in range(4)]


def kept_stiffness(geo, lines, stiffness):
    row = iota((8, LANES), 0)
    last = jnp.zeros((8, LANES), jnp.float32)
    for j in range(8):
        last = jnp.where(row == j, stiffness[j * 8 + 7 : j * 8 + 8, :], last)
    both = jnp.stack([lines[0], lines[0] - last])
    return jnp.concatenate([both] * (WIDE // LANES), axis=2)


def ready_kernel(factors, stiffness, lines, upper, lower, pieces, waves, stiff_keep):
    geo = Geometry(WIDE)
    functions, turned = wide_functions(upper, lower)
    for b in range(4):
        waves[b : b + 1], waves[4 + b : 5 + b] = functions[b], turned[b]
    along_y = kept_stiffness(geo, lines, stiffness)
    stiff_keep[...] = solid(along_y)
    for element in range(2):
        made = coarse_pieces(geo, stored_factors(factors, element), along_y, functions, turned)
        for b in range(4):
            for k in range(2):
                pieces[element, k, b] = solid(own(made[b][k]))


def solve_kernel(
    known, factors, halves, remainder, spectrum, inverse, got_a, got_b, got_c, _,
    stiffness, vectors, bend, lam, upper, lower, diagonals,
    start_faces, residual, local, beside, face_factors, sums,
):
    even = even_index("gx")
    geo = Geometry(WIDE)
    sides = both_sides(even, got_a, got_b)
    beyond = got_c[...]
    near = [read_first(side) for side in sides]
    far = [read_far(side) for side in sides]
    last = [read_first(beyond[FIRST_ROWS : 2 * FIRST_ROWS]), read_first(beyond[:FIRST_ROWS])]
    mine = [stored_factors(factors, e) for e in range(2)]
    near_factors, far_factors, last_factors = (
        [scaled_metrics(geo, v[-1]) for v in group] for group in (near, far, last)
    )
    for side in range(2):
        for c in range(3):
            face_factors[side, c] = solid(near_factors[side][c])
    half = [split(halves[side]) for side in range(2)]
    remain = [split(remainder[x]) for x in (0, 15)]
    left_half = [near[0][0], half[1], last[0][0], far[1][0]]
    right_half = [half[0], near[1][0], far[0][0], last[1][0]]
    left_factors = [near_factors[0], mine[1], last_factors[0], far_factors[1]]
    right_factors = [mine[0], near_factors[1], far_factors[0], last_factors[1]]
    stiff = wide_diagonals(diagonals, 0)
    along_z = contract_z(jnp.concatenate([solid(v) for v in left_half + right_half], axis=0), upper, lower, 0)
    first, last_corner = line_of(stiffness, 0, WIDE), line_of(stiffness, 63, WIDE)
    cross = line_of(stiffness, 7, WIDE)
    taken, into_left, into_right = [], [], []
    for k in range(4):
        left, right = left_factors[k][0] * right_half[k], right_factors[k][0] * left_half[k]
        from_left, from_right = split(along_z[k * 16 : k * 16 + 16]), split(along_z[k * 16 + 64 : k * 16 + 80])
        rest = left_factors[k][1] * contract_y(right_half[k], stiff) + right_factors[k][1] * contract_y(left_half[k], stiff)
        rest = rest + left_factors[k][2] * from_right + right_factors[k][2] * from_left
        taken.append(last_corner * left + first * right + WEIGHTS[0] * rest)
        into_left.append(geo.assemble(left) if k != 2 else None)
        into_right.append(geo.assemble(right) if k != 3 else None)
    to_right = [geo.assemble(v - t) for v, t in zip((near[0][1], remain[1], last[0][1]), taken[:3])]
    to_left = [geo.assemble(v - taken[k]) for k, v in ((0, remain[0]), (1, near[1][1]), (3, last[1][1]))]
    for side in range(2):
        start_faces[side] = solid(own(left_half[side] + right_half[side]))

    moved = [into_right[0], into_left[1]]
    rows = [own(split(known[x])) for x in range(ROWS)]
    rows[0], rows[15] = rows[0] + own(to_right[0]), rows[15] + own(to_left[1])
    for side, face in ((0, 0), (1, 7)):
        for i in range(8):
            if i != face:
                change = line_of(stiffness, i * 8 + face, LANES) * own(moved[side])
                x = side * 8 + i
                rows[x] = rows[x] - change
                if x in (7, 8):
                    rows[15 - x] = rows[15 - x] - change
    parts = [None, None]
    for x in range(ROWS):
        residual[x] = solid(rows[x])
        for a in range(2):
            if GROUP_X[a][x] * INVERSE_X[x] != 0.0:
                term = (GROUP_X[a][x] * INVERSE_X[x]) * rows[x]
                parts[a] = term if parts[a] is None else parts[a] + term
    weight = own(geo.inverse_y * geo.inverse_z)
    for a in range(2):
        sums[a : a + 1] = down(parts[a] * weight)

    forward, backward = wide_diagonals(diagonals, 1), wide_diagonals(diagonals, 2)
    fields = to_right + to_left + [into_left[0], into_left[1], into_left[3], into_right[0], into_right[1], into_right[2]]
    flat = jnp.concatenate([solid(contract_y(v, forward)) for v in fields], axis=0)
    flat = contract_z(flat, upper, lower, 1)
    flat = [split(flat[k * 16 : k * 16 + 16]) for k in range(len(fields))]
    to_right, to_left = flat[:3], flat[3:6]
    into_left, into_right = {0: flat[6], 1: flat[7], 3: flat[8]}, {0: flat[9], 1: flat[10], 2: flat[11]}

    def vector(p, i):
        return line_of(vectors, p * 8 + i, WIDE)

    def changes(element, total, close, distant):
        face, other = 7 * element, 7 - 7 * element
        crossed = cross * distant
        return [
            vector(face, i) * total - line_of(bend, element * 8 + i, WIDE) * close - vector(other, i) * crossed
            for i in range(8)
        ]

    moved = []
    for element, change in enumerate(
        (changes(0, to_right[0], into_right[0], into_left[1]), changes(1, to_left[1], into_left[1], into_right[0]))
    ):
        moved += [solid((split(spectrum[element * 8 + i]) + change[i]) * split(inverse[element * 8 + i])) for i in range(8)]
    for side in range(2):
        value, partial = (split(v) for v in read_second(sides[side][FIRST_ROWS + FAR_ROWS :]))
        near_element, far_element = 1 - side, side
        if side == 0:
            close = changes(1, to_left[0], into_left[0], into_right[2])
            distant = changes(0, to_right[2], into_right[2], into_left[0])
        else:
            close = changes(0, to_right[1], into_right[1], into_left[3])
            distant = changes(1, to_left[2], into_left[3], into_right[1])
        face = 7 * near_element
        close = [a * b for a, b in zip(close, divisors_of(geo, near[side][2], lam))]
        distant = [a * b for a, b in zip(distant, divisors_of(geo, far[side][1], lam))]
        value = value + weighted([vector(face, i) for i in range(8)], close)
        partial = partial + weighted([line_of(bend, near_element * 8 + i, WIDE) for i in range(8)], close)
        partial = partial + cross * weighted([vector(face, i) for i in range(8)], distant)
        moved += [solid(value), solid(partial)]

    back = contract_z(jnp.concatenate(moved, axis=0), upper, lower, 2)
    back = [contract_y(split(back[k * 16 : k * 16 + 16]), backward) for k in range(ROWS + 4)]
    solved = []
    for element in range(2):
        inside = back[element * 8 : element * 8 + 8]
        solved += [contract_x(inside, vectors, i) for i in range(8)]
    total = None
    for x in range(ROWS):
        term = own(solved[x]) * rows[x]
        total = term if total is None else total + term
    sums[2:3] = down(total)
    sums[3:8] = jnp.zeros((5, LANES), jnp.float32)
    solved = join_middle(solved)
    solved[0], solved[15] = solved[0] + back[16], solved[15] + back[18]
    for x in range(ROWS):
        local[x] = solid(geo.assemble(solved[x]))
    for side in range(2):
        beside[side] = solid(geo.assemble(back[17 + 2 * side]))


def image_kernel(
    local, factors, face_factors, beside, sums, fixed, stiffness, lines, upper, lower, diagonals,
    image, payload,
):
    geo = Geometry(WIDE)
    rows = [split(local[x]) for x in range(ROWS)]
    along_z = contract_z(jnp.concatenate([solid(v) for v in rows], axis=0), upper, lower, 0)
    scaled = [stored_factors(factors, e) for e in range(2)]
    stiff = wide_diagonals(diagonals, 0)
    applied = apply_rows(rows, along_z, scaled, stiffness, stiff)
    total, parts = None, [None, None]
    for x in range(ROWS):
        term = own(applied[x]) * own(rows[x])
        total = term if total is None else total + term
        for a in range(2):
            if GROUP_X[a][x] != 0.0:
                term = GROUP_X[a][x] * own(applied[x])
                parts[a] = term if parts[a] is None else parts[a] + term
    extra = [down(value * own(geo.keep)) for value in parts + [total]]
    for side, x, across in ((0, 0, 63), (1, 15, 0)):
        there = [split(face_factors[side, c]) for c in range(3)]
        other = there[0] * (split(beside[side]) + line_of(stiffness, across, WIDE) * rows[x])
        turned = split(along_z[x * 16 : x * 16 + 16])
        other = other + WEIGHTS[0] * (there[1] * contract_y(rows[x], stiff) + there[2] * turned)
        applied[x] = applied[x] + other
    applied = join_middle(applied)
    for x in range(ROWS):
        image[x] = solid(own(geo.assemble(applied[x])))
    zero = jnp.zeros((1, LANES), jnp.float32)
    table = jnp.concatenate(
        [sums[0:2], extra[0], extra[1], fixed[0:9], sums[2:3], extra[2], zero], axis=0
    )
    reduced = contract_z(table, upper, lower, 3)
    mine = (iota((16, LANES), 1) >> 3) == iota((16, LANES), 0)
    row = jnp.sum(jnp.where(mine, reduced, 0.0), axis=0, keepdims=True) + fixed[16:17]
    block = jnp.concatenate([row, fixed[17:18]] * 4, axis=0)
    copies = payload.shape[0] // 8
    payload[...] = jnp.broadcast_to(block[None], (copies, 8, LANES)).reshape(copies * 8, LANES)


def middle_kernel(
    known, factors, halves, remainder, spectrum, inverse, got_a, got_b, got_c, waves,
    stiffness, vectors, bend, lam, upper, lower, diagonals, fixed, lines,
    start_faces, residual, local, face_factors, image, payload, beside, sums,
):
    solve_kernel(
        known, factors, halves, remainder, spectrum, inverse, got_a, got_b, got_c, waves,
        stiffness, vectors, bend, lam, upper, lower, diagonals,
        start_faces, residual, local, beside, face_factors, sums,
    )
    image_kernel(
        local, factors, face_factors, beside, sums, fixed, stiffness, lines, upper, lower, diagonals, image, payload
    )


def lane_tables():
    one = np.zeros((8, LANES), np.float32)
    two = np.zeros((8, LANES), np.float32)
    top = np.zeros((8, LANES), np.float32)
    for a in range(2):
        for b in range(3):
            one[6, 8 * a + b], two[3 * a + b, 8 * a + b], top[0, 8 * a + b] = 1.0, 1.0, 1.0
            one[6, 8 * (2 + a) + b], two[3 * a + b, 8 * (2 + a) + b] = 2.0, 1.0
            top[1, 8 * (2 + a) + b] = 1.0
    for p, (a, other) in enumerate(PAIRS):
        for b in range(3):
            for c in range(3):
                at = 8 * (4 + 3 * p + b) + c
                one[3 * a + b, at] = 1.0 if a == other else 2.0
                two[3 * other + c, at] = 1.0
                top[1, at] = 1.0
    one[6, 8 * 13 + 3], two[6, 8 * 13 + 3], top[0, 8 * 13 + 3] = 1.0, 1.0, 1.0
    one[6, 8 * 14 + 3], two[6, 8 * 14 + 3], top[1, 8 * 14 + 3] = 1.0, 1.0, 1.0
    return np.stack([one, two, top])


def final_kernel(
    devices, spans, count, per,
    start, start_faces, residual, local, image, pieces, face_factors, waves, stiff_keep, lines, tables,
    gathered, given, new_solution, new_residual, values,
):
    rows = gathered[pl.ds(0, devices, stride=2), :]
    if given is None:
        spot = iota((devices, count), 1)
        hits = []
        rhs = [jnp.zeros((1, devices), jnp.float32) for _ in range(per)]
        owner = iota((devices, devices), 1)
        for k in range(6):
            label = rows[:, 8 * k + 4 : 8 * k + 5].astype(jnp.int32)
            at = 8 * (k // 3) + k % 3
            value = rows[:, at : at + 1]
            hits.append(spot == label)
            for q in range(per):
                chosen = jnp.where(owner * per + q == label, value, 0.0)
                rhs[q] = rhs[q] + jnp.sum(chosen, axis=0, keepdims=True)
        inverse = gathered[pl.ds(1, devices, stride=2), :]
        coarse = None
        for q in range(per):
            term = jnp.dot(
                rhs[q], inverse[:, q * count : q * count + count], precision=EXACT,
                preferred_element_type=jnp.float32,
            )
            coarse = term if coarse is None else coarse + term
        columns = [jnp.sum(jnp.where(hit, coarse, 0.0), axis=1, keepdims=True) for hit in hits]
        kept = jnp.zeros((devices, LANES), jnp.float32)
        for k in range(6):
            kept = jnp.where(iota((devices, LANES), 1) == k, columns[k], kept)
        values[...] = kept
    else:
        columns = [given[:, k : k + 1] for k in range(6)]
        values[...] = given[...]
    one, two = tables[0, 6:7, :], tables[1, 6:7, :]
    for k in range(6):
        one = one + columns[k] * tables[0, k : k + 1, :]
        two = two + columns[k] * tables[1, k : k + 1, :]
    product = jnp.sum(rows * one * two, axis=0, keepdims=True)
    numerator = jnp.sum(product * tables[2, 0:1, :], axis=1, keepdims=True)
    denominator = jnp.sum(product * tables[2, 1:2, :], axis=1, keepdims=True)
    alpha = numerator / denominator

    gx, gz = lax.axis_index("gx"), lax.axis_index("gz")
    before_x = lax.rem(gx + devices // spans - 1, devices // spans)
    before_z = lax.rem(gz + spans - 1, spans)
    here = values[pl.ds(gx * spans + gz, 1), :]
    behind = values[pl.ds(gx * spans + before_z, 1), :]
    aside = values[pl.ds(before_x * spans + gz, 1), :]
    corner = values[pl.ds(before_x * spans + before_z, 1), :]

    def four(line, back, a):
        return [back[:, 3 * a + 1 : 3 * a + 2]] + [line[:, 3 * a + b : 3 * a + b + 1] for b in range(3)]

    def mix(numbers, ref):
        total = numbers[0] * ref[0]
        for b in range(1, 4):
            total = total + numbers[b] * ref[b]
        return total

    near, right, left = four(here, behind, 0), four(here, behind, 1), four(aside, corner, 0)
    whole = [mix(near, pieces.at[0, k]) for k in range(2)]
    low = [mix(near, pieces.at[1, k]) for k in range(2)]
    high = [mix(right, pieces.at[1, k]) for k in range(2)]

    def stiff(line, i):
        return lines[line, i : i + 1, :]

    extra = [stiff(0, i) * whole[0] + WEIGHTS[i] * whole[1] for i in range(8)]
    for i in range(8):
        extra.append(
            stiff(1, i) * low[0] + stiff(2, i) * high[0] + WEIGHTS[i] * (LOW[i] * low[1] + HIGH[i] * high[1])
        )
    extra = join_middle(extra)
    geo = Geometry(WIDE)

    def line(numbers, at):
        total = numbers[0] * waves[at : at + 1, :]
        for b in range(1, 4):
            total = total + numbers[b] * waves[at + b : at + b + 1, :]
        return total

    def wide_stiff(k, i):
        return jnp.concatenate([stiff(k, i)] * (WIDE // LANES), axis=1)

    def beyond(side, stiff_x, plain, turned):
        fx, fy, fz = (split(face_factors[side, c]) for c in range(3))
        value = fx * geo.keep * stiff_x[None]
        value = value + WEIGHTS[0] * (fy * split(stiff_keep[...]) * plain[None] + fz * geo.keep * turned[None])
        return solid(own(geo.assemble(value)))

    wave_near, wave_right = line(near, 0), line(right, 0)
    across = wide_stiff(1, 7) * line(left, 0) + wide_stiff(2, 7) * wave_near
    extra[0] = extra[0] + beyond(0, across, wave_near, line(near, 4))
    extra[15] = extra[15] + beyond(1, wide_stiff(0, 0) * wave_right, wave_right, line(right, 4))
    keep = solid(own(geo.keep))
    line_near, line_right = wave_near[:, :LANES], wave_right[:, :LANES]
    for x in range(ROWS):
        begin = start_faces[x // 15] if x in (0, 15) else start[x]
        mine = local[x, :, :LANES]
        new_residual[x] = residual[x] - alpha * (image[x] + extra[x])
        coarse_line = GROUP_X[0][x] * line_near
        if GROUP_X[1][x] != 0.0:
            coarse_line = coarse_line + GROUP_X[1][x] * line_right
        new_solution[x] = begin + alpha * (mine + keep * coarse_line)


VMEM = pl.BlockSpec(memory_space=pltpu.VMEM)
SMEM = pl.BlockSpec(memory_space=pltpu.SMEM)
FAR = pl.BlockSpec(memory_space=pltpu.HBM)


def call(kernel, shapes, specs, name, scratch=(), cost=None):
    def leaf(shape):
        kind = jnp.float32
        if shape[0] == "half":
            shape, kind = shape[1:], jnp.bfloat16
        return jax.ShapeDtypeStruct(shape, kind)

    return pl.pallas_call(
        kernel,
        out_shape=[leaf(shape) for shape in shapes],
        in_specs=specs,
        out_specs=[VMEM] * len(shapes),
        scratch_shapes=list(scratch),
        compiler_params=pltpu.CompilerParams(vmem_limit_bytes=16 * 1024 * 1024),
        name=name,
        cost_estimate=cost,
    )


def swap(first, second, axis):
    size = lax.axis_size(axis)
    odd = [(i, (i + 1) % size) for i in range(1, size, 2)]
    one = lax.ppermute(first, axis, [(i, i ^ 1) for i in range(size)])
    two = lax.ppermute(second, axis, odd + [(b, a) for a, b in odd])
    return one, two


def second_neighbours(common, axis):
    size = lax.axis_size(axis)
    if size == 4:
        return lax.ppermute(common, axis, [(i, i ^ 2) for i in range(size)])
    left = lax.ppermute(common[:FIRST_ROWS], axis, [(i, (i - 2) % size) for i in range(size)])
    right = lax.ppermute(common[FIRST_ROWS:], axis, [(i, (i + 2) % size) for i in range(size)])
    return jnp.concatenate([left, right], axis=0)


def body(
    source, previous, coefficients, stiffness, fdm_vectors, fdm_values, coarse_inverse, vertex_map
):
    assert source.shape == (ROWS, ROWS, LANES)
    spans = lax.axis_size("gz")
    devices = lax.axis_size("gx") * spans
    per, count = coarse_inverse.shape
    small = per * count <= LANES
    block, wide, face = (ROWS, ROWS, LANES), (ROWS, ROWS, WIDE), (ROWS, LANES)
    halo = (13, 8, LANES)

    first, second, elements, source, previous = call(
        pack_kernel,
        [halo, halo, face, block, block],
        [FAR] * 3,
        "pack",
        [pltpu.VMEM(coefficients.shape, jnp.float32), pltpu.SemaphoreType.DMA((3,))],
    )(*(pltpu.with_memory_space_constraint(v, pltpu.HBM) for v in (source, previous, coefficients)))
    first, second = swap(first, second, "gz")
    own_metrics, upper, lower, diagonals, stiff, vectors, bend, lam, lines, fixed, tables = call(
        functools.partial(prepare_kernel, small),
        [
            face, ("half", 4, WIDE, WIDE), ("half", 4, WIDE, LANES), (3, 8, 8, LANES),
            (64, LANES), (64, LANES), (16, LANES), (2, 8, LANES), (3, 8, LANES), (24, LANES), (3, 8, LANES),
        ],
        [VMEM] * 3 + [SMEM] * 2 + [VMEM if small else FAR, VMEM],
        "prepare",
    )(elements, stiffness, fdm_vectors, fdm_values, vertex_map, coarse_inverse, jnp.asarray(lane_tables()))

    message = (FIRST_ROWS + FAR_ROWS + SECOND_ROWS, LANES)
    start, remainder, factors, halves, common, part, metrics = call(
        start_kernel,
        [
            block, wide, (3, 2, ROWS, WIDE), (2, ROWS, WIDE), (2 * FIRST_ROWS + 16, LANES),
            (2, FIRST_ROWS + FAR_ROWS, LANES), (16, WIDE),
        ],
        [VMEM] * 9,
        "start",
    )(source, previous, own_metrics, first, second, stiff, upper, lower, diagonals)
    beyond = second_neighbours(common, "gx")
    known, spectrum, inverse, side_a, side_b = call(
        guess_kernel, [wide, wide, wide, message, message], [VMEM] * 10, "guess",
        cost=pl.CostEstimate(flops=4000000000, bytes_accessed=4000000, transcendentals=0),
    )(remainder, metrics, part, stiff, vectors, bend, lam, upper, lower, diagonals)
    side_a, side_b = swap(side_a, side_b, "gx")
    pieces, waves, stiff_keep = call(
        ready_kernel, [(2, 2, 4, ROWS, LANES), (8, WIDE), (ROWS, WIDE)], [VMEM] * 5, "ready"
    )(factors, stiff, lines, upper, lower)

    start_faces, residual, local, face_factors, image, payload = call(
        middle_kernel,
        [(2, ROWS, LANES), block, wide, (2, 3, ROWS, WIDE), block, (2 * devices, LANES)],
        [VMEM] * 19,
        "middle",
        [pltpu.VMEM((2, ROWS, WIDE), jnp.float32), pltpu.VMEM((8, LANES), jnp.float32)],
    )(
        known, factors, halves, remainder, spectrum, inverse, side_a, side_b, beyond, waves,
        stiff, vectors, bend, lam, upper, lower, diagonals, fixed, lines,
    )
    gathered = lax.all_to_all(payload.reshape(devices, 2, LANES), ("gx", "gz"), 0, 0)
    gathered = gathered.reshape(2 * devices, LANES)

    operands = [
        start, start_faces, residual, local, image, pieces, face_factors, waves, stiff_keep, lines,
        tables, gathered,
    ]
    finish = functools.partial(final_kernel, devices, spans, count, per)
    if small:

        def kernel(*refs):
            finish(*refs[:12], None, *refs[12:])

    else:
        kernel = finish
        rows = gathered[0::2]
        labels = rows[:, jnp.array([8 * k + 4 for k in range(6)])].astype(jnp.int32)
        parts = rows[:, jnp.array([8 * (k // 3) + k % 3 for k in range(6)])]
        rhs = jnp.zeros((count,), jnp.float32).at[labels.reshape(-1)].add(parts.reshape(-1))
        mine = jnp.dot(coarse_inverse, rhs, precision=EXACT)
        coarse = lax.all_gather(mine, ("gx", "gz"), axis=0, tiled=True)
        operands.append(jnp.pad(coarse[labels], ((0, 0), (0, LANES - 6))))
    return tuple(
        call(kernel, [block, block], [VMEM] * len(operands), "finish", [pltpu.VMEM((devices, LANES), jnp.float32)])(
            *operands
        )
    )


def solution(mesh):
    placed = (
        P("gx", None, "gz"),
        P("gx", None, "gz"),
        P(None, "gx", None, "gz"),
        P(),
        P(),
        P(),
        P(("gx", "gz"), None),
        P(None, "gx", None, "gz"),
    )
    return jax.shard_map(
        body,
        mesh=mesh,
        in_specs=placed,
        out_specs=(P("gx", None, "gz"), P("gx", None, "gz")),
        check_vma=False,
    )
```

```python
import functools

import jax
import jax.numpy as jnp
import numpy as np
from jax import lax
from jax.experimental import pallas as pl
from jax.experimental.pallas import tpu as pltpu
from jax.sharding import PartitionSpec as P

POINTS = [
    -1.0,
    -0.8717401485096066,
    -0.5917001814331423,
    -0.2092992179024789,
    0.2092992179024789,
    0.5917001814331423,
    0.8717401485096066,
    1.0,
]
WEIGHTS = [
    0.03571428571428571,
    0.21070422714350603,
    0.34112269248350435,
    0.4124587946587038,
    0.4124587946587038,
    0.34112269248350435,
    0.21070422714350603,
    0.03571428571428571,
]
ONES = [1.0] * 8
LOW = [(1.0 - s) / 2.0 for s in POINTS]
HIGH = [(1.0 + s) / 2.0 for s in POINTS]
EXACT = lax.Precision.HIGHEST

ROWS = 16
LANES = 128
WIDE = 256
HALO = 32
ELEMENTS = 22
CORNERS = (58, 80)
DEEP, SHALLOW = 25, 17
SLOT = DEEP + SHALLOW
FIRST_FIELDS = ((0, 24), (41, 17))
SECOND_FIELDS = ((0, 16), (32, 16), (64, 16), (96, 16))
FAR_FIELDS = ((0, 24), (48, 24))
FIRST_ROWS, FAR_ROWS, SECOND_ROWS = 48, 24, 40
PAIRS = ((0, 0), (0, 1), (1, 1))
GROUP_X = (ONES + LOW, [0.0] * 8 + HIGH)
INVERSE_X = [0.5] + [1.0] * 6 + [0.5] + [0.5] + [1.0] * 6 + [0.5]


def iota(shape, dim):
    return lax.broadcasted_iota(jnp.int32, shape, dim)


def pick(index, values):
    result = jnp.full(index.shape, values[0], jnp.float32)
    for i in range(1, 8):
        result = jnp.where(index == i, values[i], result)
    return result


def even_index(axis):
    return lax.rem(lax.axis_index(axis), 2) == 0


class Geometry:
    def __init__(self, lanes):
        shape = (2, 8, lanes)
        self.element_y, self.row, lane = iota(shape, 0), iota(shape, 1), iota(shape, 2)
        self.position = lane & 7
        self.first = self.position == 0
        self.last = self.position == 7
        self.edge = self.first | self.last
        self.weight_y = pick(self.row, WEIGHTS)
        self.weight_z = pick(self.position, WEIGHTS)
        self.inverse_z = jnp.where(self.edge, 0.5, 1.0)
        self.wall = (self.element_y == 1) & (self.row == 7)
        inner = ((self.element_y == 0) & (self.row == 7)) | ((self.element_y == 1) & (self.row == 0))
        self.inverse_y = jnp.where(inner, 0.5, 1.0)
        self.keep = jnp.where(self.wall, 0.0, 1.0)
        self.lanes = lanes

    def pair_y(self, v):
        lower, upper = v[0], v[1]
        row = self.row[0]
        up = jnp.where(row == 7, pltpu.roll(upper, 7, 0), 0.0)
        down = jnp.where(row == 0, pltpu.roll(lower, 1, 0), 0.0)
        return jnp.stack([lower + up, upper + down])

    def pair_z(self, v):
        flat = v.reshape(16, self.lanes)
        after = pltpu.roll(flat, self.lanes - 1, 1).reshape(v.shape)
        before = pltpu.roll(flat, 1, 1).reshape(v.shape)
        return v + jnp.where(self.edge, jnp.where(self.last, after, before), 0.0)

    def pair(self, v):
        return self.pair_z(self.pair_y(v))

    def assemble(self, v):
        return self.pair(v) * self.keep


def solid(v):
    return v.reshape(ROWS, v.shape[-1])


def split(v):
    return v.reshape(2, 8, v.shape[-1])


def own(v):
    return v[..., :LANES]


def down(v):
    return jnp.sum(v.reshape(ROWS, LANES), axis=0, keepdims=True)


def line_of(ref, at, lanes):
    row = ref[at : at + 1, :]
    return jnp.concatenate([row] * (lanes // LANES), axis=1)[None]


def weighted(factors, rows):
    total = None
    for factor, row in zip(factors, rows):
        total = factor * row if total is None else total + factor * row
    return total


def divisors_of(geo, c, lam):
    lam_y = jnp.concatenate([lam[0]] * (WIDE // LANES), axis=1)[None]
    lam_z = jnp.concatenate([lam[1]] * (WIDE // LANES), axis=1)[None]
    base = c[1] * lam_y + c[2] * lam_z
    return [1.0 / (c[0] * line_of(lam.at[0], i, WIDE) + base) for i in range(8)]


def contract_x(rows, table, i, transpose=False):
    total = None
    for p in range(8):
        factor = line_of(table, p * 8 + i if transpose else i * 8 + p, WIDE)
        term = factor * rows[p]
        total = term if total is None else total + term
    return total


def contract_y(v, diagonals):
    def moved(value, rows):
        return jnp.stack([pltpu.roll(value[e], 8 - rows, 0) for e in range(2)])

    shifted = [v] + [moved(v, d) for d in range(1, 4)]
    return weighted(diagonals[:4], shifted) + moved(weighted(diagonals[4:], shifted), 4)


def thirds(v):
    high = v.astype(jnp.bfloat16)
    rest = v - high.astype(jnp.float32)
    middle = rest.astype(jnp.bfloat16)
    return high, middle, (rest - middle.astype(jnp.float32)).astype(jnp.bfloat16)


def contract_z(flat, upper, lower, which, short=False):
    pieces = []
    for at in range(0, flat.shape[1], LANES):
        high, middle, low = thirds(flat[:, at : at + LANES])
        one = jnp.dot(
            jnp.concatenate([high, middle], axis=1), upper[which], preferred_element_type=jnp.float32
        )
        if short:
            pieces.append(one[:, :LANES] + one[:, LANES:])
            continue
        two = jnp.dot(jnp.concatenate([low, high], axis=1), lower[which], preferred_element_type=jnp.float32)
        pieces.append(one[:, :LANES] + (one[:, LANES:] + two))
    return pieces[0] if len(pieces) == 1 else jnp.concatenate(pieces, axis=1)


def wide_diagonals(ref, which):
    return [jnp.concatenate([ref[which, d]] * (WIDE // LANES), axis=1)[None] for d in range(8)]


def metric(ref, component, element):
    at = (component * 2 + element) * 2
    return jnp.stack([jnp.broadcast_to(ref[at + e : at + e + 1, :], (8, WIDE)) for e in range(2)])


def scaled_metrics(geo, c):
    return c[0] * geo.weight_y * geo.weight_z, c[1] * geo.weight_z, c[2] * geo.weight_y


def stored_factors(ref, element):
    return [split(ref[c, element]) for c in range(3)]


def apply_rows(rows, along_z, factors, stiffness, diagonals):
    result = []
    for element in range(2):
        factor_x, factor_y, factor_z = factors[element]
        inside = rows[element * 8 : element * 8 + 8]
        for i in range(8):
            x = element * 8 + i
            term_y = factor_y * contract_y(inside[i], diagonals)
            term_z = factor_z * split(along_z[x * 16 : x * 16 + 16])
            result.append(factor_x * contract_x(inside, stiffness, i) + WEIGHTS[i] * (term_y + term_z))
    return result


def join_middle(rows):
    middle = rows[7] + rows[8]
    return rows[:7] + [middle, middle] + rows[9:]


def fold(parts, fields):
    lane = iota((8, LANES), 1)
    result = parts[0]
    for part, (offset, half) in list(zip(parts, fields))[1:]:
        taken = ((lane - offset + half) & (LANES - 1)) < 2 * half
        result = jnp.where(taken, pltpu.roll(part, offset, 1), result)
    return result


def unfold(packed, field, fill=0.0):
    offset, half = field
    lane = iota((8, LANES), 1)
    moved = pltpu.roll(packed, LANES - offset, 1) if offset else packed
    return jnp.where(((lane + half) & (LANES - 1)) < 2 * half, moved, fill)


def widen(tile, pieces):
    return jnp.concatenate([tile, jnp.concatenate(pieces, axis=0)], axis=1)


def group_lanes(lanes, group):
    lane = iota((1, lanes), 1)
    signed = jnp.where(lane < lanes // 2 + lanes // 4, lane, lane - lanes) if lanes > LANES else lane
    element, position = signed >> 3, lane & 7
    low, high = pick(position, LOW), pick(position, HIGH)
    here = jnp.where((element >> 3) == group, low, 0.0)
    return here + jnp.where(((element + 1) >> 3) == group, high, 0.0)


def pack_kernel(source, previous, coefficients, first, second, elements, near_source, near_previous, raw, ready):
    copies = [
        pltpu.make_async_copy(source, near_source, ready.at[0]),
        pltpu.make_async_copy(previous, near_previous, ready.at[1]),
        pltpu.make_async_copy(coefficients, raw, ready.at[2]),
    ]
    for copy in copies:
        copy.start()
    even = even_index("gz")
    elements[...] = jnp.zeros_like(elements)
    for copy in copies:
        copy.wait()
    for c in range(3):
        for element in range(2):
            at = (c * 2 + element) * 2
            elements[at : at + 2, 0:16] = raw[c, element]
    slot = iota((8, LANES), 1)
    for to_right, out in ((even, first), (jnp.logical_not(even), second)):
        for tile in range(11):
            packed = None
            for k in range(3):
                n = 3 * tile + k
                if n >= 2 * ROWS:
                    break
                for ref, width, at in ((near_previous, DEEP, SLOT * k), (near_source, SHALLOW, SLOT * k + DEEP)):
                    shift = jnp.where(to_right, (at + width) % LANES, at)
                    moved = pltpu.roll(ref[n // 2, 8 * (n % 2) : 8 * (n % 2) + 8], shift, 1)
                    packed = moved if packed is None else jnp.where(slot >= at, moved, packed)
            out[tile] = packed
        out[11] = elements[:8]
        out[12] = elements[8:]


def lanes_of(elements):
    lane = iota((24, WIDE), 1)
    beyond = lane - LANES
    right, left = LANES + 3 * 8, WIDE - 3 * 8
    index = jnp.where(lane < right, lane >> 3, jnp.where(lane >= left, 19 + ((beyond - (left - LANES)) >> 3), ELEMENTS))
    spread = (iota((24, WIDE), 0) == index).astype(jnp.float32)
    return jnp.dot(elements[:, 0:24], spread, precision=EXACT, preferred_element_type=jnp.float32)


def elements_of(folded):
    lane = iota((8, LANES), 1)
    rest = jnp.where(lane == ELEMENTS, 1.0, 0.0)
    return jnp.concatenate(
        [jnp.where(lane < ELEMENTS, pltpu.roll(folded, LANES - at, 1), rest) for at in CORNERS], axis=0
    )


def prepare_kernel(
    with_coarse, elements, stiffness, vectors, eigen, labels, coarse, tables,
    upper, lower, diagonals, stiff_table, vector_table, bend, lam, lines, fixed, near_tables,
):
    near_tables[...] = tables[...]
    widen = (iota((16, LANES), 0) == (iota((16, LANES), 1) >> 3)).astype(jnp.float32)
    metrics = jnp.dot(elements[:, 0:16], widen, precision=EXACT, preferred_element_type=jnp.float32)
    repeat = (iota((LANES, 8), 0) & 7 == iota((LANES, 8), 1)).astype(jnp.float32)
    same = (iota((LANES, LANES), 0) >> 3) == (iota((LANES, LANES), 1) >> 3)
    unit = (iota((8, 8), 0) == iota((8, 8), 1)).astype(jnp.float32)
    row, column = iota((8, 8), 0), iota((8, 8), 1)

    def dot(a, b, dims):
        return lax.dot_general(a, b, (dims, ((), ())), precision=EXACT, preferred_element_type=jnp.float32)

    def put_block(at, matrix):
        half = dot(repeat, matrix, ((1,), (0,)))
        put_thirds(at, jnp.where(same, dot(half, repeat, ((1,), (1,))), 0.0))

    def put_thirds(at, block):
        high, middle, low = thirds(block)
        both = jnp.concatenate([high, middle], axis=1)
        upper[at] = jnp.concatenate([both, both], axis=0)
        lower[at] = jnp.concatenate([high, low], axis=0)

    def put_diagonals(at, matrix):
        turned = jnp.concatenate([matrix[4:], matrix[:4]], axis=0)
        for d in range(8):
            chosen = jnp.where(column == ((row + d % 4) & 7), matrix if d < 4 else turned, 0.0)
            diagonals[at, d] = jnp.broadcast_to(jnp.sum(chosen, axis=1, keepdims=True), (8, LANES))

    def put_table(out, matrix):
        tall = (iota((64, 8), 0) >> 3 == iota((64, 8), 1)).astype(jnp.float32)
        chosen = jnp.where(iota((64, 8), 0) & 7 == iota((64, 8), 1), dot(tall, matrix, ((1,), (0,))), 0.0)
        out[...] = jnp.broadcast_to(jnp.sum(chosen, axis=1, keepdims=True), (64, LANES))

    lane = iota((LANES, LANES), 1) & 7
    node = iota((LANES, LANES), 0)
    element, position = node >> 3, node & 7
    low, high = pick(position, LOW), pick(position, HIGH)
    columns = jnp.where(lane == (element >> 3), low, 0.0) + jnp.where(lane == ((element + 1) >> 3), high, 0.0)
    columns = jnp.where(lane == 3, 1.0, jnp.where(lane < 3, columns, 0.0))
    put_thirds(3, columns)
    k, s = stiffness[...], vectors[...]
    k_turned, s_turned = dot(k, unit, ((0,), (0,))), dot(s, unit, ((0,), (0,)))
    for at, matrix in enumerate((k_turned, s, s_turned)):
        put_block(at, matrix)
    for at, matrix in enumerate((k, s_turned, s)):
        put_diagonals(at, matrix)
    put_table(stiff_table, k)
    put_table(vector_table, s)
    for side, near in ((0, 0), (1, 7)):
        chosen = jnp.where(column == near, 0.0, s_turned * k[near : near + 1, :])
        total = jnp.sum(chosen, axis=1, keepdims=True)
        bend[8 * side : 8 * side + 8] = jnp.broadcast_to(total, (8, LANES))
    values = [eigen[i] for i in range(8)]
    lam[0] = pick(iota((8, LANES), 0), values)
    lam[1] = pick(iota((8, LANES), 1) & 7, values)
    stiff_lines = []
    for at, line in enumerate((ONES, LOW, HIGH)):
        total = jnp.sum(k * pick(column, line), axis=1, keepdims=True)
        stiff_lines.append(jnp.broadcast_to(total, (8, LANES)))
        lines[at] = stiff_lines[at]

    groups = [group_lanes(LANES, b) for b in range(3)]
    stacked = jnp.concatenate(groups + [jnp.zeros((13, LANES), jnp.float32)], axis=0)
    stiff_z = contract_z(stacked, upper, lower, 0)
    weight_z = pick(iota((1, LANES), 1) & 7, WEIGHTS)
    node = iota((8, LANES), 0)
    mass_y = [sum(WEIGHTS), sum(WEIGHTS[:7])]
    last = jnp.broadcast_to(k[:, 7:8], (8, LANES))
    inner = jnp.where(node == 7, 0.0, stiff_lines[0] - last)
    stiff_y = [jnp.sum(v, axis=0, keepdims=True) for v in (stiff_lines[0], inner)]
    at = 0
    for a, b in PAIRS:
        across, along = jnp.zeros((1, LANES), jnp.float32), jnp.zeros((1, LANES), jnp.float32)
        for element in range(2):
            fa = GROUP_X[a][element * 8 : element * 8 + 8]
            fb = GROUP_X[b][element * 8 : element * 8 + 8]
            if not (any(fa) and any(fb)):
                continue
            mass_x = sum(w * p * q for w, p, q in zip(WEIGHTS, fa, fb))
            applied = stiff_lines[0 if fb == ONES else 1 + b]
            stiff_x = jnp.sum(applied * pick(node, fa), axis=0, keepdims=True)
            for e in range(2):
                cx, cy, cz = (metrics[(c * 2 + element) * 2 + e].reshape(1, LANES) for c in range(3))
                across = across + cx * (stiff_x * mass_y[e]) + cy * (stiff_y[e] * mass_x)
                along = along + cz * (mass_x * mass_y[e])
        across = across * weight_z
        for b in range(3):
            fixed[at : at + 1] = across * groups[b] + along * stiff_z[b : b + 1]
            at += 1
    fixed[9:16] = jnp.zeros((7, LANES), jnp.float32)
    place = iota((1, LANES), 1)
    numbers = jnp.zeros((1, LANES), jnp.float32)
    for a in range(2):
        for b in range(3):
            corner, x, z = 4 * a + (b == 2), a, (0, 8, 15)[b]
            number = labels[corner, x, 0, z].astype(jnp.float32)
            numbers = jnp.where(place == 8 * (3 * a + b) + 4, number, numbers)
    fixed[16:17] = numbers
    below = jnp.zeros((1, LANES), jnp.float32)
    if with_coarse:
        per, count = coarse.shape
        below = [coarse[i : i + 1, :] for i in range(per)]
        if per * count < LANES:
            below.append(jnp.zeros((1, LANES - per * count), jnp.float32))
        below = jnp.concatenate(below, axis=1)
    fixed[17:18] = below
    fixed[18:24] = jnp.zeros((6, LANES), jnp.float32)


def start_kernel(
    source, previous, elements, first, second, stiffness, upper, lower, diagonals,
    start, remainder, factors, halves, common, part, metrics,
):
    even = even_index("gz")
    lane = iota((8, LANES), 1)
    one, two = first[...], second[...]
    from_right, from_left = jnp.where(even, one, two), jnp.where(even, two, one)

    def beyond(n, at, width):
        at = at + SLOT * (n % 3)
        right, left = from_right[n // 3], from_left[n // 3]
        if at:
            right = pltpu.roll(right, LANES - at, 1)
        left = pltpu.roll(left, (LANES - width - at) % LANES, 1)
        return jnp.where(lane < width, right, jnp.where(lane >= LANES - width, left, 0.0))

    def wide(ref, x, at, width):
        return split(widen(ref[x], [beyond(2 * x + e, at, width) for e in range(2)]))

    geo = Geometry(WIDE)
    right = pltpu.roll(jnp.concatenate([from_right[11], from_right[12]], axis=0), 16, 1)
    left = pltpu.roll(jnp.concatenate([from_left[11], from_left[12]], axis=0), 6, 1)
    place = iota((16, LANES), 1)
    compact = jnp.where(place < 16, elements[...], jnp.where(place < 19, right, jnp.where(place < ELEMENTS, left, 1.0)))
    metrics[...] = lanes_of(compact)
    factor = geo.keep * geo.inverse_y * geo.inverse_z
    rows = [geo.pair(wide(previous, x, 0, DEEP)) * (factor * INVERSE_X[x]) for x in range(ROWS)]
    rows = join_middle(rows)
    faces = (rows[0], rows[15])
    for x in range(ROWS):
        start[x] = solid(own(rows[x]))
    along_z = contract_z(jnp.concatenate([solid(v) for v in rows], axis=0), upper, lower, 0)
    scaled = [scaled_metrics(geo, [metric(metrics, c, e) for c in range(3)]) for e in range(2)]
    for e in range(2):
        for c in range(3):
            factors[c, e] = solid(scaled[e][c])
    applied = apply_rows(rows, along_z, scaled, stiffness, wide_diagonals(diagonals, 0))
    rest = [wide(source, x, DEEP, SHALLOW) - applied[x] for x in range(ROWS)]
    halves[0], halves[1] = solid(faces[0]), solid(faces[1])
    for x in range(ROWS):
        remainder[x] = solid(rest[x])
    messages, distant = [], []
    for side, x in ((0, 0), (1, 15)):
        half, value = solid(faces[side]), solid(rest[x])
        lower_fold = fold([half[:8, LANES:], value[:8, LANES:]], FIRST_FIELDS)
        upper_fold = fold([half[8:, LANES:], value[8:, LANES:]], FIRST_FIELDS)
        for at, rows in zip(CORNERS, (compact[:8], compact[8:])):
            upper_fold = jnp.where((lane >= at) & (lane < at + ELEMENTS), pltpu.roll(rows, at, 1), upper_fold)
        messages.append(jnp.concatenate([half[:, :LANES], value[:, :LANES], lower_fold, upper_fold], axis=0))
        folded = fold([half[:8, LANES:], half[8:, LANES:]], FAR_FIELDS)
        distant.append(jnp.concatenate([half[:, :LANES], folded], axis=0))
    common[: 2 * FIRST_ROWS] = jnp.concatenate(messages, axis=0)
    common[2 * FIRST_ROWS :] = jnp.zeros((16, LANES), jnp.float32)
    for side in range(2):
        part[side] = jnp.concatenate([messages[side], distant[1 - side]], axis=0)


def guess_kernel(
    remainder, metrics, part, stiffness, vectors, bend, lam, upper, lower, diagonals,
    known, spectrum, inverse, message_a, message_b,
):
    geo = Geometry(WIDE)
    rest = [split(remainder[x]) for x in range(ROWS)]
    rest = [geo.assemble(v) for v in join_middle(rest)]
    forward = wide_diagonals(diagonals, 1)
    moved = []
    for element in range(2):
        inside = rest[element * 8 : element * 8 + 8]
        moved += [solid(contract_y(contract_x(inside, vectors, i, True), forward)) for i in range(8)]
    for x in range(ROWS):
        known[x] = solid(rest[x])
    transformed = contract_z(jnp.concatenate(moved, axis=0), upper, lower, 1, True)
    damped = []
    for element in range(2):
        divisors = divisors_of(geo, [metric(metrics, c, element) for c in range(3)], lam)
        for i in range(8):
            x = element * 8 + i
            value = split(transformed[x * 16 : x * 16 + 16])
            spectrum[x], inverse[x] = solid(value), solid(divisors[i])
            damped.append(value * divisors[i])
    messages = []
    for side, near in ((0, 0), (1, 7)):
        inside, across = damped[side * 8 : side * 8 + 8], damped[8 - side * 8 : 16 - side * 8]
        value = contract_x(inside, vectors, near)
        beside = weighted([line_of(bend, side * 8 + i, WIDE) for i in range(8)], inside)
        beside = beside + line_of(stiffness, near * 8 + 7 - near, WIDE) * contract_x(across, vectors, near)
        value, beside = solid(value), solid(beside)
        folded = fold([v[at : at + 8, LANES:] for v in (value, beside) for at in (0, 8)], SECOND_FIELDS)
        messages.append(jnp.concatenate([value[:, :LANES], beside[:, :LANES], folded], axis=0))
    even_x = even_index("gx")
    both = [jnp.concatenate([part[side], messages[side]], axis=0) for side in range(2)]
    message_a[...] = jnp.where(even_x, both[1], both[0])
    message_b[...] = jnp.where(even_x, both[0], both[1])


def both_sides(even, a, b):
    one, two = a[...], b[...]
    return jnp.where(even, two, one), jnp.where(even, one, two)


def read_first(message):
    lower_fold, upper_fold = message[32:40], message[40:48]
    half, value = (
        widen(message[16 * k : 16 * k + 16], [unfold(lower_fold, FIRST_FIELDS[k]), unfold(upper_fold, FIRST_FIELDS[k])])
        for k in range(2)
    )
    return split(half), split(value)


def read_far(message):
    far = message[FIRST_ROWS : FIRST_ROWS + FAR_ROWS]
    return split(widen(far[0:16], [unfold(far[16:24], field) for field in FAR_FIELDS]))


def read_second(message):
    pieces = [unfold(message[32:40], field) for field in SECOND_FIELDS]
    return widen(message[0:16], pieces[:2]), widen(message[16:32], pieces[2:])


def coarse_pieces(geo, factors, stiff_keep, functions, stiff_functions):
    factor_x, factor_y, factor_z = factors
    kept_x, kept_y, kept_z = factor_x * geo.keep, factor_y * stiff_keep, factor_z * geo.keep
    result = []
    for plain, turned in zip(functions, stiff_functions):
        result.append(
            (geo.assemble(kept_x * plain[None]), geo.assemble(kept_y * plain[None] + kept_z * turned[None]))
        )
    return result


def wide_functions(upper, lower):
    functions = [group_lanes(WIDE, b) for b in (-1, 0, 1, 2)]
    stacked = jnp.concatenate(functions + [jnp.zeros((12, WIDE), jnp.float32)], axis=0)
    turned = contract_z(stacked, upper, lower, 0)
    return functions, [turned[b : b + 1] for b in range(4)]


def kept_stiffness(geo, lines, stiffness):
    row = iota((8, LANES), 0)
    last = jnp.zeros((8, LANES), jnp.float32)
    for j in range(8):
        last = jnp.where(row == j, stiffness[j * 8 + 7 : j * 8 + 8, :], last)
    both = jnp.stack([lines[0], lines[0] - last])
    return jnp.concatenate([both] * (WIDE // LANES), axis=2)


def ready_kernel(factors, stiffness, lines, upper, lower, pieces, waves, stiff_keep):
    geo = Geometry(WIDE)
    functions, turned = wide_functions(upper, lower)
    for b in range(4):
        waves[b : b + 1], waves[4 + b : 5 + b] = functions[b], turned[b]
    along_y = kept_stiffness(geo, lines, stiffness)
    stiff_keep[...] = solid(along_y)
    for element in range(2):
        made = coarse_pieces(geo, stored_factors(factors, element), along_y, functions, turned)
        for b in range(4):
            for k in range(2):
                pieces[element, k, b] = solid(own(made[b][k]))


def solve_kernel(
    known, factors, halves, remainder, spectrum, inverse, got_a, got_b, got_c, _,
    stiffness, vectors, bend, lam, upper, lower, diagonals,
    start_faces, residual, local, beside, face_factors, sums,
):
    even = even_index("gx")
    geo = Geometry(WIDE)
    sides = both_sides(even, got_a, got_b)
    beyond = got_c[...]
    near = [read_first(side) for side in sides]
    far = [read_far(side) for side in sides]
    last = [read_first(beyond[FIRST_ROWS : 2 * FIRST_ROWS]), read_first(beyond[:FIRST_ROWS])]
    mine = [stored_factors(factors, e) for e in range(2)]
    folds = [side[40:48] for side in sides] + [beyond[FIRST_ROWS + 40 : FIRST_ROWS + 48], beyond[40:48]]
    spread = lanes_of(jnp.concatenate([elements_of(folded) for folded in folds], axis=0))

    def metrics_of(device, element):
        return [metric(spread[16 * device : 16 * device + 16], c, element) for c in range(3)]

    near_metrics, far_metrics = [metrics_of(0, 1), metrics_of(1, 0)], [metrics_of(0, 0), metrics_of(1, 1)]
    near_factors, far_factors, last_factors = (
        [scaled_metrics(geo, v) for v in group]
        for group in (near_metrics, far_metrics, [metrics_of(2, 1), metrics_of(3, 0)])
    )
    for side in range(2):
        for c in range(3):
            face_factors[side, c] = solid(near_factors[side][c])
    half = [split(halves[side]) for side in range(2)]
    remain = [split(remainder[x]) for x in (0, 15)]
    left_half = [near[0][0], half[1], last[0][0], far[1]]
    right_half = [half[0], near[1][0], far[0], last[1][0]]
    left_factors = [near_factors[0], mine[1], last_factors[0], far_factors[1]]
    right_factors = [mine[0], near_factors[1], far_factors[0], last_factors[1]]
    stiff = wide_diagonals(diagonals, 0)
    along_z = contract_z(jnp.concatenate([solid(v) for v in left_half + right_half], axis=0), upper, lower, 0)
    first, last_corner = line_of(stiffness, 0, WIDE), line_of(stiffness, 63, WIDE)
    cross = line_of(stiffness, 7, WIDE)
    taken, into_left, into_right = [], [], []
    for k in range(4):
        left, right = left_factors[k][0] * right_half[k], right_factors[k][0] * left_half[k]
        from_left, from_right = split(along_z[k * 16 : k * 16 + 16]), split(along_z[k * 16 + 64 : k * 16 + 80])
        rest = left_factors[k][1] * contract_y(right_half[k], stiff) + right_factors[k][1] * contract_y(left_half[k], stiff)
        rest = rest + left_factors[k][2] * from_right + right_factors[k][2] * from_left
        taken.append(last_corner * left + first * right + WEIGHTS[0] * rest)
        into_left.append(geo.assemble(left) if k != 2 else None)
        into_right.append(geo.assemble(right) if k != 3 else None)
    to_right = [geo.assemble(v - t) for v, t in zip((near[0][1], remain[1], last[0][1]), taken[:3])]
    to_left = [geo.assemble(v - taken[k]) for k, v in ((0, remain[0]), (1, near[1][1]), (3, last[1][1]))]
    for side in range(2):
        start_faces[side] = solid(own(left_half[side] + right_half[side]))

    moved = [into_right[0], into_left[1]]
    rows = [own(split(known[x])) for x in range(ROWS)]
    rows[0], rows[15] = rows[0] + own(to_right[0]), rows[15] + own(to_left[1])
    for side, face in ((0, 0), (1, 7)):
        for i in range(8):
            if i != face:
                change = line_of(stiffness, i * 8 + face, LANES) * own(moved[side])
                x = side * 8 + i
                rows[x] = rows[x] - change
                if x in (7, 8):
                    rows[15 - x] = rows[15 - x] - change
    parts = [None, None]
    for x in range(ROWS):
        residual[x] = solid(rows[x])
        for a in range(2):
            if GROUP_X[a][x] * INVERSE_X[x] != 0.0:
                term = (GROUP_X[a][x] * INVERSE_X[x]) * rows[x]
                parts[a] = term if parts[a] is None else parts[a] + term
    weight = own(geo.inverse_y * geo.inverse_z)
    for a in range(2):
        sums[a : a + 1] = down(parts[a] * weight)

    forward, backward = wide_diagonals(diagonals, 1), wide_diagonals(diagonals, 2)
    fields = to_right + to_left + [into_left[0], into_left[1], into_left[3], into_right[0], into_right[1], into_right[2]]
    flat = jnp.concatenate([solid(contract_y(v, forward)) for v in fields], axis=0)
    flat = contract_z(flat, upper, lower, 1, True)
    flat = [split(flat[k * 16 : k * 16 + 16]) for k in range(len(fields))]
    to_right, to_left = flat[:3], flat[3:6]
    into_left, into_right = {0: flat[6], 1: flat[7], 3: flat[8]}, {0: flat[9], 1: flat[10], 2: flat[11]}

    def vector(p, i):
        return line_of(vectors, p * 8 + i, WIDE)

    def changes(element, total, close, distant):
        face, other = 7 * element, 7 - 7 * element
        crossed = cross * distant
        return [
            vector(face, i) * total - line_of(bend, element * 8 + i, WIDE) * close - vector(other, i) * crossed
            for i in range(8)
        ]

    moved = []
    for element, change in enumerate(
        (changes(0, to_right[0], into_right[0], into_left[1]), changes(1, to_left[1], into_left[1], into_right[0]))
    ):
        moved += [solid((split(spectrum[element * 8 + i]) + change[i]) * split(inverse[element * 8 + i])) for i in range(8)]
    for side in range(2):
        value, partial = (split(v) for v in read_second(sides[side][FIRST_ROWS + FAR_ROWS :]))
        near_element, far_element = 1 - side, side
        if side == 0:
            close = changes(1, to_left[0], into_left[0], into_right[2])
            distant = changes(0, to_right[2], into_right[2], into_left[0])
        else:
            close = changes(0, to_right[1], into_right[1], into_left[3])
            distant = changes(1, to_left[2], into_left[3], into_right[1])
        face = 7 * near_element
        close = [a * b for a, b in zip(close, divisors_of(geo, near_metrics[side], lam))]
        distant = [a * b for a, b in zip(distant, divisors_of(geo, far_metrics[side], lam))]
        value = value + weighted([vector(face, i) for i in range(8)], close)
        partial = partial + weighted([line_of(bend, near_element * 8 + i, WIDE) for i in range(8)], close)
        partial = partial + cross * weighted([vector(face, i) for i in range(8)], distant)
        moved += [solid(value), solid(partial)]

    back = contract_z(jnp.concatenate(moved, axis=0), upper, lower, 2, True)
    back = [contract_y(split(back[k * 16 : k * 16 + 16]), backward) for k in range(ROWS + 4)]
    solved = []
    for element in range(2):
        inside = back[element * 8 : element * 8 + 8]
        solved += [contract_x(inside, vectors, i) for i in range(8)]
    total = None
    for x in range(ROWS):
        term = own(solved[x]) * rows[x]
        total = term if total is None else total + term
    sums[2:3] = down(total)
    sums[3:8] = jnp.zeros((5, LANES), jnp.float32)
    solved = join_middle(solved)
    solved[0], solved[15] = solved[0] + back[16], solved[15] + back[18]
    for x in range(ROWS):
        local[x] = solid(geo.assemble(solved[x]))
    for side in range(2):
        beside[side] = solid(geo.assemble(back[17 + 2 * side]))


def image_kernel(
    local, factors, face_factors, beside, sums, fixed, stiffness, lines, upper, lower, diagonals,
    image, payload,
):
    geo = Geometry(WIDE)
    rows = [split(local[x]) for x in range(ROWS)]
    along_z = contract_z(jnp.concatenate([solid(v) for v in rows], axis=0), upper, lower, 0, True)
    scaled = [stored_factors(factors, e) for e in range(2)]
    stiff = wide_diagonals(diagonals, 0)
    applied = apply_rows(rows, along_z, scaled, stiffness, stiff)
    total, parts = None, [None, None]
    for x in range(ROWS):
        term = own(applied[x]) * own(rows[x])
        total = term if total is None else total + term
        for a in range(2):
            if GROUP_X[a][x] != 0.0:
                term = GROUP_X[a][x] * own(applied[x])
                parts[a] = term if parts[a] is None else parts[a] + term
    extra = [down(value * own(geo.keep)) for value in parts + [total]]
    for side, x, across in ((0, 0, 63), (1, 15, 0)):
        there = [split(face_factors[side, c]) for c in range(3)]
        other = there[0] * (split(beside[side]) + line_of(stiffness, across, WIDE) * rows[x])
        turned = split(along_z[x * 16 : x * 16 + 16])
        other = other + WEIGHTS[0] * (there[1] * contract_y(rows[x], stiff) + there[2] * turned)
        applied[x] = applied[x] + other
    applied = join_middle(applied)
    for x in range(ROWS):
        image[x] = solid(own(geo.assemble(applied[x])))
    zero = jnp.zeros((1, LANES), jnp.float32)
    table = jnp.concatenate(
        [sums[0:2], extra[0], extra[1], fixed[0:9], sums[2:3], extra[2], zero], axis=0
    )
    reduced = contract_z(table, upper, lower, 3)
    mine = (iota((16, LANES), 1) >> 3) == iota((16, LANES), 0)
    row = jnp.sum(jnp.where(mine, reduced, 0.0), axis=0, keepdims=True) + fixed[16:17]
    block = jnp.concatenate([row, fixed[17:18]] * 4, axis=0)
    copies = payload.shape[0] // 8
    payload[...] = jnp.broadcast_to(block[None], (copies, 8, LANES)).reshape(copies * 8, LANES)


def middle_kernel(
    known, factors, halves, remainder, spectrum, inverse, got_a, got_b, got_c, waves,
    stiffness, vectors, bend, lam, upper, lower, diagonals, fixed, lines,
    start_faces, residual, local, face_factors, image, payload, beside, sums,
):
    solve_kernel(
        known, factors, halves, remainder, spectrum, inverse, got_a, got_b, got_c, waves,
        stiffness, vectors, bend, lam, upper, lower, diagonals,
        start_faces, residual, local, beside, face_factors, sums,
    )
    image_kernel(
        local, factors, face_factors, beside, sums, fixed, stiffness, lines, upper, lower, diagonals, image, payload
    )


def lane_tables():
    one = np.zeros((8, LANES), np.float32)
    two = np.zeros((8, LANES), np.float32)
    top = np.zeros((8, LANES), np.float32)
    for a in range(2):
        for b in range(3):
            one[6, 8 * a + b], two[3 * a + b, 8 * a + b], top[0, 8 * a + b] = 1.0, 1.0, 1.0
            one[6, 8 * (2 + a) + b], two[3 * a + b, 8 * (2 + a) + b] = 2.0, 1.0
            top[1, 8 * (2 + a) + b] = 1.0
    for p, (a, other) in enumerate(PAIRS):
        for b in range(3):
            for c in range(3):
                at = 8 * (4 + 3 * p + b) + c
                one[3 * a + b, at] = 1.0 if a == other else 2.0
                two[3 * other + c, at] = 1.0
                top[1, at] = 1.0
    one[6, 8 * 13 + 3], two[6, 8 * 13 + 3], top[0, 8 * 13 + 3] = 1.0, 1.0, 1.0
    one[6, 8 * 14 + 3], two[6, 8 * 14 + 3], top[1, 8 * 14 + 3] = 1.0, 1.0, 1.0
    return np.stack([one, two, top])


def final_kernel(
    devices, spans, count, per,
    start, start_faces, residual, local, image, pieces, face_factors, waves, stiff_keep, lines, tables,
    gathered, given, new_solution, new_residual, values,
):
    rows = gathered[pl.ds(0, devices, stride=2), :]
    if given is None:
        spot = iota((devices, count), 1)
        hits = []
        rhs = [jnp.zeros((1, devices), jnp.float32) for _ in range(per)]
        owner = iota((devices, devices), 1)
        for k in range(6):
            label = rows[:, 8 * k + 4 : 8 * k + 5].astype(jnp.int32)
            at = 8 * (k // 3) + k % 3
            value = rows[:, at : at + 1]
            hits.append(spot == label)
            for q in range(per):
                chosen = jnp.where(owner * per + q == label, value, 0.0)
                rhs[q] = rhs[q] + jnp.sum(chosen, axis=0, keepdims=True)
        inverse = gathered[pl.ds(1, devices, stride=2), :]
        coarse = None
        for q in range(per):
            term = jnp.dot(
                rhs[q], inverse[:, q * count : q * count + count], precision=EXACT,
                preferred_element_type=jnp.float32,
            )
            coarse = term if coarse is None else coarse + term
        columns = [jnp.sum(jnp.where(hit, coarse, 0.0), axis=1, keepdims=True) for hit in hits]
        kept = jnp.zeros((devices, LANES), jnp.float32)
        for k in range(6):
            kept = jnp.where(iota((devices, LANES), 1) == k, columns[k], kept)
        values[...] = kept
    else:
        columns = [given[:, k : k + 1] for k in range(6)]
        values[...] = given[...]
    one, two = tables[0, 6:7, :], tables[1, 6:7, :]
    for k in range(6):
        one = one + columns[k] * tables[0, k : k + 1, :]
        two = two + columns[k] * tables[1, k : k + 1, :]
    product = jnp.sum(rows * one * two, axis=0, keepdims=True)
    numerator = jnp.sum(product * tables[2, 0:1, :], axis=1, keepdims=True)
    denominator = jnp.sum(product * tables[2, 1:2, :], axis=1, keepdims=True)
    alpha = numerator / denominator

    gx, gz = lax.axis_index("gx"), lax.axis_index("gz")
    before_x = lax.rem(gx + devices // spans - 1, devices // spans)
    before_z = lax.rem(gz + spans - 1, spans)
    here = values[pl.ds(gx * spans + gz, 1), :]
    behind = values[pl.ds(gx * spans + before_z, 1), :]
    aside = values[pl.ds(before_x * spans + gz, 1), :]
    corner = values[pl.ds(before_x * spans + before_z, 1), :]

    def four(line, back, a):
        return [back[:, 3 * a + 1 : 3 * a + 2]] + [line[:, 3 * a + b : 3 * a + b + 1] for b in range(3)]

    def mix(numbers, ref):
        total = numbers[0] * ref[0]
        for b in range(1, 4):
            total = total + numbers[b] * ref[b]
        return total

    near, right, left = four(here, behind, 0), four(here, behind, 1), four(aside, corner, 0)
    whole = [mix(near, pieces.at[0, k]) for k in range(2)]
    low = [mix(near, pieces.at[1, k]) for k in range(2)]
    high = [mix(right, pieces.at[1, k]) for k in range(2)]

    def stiff(line, i):
        return lines[line, i : i + 1, :]

    extra = [stiff(0, i) * whole[0] + WEIGHTS[i] * whole[1] for i in range(8)]
    for i in range(8):
        extra.append(
            stiff(1, i) * low[0] + stiff(2, i) * high[0] + WEIGHTS[i] * (LOW[i] * low[1] + HIGH[i] * high[1])
        )
    extra = join_middle(extra)
    geo = Geometry(WIDE)

    def line(numbers, at):
        total = numbers[0] * waves[at : at + 1, :]
        for b in range(1, 4):
            total = total + numbers[b] * waves[at + b : at + b + 1, :]
        return total

    def wide_stiff(k, i):
        return jnp.concatenate([stiff(k, i)] * (WIDE // LANES), axis=1)

    def beyond(side, stiff_x, plain, turned):
        fx, fy, fz = (split(face_factors[side, c]) for c in range(3))
        value = fx * geo.keep * stiff_x[None]
        value = value + WEIGHTS[0] * (fy * split(stiff_keep[...]) * plain[None] + fz * geo.keep * turned[None])
        return solid(own(geo.assemble(value)))

    wave_near, wave_right = line(near, 0), line(right, 0)
    across = wide_stiff(1, 7) * line(left, 0) + wide_stiff(2, 7) * wave_near
    extra[0] = extra[0] + beyond(0, across, wave_near, line(near, 4))
    extra[15] = extra[15] + beyond(1, wide_stiff(0, 0) * wave_right, wave_right, line(right, 4))
    keep = solid(own(geo.keep))
    line_near, line_right = wave_near[:, :LANES], wave_right[:, :LANES]
    for x in range(ROWS):
        begin = start_faces[x // 15] if x in (0, 15) else start[x]
        mine = local[x, :, :LANES]
        new_residual[x] = residual[x] - alpha * (image[x] + extra[x])
        coarse_line = GROUP_X[0][x] * line_near
        if GROUP_X[1][x] != 0.0:
            coarse_line = coarse_line + GROUP_X[1][x] * line_right
        new_solution[x] = begin + alpha * (mine + keep * coarse_line)


VMEM = pl.BlockSpec(memory_space=pltpu.VMEM)
SMEM = pl.BlockSpec(memory_space=pltpu.SMEM)
FAR = pl.BlockSpec(memory_space=pltpu.HBM)


def call(kernel, shapes, specs, name, scratch=(), cost=None):
    def leaf(shape):
        kind = jnp.float32
        if shape[0] == "half":
            shape, kind = shape[1:], jnp.bfloat16
        return jax.ShapeDtypeStruct(shape, kind)

    return pl.pallas_call(
        kernel,
        out_shape=[leaf(shape) for shape in shapes],
        in_specs=specs,
        out_specs=[VMEM] * len(shapes),
        scratch_shapes=list(scratch),
        compiler_params=pltpu.CompilerParams(vmem_limit_bytes=16 * 1024 * 1024),
        name=name,
        cost_estimate=cost,
    )


def swap(first, second, axis):
    size = lax.axis_size(axis)
    odd = [(i, (i + 1) % size) for i in range(1, size, 2)]
    one = lax.ppermute(first, axis, [(i, i ^ 1) for i in range(size)])
    two = lax.ppermute(second, axis, odd + [(b, a) for a, b in odd])
    return one, two


def second_neighbours(common, axis):
    size = lax.axis_size(axis)
    if size == 4:
        return lax.ppermute(common, axis, [(i, i ^ 2) for i in range(size)])
    left = lax.ppermute(common[:FIRST_ROWS], axis, [(i, (i - 2) % size) for i in range(size)])
    right = lax.ppermute(common[FIRST_ROWS:], axis, [(i, (i + 2) % size) for i in range(size)])
    return jnp.concatenate([left, right], axis=0)


def body(
    source, previous, coefficients, stiffness, fdm_vectors, fdm_values, coarse_inverse, vertex_map
):
    assert source.shape == (ROWS, ROWS, LANES)
    spans = lax.axis_size("gz")
    devices = lax.axis_size("gx") * spans
    per, count = coarse_inverse.shape
    small = per * count <= LANES
    block, wide, face = (ROWS, ROWS, LANES), (ROWS, ROWS, WIDE), (ROWS, LANES)
    halo = (13, 8, LANES)

    first, second, elements, source, previous = call(
        pack_kernel,
        [halo, halo, face, block, block],
        [FAR] * 3,
        "pack",
        [pltpu.VMEM(coefficients.shape, jnp.float32), pltpu.SemaphoreType.DMA((3,))],
    )(*(pltpu.with_memory_space_constraint(v, pltpu.HBM) for v in (source, previous, coefficients)))
    first, second = swap(first, second, "gz")
    upper, lower, diagonals, stiff, vectors, bend, lam, lines, fixed, tables = call(
        functools.partial(prepare_kernel, small),
        [
            ("half", 4, WIDE, WIDE), ("half", 4, WIDE, LANES), (3, 8, 8, LANES),
            (64, LANES), (64, LANES), (16, LANES), (2, 8, LANES), (3, 8, LANES), (24, LANES), (3, 8, LANES),
        ],
        [VMEM] * 3 + [SMEM] * 2 + [VMEM if small else FAR, VMEM],
        "prepare",
    )(elements, stiffness, fdm_vectors, fdm_values, vertex_map, coarse_inverse, jnp.asarray(lane_tables()))

    message = (FIRST_ROWS + FAR_ROWS + SECOND_ROWS, LANES)
    start, remainder, factors, halves, common, part, metrics = call(
        start_kernel,
        [
            block, wide, (3, 2, ROWS, WIDE), (2, ROWS, WIDE), (2 * FIRST_ROWS + 16, LANES),
            (2, FIRST_ROWS + FAR_ROWS, LANES), (16, WIDE),
        ],
        [VMEM] * 9,
        "start",
    )(source, previous, elements, first, second, stiff, upper, lower, diagonals)
    beyond = second_neighbours(common, "gx")
    known, spectrum, inverse, side_a, side_b = call(
        guess_kernel, [wide, wide, wide, message, message], [VMEM] * 10, "guess",
        cost=pl.CostEstimate(flops=4000000000, bytes_accessed=4000000, transcendentals=0),
    )(remainder, metrics, part, stiff, vectors, bend, lam, upper, lower, diagonals)
    side_a, side_b = swap(side_a, side_b, "gx")
    pieces, waves, stiff_keep = call(
        ready_kernel, [(2, 2, 4, ROWS, LANES), (8, WIDE), (ROWS, WIDE)], [VMEM] * 5, "ready"
    )(factors, stiff, lines, upper, lower)

    start_faces, residual, local, face_factors, image, payload = call(
        middle_kernel,
        [(2, ROWS, LANES), block, wide, (2, 3, ROWS, WIDE), block, (2 * devices, LANES)],
        [VMEM] * 19,
        "middle",
        [pltpu.VMEM((2, ROWS, WIDE), jnp.float32), pltpu.VMEM((8, LANES), jnp.float32)],
    )(
        known, factors, halves, remainder, spectrum, inverse, side_a, side_b, beyond, waves,
        stiff, vectors, bend, lam, upper, lower, diagonals, fixed, lines,
    )
    gathered = lax.all_to_all(payload.reshape(devices, 2, LANES), ("gx", "gz"), 0, 0)
    gathered = gathered.reshape(2 * devices, LANES)

    operands = [
        start, start_faces, residual, local, image, pieces, face_factors, waves, stiff_keep, lines,
        tables, gathered,
    ]
    finish = functools.partial(final_kernel, devices, spans, count, per)
    if small:

        def kernel(*refs):
            finish(*refs[:12], None, *refs[12:])

    else:
        kernel = finish
        rows = gathered[0::2]
        labels = rows[:, jnp.array([8 * k + 4 for k in range(6)])].astype(jnp.int32)
        parts = rows[:, jnp.array([8 * (k // 3) + k % 3 for k in range(6)])]
        rhs = jnp.zeros((count,), jnp.float32).at[labels.reshape(-1)].add(parts.reshape(-1))
        mine = jnp.dot(coarse_inverse, rhs, precision=EXACT)
        coarse = lax.all_gather(mine, ("gx", "gz"), axis=0, tiled=True)
        operands.append(jnp.pad(coarse[labels], ((0, 0), (0, LANES - 6))))
    return tuple(
        call(kernel, [block, block], [VMEM] * len(operands), "finish", [pltpu.VMEM((devices, LANES), jnp.float32)])(
            *operands
        )
    )


def solution(mesh):
    placed = (
        P("gx", None, "gz"),
        P("gx", None, "gz"),
        P(None, "gx", None, "gz"),
        P(),
        P(),
        P(),
        P(("gx", "gz"), None),
        P(None, "gx", None, "gz"),
    )
    return jax.shard_map(
        body,
        mesh=mesh,
        in_specs=placed,
        out_specs=(P("gx", None, "gz"), P("gx", None, "gz")),
        check_vma=False,
    )
```

```python
import functools

import jax
import jax.numpy as jnp
import numpy as np
from jax import lax
from jax.experimental import pallas as pl
from jax.experimental.pallas import tpu as pltpu
from jax.sharding import PartitionSpec as P

POINTS = [
    -1.0,
    -0.8717401485096066,
    -0.5917001814331423,
    -0.2092992179024789,
    0.2092992179024789,
    0.5917001814331423,
    0.8717401485096066,
    1.0,
]
WEIGHTS = [
    0.03571428571428571,
    0.21070422714350603,
    0.34112269248350435,
    0.4124587946587038,
    0.4124587946587038,
    0.34112269248350435,
    0.21070422714350603,
    0.03571428571428571,
]
ONES = [1.0] * 8
LOW = [(1.0 - s) / 2.0 for s in POINTS]
HIGH = [(1.0 + s) / 2.0 for s in POINTS]
EXACT = lax.Precision.HIGHEST

ROWS = 16
LANES = 128
WIDE = 256
BOTH = 384
HALO = 32
ELEMENTS = 22
CORNERS = (58, 80)
DEEP, SHALLOW = 25, 17
SLOT = DEEP + SHALLOW
FIRST_FIELDS = ((0, 24), (41, 17))
SECOND_FIELDS = ((0, 16), (32, 16), (64, 16), (96, 16))
FAR_FIELDS = ((0, 24), (48, 24))
FIRST_ROWS, FAR_ROWS, SECOND_ROWS = 48, 24, 40
PAIRS = ((0, 0), (0, 1), (1, 1))
GROUP_X = (ONES + LOW, [0.0] * 8 + HIGH)
INVERSE_X = [0.5] + [1.0] * 6 + [0.5] + [0.5] + [1.0] * 6 + [0.5]


def iota(shape, dim):
    return lax.broadcasted_iota(jnp.int32, shape, dim)


def pick(index, values):
    result = jnp.full(index.shape, values[0], jnp.float32)
    for i in range(1, 8):
        result = jnp.where(index == i, values[i], result)
    return result


def even_index(axis):
    return lax.rem(lax.axis_index(axis), 2) == 0


class Geometry:
    def __init__(self, lanes):
        shape = (2, 8, lanes)
        self.element_y, self.row, lane = iota(shape, 0), iota(shape, 1), iota(shape, 2)
        self.position = lane & 7
        self.first = self.position == 0
        self.last = self.position == 7
        self.edge = self.first | self.last
        self.weight_y = pick(self.row, WEIGHTS)
        self.weight_z = pick(self.position, WEIGHTS)
        self.inverse_z = jnp.where(self.edge, 0.5, 1.0)
        self.wall = (self.element_y == 1) & (self.row == 7)
        inner = ((self.element_y == 0) & (self.row == 7)) | ((self.element_y == 1) & (self.row == 0))
        self.inverse_y = jnp.where(inner, 0.5, 1.0)
        self.keep = jnp.where(self.wall, 0.0, 1.0)
        self.lanes = lanes

    def pair_y(self, v):
        lower, upper = v[0], v[1]
        row = self.row[0]
        up = jnp.where(row == 7, pltpu.roll(upper, 7, 0), 0.0)
        down = jnp.where(row == 0, pltpu.roll(lower, 1, 0), 0.0)
        return jnp.stack([lower + up, upper + down])

    def pair_z(self, v):
        flat = v.reshape(16, self.lanes)
        after = pltpu.roll(flat, self.lanes - 1, 1).reshape(v.shape)
        before = pltpu.roll(flat, 1, 1).reshape(v.shape)
        return v + jnp.where(self.edge, jnp.where(self.last, after, before), 0.0)

    def pair(self, v):
        return self.pair_z(self.pair_y(v))

    def assemble(self, v):
        return self.pair(v) * self.keep


def solid(v):
    return v.reshape(ROWS, v.shape[-1])


def split(v):
    return v.reshape(2, 8, v.shape[-1])


def own(v):
    return v[..., :LANES]


def down(v):
    return jnp.sum(v.reshape(ROWS, LANES), axis=0, keepdims=True)


def line_of(ref, at, lanes):
    row = ref[at : at + 1, :]
    return jnp.concatenate([row] * (lanes // LANES), axis=1)[None]


def weighted(factors, rows):
    total = None
    for factor, row in zip(factors, rows):
        total = factor * row if total is None else total + factor * row
    return total


def divisors_of(c, lam):
    lanes = c[0].shape[-1]
    lam_y = jnp.concatenate([lam[0]] * (lanes // LANES), axis=1)[None]
    lam_z = jnp.concatenate([lam[1]] * (lanes // LANES), axis=1)[None]
    base = c[1] * lam_y + c[2] * lam_z
    return [1.0 / (c[0] * line_of(lam.at[0], i, lanes) + base) for i in range(8)]


def halo_lanes():
    lane = iota((1, 1, LANES), 2)
    return (lane < HALO) | (lane >= LANES - HALO)


def join_pair(low, high):
    other = pltpu.roll(solid(high[:, :, LANES:]), LANES // 2, 1).reshape(2, 8, LANES)
    return jnp.concatenate([own(low), own(high), jnp.where(halo_lanes(), low[:, :, LANES:], other)], axis=2)


def part_pair(v):
    last = v[:, :, WIDE:]
    other = pltpu.roll(solid(last), LANES // 2, 1).reshape(2, 8, LANES)
    return jnp.concatenate([own(v), last], axis=2), jnp.concatenate([v[:, :, LANES:WIDE], other], axis=2)


def join_pairs(rows):
    return [join_pair(rows[x], rows[x + 8]) for x in range(8)]


def part_pairs(pairs):
    parted = [part_pair(v) for v in pairs]
    return [v[0] for v in parted] + [v[1] for v in parted]


def pair_line(ref, low, high):
    one, two = ref[low : low + 1, :], ref[high : high + 1, :]
    mixed = jnp.where(halo_lanes()[0], one, two)
    return jnp.concatenate([one, two, mixed], axis=1)[None]


def contract_x(rows, table, i, transpose=False):
    total = None
    for p in range(8):
        factor = line_of(table, p * 8 + i if transpose else i * 8 + p, rows[p].shape[-1])
        term = factor * rows[p]
        total = term if total is None else total + term
    return total


def contract_y(v, diagonals):
    def moved(value, rows):
        return jnp.stack([pltpu.roll(value[e], 8 - rows, 0) for e in range(2)])

    shifted = [v] + [moved(v, d) for d in range(1, 4)]
    return weighted(diagonals[:4], shifted) + moved(weighted(diagonals[4:], shifted), 4)


def thirds(v):
    high = v.astype(jnp.bfloat16)
    rest = v - high.astype(jnp.float32)
    middle = rest.astype(jnp.bfloat16)
    return high, middle, (rest - middle.astype(jnp.float32)).astype(jnp.bfloat16)


def contract_z(flat, upper, lower, which, short=False):
    pieces = []
    for at in range(0, flat.shape[1], LANES):
        high, middle, low = thirds(flat[:, at : at + LANES])
        one = jnp.dot(
            jnp.concatenate([high, middle], axis=1), upper[which], preferred_element_type=jnp.float32
        )
        if short:
            pieces.append(one[:, :LANES] + one[:, LANES:])
            continue
        two = jnp.dot(jnp.concatenate([low, high], axis=1), lower[which], preferred_element_type=jnp.float32)
        pieces.append(one[:, :LANES] + (one[:, LANES:] + two))
    return pieces[0] if len(pieces) == 1 else jnp.concatenate(pieces, axis=1)


def wide_diagonals(ref, which, lanes=WIDE):
    return [jnp.concatenate([ref[which, d]] * (lanes // LANES), axis=1)[None] for d in range(8)]


def metric(ref, component, element):
    at = (component * 2 + element) * 2
    return jnp.stack([jnp.broadcast_to(ref[at + e : at + e + 1, :], (8, WIDE)) for e in range(2)])


def scaled_metrics(geo, c):
    return c[0] * geo.weight_y * geo.weight_z, c[1] * geo.weight_z, c[2] * geo.weight_y


def stored_factors(ref, element):
    return [split(ref[c, element]) for c in range(3)]


def apply_pairs(pairs, factors, stiffness, upper, lower, diagonals, short=False):
    factor_x, factor_y, factor_z = factors
    along_z = contract_z(jnp.concatenate([solid(v) for v in pairs], axis=0), upper, lower, 0, short)
    along_z = [split(along_z[x * 16 : x * 16 + 16]) for x in range(8)]
    result = []
    for i in range(8):
        terms = factor_y * contract_y(pairs[i], diagonals) + factor_z * along_z[i]
        result.append(factor_x * contract_x(pairs, stiffness, i) + WEIGHTS[i] * terms)
    return result, along_z


def join_middle(rows):
    middle = rows[7] + rows[8]
    return rows[:7] + [middle, middle] + rows[9:]


def fold(parts, fields):
    lane = iota((8, LANES), 1)
    result = parts[0]
    for part, (offset, half) in list(zip(parts, fields))[1:]:
        taken = ((lane - offset + half) & (LANES - 1)) < 2 * half
        result = jnp.where(taken, pltpu.roll(part, offset, 1), result)
    return result


def unfold(packed, field, fill=0.0):
    offset, half = field
    lane = iota((8, LANES), 1)
    moved = pltpu.roll(packed, LANES - offset, 1) if offset else packed
    return jnp.where(((lane + half) & (LANES - 1)) < 2 * half, moved, fill)


def widen(tile, pieces):
    return jnp.concatenate([tile, jnp.concatenate(pieces, axis=0)], axis=1)


def group_lanes(lanes, group):
    lane = iota((1, lanes), 1)
    signed = jnp.where(lane < lanes // 2 + lanes // 4, lane, lane - lanes) if lanes > LANES else lane
    element, position = signed >> 3, lane & 7
    low, high = pick(position, LOW), pick(position, HIGH)
    here = jnp.where((element >> 3) == group, low, 0.0)
    return here + jnp.where(((element + 1) >> 3) == group, high, 0.0)


def pack_kernel(source, previous, coefficients, first, second, elements, near_source, near_previous, raw, ready):
    copies = [
        pltpu.make_async_copy(source, near_source, ready.at[0]),
        pltpu.make_async_copy(previous, near_previous, ready.at[1]),
        pltpu.make_async_copy(coefficients, raw, ready.at[2]),
    ]
    for copy in copies:
        copy.start()
    even = even_index("gz")
    elements[...] = jnp.zeros_like(elements)
    for copy in copies:
        copy.wait()
    for c in range(3):
        for element in range(2):
            at = (c * 2 + element) * 2
            elements[at : at + 2, 0:16] = raw[c, element]
    slot = iota((8, LANES), 1)
    for to_right, out in ((even, first), (jnp.logical_not(even), second)):
        for tile in range(11):
            packed = None
            for k in range(3):
                n = 3 * tile + k
                if n >= 2 * ROWS:
                    break
                for ref, width, at in ((near_previous, DEEP, SLOT * k), (near_source, SHALLOW, SLOT * k + DEEP)):
                    shift = jnp.where(to_right, (at + width) % LANES, at)
                    moved = pltpu.roll(ref[n // 2, 8 * (n % 2) : 8 * (n % 2) + 8], shift, 1)
                    packed = moved if packed is None else jnp.where(slot >= at, moved, packed)
            out[tile] = packed
        out[11] = elements[:8]
        out[12] = elements[8:]


def lanes_of(elements):
    lane = iota((24, WIDE), 1)
    beyond = lane - LANES
    right, left = LANES + 3 * 8, WIDE - 3 * 8
    index = jnp.where(lane < right, lane >> 3, jnp.where(lane >= left, 19 + ((beyond - (left - LANES)) >> 3), ELEMENTS))
    spread = (iota((24, WIDE), 0) == index).astype(jnp.bfloat16)
    high, middle, low = (jnp.dot(v, spread, preferred_element_type=jnp.float32) for v in thirds(elements[:, 0:24]))
    return high + (middle + low)


def elements_of(folded):
    lane = iota((8, LANES), 1)
    rest = jnp.where(lane == ELEMENTS, 1.0, 0.0)
    return jnp.concatenate(
        [jnp.where(lane < ELEMENTS, pltpu.roll(folded, LANES - at, 1), rest) for at in CORNERS], axis=0
    )


def prepare_kernel(
    with_coarse, elements, stiffness, vectors, eigen, labels, coarse, tables,
    upper, lower, diagonals, stiff_table, vector_table, bend, lam, lines, fixed, near_tables,
):
    near_tables[...] = tables[...]
    widen = (iota((16, LANES), 0) == (iota((16, LANES), 1) >> 3)).astype(jnp.float32)
    metrics = jnp.dot(elements[:, 0:16], widen, precision=EXACT, preferred_element_type=jnp.float32)
    repeat = (iota((LANES, 8), 0) & 7 == iota((LANES, 8), 1)).astype(jnp.float32)
    same = (iota((LANES, LANES), 0) >> 3) == (iota((LANES, LANES), 1) >> 3)
    unit = (iota((8, 8), 0) == iota((8, 8), 1)).astype(jnp.float32)
    row, column = iota((8, 8), 0), iota((8, 8), 1)

    def dot(a, b, dims):
        return lax.dot_general(a, b, (dims, ((), ())), precision=EXACT, preferred_element_type=jnp.float32)

    def put_block(at, matrix):
        half = dot(repeat, matrix, ((1,), (0,)))
        put_thirds(at, jnp.where(same, dot(half, repeat, ((1,), (1,))), 0.0))

    def put_thirds(at, block):
        high, middle, low = thirds(block)
        both = jnp.concatenate([high, middle], axis=1)
        upper[at] = jnp.concatenate([both, both], axis=0)
        lower[at] = jnp.concatenate([high, low], axis=0)

    def put_diagonals(at, matrix):
        turned = jnp.concatenate([matrix[4:], matrix[:4]], axis=0)
        for d in range(8):
            chosen = jnp.where(column == ((row + d % 4) & 7), matrix if d < 4 else turned, 0.0)
            diagonals[at, d] = jnp.broadcast_to(jnp.sum(chosen, axis=1, keepdims=True), (8, LANES))

    def put_table(out, matrix):
        tall = (iota((64, 8), 0) >> 3 == iota((64, 8), 1)).astype(jnp.float32)
        chosen = jnp.where(iota((64, 8), 0) & 7 == iota((64, 8), 1), dot(tall, matrix, ((1,), (0,))), 0.0)
        out[...] = jnp.broadcast_to(jnp.sum(chosen, axis=1, keepdims=True), (64, LANES))

    lane = iota((LANES, LANES), 1) & 7
    node = iota((LANES, LANES), 0)
    element, position = node >> 3, node & 7
    low, high = pick(position, LOW), pick(position, HIGH)
    columns = jnp.where(lane == (element >> 3), low, 0.0) + jnp.where(lane == ((element + 1) >> 3), high, 0.0)
    columns = jnp.where(lane == 3, 1.0, jnp.where(lane < 3, columns, 0.0))
    put_thirds(3, columns)
    k, s = stiffness[...], vectors[...]
    k_turned, s_turned = dot(k, unit, ((0,), (0,))), dot(s, unit, ((0,), (0,)))
    for at, matrix in enumerate((k_turned, s, s_turned)):
        put_block(at, matrix)
    for at, matrix in enumerate((k, s_turned, s)):
        put_diagonals(at, matrix)
    put_table(stiff_table, k)
    put_table(vector_table, s)
    for side, near in ((0, 0), (1, 7)):
        chosen = jnp.where(column == near, 0.0, s_turned * k[near : near + 1, :])
        total = jnp.sum(chosen, axis=1, keepdims=True)
        bend[8 * side : 8 * side + 8] = jnp.broadcast_to(total, (8, LANES))
    values = [eigen[i] for i in range(8)]
    lam[0] = pick(iota((8, LANES), 0), values)
    lam[1] = pick(iota((8, LANES), 1) & 7, values)
    stiff_lines = []
    for at, line in enumerate((ONES, LOW, HIGH)):
        total = jnp.sum(k * pick(column, line), axis=1, keepdims=True)
        stiff_lines.append(jnp.broadcast_to(total, (8, LANES)))
        lines[at] = stiff_lines[at]

    groups = [group_lanes(LANES, b) for b in range(3)]
    stacked = jnp.concatenate(groups + [jnp.zeros((13, LANES), jnp.float32)], axis=0)
    stiff_z = contract_z(stacked, upper, lower, 0)
    weight_z = pick(iota((1, LANES), 1) & 7, WEIGHTS)
    node = iota((8, LANES), 0)
    mass_y = [sum(WEIGHTS), sum(WEIGHTS[:7])]
    last = jnp.broadcast_to(k[:, 7:8], (8, LANES))
    inner = jnp.where(node == 7, 0.0, stiff_lines[0] - last)
    stiff_y = [jnp.sum(v, axis=0, keepdims=True) for v in (stiff_lines[0], inner)]
    at = 0
    for a, b in PAIRS:
        across, along = jnp.zeros((1, LANES), jnp.float32), jnp.zeros((1, LANES), jnp.float32)
        for element in range(2):
            fa = GROUP_X[a][element * 8 : element * 8 + 8]
            fb = GROUP_X[b][element * 8 : element * 8 + 8]
            if not (any(fa) and any(fb)):
                continue
            mass_x = sum(w * p * q for w, p, q in zip(WEIGHTS, fa, fb))
            applied = stiff_lines[0 if fb == ONES else 1 + b]
            stiff_x = jnp.sum(applied * pick(node, fa), axis=0, keepdims=True)
            for e in range(2):
                cx, cy, cz = (metrics[(c * 2 + element) * 2 + e].reshape(1, LANES) for c in range(3))
                across = across + cx * (stiff_x * mass_y[e]) + cy * (stiff_y[e] * mass_x)
                along = along + cz * (mass_x * mass_y[e])
        across = across * weight_z
        for b in range(3):
            fixed[at : at + 1] = across * groups[b] + along * stiff_z[b : b + 1]
            at += 1
    fixed[9:16] = jnp.zeros((7, LANES), jnp.float32)
    place = iota((1, LANES), 1)
    numbers = jnp.zeros((1, LANES), jnp.float32)
    for a in range(2):
        for b in range(3):
            corner, x, z = 4 * a + (b == 2), a, (0, 8, 15)[b]
            number = labels[corner, x, 0, z].astype(jnp.float32)
            numbers = jnp.where(place == 8 * (3 * a + b) + 4, number, numbers)
    fixed[16:17] = numbers
    below = jnp.zeros((1, LANES), jnp.float32)
    if with_coarse:
        per, count = coarse.shape
        below = [coarse[i : i + 1, :] for i in range(per)]
        if per * count < LANES:
            below.append(jnp.zeros((1, LANES - per * count), jnp.float32))
        below = jnp.concatenate(below, axis=1)
    fixed[17:18] = below
    fixed[18:24] = jnp.zeros((6, LANES), jnp.float32)


def start_kernel(
    source, previous, elements, first, second, stiffness, upper, lower, diagonals,
    start, remainder, factors, pair_factors, halves, common, part, metrics,
):
    even = even_index("gz")
    lane = iota((8, LANES), 1)
    one, two = first[...], second[...]
    from_right, from_left = jnp.where(even, one, two), jnp.where(even, two, one)

    def beyond(n, at, width):
        at = at + SLOT * (n % 3)
        right, left = from_right[n // 3], from_left[n // 3]
        if at:
            right = pltpu.roll(right, LANES - at, 1)
        left = pltpu.roll(left, (LANES - width - at) % LANES, 1)
        return jnp.where(lane < width, right, jnp.where(lane >= LANES - width, left, 0.0))

    def wide(ref, x, at, width):
        return split(widen(ref[x], [beyond(2 * x + e, at, width) for e in range(2)]))

    geo = Geometry(WIDE)
    right = pltpu.roll(jnp.concatenate([from_right[11], from_right[12]], axis=0), 16, 1)
    left = pltpu.roll(jnp.concatenate([from_left[11], from_left[12]], axis=0), 6, 1)
    place = iota((16, LANES), 1)
    compact = jnp.where(place < 16, elements[...], jnp.where(place < 19, right, jnp.where(place < ELEMENTS, left, 1.0)))
    metrics[...] = lanes_of(compact)
    factor = geo.keep * geo.inverse_y * geo.inverse_z
    rows = [geo.pair(wide(previous, x, 0, DEEP)) * (factor * INVERSE_X[x]) for x in range(ROWS)]
    rows = join_middle(rows)
    faces = (rows[0], rows[15])
    for x in range(ROWS):
        start[x] = solid(own(rows[x]))
    scaled = [scaled_metrics(geo, [metric(metrics, c, e) for c in range(3)]) for e in range(2)]
    joined = [join_pair(scaled[0][c], scaled[1][c]) for c in range(3)]
    for c in range(3):
        pair_factors[c] = solid(joined[c])
        for e in range(2):
            factors[c, e] = solid(scaled[e][c])
    applied, _ = apply_pairs(join_pairs(rows), joined, stiffness, upper, lower, wide_diagonals(diagonals, 0, BOTH))
    applied = part_pairs(applied)
    rest = [wide(source, x, DEEP, SHALLOW) - applied[x] for x in range(ROWS)]
    halves[0], halves[1] = solid(faces[0]), solid(faces[1])
    for x in range(ROWS):
        remainder[x] = solid(rest[x])
    messages, distant = [], []
    for side, x in ((0, 0), (1, 15)):
        half, value = solid(faces[side]), solid(rest[x])
        lower_fold = fold([half[:8, LANES:], value[:8, LANES:]], FIRST_FIELDS)
        upper_fold = fold([half[8:, LANES:], value[8:, LANES:]], FIRST_FIELDS)
        for at, rows in zip(CORNERS, (compact[:8], compact[8:])):
            upper_fold = jnp.where((lane >= at) & (lane < at + ELEMENTS), pltpu.roll(rows, at, 1), upper_fold)
        messages.append(jnp.concatenate([half[:, :LANES], value[:, :LANES], lower_fold, upper_fold], axis=0))
        folded = fold([half[:8, LANES:], half[8:, LANES:]], FAR_FIELDS)
        distant.append(jnp.concatenate([half[:, :LANES], folded], axis=0))
    common[: 2 * FIRST_ROWS] = jnp.concatenate(messages, axis=0)
    common[2 * FIRST_ROWS :] = jnp.zeros((16, LANES), jnp.float32)
    for side in range(2):
        part[side] = jnp.concatenate([messages[side], distant[1 - side]], axis=0)


def guess_kernel(
    remainder, metrics, part, stiffness, vectors, bend, lam, upper, lower, diagonals,
    known, spectrum, inverse, message_a, message_b,
):
    geo = Geometry(WIDE)
    rest = [split(remainder[x]) for x in range(ROWS)]
    rest = [geo.assemble(v) for v in join_middle(rest)]
    for x in range(ROWS):
        known[x] = solid(own(rest[x]))
    pairs = join_pairs(rest)
    forward = wide_diagonals(diagonals, 1, BOTH)
    moved = [solid(contract_y(contract_x(pairs, vectors, i, True), forward)) for i in range(8)]
    transformed = contract_z(jnp.concatenate(moved, axis=0), upper, lower, 1, True)
    divisors = divisors_of([join_pair(metric(metrics, c, 0), metric(metrics, c, 1)) for c in range(3)], lam)
    damped = []
    for i in range(8):
        value = split(transformed[i * 16 : i * 16 + 16])
        spectrum[i], inverse[i] = solid(value), solid(divisors[i])
        damped.append(value * divisors[i])
    ends = [part_pair(contract_x(damped, vectors, near)) for near in (0, 7)]
    messages = []
    for side, near in ((0, 0), (1, 7)):
        value = ends[side][side]
        beside = part_pair(weighted([line_of(bend, side * 8 + i, BOTH) for i in range(8)], damped))[side]
        beside = beside + line_of(stiffness, near * 8 + 7 - near, WIDE) * ends[side][1 - side]
        value, beside = solid(value), solid(beside)
        folded = fold([v[at : at + 8, LANES:] for v in (value, beside) for at in (0, 8)], SECOND_FIELDS)
        messages.append(jnp.concatenate([value[:, :LANES], beside[:, :LANES], folded], axis=0))
    even_x = even_index("gx")
    both = [jnp.concatenate([part[side], messages[side]], axis=0) for side in range(2)]
    message_a[...] = jnp.where(even_x, both[1], both[0])
    message_b[...] = jnp.where(even_x, both[0], both[1])


def read_first(message):
    lower_fold, upper_fold = message[32:40], message[40:48]
    half, value = (
        widen(message[16 * k : 16 * k + 16], [unfold(lower_fold, FIRST_FIELDS[k]), unfold(upper_fold, FIRST_FIELDS[k])])
        for k in range(2)
    )
    return split(half), split(value)


def read_far(message):
    far = message[FIRST_ROWS : FIRST_ROWS + FAR_ROWS]
    return split(widen(far[0:16], [unfold(far[16:24], field) for field in FAR_FIELDS]))


def read_second(message):
    pieces = [unfold(message[32:40], field) for field in SECOND_FIELDS]
    return widen(message[0:16], pieces[:2]), widen(message[16:32], pieces[2:])


def coarse_pieces(geo, factors, stiff_keep, functions, stiff_functions):
    factor_x, factor_y, factor_z = factors
    kept_x, kept_y, kept_z = factor_x * geo.keep, factor_y * stiff_keep, factor_z * geo.keep
    result = []
    for plain, turned in zip(functions, stiff_functions):
        result.append(
            (geo.assemble(kept_x * plain[None]), geo.assemble(kept_y * plain[None] + kept_z * turned[None]))
        )
    return result


def wide_functions(upper, lower):
    functions = [group_lanes(WIDE, b) for b in (-1, 0, 1, 2)]
    stacked = jnp.concatenate(functions + [jnp.zeros((12, WIDE), jnp.float32)], axis=0)
    turned = contract_z(stacked, upper, lower, 0)
    return functions, [turned[b : b + 1] for b in range(4)]


def kept_stiffness(geo, lines, stiffness):
    row = iota((8, LANES), 0)
    last = jnp.zeros((8, LANES), jnp.float32)
    for j in range(8):
        last = jnp.where(row == j, stiffness[j * 8 + 7 : j * 8 + 8, :], last)
    both = jnp.stack([lines[0], lines[0] - last])
    return jnp.concatenate([both] * (WIDE // LANES), axis=2)


def ready_kernel(factors, stiffness, lines, upper, lower, pieces, waves, stiff_keep):
    geo = Geometry(WIDE)
    functions, turned = wide_functions(upper, lower)
    for b in range(4):
        waves[b : b + 1], waves[4 + b : 5 + b] = functions[b], turned[b]
    along_y = kept_stiffness(geo, lines, stiffness)
    stiff_keep[...] = solid(along_y)
    for element in range(2):
        made = coarse_pieces(geo, stored_factors(factors, element), along_y, functions, turned)
        for b in range(4):
            for k in range(2):
                pieces[element, k, b] = solid(own(made[b][k]))


def side_kernel(
    first, halves, remainder, factors, got, beyond, stiffness, vectors, bend, lam, upper, lower, diagonals,
    start_face, additions, fields, answers, near_factors,
):
    right = even_index("gx") if first else jnp.logical_not(even_index("gx"))
    side = jnp.where(right, 1, 0)
    other = 1 - side
    geo = Geometry(WIDE)
    message = got[...]
    near_half, near_value = read_first(message)
    far_half = read_far(message)
    block = beyond[pl.ds(pl.multiple_of(FIRST_ROWS * other, 8), FIRST_ROWS), :]
    last_half, last_value = read_first(block)
    spread = lanes_of(jnp.concatenate([elements_of(message[40:48]), elements_of(block[40:48])], axis=0))

    def metrics_of(device, of_right, of_left):
        rows = spread[16 * device : 16 * device + 16]
        return [jnp.where(right, metric(rows, c, of_right), metric(rows, c, of_left)) for c in range(3)]

    def row_of(ref, at):
        row = ref[pl.ds(at, 1), :]
        return jnp.concatenate([row] * (WIDE // LANES), axis=1)[None]

    near, far, last = metrics_of(0, 0, 1), metrics_of(0, 1, 0), metrics_of(1, 0, 1)
    near_scaled, far_scaled, last_scaled = (scaled_metrics(geo, c) for c in (near, far, last))
    mine = [split(factors[c, side]) for c in range(3)]
    for c in range(3):
        near_factors[c] = solid(near_scaled[c])
    half, value = split(halves[side]), split(remainder[15 * side])
    start_face[...] = solid(own(half + near_half))
    stiff = wide_diagonals(diagonals, 0)
    parts = [half, near_half, far_half, last_half]
    along_z = contract_z(jnp.concatenate([solid(v) for v in parts], axis=0), upper, lower, 0)
    here, there = row_of(stiffness, 63 * side), row_of(stiffness, 63 * other)

    def face_row(c, corner, k):
        term = c[1] * contract_y(parts[k], stiff) + c[2] * split(along_z[k * 16 : k * 16 + 16])
        return corner * (c[0] * parts[k]) + WEIGHTS[0] * term

    taken = face_row(mine, here, 1) + face_row(near_scaled, there, 0)
    taken_far = face_row(far_scaled, here, 3) + face_row(last_scaled, there, 2)
    made = [
        geo.assemble(v)
        for v in (
            near_value - taken, mine[0] * near_half, value - taken, near_scaled[0] * half,
            last_value - taken_far, far_scaled[0] * last_half,
        )
    ]
    for k in range(2):
        additions[k] = solid(own(made[k]))
    forward = wide_diagonals(diagonals, 1)
    flat = jnp.concatenate([solid(contract_y(v, forward)) for v in made], axis=0)
    flat = contract_z(flat, upper, lower, 1, True)
    fields[0], fields[1] = flat[0:16], flat[16:32]
    near_total, near_field, far_total, far_field = (split(flat[k * 16 : k * 16 + 16]) for k in range(2, 6))

    cross = line_of(stiffness, 7, WIDE)
    ends = [[row_of(vectors, 56 * at + i) for i in range(8)] for at in (other, side)]
    bends = [[row_of(bend, 8 * at + i) for i in range(8)] for at in (other, side)]
    result, partial = (split(v) for v in read_second(message[FIRST_ROWS + FAR_ROWS :]))
    crossed, divisors = cross * far_field, divisors_of(near, lam)
    close = [
        (ends[0][i] * near_total - bends[0][i] * near_field - ends[1][i] * crossed) * divisors[i] for i in range(8)
    ]
    crossed, divisors = cross * near_field, divisors_of(far, lam)
    distant = [
        (ends[1][i] * far_total - bends[1][i] * far_field - ends[0][i] * crossed) * divisors[i] for i in range(8)
    ]
    result = result + weighted(ends[0], close)
    partial = partial + weighted(bends[0], close) + cross * weighted(ends[0], distant)
    answers[0], answers[1] = solid(result), solid(partial)


def solve_kernel(
    known, spectrum, inverse, sides, stiffness, vectors, bend, upper, lower, diagonals,
    start_faces, residual, local, beside, face_factors, sums,
):
    even = even_index("gx")
    geo = Geometry(WIDE)

    def both(which, *at):
        one, two = sides[0][which][at], sides[1][which][at]
        return jnp.where(even, two, one), jnp.where(even, one, two)

    start_faces[0], start_faces[1] = both(0)
    for c in range(3):
        face_factors[0, c], face_factors[1, c] = both(4, c)
    totals, moved = both(1, 0), both(1, 1)

    rows = [split(known[x]) for x in range(ROWS)]
    rows[0], rows[15] = rows[0] + split(totals[0]), rows[15] + split(totals[1])
    for side, face in ((0, 0), (1, 7)):
        for i in range(8):
            if i != face:
                change = line_of(stiffness, i * 8 + face, LANES) * split(moved[side])
                x = side * 8 + i
                rows[x] = rows[x] - change
                if x in (7, 8):
                    rows[15 - x] = rows[15 - x] - change
    parts = [None, None]
    for x in range(ROWS):
        residual[x] = solid(rows[x])
        for a in range(2):
            if GROUP_X[a][x] * INVERSE_X[x] != 0.0:
                term = (GROUP_X[a][x] * INVERSE_X[x]) * rows[x]
                parts[a] = term if parts[a] is None else parts[a] + term
    weight = own(geo.inverse_y * geo.inverse_z)
    for a in range(2):
        sums[a : a + 1] = down(parts[a] * weight)

    backward = wide_diagonals(diagonals, 2)
    totals, moved = [split(v) for v in both(2, 0)], [split(v) for v in both(2, 1)]

    total, close = join_pair(*totals), join_pair(*moved)
    crossed = line_of(stiffness, 7, BOTH) * join_pair(moved[1], moved[0])
    ready = []
    for i in range(8):
        change = pair_line(vectors, i, 56 + i) * total - pair_line(bend, i, 8 + i) * close
        change = change - pair_line(vectors, 56 + i, i) * crossed
        ready.append(solid((split(spectrum[i]) + change) * split(inverse[i])))
    answers = [both(3, k) for k in range(2)]
    answers = jnp.concatenate([answers[k][side] for side in range(2) for k in range(2)], axis=0)
    back = contract_z(jnp.concatenate(ready, axis=0), upper, lower, 2, True)
    answers = contract_z(answers, upper, lower, 2, True)
    wide_backward = wide_diagonals(diagonals, 2, BOTH)
    back = [contract_y(split(back[k * 16 : k * 16 + 16]), wide_backward) for k in range(8)]
    answers = [contract_y(split(answers[k * 16 : k * 16 + 16]), backward) for k in range(4)]
    solved = part_pairs([contract_x(back, vectors, i) for i in range(8)])
    total = None
    for x in range(ROWS):
        term = own(solved[x]) * rows[x]
        total = term if total is None else total + term
    sums[2:3] = down(total)
    sums[3:8] = jnp.zeros((5, LANES), jnp.float32)
    solved = join_middle(solved)
    solved[0], solved[15] = solved[0] + answers[0], solved[15] + answers[2]
    for x in range(ROWS):
        local[x] = solid(geo.assemble(solved[x]))
    for side in range(2):
        beside[side] = solid(geo.assemble(answers[1 + 2 * side]))


def image_kernel(
    local, factors, face_factors, beside, sums, fixed, stiffness, lines, upper, lower, diagonals,
    image, payload,
):
    geo = Geometry(WIDE)
    rows = [split(local[x]) for x in range(ROWS)]
    stiff = wide_diagonals(diagonals, 0)
    applied, along_z = apply_pairs(
        join_pairs(rows), [split(factors[c]) for c in range(3)], stiffness, upper, lower,
        wide_diagonals(diagonals, 0, BOTH), True,
    )
    applied = part_pairs(applied)
    along_z = (part_pair(along_z[0])[0], part_pair(along_z[7])[1])
    total, parts = None, [None, None]
    for x in range(ROWS):
        term = own(applied[x]) * own(rows[x])
        total = term if total is None else total + term
        for a in range(2):
            if GROUP_X[a][x] != 0.0:
                term = GROUP_X[a][x] * own(applied[x])
                parts[a] = term if parts[a] is None else parts[a] + term
    extra = [down(value * own(geo.keep)) for value in parts + [total]]
    for side, x, across in ((0, 0, 63), (1, 15, 0)):
        there = [split(face_factors[side, c]) for c in range(3)]
        other = there[0] * (split(beside[side]) + line_of(stiffness, across, WIDE) * rows[x])
        other = other + WEIGHTS[0] * (there[1] * contract_y(rows[x], stiff) + there[2] * along_z[side])
        applied[x] = applied[x] + other
    applied = join_middle(applied)
    for x in range(ROWS):
        image[x] = solid(own(geo.assemble(applied[x])))
    zero = jnp.zeros((1, LANES), jnp.float32)
    table = jnp.concatenate(
        [sums[0:2], extra[0], extra[1], fixed[0:9], sums[2:3], extra[2], zero], axis=0
    )
    reduced = contract_z(table, upper, lower, 3)
    mine = (iota((16, LANES), 1) >> 3) == iota((16, LANES), 0)
    row = jnp.sum(jnp.where(mine, reduced, 0.0), axis=0, keepdims=True) + fixed[16:17]
    block = jnp.concatenate([row, fixed[17:18]] * 4, axis=0)
    copies = payload.shape[0] // 8
    payload[...] = jnp.broadcast_to(block[None], (copies, 8, LANES)).reshape(copies * 8, LANES)


def middle_kernel(
    known, factors, spectrum, inverse, _, stiffness, vectors, bend, upper, lower, diagonals, fixed, lines, *refs
):
    sides, (start_faces, residual, local, face_factors, image, payload, beside, sums) = (refs[5:10], refs[:5]), refs[10:]
    solve_kernel(
        known, spectrum, inverse, sides, stiffness, vectors, bend, upper, lower, diagonals,
        start_faces, residual, local, beside, face_factors, sums,
    )
    image_kernel(
        local, factors, face_factors, beside, sums, fixed, stiffness, lines, upper, lower, diagonals, image, payload
    )


def lane_tables():
    one = np.zeros((8, LANES), np.float32)
    two = np.zeros((8, LANES), np.float32)
    top = np.zeros((8, LANES), np.float32)
    for a in range(2):
        for b in range(3):
            one[6, 8 * a + b], two[3 * a + b, 8 * a + b], top[0, 8 * a + b] = 1.0, 1.0, 1.0
            one[6, 8 * (2 + a) + b], two[3 * a + b, 8 * (2 + a) + b] = 2.0, 1.0
            top[1, 8 * (2 + a) + b] = 1.0
    for p, (a, other) in enumerate(PAIRS):
        for b in range(3):
            for c in range(3):
                at = 8 * (4 + 3 * p + b) + c
                one[3 * a + b, at] = 1.0 if a == other else 2.0
                two[3 * other + c, at] = 1.0
                top[1, at] = 1.0
    one[6, 8 * 13 + 3], two[6, 8 * 13 + 3], top[0, 8 * 13 + 3] = 1.0, 1.0, 1.0
    one[6, 8 * 14 + 3], two[6, 8 * 14 + 3], top[1, 8 * 14 + 3] = 1.0, 1.0, 1.0
    return np.stack([one, two, top])


def final_kernel(
    devices, spans, count, per,
    start, start_faces, residual, local, image, pieces, face_factors, waves, stiff_keep, lines, tables,
    gathered, given, new_solution, new_residual, values,
):
    rows = gathered[pl.ds(0, devices, stride=2), :]
    if given is None:
        spot = iota((devices, count), 1)
        hits = []
        rhs = [jnp.zeros((1, devices), jnp.float32) for _ in range(per)]
        owner = iota((devices, devices), 1)
        for k in range(6):
            label = rows[:, 8 * k + 4 : 8 * k + 5].astype(jnp.int32)
            at = 8 * (k // 3) + k % 3
            value = rows[:, at : at + 1]
            hits.append(spot == label)
            for q in range(per):
                chosen = jnp.where(owner * per + q == label, value, 0.0)
                rhs[q] = rhs[q] + jnp.sum(chosen, axis=0, keepdims=True)
        inverse = gathered[pl.ds(1, devices, stride=2), :]
        coarse = None
        for q in range(per):
            term = jnp.dot(
                rhs[q], inverse[:, q * count : q * count + count], precision=EXACT,
                preferred_element_type=jnp.float32,
            )
            coarse = term if coarse is None else coarse + term
        columns = [jnp.sum(jnp.where(hit, coarse, 0.0), axis=1, keepdims=True) for hit in hits]
        kept = jnp.zeros((devices, LANES), jnp.float32)
        for k in range(6):
            kept = jnp.where(iota((devices, LANES), 1) == k, columns[k], kept)
        values[...] = kept
    else:
        columns = [given[:, k : k + 1] for k in range(6)]
        values[...] = given[...]
    one, two = tables[0, 6:7, :], tables[1, 6:7, :]
    for k in range(6):
        one = one + columns[k] * tables[0, k : k + 1, :]
        two = two + columns[k] * tables[1, k : k + 1, :]
    product = jnp.sum(rows * one * two, axis=0, keepdims=True)
    numerator = jnp.sum(product * tables[2, 0:1, :], axis=1, keepdims=True)
    denominator = jnp.sum(product * tables[2, 1:2, :], axis=1, keepdims=True)
    alpha = numerator / denominator

    gx, gz = lax.axis_index("gx"), lax.axis_index("gz")
    before_x = lax.rem(gx + devices // spans - 1, devices // spans)
    before_z = lax.rem(gz + spans - 1, spans)
    here = values[pl.ds(gx * spans + gz, 1), :]
    behind = values[pl.ds(gx * spans + before_z, 1), :]
    aside = values[pl.ds(before_x * spans + gz, 1), :]
    corner = values[pl.ds(before_x * spans + before_z, 1), :]

    def four(line, back, a):
        return [back[:, 3 * a + 1 : 3 * a + 2]] + [line[:, 3 * a + b : 3 * a + b + 1] for b in range(3)]

    def mix(numbers, ref):
        total = numbers[0] * ref[0]
        for b in range(1, 4):
            total = total + numbers[b] * ref[b]
        return total

    near, right, left = four(here, behind, 0), four(here, behind, 1), four(aside, corner, 0)
    whole = [mix(near, pieces.at[0, k]) for k in range(2)]
    low = [mix(near, pieces.at[1, k]) for k in range(2)]
    high = [mix(right, pieces.at[1, k]) for k in range(2)]

    def stiff(line, i):
        return lines[line, i : i + 1, :]

    extra = [stiff(0, i) * whole[0] + WEIGHTS[i] * whole[1] for i in range(8)]
    for i in range(8):
        extra.append(
            stiff(1, i) * low[0] + stiff(2, i) * high[0] + WEIGHTS[i] * (LOW[i] * low[1] + HIGH[i] * high[1])
        )
    extra = join_middle(extra)
    geo = Geometry(WIDE)

    def line(numbers, at):
        total = numbers[0] * waves[at : at + 1, :]
        for b in range(1, 4):
            total = total + numbers[b] * waves[at + b : at + b + 1, :]
        return total

    def wide_stiff(k, i):
        return jnp.concatenate([stiff(k, i)] * (WIDE // LANES), axis=1)

    def beyond(side, stiff_x, plain, turned):
        fx, fy, fz = (split(face_factors[side, c]) for c in range(3))
        value = fx * geo.keep * stiff_x[None]
        value = value + WEIGHTS[0] * (fy * split(stiff_keep[...]) * plain[None] + fz * geo.keep * turned[None])
        return solid(own(geo.assemble(value)))

    wave_near, wave_right = line(near, 0), line(right, 0)
    across = wide_stiff(1, 7) * line(left, 0) + wide_stiff(2, 7) * wave_near
    extra[0] = extra[0] + beyond(0, across, wave_near, line(near, 4))
    extra[15] = extra[15] + beyond(1, wide_stiff(0, 0) * wave_right, wave_right, line(right, 4))
    keep = solid(own(geo.keep))
    line_near, line_right = wave_near[:, :LANES], wave_right[:, :LANES]
    for x in range(ROWS):
        begin = start_faces[x // 15] if x in (0, 15) else start[x]
        mine = local[x, :, :LANES]
        new_residual[x] = residual[x] - alpha * (image[x] + extra[x])
        coarse_line = GROUP_X[0][x] * line_near
        if GROUP_X[1][x] != 0.0:
            coarse_line = coarse_line + GROUP_X[1][x] * line_right
        new_solution[x] = begin + alpha * (mine + keep * coarse_line)


VMEM = pl.BlockSpec(memory_space=pltpu.VMEM)
SMEM = pl.BlockSpec(memory_space=pltpu.SMEM)
FAR = pl.BlockSpec(memory_space=pltpu.HBM)


def call(kernel, shapes, specs, name, scratch=(), cost=None):
    def leaf(shape):
        kind = jnp.float32
        if shape[0] == "half":
            shape, kind = shape[1:], jnp.bfloat16
        return jax.ShapeDtypeStruct(shape, kind)

    return pl.pallas_call(
        kernel,
        out_shape=[leaf(shape) for shape in shapes],
        in_specs=specs,
        out_specs=[VMEM] * len(shapes),
        scratch_shapes=list(scratch),
        compiler_params=pltpu.CompilerParams(vmem_limit_bytes=16 * 1024 * 1024),
        name=name,
        cost_estimate=cost,
    )


def swap(first, second, axis):
    size = lax.axis_size(axis)
    odd = [(i, (i + 1) % size) for i in range(1, size, 2)]
    one = lax.ppermute(first, axis, [(i, i ^ 1) for i in range(size)])
    two = lax.ppermute(second, axis, odd + [(b, a) for a, b in odd])
    return one, two


def second_neighbours(common, axis):
    size = lax.axis_size(axis)
    if size == 4:
        return lax.ppermute(common, axis, [(i, i ^ 2) for i in range(size)])
    left = lax.ppermute(common[:FIRST_ROWS], axis, [(i, (i - 2) % size) for i in range(size)])
    right = lax.ppermute(common[FIRST_ROWS:], axis, [(i, (i + 2) % size) for i in range(size)])
    return jnp.concatenate([left, right], axis=0)


def body(
    source, previous, coefficients, stiffness, fdm_vectors, fdm_values, coarse_inverse, vertex_map
):
    assert source.shape == (ROWS, ROWS, LANES)
    spans = lax.axis_size("gz")
    devices = lax.axis_size("gx") * spans
    per, count = coarse_inverse.shape
    small = per * count <= LANES
    block, wide, face = (ROWS, ROWS, LANES), (ROWS, ROWS, WIDE), (ROWS, LANES)
    halo = (13, 8, LANES)

    first, second, elements, source, previous = call(
        pack_kernel,
        [halo, halo, face, block, block],
        [FAR] * 3,
        "pack",
        [pltpu.VMEM(coefficients.shape, jnp.float32), pltpu.SemaphoreType.DMA((3,))],
    )(*(pltpu.with_memory_space_constraint(v, pltpu.HBM) for v in (source, previous, coefficients)))
    first, second = swap(first, second, "gz")
    upper, lower, diagonals, stiff, vectors, bend, lam, lines, fixed, tables = call(
        functools.partial(prepare_kernel, small),
        [
            ("half", 4, WIDE, WIDE), ("half", 4, WIDE, LANES), (3, 8, 8, LANES),
            (64, LANES), (64, LANES), (16, LANES), (2, 8, LANES), (3, 8, LANES), (24, LANES), (3, 8, LANES),
        ],
        [VMEM] * 3 + [SMEM] * 2 + [VMEM if small else FAR, VMEM],
        "prepare",
    )(elements, stiffness, fdm_vectors, fdm_values, vertex_map, coarse_inverse, jnp.asarray(lane_tables()))

    message = (FIRST_ROWS + FAR_ROWS + SECOND_ROWS, LANES)
    start, remainder, factors, pair_factors, halves, common, part, metrics = call(
        start_kernel,
        [
            block, wide, (3, 2, ROWS, WIDE), (3, ROWS, BOTH), (2, ROWS, WIDE), (2 * FIRST_ROWS + 16, LANES),
            (2, FIRST_ROWS + FAR_ROWS, LANES), (16, WIDE),
        ],
        [VMEM] * 9,
        "start",
    )(source, previous, elements, first, second, stiff, upper, lower, diagonals)
    beyond = second_neighbours(common, "gx")
    known, spectrum, inverse, side_a, side_b = call(
        guess_kernel, [block, (8, ROWS, BOTH), (8, ROWS, BOTH), message, message], [VMEM] * 10, "guess",
        cost=pl.CostEstimate(flops=4000000000, bytes_accessed=4000000, transcendentals=0),
    )(remainder, metrics, part, stiff, vectors, bend, lam, upper, lower, diagonals)
    side_a, side_b = swap(side_a, side_b, "gx")
    pieces, waves, stiff_keep = call(
        ready_kernel, [(2, 2, 4, ROWS, LANES), (8, WIDE), (ROWS, WIDE)], [VMEM] * 5, "ready"
    )(factors, stiff, lines, upper, lower)

    sides = []
    for at, got in ((1, side_b), (0, side_a)):
        sides += call(
            functools.partial(side_kernel, at == 0),
            [face, (2, ROWS, LANES), (2, ROWS, WIDE), (2, ROWS, WIDE), (3, ROWS, WIDE)],
            [VMEM] * 12,
            ("side_first", "side_second")[at],
        )(halves, remainder, factors, got, beyond, stiff, vectors, bend, lam, upper, lower, diagonals)
    start_faces, residual, local, face_factors, image, payload = call(
        middle_kernel,
        [(2, ROWS, LANES), block, wide, (2, 3, ROWS, WIDE), block, (2 * devices, LANES)],
        [VMEM] * 23,
        "middle",
        [pltpu.VMEM((2, ROWS, WIDE), jnp.float32), pltpu.VMEM((8, LANES), jnp.float32)],
    )(known, pair_factors, spectrum, inverse, waves, stiff, vectors, bend, upper, lower, diagonals, fixed, lines, *sides)
    gathered = lax.all_to_all(payload.reshape(devices, 2, LANES), ("gx", "gz"), 0, 0)
    gathered = gathered.reshape(2 * devices, LANES)

    operands = [
        start, start_faces, residual, local, image, pieces, face_factors, waves, stiff_keep, lines,
        tables, gathered,
    ]
    finish = functools.partial(final_kernel, devices, spans, count, per)
    if small:

        def kernel(*refs):
            finish(*refs[:12], None, *refs[12:])

    else:
        kernel = finish
        rows = gathered[0::2]
        labels = rows[:, jnp.array([8 * k + 4 for k in range(6)])].astype(jnp.int32)
        parts = rows[:, jnp.array([8 * (k // 3) + k % 3 for k in range(6)])]
        rhs = jnp.zeros((count,), jnp.float32).at[labels.reshape(-1)].add(parts.reshape(-1))
        mine = jnp.dot(coarse_inverse, rhs, precision=EXACT)
        coarse = lax.all_gather(mine, ("gx", "gz"), axis=0, tiled=True)
        operands.append(jnp.pad(coarse[labels], ((0, 0), (0, LANES - 6))))
    return tuple(
        call(kernel, [block, block], [VMEM] * len(operands), "finish", [pltpu.VMEM((devices, LANES), jnp.float32)])(
            *operands
        )
    )


def solution(mesh):
    placed = (
        P("gx", None, "gz"),
        P("gx", None, "gz"),
        P(None, "gx", None, "gz"),
        P(),
        P(),
        P(),
        P(("gx", "gz"), None),
        P(None, "gx", None, "gz"),
    )
    return jax.shard_map(
        body,
        mesh=mesh,
        in_specs=placed,
        out_specs=(P("gx", None, "gz"), P("gx", None, "gz")),
        check_vma=False,
    )
```

```python
import functools

import jax
import jax.numpy as jnp
import numpy as np
from jax import lax
from jax.experimental import pallas as pl
from jax.experimental.pallas import tpu as pltpu
from jax.sharding import PartitionSpec as P

POINTS = [
    -1.0,
    -0.8717401485096066,
    -0.5917001814331423,
    -0.2092992179024789,
    0.2092992179024789,
    0.5917001814331423,
    0.8717401485096066,
    1.0,
]
WEIGHTS = [
    0.03571428571428571,
    0.21070422714350603,
    0.34112269248350435,
    0.4124587946587038,
    0.4124587946587038,
    0.34112269248350435,
    0.21070422714350603,
    0.03571428571428571,
]
ONES = [1.0] * 8
LOW = [(1.0 - s) / 2.0 for s in POINTS]
HIGH = [(1.0 + s) / 2.0 for s in POINTS]
EXACT = lax.Precision.HIGHEST

ROWS = 16
LANES = 128
WIDE = 256
BOTH = 384
HALO = 32
ELEMENTS = 22
CORNERS = (58, 80)
SPARE = (84, 100)
DEEP, SHALLOW = 25, 17
SLOT = DEEP + SHALLOW
FIRST_FIELDS = ((0, 24), (41, 17))
SECOND_FIELDS = ((0, 16), (32, 16), (64, 16), (96, 16))
FAR_FIELDS = ((0, 24), (48, 24))
FIRST_ROWS, FAR_ROWS, SECOND_ROWS = 48, 24, 40
PAIRS = ((0, 0), (0, 1), (1, 1))
GROUP_X = (ONES + LOW, [0.0] * 8 + HIGH)
INVERSE_X = [0.5] + [1.0] * 6 + [0.5] + [0.5] + [1.0] * 6 + [0.5]


def iota(shape, dim):
    return lax.broadcasted_iota(jnp.int32, shape, dim)


def pick(index, values):
    result = jnp.full(index.shape, values[0], jnp.float32)
    for i in range(1, 8):
        result = jnp.where(index == i, values[i], result)
    return result


def even_index(axis):
    return lax.rem(lax.axis_index(axis), 2) == 0


class Geometry:
    def __init__(self, lanes):
        shape = (2, 8, lanes)
        self.element_y, self.row, lane = iota(shape, 0), iota(shape, 1), iota(shape, 2)
        self.position = lane & 7
        self.first = self.position == 0
        self.last = self.position == 7
        self.edge = self.first | self.last
        self.weight_y = pick(self.row, WEIGHTS)
        self.weight_z = pick(self.position, WEIGHTS)
        self.inverse_z = jnp.where(self.edge, 0.5, 1.0)
        self.wall = (self.element_y == 1) & (self.row == 7)
        inner = ((self.element_y == 0) & (self.row == 7)) | ((self.element_y == 1) & (self.row == 0))
        self.inverse_y = jnp.where(inner, 0.5, 1.0)
        self.keep = jnp.where(self.wall, 0.0, 1.0)
        self.lanes = lanes

    def pair_y(self, v):
        lower, upper = v[0], v[1]
        row = self.row[0]
        up = jnp.where(row == 7, pltpu.roll(upper, 7, 0), 0.0)
        down = jnp.where(row == 0, pltpu.roll(lower, 1, 0), 0.0)
        return jnp.stack([lower + up, upper + down])

    def pair_z(self, v):
        flat = v.reshape(16, self.lanes)
        after = pltpu.roll(flat, self.lanes - 1, 1).reshape(v.shape)
        before = pltpu.roll(flat, 1, 1).reshape(v.shape)
        return v + jnp.where(self.edge, jnp.where(self.last, after, before), 0.0)

    def pair(self, v):
        return self.pair_z(self.pair_y(v))

    def assemble(self, v):
        return self.pair(v) * self.keep


def solid(v):
    return v.reshape(ROWS, v.shape[-1])


def split(v):
    return v.reshape(2, 8, v.shape[-1])


def own(v):
    return v[..., :LANES]


def down(v):
    return jnp.sum(v.reshape(ROWS, LANES), axis=0, keepdims=True)


def line_of(ref, at, lanes):
    row = ref[at : at + 1, :]
    return jnp.concatenate([row] * (lanes // LANES), axis=1)[None]


def weighted(factors, rows):
    total = None
    for factor, row in zip(factors, rows):
        total = factor * row if total is None else total + factor * row
    return total


def divisors_of(c, lam):
    lanes = c[0].shape[-1]
    lam_y = jnp.concatenate([lam[0]] * (lanes // LANES), axis=1)[None]
    lam_z = jnp.concatenate([lam[1]] * (lanes // LANES), axis=1)[None]
    base = c[1] * lam_y + c[2] * lam_z
    return [1.0 / (c[0] * line_of(lam.at[0], i, lanes) + base) for i in range(8)]


def halo_lanes():
    lane = iota((1, 1, LANES), 2)
    return (lane < HALO) | (lane >= LANES - HALO)


def join_pair(low, high):
    other = pltpu.roll(solid(high[:, :, LANES:]), LANES // 2, 1).reshape(2, 8, LANES)
    return jnp.concatenate([own(low), own(high), jnp.where(halo_lanes(), low[:, :, LANES:], other)], axis=2)


def part_pair(v):
    last = v[:, :, WIDE:]
    other = pltpu.roll(solid(last), LANES // 2, 1).reshape(2, 8, LANES)
    return jnp.concatenate([own(v), last], axis=2), jnp.concatenate([v[:, :, LANES:WIDE], other], axis=2)


def join_pairs(rows):
    return [join_pair(rows[x], rows[x + 8]) for x in range(8)]


def part_pairs(pairs):
    parted = [part_pair(v) for v in pairs]
    return [v[0] for v in parted] + [v[1] for v in parted]


def pair_line(ref, low, high):
    one, two = ref[low : low + 1, :], ref[high : high + 1, :]
    mixed = jnp.where(halo_lanes()[0], one, two)
    return jnp.concatenate([one, two, mixed], axis=1)[None]


def contract_x(rows, table, i, transpose=False):
    total = None
    for p in range(8):
        factor = line_of(table, p * 8 + i if transpose else i * 8 + p, rows[p].shape[-1])
        term = factor * rows[p]
        total = term if total is None else total + term
    return total


def contract_y(v, diagonals):
    def moved(value, rows):
        return jnp.stack([pltpu.roll(value[e], 8 - rows, 0) for e in range(2)])

    shifted = [v] + [moved(v, d) for d in range(1, 4)]
    return weighted(diagonals[:4], shifted) + moved(weighted(diagonals[4:], shifted), 4)


def thirds(v):
    high = v.astype(jnp.bfloat16)
    rest = v - high.astype(jnp.float32)
    middle = rest.astype(jnp.bfloat16)
    return high, middle, (rest - middle.astype(jnp.float32)).astype(jnp.bfloat16)


def contract_z(flat, upper, lower, which, short=False):
    pieces = []
    for at in range(0, flat.shape[1], LANES):
        high, middle, low = thirds(flat[:, at : at + LANES])
        one = jnp.dot(
            jnp.concatenate([high, middle], axis=1), upper[which], preferred_element_type=jnp.float32
        )
        if short:
            pieces.append(one[:, :LANES] + one[:, LANES:])
            continue
        two = jnp.dot(jnp.concatenate([low, high], axis=1), lower[which], preferred_element_type=jnp.float32)
        pieces.append(one[:, :LANES] + (one[:, LANES:] + two))
    return pieces[0] if len(pieces) == 1 else jnp.concatenate(pieces, axis=1)


def wide_diagonals(ref, which, lanes=WIDE):
    return [jnp.concatenate([ref[which, d]] * (lanes // LANES), axis=1)[None] for d in range(8)]


def metric(ref, component, element):
    at = (component * 2 + element) * 2
    return jnp.stack([jnp.broadcast_to(ref[at + e : at + e + 1, :], (8, WIDE)) for e in range(2)])


def scaled_metrics(geo, c):
    return c[0] * geo.weight_y * geo.weight_z, c[1] * geo.weight_z, c[2] * geo.weight_y


def stored_factors(ref, element):
    return [split(ref[c, element]) for c in range(3)]


def apply_pairs(pairs, factors, stiffness, upper, lower, diagonals, short=False):
    factor_x, factor_y, factor_z = factors
    along_z = contract_z(jnp.concatenate([solid(v) for v in pairs], axis=0), upper, lower, 0, short)
    along_z = [split(along_z[x * 16 : x * 16 + 16]) for x in range(8)]
    result = []
    for i in range(8):
        terms = factor_y * contract_y(pairs[i], diagonals) + factor_z * along_z[i]
        result.append(factor_x * contract_x(pairs, stiffness, i) + WEIGHTS[i] * terms)
    return result, along_z


def join_middle(rows):
    middle = rows[7] + rows[8]
    return rows[:7] + [middle, middle] + rows[9:]


def fold(parts, fields):
    lane = iota((8, LANES), 1)
    result = parts[0]
    for part, (offset, half) in list(zip(parts, fields))[1:]:
        taken = ((lane - offset + half) & (LANES - 1)) < 2 * half
        result = jnp.where(taken, pltpu.roll(part, offset, 1), result)
    return result


def unfold(packed, field, fill=0.0):
    offset, half = field
    lane = iota((8, LANES), 1)
    moved = pltpu.roll(packed, LANES - offset, 1) if offset else packed
    return jnp.where(((lane + half) & (LANES - 1)) < 2 * half, moved, fill)


def widen(tile, pieces):
    return jnp.concatenate([tile, jnp.concatenate(pieces, axis=0)], axis=1)


def group_lanes(lanes, group):
    lane = iota((1, lanes), 1)
    signed = jnp.where(lane < lanes // 2 + lanes // 4, lane, lane - lanes) if lanes > LANES else lane
    element, position = signed >> 3, lane & 7
    low, high = pick(position, LOW), pick(position, HIGH)
    here = jnp.where((element >> 3) == group, low, 0.0)
    return here + jnp.where(((element + 1) >> 3) == group, high, 0.0)


def pack_kernel(source, previous, coefficients, first, second, elements, near_source, near_previous, raw, ready):
    copies = [
        pltpu.make_async_copy(source, near_source, ready.at[0]),
        pltpu.make_async_copy(previous, near_previous, ready.at[1]),
        pltpu.make_async_copy(coefficients, raw, ready.at[2]),
    ]
    for copy in copies:
        copy.start()
    even = even_index("gz")
    elements[...] = jnp.zeros_like(elements)
    for copy in copies:
        copy.wait()
    for c in range(3):
        for element in range(2):
            at = (c * 2 + element) * 2
            elements[at : at + 2, 0:16] = raw[c, element]
    slot = iota((8, LANES), 1)
    for to_right, out in ((even, first), (jnp.logical_not(even), second)):
        for tile in range(11):
            packed = None
            for k in range(3):
                n = 3 * tile + k
                if n >= 2 * ROWS:
                    break
                for ref, width, at in ((near_previous, DEEP, SLOT * k), (near_source, SHALLOW, SLOT * k + DEEP)):
                    shift = jnp.where(to_right, (at + width) % LANES, at)
                    moved = pltpu.roll(ref[n // 2, 8 * (n % 2) : 8 * (n % 2) + 8], shift, 1)
                    packed = moved if packed is None else jnp.where(slot >= at, moved, packed)
            if tile == 10:
                for at, rows in zip(SPARE, (elements[:8], elements[8:])):
                    packed = jnp.where(slot >= at, pltpu.roll(rows, at, 1), packed)
            out[tile] = packed


def lanes_of(elements):
    lane = iota((24, WIDE), 1)
    beyond = lane - LANES
    right, left = LANES + 3 * 8, WIDE - 3 * 8
    index = jnp.where(lane < right, lane >> 3, jnp.where(lane >= left, 19 + ((beyond - (left - LANES)) >> 3), ELEMENTS))
    spread = (iota((24, WIDE), 0) == index).astype(jnp.bfloat16)
    high, middle, low = (jnp.dot(v, spread, preferred_element_type=jnp.float32) for v in thirds(elements[:, 0:24]))
    return high + (middle + low)


def elements_of(folded):
    lane = iota((8, LANES), 1)
    rest = jnp.where(lane == ELEMENTS, 1.0, 0.0)
    return jnp.concatenate(
        [jnp.where(lane < ELEMENTS, pltpu.roll(folded, LANES - at, 1), rest) for at in CORNERS], axis=0
    )


def prepare_kernel(
    with_coarse, elements, stiffness, vectors, eigen, labels, coarse, tables,
    upper, lower, diagonals, stiff_table, vector_table, bend, lam, lines, fixed, near_tables,
):
    near_tables[...] = tables[...]
    widen = (iota((16, LANES), 0) == (iota((16, LANES), 1) >> 3)).astype(jnp.float32)
    metrics = jnp.dot(elements[:, 0:16], widen, precision=EXACT, preferred_element_type=jnp.float32)
    repeat = (iota((LANES, 8), 0) & 7 == iota((LANES, 8), 1)).astype(jnp.float32)
    same = (iota((LANES, LANES), 0) >> 3) == (iota((LANES, LANES), 1) >> 3)
    unit = (iota((8, 8), 0) == iota((8, 8), 1)).astype(jnp.float32)
    row, column = iota((8, 8), 0), iota((8, 8), 1)

    def dot(a, b, dims):
        return lax.dot_general(a, b, (dims, ((), ())), precision=EXACT, preferred_element_type=jnp.float32)

    def put_block(at, matrix):
        half = dot(repeat, matrix, ((1,), (0,)))
        put_thirds(at, jnp.where(same, dot(half, repeat, ((1,), (1,))), 0.0))

    def put_thirds(at, block):
        high, middle, low = thirds(block)
        both = jnp.concatenate([high, middle], axis=1)
        upper[at] = jnp.concatenate([both, both], axis=0)
        lower[at] = jnp.concatenate([high, low], axis=0)

    def put_diagonals(at, matrix):
        turned = jnp.concatenate([matrix[4:], matrix[:4]], axis=0)
        for d in range(8):
            chosen = jnp.where(column == ((row + d % 4) & 7), matrix if d < 4 else turned, 0.0)
            diagonals[at, d] = jnp.broadcast_to(jnp.sum(chosen, axis=1, keepdims=True), (8, LANES))

    def put_table(out, matrix):
        tall = (iota((64, 8), 0) >> 3 == iota((64, 8), 1)).astype(jnp.float32)
        chosen = jnp.where(iota((64, 8), 0) & 7 == iota((64, 8), 1), dot(tall, matrix, ((1,), (0,))), 0.0)
        out[...] = jnp.broadcast_to(jnp.sum(chosen, axis=1, keepdims=True), (64, LANES))

    lane = iota((LANES, LANES), 1) & 7
    node = iota((LANES, LANES), 0)
    element, position = node >> 3, node & 7
    low, high = pick(position, LOW), pick(position, HIGH)
    columns = jnp.where(lane == (element >> 3), low, 0.0) + jnp.where(lane == ((element + 1) >> 3), high, 0.0)
    columns = jnp.where(lane == 3, 1.0, jnp.where(lane < 3, columns, 0.0))
    put_thirds(3, columns)
    k, s = stiffness[...], vectors[...]
    k_turned, s_turned = dot(k, unit, ((0,), (0,))), dot(s, unit, ((0,), (0,)))
    for at, matrix in enumerate((k_turned, s, s_turned)):
        put_block(at, matrix)
    for at, matrix in enumerate((k, s_turned, s)):
        put_diagonals(at, matrix)
    put_table(stiff_table, k)
    put_table(vector_table, s)
    for side, near in ((0, 0), (1, 7)):
        chosen = jnp.where(column == near, 0.0, s_turned * k[near : near + 1, :])
        total = jnp.sum(chosen, axis=1, keepdims=True)
        bend[8 * side : 8 * side + 8] = jnp.broadcast_to(total, (8, LANES))
    values = [eigen[i] for i in range(8)]
    lam[0] = pick(iota((8, LANES), 0), values)
    lam[1] = pick(iota((8, LANES), 1) & 7, values)
    stiff_lines = []
    for at, line in enumerate((ONES, LOW, HIGH)):
        total = jnp.sum(k * pick(column, line), axis=1, keepdims=True)
        stiff_lines.append(jnp.broadcast_to(total, (8, LANES)))
        lines[at] = stiff_lines[at]

    groups = [group_lanes(LANES, b) for b in range(3)]
    stacked = jnp.concatenate(groups + [jnp.zeros((13, LANES), jnp.float32)], axis=0)
    stiff_z = contract_z(stacked, upper, lower, 0)
    weight_z = pick(iota((1, LANES), 1) & 7, WEIGHTS)
    node = iota((8, LANES), 0)
    mass_y = [sum(WEIGHTS), sum(WEIGHTS[:7])]
    last = jnp.broadcast_to(k[:, 7:8], (8, LANES))
    inner = jnp.where(node == 7, 0.0, stiff_lines[0] - last)
    stiff_y = [jnp.sum(v, axis=0, keepdims=True) for v in (stiff_lines[0], inner)]
    at = 0
    for a, b in PAIRS:
        across, along = jnp.zeros((1, LANES), jnp.float32), jnp.zeros((1, LANES), jnp.float32)
        for element in range(2):
            fa = GROUP_X[a][element * 8 : element * 8 + 8]
            fb = GROUP_X[b][element * 8 : element * 8 + 8]
            if not (any(fa) and any(fb)):
                continue
            mass_x = sum(w * p * q for w, p, q in zip(WEIGHTS, fa, fb))
            applied = stiff_lines[0 if fb == ONES else 1 + b]
            stiff_x = jnp.sum(applied * pick(node, fa), axis=0, keepdims=True)
            for e in range(2):
                cx, cy, cz = (metrics[(c * 2 + element) * 2 + e].reshape(1, LANES) for c in range(3))
                across = across + cx * (stiff_x * mass_y[e]) + cy * (stiff_y[e] * mass_x)
                along = along + cz * (mass_x * mass_y[e])
        across = across * weight_z
        for b in range(3):
            fixed[at : at + 1] = across * groups[b] + along * stiff_z[b : b + 1]
            at += 1
    fixed[9:16] = jnp.zeros((7, LANES), jnp.float32)
    place = iota((1, LANES), 1)
    numbers = jnp.zeros((1, LANES), jnp.float32)
    for a in range(2):
        for b in range(3):
            corner, x, z = 4 * a + (b == 2), a, (0, 8, 15)[b]
            number = labels[corner, x, 0, z].astype(jnp.float32)
            numbers = jnp.where(place == 8 * (3 * a + b) + 4, number, numbers)
    fixed[16:17] = numbers
    below = jnp.zeros((1, LANES), jnp.float32)
    if with_coarse:
        per, count = coarse.shape
        below = [coarse[i : i + 1, :] for i in range(per)]
        if per * count < LANES:
            below.append(jnp.zeros((1, LANES - per * count), jnp.float32))
        below = jnp.concatenate(below, axis=1)
    fixed[17:18] = below
    fixed[18:24] = jnp.zeros((6, LANES), jnp.float32)


def start_kernel(
    source, previous, elements, first, second, stiffness, upper, lower, diagonals,
    start, remainder, factors, pair_factors, halves, common, part, metrics,
):
    even = even_index("gz")
    lane = iota((8, LANES), 1)
    one, two = first[...], second[...]
    from_right, from_left = jnp.where(even, one, two), jnp.where(even, two, one)

    def beyond(n, at, width):
        at = at + SLOT * (n % 3)
        right, left = from_right[n // 3], from_left[n // 3]
        if at:
            right = pltpu.roll(right, LANES - at, 1)
        left = pltpu.roll(left, (LANES - width - at) % LANES, 1)
        return jnp.where(lane < width, right, jnp.where(lane >= LANES - width, left, 0.0))

    def wide(ref, x, at, width):
        return split(widen(ref[x], [beyond(2 * x + e, at, width) for e in range(2)]))

    geo = Geometry(WIDE)
    right, left = (
        jnp.concatenate([pltpu.roll(tiles[10], (LANES + to - at) % LANES, 1) for at in SPARE], axis=0)
        for tiles, to in ((from_right, 16), (from_left, 6))
    )
    place = iota((16, LANES), 1)
    compact = jnp.where(place < 16, elements[...], jnp.where(place < 19, right, jnp.where(place < ELEMENTS, left, 1.0)))
    metrics[...] = lanes_of(compact)
    factor = geo.keep * geo.inverse_y * geo.inverse_z
    rows = [geo.pair(wide(previous, x, 0, DEEP)) * (factor * INVERSE_X[x]) for x in range(ROWS)]
    rows = join_middle(rows)
    faces = (rows[0], rows[15])
    for x in range(ROWS):
        start[x] = solid(own(rows[x]))
    scaled = [scaled_metrics(geo, [metric(metrics, c, e) for c in range(3)]) for e in range(2)]
    joined = [join_pair(scaled[0][c], scaled[1][c]) for c in range(3)]
    for c in range(3):
        pair_factors[c] = solid(joined[c])
        for e in range(2):
            factors[c, e] = solid(scaled[e][c])
    applied, _ = apply_pairs(join_pairs(rows), joined, stiffness, upper, lower, wide_diagonals(diagonals, 0, BOTH))
    applied = part_pairs(applied)
    rest = [wide(source, x, DEEP, SHALLOW) - applied[x] for x in range(ROWS)]
    halves[0], halves[1] = solid(faces[0]), solid(faces[1])
    for x in range(ROWS):
        remainder[x] = solid(rest[x])
    messages, distant = [], []
    for side, x in ((0, 0), (1, 15)):
        half, value = solid(faces[side]), solid(rest[x])
        lower_fold = fold([half[:8, LANES:], value[:8, LANES:]], FIRST_FIELDS)
        upper_fold = fold([half[8:, LANES:], value[8:, LANES:]], FIRST_FIELDS)
        for at, rows in zip(CORNERS, (compact[:8], compact[8:])):
            upper_fold = jnp.where((lane >= at) & (lane < at + ELEMENTS), pltpu.roll(rows, at, 1), upper_fold)
        messages.append(jnp.concatenate([half[:, :LANES], value[:, :LANES], lower_fold, upper_fold], axis=0))
        folded = fold([half[:8, LANES:], half[8:, LANES:]], FAR_FIELDS)
        distant.append(jnp.concatenate([half[:, :LANES], folded], axis=0))
    common[: 2 * FIRST_ROWS] = jnp.concatenate(messages, axis=0)
    common[2 * FIRST_ROWS :] = jnp.zeros((16, LANES), jnp.float32)
    for side in range(2):
        part[side] = jnp.concatenate([messages[side], distant[1 - side]], axis=0)


def guess_kernel(
    remainder, metrics, part, stiffness, vectors, bend, lam, upper, lower, diagonals,
    known, spectrum, inverse, message_a, message_b,
):
    geo = Geometry(WIDE)
    rest = [split(remainder[x]) for x in range(ROWS)]
    rest = [geo.assemble(v) for v in join_middle(rest)]
    for x in range(ROWS):
        known[x] = solid(own(rest[x]))
    pairs = join_pairs(rest)
    forward = wide_diagonals(diagonals, 1, BOTH)
    moved = [solid(contract_y(contract_x(pairs, vectors, i, True), forward)) for i in range(8)]
    transformed = contract_z(jnp.concatenate(moved, axis=0), upper, lower, 1, True)
    divisors = divisors_of([join_pair(metric(metrics, c, 0), metric(metrics, c, 1)) for c in range(3)], lam)
    damped = []
    for i in range(8):
        value = split(transformed[i * 16 : i * 16 + 16])
        spectrum[i], inverse[i] = solid(value), solid(divisors[i])
        damped.append(value * divisors[i])
    ends = [part_pair(contract_x(damped, vectors, near)) for near in (0, 7)]
    messages = []
    for side, near in ((0, 0), (1, 7)):
        value = ends[side][side]
        beside = part_pair(weighted([line_of(bend, side * 8 + i, BOTH) for i in range(8)], damped))[side]
        beside = beside + line_of(stiffness, near * 8 + 7 - near, WIDE) * ends[side][1 - side]
        value, beside = solid(value), solid(beside)
        folded = fold([v[at : at + 8, LANES:] for v in (value, beside) for at in (0, 8)], SECOND_FIELDS)
        messages.append(jnp.concatenate([value[:, :LANES], beside[:, :LANES], folded], axis=0))
    even_x = even_index("gx")
    both = [jnp.concatenate([part[side], messages[side]], axis=0) for side in range(2)]
    message_a[...] = jnp.where(even_x, both[1], both[0])
    message_b[...] = jnp.where(even_x, both[0], both[1])


def read_first(message):
    lower_fold, upper_fold = message[32:40], message[40:48]
    half, value = (
        widen(message[16 * k : 16 * k + 16], [unfold(lower_fold, FIRST_FIELDS[k]), unfold(upper_fold, FIRST_FIELDS[k])])
        for k in range(2)
    )
    return split(half), split(value)


def read_far(message):
    far = message[FIRST_ROWS : FIRST_ROWS + FAR_ROWS]
    return split(widen(far[0:16], [unfold(far[16:24], field) for field in FAR_FIELDS]))


def read_second(message):
    pieces = [unfold(message[32:40], field) for field in SECOND_FIELDS]
    return widen(message[0:16], pieces[:2]), widen(message[16:32], pieces[2:])


def coarse_pieces(geo, factors, stiff_keep, functions, stiff_functions):
    factor_x, factor_y, factor_z = factors
    kept_x, kept_y, kept_z = factor_x * geo.keep, factor_y * stiff_keep, factor_z * geo.keep
    result = []
    for plain, turned in zip(functions, stiff_functions):
        result.append(
            (geo.assemble(kept_x * plain[None]), geo.assemble(kept_y * plain[None] + kept_z * turned[None]))
        )
    return result


def wide_functions(upper, lower):
    functions = [group_lanes(WIDE, b) for b in (-1, 0, 1, 2)]
    stacked = jnp.concatenate(functions + [jnp.zeros((12, WIDE), jnp.float32)], axis=0)
    turned = contract_z(stacked, upper, lower, 0)
    return functions, [turned[b : b + 1] for b in range(4)]


def kept_stiffness(geo, lines, stiffness):
    row = iota((8, LANES), 0)
    last = jnp.zeros((8, LANES), jnp.float32)
    for j in range(8):
        last = jnp.where(row == j, stiffness[j * 8 + 7 : j * 8 + 8, :], last)
    both = jnp.stack([lines[0], lines[0] - last])
    return jnp.concatenate([both] * (WIDE // LANES), axis=2)


def ready_kernel(factors, stiffness, lines, upper, lower, pieces, waves, stiff_keep):
    geo = Geometry(WIDE)
    functions, turned = wide_functions(upper, lower)
    for b in range(4):
        waves[b : b + 1], waves[4 + b : 5 + b] = functions[b], turned[b]
    along_y = kept_stiffness(geo, lines, stiffness)
    stiff_keep[...] = solid(along_y)
    for element in range(2):
        made = coarse_pieces(geo, stored_factors(factors, element), along_y, functions, turned)
        for b in range(4):
            for k in range(2):
                pieces[element, k, b] = solid(own(made[b][k]))


def side_kernel(
    first, halves, remainder, factors, got, beyond, stiffness, vectors, bend, lam, upper, lower, diagonals,
    start_face, additions, fields, answers, near_factors,
):
    right = even_index("gx") if first else jnp.logical_not(even_index("gx"))
    side = jnp.where(right, 1, 0)
    other = 1 - side
    geo = Geometry(WIDE)
    message = got[...]
    near_half, near_value = read_first(message)
    far_half = read_far(message)
    block = beyond[pl.ds(pl.multiple_of(FIRST_ROWS * other, 8), FIRST_ROWS), :]
    last_half, last_value = read_first(block)
    spread = lanes_of(jnp.concatenate([elements_of(message[40:48]), elements_of(block[40:48])], axis=0))

    def metrics_of(device, of_right, of_left):
        rows = spread[16 * device : 16 * device + 16]
        return [jnp.where(right, metric(rows, c, of_right), metric(rows, c, of_left)) for c in range(3)]

    def row_of(ref, at):
        row = ref[pl.ds(at, 1), :]
        return jnp.concatenate([row] * (WIDE // LANES), axis=1)[None]

    near, far, last = metrics_of(0, 0, 1), metrics_of(0, 1, 0), metrics_of(1, 0, 1)
    near_scaled, far_scaled, last_scaled = (scaled_metrics(geo, c) for c in (near, far, last))
    mine = [split(factors[c, side]) for c in range(3)]
    for c in range(3):
        near_factors[c] = solid(near_scaled[c])
    half, value = split(halves[side]), split(remainder[15 * side])
    start_face[...] = solid(own(half + near_half))
    stiff = wide_diagonals(diagonals, 0)
    parts = [half, near_half, far_half, last_half]
    along_z = contract_z(jnp.concatenate([solid(v) for v in parts], axis=0), upper, lower, 0)
    here, there = row_of(stiffness, 63 * side), row_of(stiffness, 63 * other)

    def face_row(c, corner, k):
        term = c[1] * contract_y(parts[k], stiff) + c[2] * split(along_z[k * 16 : k * 16 + 16])
        return corner * (c[0] * parts[k]) + WEIGHTS[0] * term

    taken = face_row(mine, here, 1) + face_row(near_scaled, there, 0)
    taken_far = face_row(far_scaled, here, 3) + face_row(last_scaled, there, 2)
    made = [
        geo.assemble(v)
        for v in (
            near_value - taken, mine[0] * near_half, value - taken, near_scaled[0] * half,
            last_value - taken_far, far_scaled[0] * last_half,
        )
    ]
    for k in range(2):
        additions[k] = solid(own(made[k]))
    forward = wide_diagonals(diagonals, 1)
    flat = jnp.concatenate([solid(contract_y(v, forward)) for v in made], axis=0)
    flat = contract_z(flat, upper, lower, 1, True)
    fields[0], fields[1] = flat[0:16], flat[16:32]
    near_total, near_field, far_total, far_field = (split(flat[k * 16 : k * 16 + 16]) for k in range(2, 6))

    cross = line_of(stiffness, 7, WIDE)
    ends = [[row_of(vectors, 56 * at + i) for i in range(8)] for at in (other, side)]
    bends = [[row_of(bend, 8 * at + i) for i in range(8)] for at in (other, side)]
    result, partial = (split(v) for v in read_second(message[FIRST_ROWS + FAR_ROWS :]))
    crossed, divisors = cross * far_field, divisors_of(near, lam)
    close = [
        (ends[0][i] * near_total - bends[0][i] * near_field - ends[1][i] * crossed) * divisors[i] for i in range(8)
    ]
    crossed, divisors = cross * near_field, divisors_of(far, lam)
    distant = [
        (ends[1][i] * far_total - bends[1][i] * far_field - ends[0][i] * crossed) * divisors[i] for i in range(8)
    ]
    result = result + weighted(ends[0], close)
    partial = partial + weighted(bends[0], close) + cross * weighted(ends[0], distant)
    answers[0], answers[1] = solid(result), solid(partial)


def solve_kernel(
    known, spectrum, inverse, sides, stiffness, vectors, bend, upper, lower, diagonals,
    start_faces, residual, local, beside, face_factors, sums,
):
    even = even_index("gx")
    geo = Geometry(WIDE)

    def both(which, *at):
        one, two = sides[0][which][at], sides[1][which][at]
        return jnp.where(even, two, one), jnp.where(even, one, two)

    start_faces[0], start_faces[1] = both(0)
    for c in range(3):
        face_factors[0, c], face_factors[1, c] = both(4, c)
    totals, moved = both(1, 0), both(1, 1)

    rows = [split(known[x]) for x in range(ROWS)]
    rows[0], rows[15] = rows[0] + split(totals[0]), rows[15] + split(totals[1])
    for side, face in ((0, 0), (1, 7)):
        for i in range(8):
            if i != face:
                change = line_of(stiffness, i * 8 + face, LANES) * split(moved[side])
                x = side * 8 + i
                rows[x] = rows[x] - change
                if x in (7, 8):
                    rows[15 - x] = rows[15 - x] - change
    parts = [None, None]
    for x in range(ROWS):
        residual[x] = solid(rows[x])
        for a in range(2):
            if GROUP_X[a][x] * INVERSE_X[x] != 0.0:
                term = (GROUP_X[a][x] * INVERSE_X[x]) * rows[x]
                parts[a] = term if parts[a] is None else parts[a] + term
    weight = own(geo.inverse_y * geo.inverse_z)
    for a in range(2):
        sums[a : a + 1] = down(parts[a] * weight)

    backward = wide_diagonals(diagonals, 2)
    totals, moved = [split(v) for v in both(2, 0)], [split(v) for v in both(2, 1)]

    total, close = join_pair(*totals), join_pair(*moved)
    crossed = line_of(stiffness, 7, BOTH) * join_pair(moved[1], moved[0])
    ready = []
    for i in range(8):
        change = pair_line(vectors, i, 56 + i) * total - pair_line(bend, i, 8 + i) * close
        change = change - pair_line(vectors, 56 + i, i) * crossed
        ready.append(solid((split(spectrum[i]) + change) * split(inverse[i])))
    answers = [both(3, k) for k in range(2)]
    answers = jnp.concatenate([answers[k][side] for side in range(2) for k in range(2)], axis=0)
    back = contract_z(jnp.concatenate(ready, axis=0), upper, lower, 2, True)
    answers = contract_z(answers, upper, lower, 2, True)
    wide_backward = wide_diagonals(diagonals, 2, BOTH)
    back = [contract_y(split(back[k * 16 : k * 16 + 16]), wide_backward) for k in range(8)]
    answers = [contract_y(split(answers[k * 16 : k * 16 + 16]), backward) for k in range(4)]
    solved = part_pairs([contract_x(back, vectors, i) for i in range(8)])
    total = None
    for x in range(ROWS):
        term = own(solved[x]) * rows[x]
        total = term if total is None else total + term
    sums[2:3] = down(total)
    sums[3:8] = jnp.zeros((5, LANES), jnp.float32)
    solved = join_middle(solved)
    solved[0], solved[15] = solved[0] + answers[0], solved[15] + answers[2]
    for x in range(ROWS):
        local[x] = solid(geo.assemble(solved[x]))
    for side in range(2):
        beside[side] = solid(geo.assemble(answers[1 + 2 * side]))


def image_kernel(
    local, factors, face_factors, beside, sums, fixed, stiffness, lines, upper, lower, diagonals,
    image, payload,
):
    geo = Geometry(WIDE)
    rows = [split(local[x]) for x in range(ROWS)]
    stiff = wide_diagonals(diagonals, 0)
    applied, along_z = apply_pairs(
        join_pairs(rows), [split(factors[c]) for c in range(3)], stiffness, upper, lower,
        wide_diagonals(diagonals, 0, BOTH), True,
    )
    applied = part_pairs(applied)
    along_z = (part_pair(along_z[0])[0], part_pair(along_z[7])[1])
    total, parts = None, [None, None]
    for x in range(ROWS):
        term = own(applied[x]) * own(rows[x])
        total = term if total is None else total + term
        for a in range(2):
            if GROUP_X[a][x] != 0.0:
                term = GROUP_X[a][x] * own(applied[x])
                parts[a] = term if parts[a] is None else parts[a] + term
    extra = [down(value * own(geo.keep)) for value in parts + [total]]
    for side, x, across in ((0, 0, 63), (1, 15, 0)):
        there = [split(face_factors[side, c]) for c in range(3)]
        other = there[0] * (split(beside[side]) + line_of(stiffness, across, WIDE) * rows[x])
        other = other + WEIGHTS[0] * (there[1] * contract_y(rows[x], stiff) + there[2] * along_z[side])
        applied[x] = applied[x] + other
    applied = join_middle(applied)
    for x in range(ROWS):
        image[x] = solid(own(geo.assemble(applied[x])))
    zero = jnp.zeros((1, LANES), jnp.float32)
    table = jnp.concatenate(
        [sums[0:2], extra[0], extra[1], fixed[0:9], sums[2:3], extra[2], zero], axis=0
    )
    reduced = contract_z(table, upper, lower, 3)
    mine = (iota((16, LANES), 1) >> 3) == iota((16, LANES), 0)
    row = jnp.sum(jnp.where(mine, reduced, 0.0), axis=0, keepdims=True) + fixed[16:17]
    block = jnp.concatenate([row, fixed[17:18]] * 4, axis=0)
    copies = payload.shape[0] // 8
    payload[...] = jnp.broadcast_to(block[None], (copies, 8, LANES)).reshape(copies * 8, LANES)


def middle_kernel(
    known, pair_factors, spectrum, inverse, _, stiffness, vectors, bend, upper, lower, diagonals, fixed, lines,
    halves, remainder, factors, got, beyond, lam, *refs
):
    one, refs = refs[:5], refs[5:]
    (start_faces, residual, local, face_factors, image, payload, beside, sums), two = refs[:8], refs[8:]
    side_kernel(
        False, halves, remainder, factors, got, beyond, stiffness, vectors, bend, lam, upper, lower, diagonals, *two
    )
    solve_kernel(
        known, spectrum, inverse, (one, two), stiffness, vectors, bend, upper, lower, diagonals,
        start_faces, residual, local, beside, face_factors, sums,
    )
    image_kernel(
        local, pair_factors, face_factors, beside, sums, fixed, stiffness, lines, upper, lower, diagonals, image, payload
    )


def lane_tables():
    one = np.zeros((8, LANES), np.float32)
    two = np.zeros((8, LANES), np.float32)
    top = np.zeros((8, LANES), np.float32)
    for a in range(2):
        for b in range(3):
            one[6, 8 * a + b], two[3 * a + b, 8 * a + b], top[0, 8 * a + b] = 1.0, 1.0, 1.0
            one[6, 8 * (2 + a) + b], two[3 * a + b, 8 * (2 + a) + b] = 2.0, 1.0
            top[1, 8 * (2 + a) + b] = 1.0
    for p, (a, other) in enumerate(PAIRS):
        for b in range(3):
            for c in range(3):
                at = 8 * (4 + 3 * p + b) + c
                one[3 * a + b, at] = 1.0 if a == other else 2.0
                two[3 * other + c, at] = 1.0
                top[1, at] = 1.0
    one[6, 8 * 13 + 3], two[6, 8 * 13 + 3], top[0, 8 * 13 + 3] = 1.0, 1.0, 1.0
    one[6, 8 * 14 + 3], two[6, 8 * 14 + 3], top[1, 8 * 14 + 3] = 1.0, 1.0, 1.0
    return np.stack([one, two, top])


def final_kernel(
    devices, spans, count, per,
    start, start_faces, residual, local, image, pieces, face_factors, waves, stiff_keep, lines, tables,
    gathered, given, new_solution, new_residual, values,
):
    rows = gathered[pl.ds(0, devices, stride=2), :]
    if given is None:
        spot = iota((devices, count), 1)
        hits = []
        rhs = [jnp.zeros((1, devices), jnp.float32) for _ in range(per)]
        owner = iota((devices, devices), 1)
        for k in range(6):
            label = rows[:, 8 * k + 4 : 8 * k + 5].astype(jnp.int32)
            at = 8 * (k // 3) + k % 3
            value = rows[:, at : at + 1]
            hits.append(spot == label)
            for q in range(per):
                chosen = jnp.where(owner * per + q == label, value, 0.0)
                rhs[q] = rhs[q] + jnp.sum(chosen, axis=0, keepdims=True)
        inverse = gathered[pl.ds(1, devices, stride=2), :]
        coarse = None
        for q in range(per):
            term = jnp.dot(
                rhs[q], inverse[:, q * count : q * count + count], precision=EXACT,
                preferred_element_type=jnp.float32,
            )
            coarse = term if coarse is None else coarse + term
        columns = [jnp.sum(jnp.where(hit, coarse, 0.0), axis=1, keepdims=True) for hit in hits]
        kept = jnp.zeros((devices, LANES), jnp.float32)
        for k in range(6):
            kept = jnp.where(iota((devices, LANES), 1) == k, columns[k], kept)
        values[...] = kept
    else:
        columns = [given[:, k : k + 1] for k in range(6)]
        values[...] = given[...]
    one, two = tables[0, 6:7, :], tables[1, 6:7, :]
    for k in range(6):
        one = one + columns[k] * tables[0, k : k + 1, :]
        two = two + columns[k] * tables[1, k : k + 1, :]
    product = jnp.sum(rows * one * two, axis=0, keepdims=True)
    numerator = jnp.sum(product * tables[2, 0:1, :], axis=1, keepdims=True)
    denominator = jnp.sum(product * tables[2, 1:2, :], axis=1, keepdims=True)
    alpha = numerator / denominator

    gx, gz = lax.axis_index("gx"), lax.axis_index("gz")
    before_x = lax.rem(gx + devices // spans - 1, devices // spans)
    before_z = lax.rem(gz + spans - 1, spans)
    here = values[pl.ds(gx * spans + gz, 1), :]
    behind = values[pl.ds(gx * spans + before_z, 1), :]
    aside = values[pl.ds(before_x * spans + gz, 1), :]
    corner = values[pl.ds(before_x * spans + before_z, 1), :]

    def four(line, back, a):
        return [back[:, 3 * a + 1 : 3 * a + 2]] + [line[:, 3 * a + b : 3 * a + b + 1] for b in range(3)]

    def mix(numbers, ref):
        total = numbers[0] * ref[0]
        for b in range(1, 4):
            total = total + numbers[b] * ref[b]
        return total

    near, right, left = four(here, behind, 0), four(here, behind, 1), four(aside, corner, 0)
    whole = [mix(near, pieces.at[0, k]) for k in range(2)]
    low = [mix(near, pieces.at[1, k]) for k in range(2)]
    high = [mix(right, pieces.at[1, k]) for k in range(2)]

    def stiff(line, i):
        return lines[line, i : i + 1, :]

    extra = [stiff(0, i) * whole[0] + WEIGHTS[i] * whole[1] for i in range(8)]
    for i in range(8):
        extra.append(
            stiff(1, i) * low[0] + stiff(2, i) * high[0] + WEIGHTS[i] * (LOW[i] * low[1] + HIGH[i] * high[1])
        )
    extra = join_middle(extra)
    geo = Geometry(WIDE)

    def line(numbers, at):
        total = numbers[0] * waves[at : at + 1, :]
        for b in range(1, 4):
            total = total + numbers[b] * waves[at + b : at + b + 1, :]
        return total

    def wide_stiff(k, i):
        return jnp.concatenate([stiff(k, i)] * (WIDE // LANES), axis=1)

    def beyond(side, stiff_x, plain, turned):
        fx, fy, fz = (split(face_factors[side, c]) for c in range(3))
        value = fx * geo.keep * stiff_x[None]
        value = value + WEIGHTS[0] * (fy * split(stiff_keep[...]) * plain[None] + fz * geo.keep * turned[None])
        return solid(own(geo.assemble(value)))

    wave_near, wave_right = line(near, 0), line(right, 0)
    across = wide_stiff(1, 7) * line(left, 0) + wide_stiff(2, 7) * wave_near
    extra[0] = extra[0] + beyond(0, across, wave_near, line(near, 4))
    extra[15] = extra[15] + beyond(1, wide_stiff(0, 0) * wave_right, wave_right, line(right, 4))
    keep = solid(own(geo.keep))
    line_near, line_right = wave_near[:, :LANES], wave_right[:, :LANES]
    for x in range(ROWS):
        begin = start_faces[x // 15] if x in (0, 15) else start[x]
        mine = local[x, :, :LANES]
        new_residual[x] = residual[x] - alpha * (image[x] + extra[x])
        coarse_line = GROUP_X[0][x] * line_near
        if GROUP_X[1][x] != 0.0:
            coarse_line = coarse_line + GROUP_X[1][x] * line_right
        new_solution[x] = begin + alpha * (mine + keep * coarse_line)


VMEM = pl.BlockSpec(memory_space=pltpu.VMEM)
SMEM = pl.BlockSpec(memory_space=pltpu.SMEM)
FAR = pl.BlockSpec(memory_space=pltpu.HBM)


def call(kernel, shapes, specs, name, scratch=(), cost=None):
    def leaf(shape):
        kind = jnp.float32
        if shape[0] == "half":
            shape, kind = shape[1:], jnp.bfloat16
        return jax.ShapeDtypeStruct(shape, kind)

    return pl.pallas_call(
        kernel,
        out_shape=[leaf(shape) for shape in shapes],
        in_specs=specs,
        out_specs=[VMEM] * len(shapes),
        scratch_shapes=list(scratch),
        compiler_params=pltpu.CompilerParams(vmem_limit_bytes=16 * 1024 * 1024),
        name=name,
        cost_estimate=cost,
    )


def swap(first, second, axis):
    size = lax.axis_size(axis)
    odd = [(i, (i + 1) % size) for i in range(1, size, 2)]
    one = lax.ppermute(first, axis, [(i, i ^ 1) for i in range(size)])
    two = lax.ppermute(second, axis, odd + [(b, a) for a, b in odd])
    return one, two


def second_neighbours(common, axis):
    size = lax.axis_size(axis)
    if size == 4:
        return lax.ppermute(common, axis, [(i, i ^ 2) for i in range(size)])
    left = lax.ppermute(common[:FIRST_ROWS], axis, [(i, (i - 2) % size) for i in range(size)])
    right = lax.ppermute(common[FIRST_ROWS:], axis, [(i, (i + 2) % size) for i in range(size)])
    return jnp.concatenate([left, right], axis=0)


def body(
    source, previous, coefficients, stiffness, fdm_vectors, fdm_values, coarse_inverse, vertex_map
):
    assert source.shape == (ROWS, ROWS, LANES)
    spans = lax.axis_size("gz")
    devices = lax.axis_size("gx") * spans
    per, count = coarse_inverse.shape
    small = per * count <= LANES
    block, wide, face = (ROWS, ROWS, LANES), (ROWS, ROWS, WIDE), (ROWS, LANES)
    halo = (11, 8, LANES)

    first, second, elements, source, previous = call(
        pack_kernel,
        [halo, halo, face, block, block],
        [FAR] * 3,
        "pack",
        [pltpu.VMEM(coefficients.shape, jnp.float32), pltpu.SemaphoreType.DMA((3,))],
    )(*(pltpu.with_memory_space_constraint(v, pltpu.HBM) for v in (source, previous, coefficients)))
    first, second = swap(first, second, "gz")
    upper, lower, diagonals, stiff, vectors, bend, lam, lines, fixed, tables = call(
        functools.partial(prepare_kernel, small),
        [
            ("half", 4, WIDE, WIDE), ("half", 4, WIDE, LANES), (3, 8, 8, LANES),
            (64, LANES), (64, LANES), (16, LANES), (2, 8, LANES), (3, 8, LANES), (24, LANES), (3, 8, LANES),
        ],
        [VMEM] * 3 + [SMEM] * 2 + [VMEM if small else FAR, VMEM],
        "prepare",
    )(elements, stiffness, fdm_vectors, fdm_values, vertex_map, coarse_inverse, jnp.asarray(lane_tables()))

    message = (FIRST_ROWS + FAR_ROWS + SECOND_ROWS, LANES)
    start, remainder, factors, pair_factors, halves, common, part, metrics = call(
        start_kernel,
        [
            block, wide, (3, 2, ROWS, WIDE), (3, ROWS, BOTH), (2, ROWS, WIDE), (2 * FIRST_ROWS + 16, LANES),
            (2, FIRST_ROWS + FAR_ROWS, LANES), (16, WIDE),
        ],
        [VMEM] * 9,
        "start",
    )(source, previous, elements, first, second, stiff, upper, lower, diagonals)
    beyond = second_neighbours(common, "gx")
    known, spectrum, inverse, side_a, side_b = call(
        guess_kernel, [block, (8, ROWS, BOTH), (8, ROWS, BOTH), message, message], [VMEM] * 10, "guess",
        cost=pl.CostEstimate(flops=4000000000, bytes_accessed=4000000, transcendentals=0),
    )(remainder, metrics, part, stiff, vectors, bend, lam, upper, lower, diagonals)
    side_a, side_b = swap(side_a, side_b, "gx")
    pieces, waves, stiff_keep = call(
        ready_kernel, [(2, 2, 4, ROWS, LANES), (8, WIDE), (ROWS, WIDE)], [VMEM] * 5, "ready"
    )(factors, stiff, lines, upper, lower)

    shapes = [face, (2, ROWS, LANES), (2, ROWS, WIDE), (2, ROWS, WIDE), (3, ROWS, WIDE)]
    one = call(functools.partial(side_kernel, True), shapes, [VMEM] * 12, "side")(
        halves, remainder, factors, side_a, beyond, stiff, vectors, bend, lam, upper, lower, diagonals
    )
    start_faces, residual, local, face_factors, image, payload = call(
        middle_kernel,
        [(2, ROWS, LANES), block, wide, (2, 3, ROWS, WIDE), block, (2 * devices, LANES)],
        [VMEM] * 24,
        "middle",
        [pltpu.VMEM(shape, jnp.float32) for shape in [(2, ROWS, WIDE), (8, LANES)] + shapes],
    )(
        known, pair_factors, spectrum, inverse, waves, stiff, vectors, bend, upper, lower, diagonals, fixed, lines,
        halves, remainder, factors, side_b, beyond, lam, *one,
    )
    gathered = lax.all_to_all(payload.reshape(devices, 2, LANES), ("gx", "gz"), 0, 0)
    gathered = gathered.reshape(2 * devices, LANES)

    operands = [
        start, start_faces, residual, local, image, pieces, face_factors, waves, stiff_keep, lines,
        tables, gathered,
    ]
    finish = functools.partial(final_kernel, devices, spans, count, per)
    if small:

        def kernel(*refs):
            finish(*refs[:12], None, *refs[12:])

    else:
        kernel = finish
        rows = gathered[0::2]
        labels = rows[:, jnp.array([8 * k + 4 for k in range(6)])].astype(jnp.int32)
        parts = rows[:, jnp.array([8 * (k // 3) + k % 3 for k in range(6)])]
        rhs = jnp.zeros((count,), jnp.float32).at[labels.reshape(-1)].add(parts.reshape(-1))
        mine = jnp.dot(coarse_inverse, rhs, precision=EXACT)
        coarse = lax.all_gather(mine, ("gx", "gz"), axis=0, tiled=True)
        operands.append(jnp.pad(coarse[labels], ((0, 0), (0, LANES - 6))))
    return tuple(
        call(kernel, [block, block], [VMEM] * len(operands), "finish", [pltpu.VMEM((devices, LANES), jnp.float32)])(
            *operands
        )
    )


def solution(mesh):
    placed = (
        P("gx", None, "gz"),
        P("gx", None, "gz"),
        P(None, "gx", None, "gz"),
        P(),
        P(),
        P(),
        P(("gx", "gz"), None),
        P(None, "gx", None, "gz"),
    )
    return jax.shard_map(
        body,
        mesh=mesh,
        in_specs=placed,
        out_specs=(P("gx", None, "gz"), P("gx", None, "gz")),
        check_vma=False,
    )
```

```python
import functools

import jax
import jax.numpy as jnp
import numpy as np
from jax import lax
from jax.experimental import pallas as pl
from jax.experimental.pallas import tpu as pltpu
from jax.sharding import PartitionSpec as P

POINTS = [
    -1.0,
    -0.8717401485096066,
    -0.5917001814331423,
    -0.2092992179024789,
    0.2092992179024789,
    0.5917001814331423,
    0.8717401485096066,
    1.0,
]
WEIGHTS = [
    0.03571428571428571,
    0.21070422714350603,
    0.34112269248350435,
    0.4124587946587038,
    0.4124587946587038,
    0.34112269248350435,
    0.21070422714350603,
    0.03571428571428571,
]
ONES = [1.0] * 8
LOW = [(1.0 - s) / 2.0 for s in POINTS]
HIGH = [(1.0 + s) / 2.0 for s in POINTS]
EXACT = lax.Precision.HIGHEST

ROWS = 16
LANES = 128
WIDE = 256
BOTH = 384
HALO = 32
ELEMENTS = 22
CORNERS = (58, 80)
SPARE = (84, 100)
DEEP, SHALLOW = 25, 17
SLOT = DEEP + SHALLOW
FIRST_FIELDS = ((0, 24), (41, 17))
SECOND_FIELDS = ((0, 16), (32, 16), (64, 16), (96, 16))
FAR_FIELDS = ((0, 24), (48, 24))
FIRST_ROWS, FAR_ROWS, SECOND_ROWS = 48, 24, 40
PAIRS = ((0, 0), (0, 1), (1, 1))
GROUP_X = (ONES + LOW, [0.0] * 8 + HIGH)
INVERSE_X = [0.5] + [1.0] * 6 + [0.5] + [0.5] + [1.0] * 6 + [0.5]


def iota(shape, dim):
    return lax.broadcasted_iota(jnp.int32, shape, dim)


def pick(index, values):
    result = jnp.full(index.shape, values[0], jnp.float32)
    for i in range(1, 8):
        result = jnp.where(index == i, values[i], result)
    return result


def even_index(axis):
    return lax.rem(lax.axis_index(axis), 2) == 0


class Geometry:
    def __init__(self, lanes):
        shape = (2, 8, lanes)
        self.element_y, self.row, lane = iota(shape, 0), iota(shape, 1), iota(shape, 2)
        self.position = lane & 7
        self.first = self.position == 0
        self.last = self.position == 7
        self.edge = self.first | self.last
        self.weight_y = pick(self.row, WEIGHTS)
        self.weight_z = pick(self.position, WEIGHTS)
        self.inverse_z = jnp.where(self.edge, 0.5, 1.0)
        self.wall = (self.element_y == 1) & (self.row == 7)
        inner = ((self.element_y == 0) & (self.row == 7)) | ((self.element_y == 1) & (self.row == 0))
        self.inverse_y = jnp.where(inner, 0.5, 1.0)
        self.keep = jnp.where(self.wall, 0.0, 1.0)
        self.lanes = lanes

    def pair_y(self, v):
        lower, upper = v[0], v[1]
        row = self.row[0]
        up = jnp.where(row == 7, pltpu.roll(upper, 7, 0), 0.0)
        down = jnp.where(row == 0, pltpu.roll(lower, 1, 0), 0.0)
        return jnp.stack([lower + up, upper + down])

    def pair_z(self, v):
        flat = v.reshape(16, self.lanes)
        after = pltpu.roll(flat, self.lanes - 1, 1).reshape(v.shape)
        before = pltpu.roll(flat, 1, 1).reshape(v.shape)
        return v + jnp.where(self.edge, jnp.where(self.last, after, before), 0.0)

    def pair(self, v):
        return self.pair_z(self.pair_y(v))

    def assemble(self, v):
        return self.pair(v) * self.keep


def solid(v):
    return v.reshape(ROWS, v.shape[-1])


def split(v):
    return v.reshape(2, 8, v.shape[-1])


def own(v):
    return v[..., :LANES]


def down(v):
    return jnp.sum(v.reshape(ROWS, LANES), axis=0, keepdims=True)


def line_of(ref, at, lanes):
    row = ref[at : at + 1, :]
    return jnp.concatenate([row] * (lanes // LANES), axis=1)[None]


def weighted(factors, rows):
    total = None
    for factor, row in zip(factors, rows):
        total = factor * row if total is None else total + factor * row
    return total


def divisors_of(c, lam):
    lanes = c[0].shape[-1]
    lam_y = jnp.concatenate([lam[0]] * (lanes // LANES), axis=1)[None]
    lam_z = jnp.concatenate([lam[1]] * (lanes // LANES), axis=1)[None]
    base = c[1] * lam_y + c[2] * lam_z
    return [1.0 / (c[0] * line_of(lam.at[0], i, lanes) + base) for i in range(8)]


def halo_lanes():
    lane = iota((1, 1, LANES), 2)
    return (lane < HALO) | (lane >= LANES - HALO)


def join_pair(low, high):
    other = pltpu.roll(solid(high[:, :, LANES:]), LANES // 2, 1).reshape(2, 8, LANES)
    return jnp.concatenate([own(low), own(high), jnp.where(halo_lanes(), low[:, :, LANES:], other)], axis=2)


def part_pair(v):
    last = v[:, :, WIDE:]
    other = pltpu.roll(solid(last), LANES // 2, 1).reshape(2, 8, LANES)
    return jnp.concatenate([own(v), last], axis=2), jnp.concatenate([v[:, :, LANES:WIDE], other], axis=2)


def join_pairs(rows):
    return [join_pair(rows[x], rows[x + 8]) for x in range(8)]


def part_pairs(pairs):
    parted = [part_pair(v) for v in pairs]
    return [v[0] for v in parted] + [v[1] for v in parted]


def pair_line(ref, low, high):
    one, two = ref[low : low + 1, :], ref[high : high + 1, :]
    mixed = jnp.where(halo_lanes()[0], one, two)
    return jnp.concatenate([one, two, mixed], axis=1)[None]


def contract_x(rows, table, i, transpose=False):
    total = None
    for p in range(8):
        factor = line_of(table, p * 8 + i if transpose else i * 8 + p, rows[p].shape[-1])
        term = factor * rows[p]
        total = term if total is None else total + term
    return total


def contract_y(v, diagonals):
    def moved(value, rows):
        return jnp.stack([pltpu.roll(value[e], 8 - rows, 0) for e in range(2)])

    shifted = [v] + [moved(v, d) for d in range(1, 4)]
    return weighted(diagonals[:4], shifted) + moved(weighted(diagonals[4:], shifted), 4)


def thirds(v):
    high = v.astype(jnp.bfloat16)
    rest = v - high.astype(jnp.float32)
    middle = rest.astype(jnp.bfloat16)
    return high, middle, (rest - middle.astype(jnp.float32)).astype(jnp.bfloat16)


def contract_z(flat, upper, lower, which, short=False):
    pieces = []
    for at in range(0, flat.shape[1], LANES):
        high, middle, low = thirds(flat[:, at : at + LANES])
        one = jnp.dot(
            jnp.concatenate([high, middle], axis=1), upper[which], preferred_element_type=jnp.float32
        )
        if short:
            pieces.append(one[:, :LANES] + one[:, LANES:])
            continue
        two = jnp.dot(jnp.concatenate([low, high], axis=1), lower[which], preferred_element_type=jnp.float32)
        pieces.append(one[:, :LANES] + (one[:, LANES:] + two))
    return pieces[0] if len(pieces) == 1 else jnp.concatenate(pieces, axis=1)


def wide_diagonals(ref, which, lanes=WIDE):
    return [jnp.concatenate([ref[which, d]] * (lanes // LANES), axis=1)[None] for d in range(8)]


def metric(ref, component, element):
    at = (component * 2 + element) * 2
    return jnp.stack([jnp.broadcast_to(ref[at + e : at + e + 1, :], (8, WIDE)) for e in range(2)])


def scaled_metrics(geo, c):
    return c[0] * geo.weight_y * geo.weight_z, c[1] * geo.weight_z, c[2] * geo.weight_y


def stored_factors(ref, element):
    return [split(ref[c, element]) for c in range(3)]


def apply_pairs(pairs, factors, stiffness, upper, lower, diagonals, short=False):
    factor_x, factor_y, factor_z = factors
    along_z = contract_z(jnp.concatenate([solid(v) for v in pairs], axis=0), upper, lower, 0, short)
    along_z = [split(along_z[x * 16 : x * 16 + 16]) for x in range(8)]
    result = []
    for i in range(8):
        terms = factor_y * contract_y(pairs[i], diagonals) + factor_z * along_z[i]
        result.append(factor_x * contract_x(pairs, stiffness, i) + WEIGHTS[i] * terms)
    return result, along_z


def join_middle(rows):
    middle = rows[7] + rows[8]
    return rows[:7] + [middle, middle] + rows[9:]


def fold(parts, fields):
    lane = iota((8, LANES), 1)
    result = parts[0]
    for part, (offset, half) in list(zip(parts, fields))[1:]:
        taken = ((lane - offset + half) & (LANES - 1)) < 2 * half
        result = jnp.where(taken, pltpu.roll(part, offset, 1), result)
    return result


def unfold(packed, field, fill=0.0):
    offset, half = field
    lane = iota((8, LANES), 1)
    moved = pltpu.roll(packed, LANES - offset, 1) if offset else packed
    return jnp.where(((lane + half) & (LANES - 1)) < 2 * half, moved, fill)


def widen(tile, pieces):
    return jnp.concatenate([tile, jnp.concatenate(pieces, axis=0)], axis=1)


def group_lanes(lanes, group):
    lane = iota((1, lanes), 1)
    signed = jnp.where(lane < lanes // 2 + lanes // 4, lane, lane - lanes) if lanes > LANES else lane
    element, position = signed >> 3, lane & 7
    low, high = pick(position, LOW), pick(position, HIGH)
    here = jnp.where((element >> 3) == group, low, 0.0)
    return here + jnp.where(((element + 1) >> 3) == group, high, 0.0)


def pack_kernel(
    source, previous, coefficients, eigen, coarse,
    first, second, elements, near_source, near_previous, near_eigen, near_coarse, raw, ready,
):
    copies = [
        pltpu.make_async_copy(source, near_source, ready.at[0]),
        pltpu.make_async_copy(previous, near_previous, ready.at[1]),
        pltpu.make_async_copy(coefficients, raw, ready.at[2]),
        pltpu.make_async_copy(eigen, near_eigen, ready.at[3]),
        pltpu.make_async_copy(coarse, near_coarse, ready.at[4]),
    ]
    for copy in copies:
        copy.start()
    even = even_index("gz")
    elements[...] = jnp.zeros_like(elements)
    for copy in copies:
        copy.wait()
    for c in range(3):
        for element in range(2):
            at = (c * 2 + element) * 2
            elements[at : at + 2, 0:16] = raw[c, element]
    slot = iota((8, LANES), 1)
    for to_right, out in ((even, first), (jnp.logical_not(even), second)):
        for tile in range(11):
            packed = None
            for k in range(3):
                n = 3 * tile + k
                if n >= 2 * ROWS:
                    break
                for ref, width, at in ((near_previous, DEEP, SLOT * k), (near_source, SHALLOW, SLOT * k + DEEP)):
                    shift = jnp.where(to_right, (at + width) % LANES, at)
                    moved = pltpu.roll(ref[n // 2, 8 * (n % 2) : 8 * (n % 2) + 8], shift, 1)
                    packed = moved if packed is None else jnp.where(slot >= at, moved, packed)
            if tile == 10:
                for at, rows in zip(SPARE, (elements[:8], elements[8:])):
                    packed = jnp.where(slot >= at, pltpu.roll(rows, at, 1), packed)
            out[tile] = packed


def lanes_of(elements):
    lane = iota((24, WIDE), 1)
    beyond = lane - LANES
    right, left = LANES + 3 * 8, WIDE - 3 * 8
    index = jnp.where(lane < right, lane >> 3, jnp.where(lane >= left, 19 + ((beyond - (left - LANES)) >> 3), ELEMENTS))
    spread = (iota((24, WIDE), 0) == index).astype(jnp.bfloat16)
    high, middle, low = (jnp.dot(v, spread, preferred_element_type=jnp.float32) for v in thirds(elements[:, 0:24]))
    return high + (middle + low)


def elements_of(folded):
    lane = iota((8, LANES), 1)
    rest = jnp.where(lane == ELEMENTS, 1.0, 0.0)
    return jnp.concatenate(
        [jnp.where(lane < ELEMENTS, pltpu.roll(folded, LANES - at, 1), rest) for at in CORNERS], axis=0
    )


def prepare_kernel(
    with_coarse, elements, stiffness, vectors, eigen, labels, coarse, tables,
    upper, lower, diagonals, stiff_table, vector_table, bend, lam, lines, fixed, near_tables,
):
    near_tables[...] = tables[...]
    widen = (iota((16, LANES), 0) == (iota((16, LANES), 1) >> 3)).astype(jnp.float32)
    metrics = jnp.dot(elements[:, 0:16], widen, precision=EXACT, preferred_element_type=jnp.float32)
    repeat = (iota((LANES, 8), 0) & 7 == iota((LANES, 8), 1)).astype(jnp.float32)
    same = (iota((LANES, LANES), 0) >> 3) == (iota((LANES, LANES), 1) >> 3)
    unit = (iota((8, 8), 0) == iota((8, 8), 1)).astype(jnp.float32)
    row, column = iota((8, 8), 0), iota((8, 8), 1)

    def dot(a, b, dims):
        return lax.dot_general(a, b, (dims, ((), ())), precision=EXACT, preferred_element_type=jnp.float32)

    def put_block(at, matrix):
        half = dot(repeat, matrix, ((1,), (0,)))
        put_thirds(at, jnp.where(same, dot(half, repeat, ((1,), (1,))), 0.0))

    def put_thirds(at, block):
        high, middle, low = thirds(block)
        both = jnp.concatenate([high, middle], axis=1)
        upper[at] = jnp.concatenate([both, both], axis=0)
        lower[at] = jnp.concatenate([high, low], axis=0)

    def put_diagonals(at, matrix):
        turned = jnp.concatenate([matrix[4:], matrix[:4]], axis=0)
        for d in range(8):
            chosen = jnp.where(column == ((row + d % 4) & 7), matrix if d < 4 else turned, 0.0)
            diagonals[at, d] = jnp.broadcast_to(jnp.sum(chosen, axis=1, keepdims=True), (8, LANES))

    def put_table(out, matrix):
        tall = (iota((64, 8), 0) >> 3 == iota((64, 8), 1)).astype(jnp.float32)
        chosen = jnp.where(iota((64, 8), 0) & 7 == iota((64, 8), 1), dot(tall, matrix, ((1,), (0,))), 0.0)
        out[...] = jnp.broadcast_to(jnp.sum(chosen, axis=1, keepdims=True), (64, LANES))

    lane = iota((LANES, LANES), 1) & 7
    node = iota((LANES, LANES), 0)
    element, position = node >> 3, node & 7
    low, high = pick(position, LOW), pick(position, HIGH)
    columns = jnp.where(lane == (element >> 3), low, 0.0) + jnp.where(lane == ((element + 1) >> 3), high, 0.0)
    columns = jnp.where(lane == 3, 1.0, jnp.where(lane < 3, columns, 0.0))
    put_thirds(3, columns)
    k, s = stiffness[...], vectors[...]
    k_turned, s_turned = dot(k, unit, ((0,), (0,))), dot(s, unit, ((0,), (0,)))
    for at, matrix in enumerate((k_turned, s, s_turned)):
        put_block(at, matrix)
    for at, matrix in enumerate((k, s_turned, s)):
        put_diagonals(at, matrix)
    put_table(stiff_table, k)
    put_table(vector_table, s)
    for side, near in ((0, 0), (1, 7)):
        chosen = jnp.where(column == near, 0.0, s_turned * k[near : near + 1, :])
        total = jnp.sum(chosen, axis=1, keepdims=True)
        bend[8 * side : 8 * side + 8] = jnp.broadcast_to(total, (8, LANES))
    values = eigen[...]
    total = jnp.sum(jnp.where(row == column, values, 0.0), axis=1, keepdims=True)
    lam[0] = jnp.broadcast_to(total, (8, LANES))
    lam[1] = jnp.broadcast_to(dot(values, repeat, ((1,), (1,))), (8, LANES))
    stiff_lines = []
    for at, line in enumerate((ONES, LOW, HIGH)):
        total = jnp.sum(k * pick(column, line), axis=1, keepdims=True)
        stiff_lines.append(jnp.broadcast_to(total, (8, LANES)))
        lines[at] = stiff_lines[at]

    groups = [group_lanes(LANES, b) for b in range(3)]
    stacked = jnp.concatenate(groups + [jnp.zeros((13, LANES), jnp.float32)], axis=0)
    stiff_z = contract_z(stacked, upper, lower, 0)
    weight_z = pick(iota((1, LANES), 1) & 7, WEIGHTS)
    node = iota((8, LANES), 0)
    mass_y = [sum(WEIGHTS), sum(WEIGHTS[:7])]
    last = jnp.broadcast_to(k[:, 7:8], (8, LANES))
    inner = jnp.where(node == 7, 0.0, stiff_lines[0] - last)
    stiff_y = [jnp.sum(v, axis=0, keepdims=True) for v in (stiff_lines[0], inner)]
    at = 0
    for a, b in PAIRS:
        across, along = jnp.zeros((1, LANES), jnp.float32), jnp.zeros((1, LANES), jnp.float32)
        for element in range(2):
            fa = GROUP_X[a][element * 8 : element * 8 + 8]
            fb = GROUP_X[b][element * 8 : element * 8 + 8]
            if not (any(fa) and any(fb)):
                continue
            mass_x = sum(w * p * q for w, p, q in zip(WEIGHTS, fa, fb))
            applied = stiff_lines[0 if fb == ONES else 1 + b]
            stiff_x = jnp.sum(applied * pick(node, fa), axis=0, keepdims=True)
            for e in range(2):
                cx, cy, cz = (metrics[(c * 2 + element) * 2 + e].reshape(1, LANES) for c in range(3))
                across = across + cx * (stiff_x * mass_y[e]) + cy * (stiff_y[e] * mass_x)
                along = along + cz * (mass_x * mass_y[e])
        across = across * weight_z
        for b in range(3):
            fixed[at : at + 1] = across * groups[b] + along * stiff_z[b : b + 1]
            at += 1
    fixed[9:16] = jnp.zeros((7, LANES), jnp.float32)
    place = iota((1, LANES), 1)
    numbers = jnp.zeros((1, LANES), jnp.float32)
    for a in range(2):
        for b in range(3):
            corner, x, z = 4 * a + (b == 2), a, (0, 8, 15)[b]
            number = labels[corner, x][0:1, z : z + 1].astype(jnp.float32)
            numbers = jnp.where(place == 8 * (3 * a + b) + 4, number, numbers)
    fixed[16:17] = numbers
    below = jnp.zeros((1, LANES), jnp.float32)
    if with_coarse:
        per, count = coarse.shape
        below = [coarse[i : i + 1, :] for i in range(per)]
        if per * count < LANES:
            below.append(jnp.zeros((1, LANES - per * count), jnp.float32))
        below = jnp.concatenate(below, axis=1)
    fixed[17:18] = below
    fixed[18:24] = jnp.zeros((6, LANES), jnp.float32)


def start_kernel(
    source, previous, elements, first, second, stiffness, upper, lower, diagonals,
    start, remainder, factors, pair_factors, halves, common, part, metrics,
):
    even = even_index("gz")
    lane = iota((8, LANES), 1)
    one, two = first[...], second[...]
    from_right, from_left = jnp.where(even, one, two), jnp.where(even, two, one)

    def beyond(n, at, width):
        at = at + SLOT * (n % 3)
        right, left = from_right[n // 3], from_left[n // 3]
        if at:
            right = pltpu.roll(right, LANES - at, 1)
        left = pltpu.roll(left, (LANES - width - at) % LANES, 1)
        return jnp.where(lane < width, right, jnp.where(lane >= LANES - width, left, 0.0))

    def wide(ref, x, at, width):
        return split(widen(ref[x], [beyond(2 * x + e, at, width) for e in range(2)]))

    geo = Geometry(WIDE)
    right, left = (
        jnp.concatenate([pltpu.roll(tiles[10], (LANES + to - at) % LANES, 1) for at in SPARE], axis=0)
        for tiles, to in ((from_right, 16), (from_left, 6))
    )
    place = iota((16, LANES), 1)
    compact = jnp.where(place < 16, elements[...], jnp.where(place < 19, right, jnp.where(place < ELEMENTS, left, 1.0)))
    metrics[...] = lanes_of(compact)
    factor = geo.keep * geo.inverse_y * geo.inverse_z
    rows = [geo.pair(wide(previous, x, 0, DEEP)) * (factor * INVERSE_X[x]) for x in range(ROWS)]
    rows = join_middle(rows)
    faces = (rows[0], rows[15])
    for x in range(ROWS):
        start[x] = solid(own(rows[x]))
    scaled = [scaled_metrics(geo, [metric(metrics, c, e) for c in range(3)]) for e in range(2)]
    joined = [join_pair(scaled[0][c], scaled[1][c]) for c in range(3)]
    for c in range(3):
        pair_factors[c] = solid(joined[c])
        for e in range(2):
            factors[c, e] = solid(scaled[e][c])
    applied, _ = apply_pairs(join_pairs(rows), joined, stiffness, upper, lower, wide_diagonals(diagonals, 0, BOTH))
    applied = part_pairs(applied)
    rest = [wide(source, x, DEEP, SHALLOW) - applied[x] for x in range(ROWS)]
    halves[0], halves[1] = solid(faces[0]), solid(faces[1])
    for x in range(ROWS):
        remainder[x] = solid(rest[x])
    messages, distant = [], []
    for side, x in ((0, 0), (1, 15)):
        half, value = solid(faces[side]), solid(rest[x])
        lower_fold = fold([half[:8, LANES:], value[:8, LANES:]], FIRST_FIELDS)
        upper_fold = fold([half[8:, LANES:], value[8:, LANES:]], FIRST_FIELDS)
        for at, rows in zip(CORNERS, (compact[:8], compact[8:])):
            upper_fold = jnp.where((lane >= at) & (lane < at + ELEMENTS), pltpu.roll(rows, at, 1), upper_fold)
        messages.append(jnp.concatenate([half[:, :LANES], value[:, :LANES], lower_fold, upper_fold], axis=0))
        folded = fold([half[:8, LANES:], half[8:, LANES:]], FAR_FIELDS)
        distant.append(jnp.concatenate([half[:, :LANES], folded], axis=0))
    common[: 2 * FIRST_ROWS] = jnp.concatenate(messages, axis=0)
    common[2 * FIRST_ROWS :] = jnp.zeros((16, LANES), jnp.float32)
    for side in range(2):
        part[side] = jnp.concatenate([messages[side], distant[1 - side]], axis=0)


def guess_kernel(
    remainder, metrics, part, stiffness, vectors, bend, lam, upper, lower, diagonals,
    known, spectrum, inverse, message_a, message_b,
):
    geo = Geometry(WIDE)
    rest = [split(remainder[x]) for x in range(ROWS)]
    rest = [geo.assemble(v) for v in join_middle(rest)]
    for x in range(ROWS):
        known[x] = solid(own(rest[x]))
    pairs = join_pairs(rest)
    forward = wide_diagonals(diagonals, 1, BOTH)
    moved = [solid(contract_y(contract_x(pairs, vectors, i, True), forward)) for i in range(8)]
    transformed = contract_z(jnp.concatenate(moved, axis=0), upper, lower, 1, True)
    divisors = divisors_of([join_pair(metric(metrics, c, 0), metric(metrics, c, 1)) for c in range(3)], lam)
    damped = []
    for i in range(8):
        value = split(transformed[i * 16 : i * 16 + 16])
        spectrum[i], inverse[i] = solid(value), solid(divisors[i])
        damped.append(value * divisors[i])
    ends = [part_pair(contract_x(damped, vectors, near)) for near in (0, 7)]
    messages = []
    for side, near in ((0, 0), (1, 7)):
        value = ends[side][side]
        beside = part_pair(weighted([line_of(bend, side * 8 + i, BOTH) for i in range(8)], damped))[side]
        beside = beside + line_of(stiffness, near * 8 + 7 - near, WIDE) * ends[side][1 - side]
        value, beside = solid(value), solid(beside)
        folded = fold([v[at : at + 8, LANES:] for v in (value, beside) for at in (0, 8)], SECOND_FIELDS)
        messages.append(jnp.concatenate([value[:, :LANES], beside[:, :LANES], folded], axis=0))
    even_x = even_index("gx")
    both = [jnp.concatenate([part[side], messages[side]], axis=0) for side in range(2)]
    message_a[...] = jnp.where(even_x, both[1], both[0])
    message_b[...] = jnp.where(even_x, both[0], both[1])


def read_first(message):
    lower_fold, upper_fold = message[32:40], message[40:48]
    half, value = (
        widen(message[16 * k : 16 * k + 16], [unfold(lower_fold, FIRST_FIELDS[k]), unfold(upper_fold, FIRST_FIELDS[k])])
        for k in range(2)
    )
    return split(half), split(value)


def read_far(message):
    far = message[FIRST_ROWS : FIRST_ROWS + FAR_ROWS]
    return split(widen(far[0:16], [unfold(far[16:24], field) for field in FAR_FIELDS]))


def read_second(message):
    pieces = [unfold(message[32:40], field) for field in SECOND_FIELDS]
    return widen(message[0:16], pieces[:2]), widen(message[16:32], pieces[2:])


def coarse_pieces(geo, factors, stiff_keep, functions, stiff_functions):
    factor_x, factor_y, factor_z = factors
    kept_x, kept_y, kept_z = factor_x * geo.keep, factor_y * stiff_keep, factor_z * geo.keep
    result = []
    for plain, turned in zip(functions, stiff_functions):
        result.append(
            (geo.assemble(kept_x * plain[None]), geo.assemble(kept_y * plain[None] + kept_z * turned[None]))
        )
    return result


def wide_functions(upper, lower):
    functions = [group_lanes(WIDE, b) for b in (-1, 0, 1, 2)]
    stacked = jnp.concatenate(functions + [jnp.zeros((12, WIDE), jnp.float32)], axis=0)
    turned = contract_z(stacked, upper, lower, 0)
    return functions, [turned[b : b + 1] for b in range(4)]


def kept_stiffness(geo, lines, stiffness):
    row = iota((8, LANES), 0)
    last = jnp.zeros((8, LANES), jnp.float32)
    for j in range(8):
        last = jnp.where(row == j, stiffness[j * 8 + 7 : j * 8 + 8, :], last)
    both = jnp.stack([lines[0], lines[0] - last])
    return jnp.concatenate([both] * (WIDE // LANES), axis=2)


def ready_kernel(factors, stiffness, lines, upper, lower, pieces, waves, stiff_keep):
    geo = Geometry(WIDE)
    functions, turned = wide_functions(upper, lower)
    for b in range(4):
        waves[b : b + 1], waves[4 + b : 5 + b] = functions[b], turned[b]
    along_y = kept_stiffness(geo, lines, stiffness)
    stiff_keep[...] = solid(along_y)
    for element in range(2):
        made = coarse_pieces(geo, stored_factors(factors, element), along_y, functions, turned)
        for b in range(4):
            for k in range(2):
                pieces[element, k, b] = solid(own(made[b][k]))


def side_kernel(
    first, halves, remainder, factors, got, beyond, stiffness, vectors, bend, lam, upper, lower, diagonals,
    start_face, additions, fields, answers, near_factors,
):
    right = even_index("gx") if first else jnp.logical_not(even_index("gx"))
    side = jnp.where(right, 1, 0)
    other = 1 - side
    geo = Geometry(WIDE)
    message = got[...]
    near_half, near_value = read_first(message)
    far_half = read_far(message)
    block = beyond[pl.ds(pl.multiple_of(FIRST_ROWS * other, 8), FIRST_ROWS), :]
    last_half, last_value = read_first(block)
    spread = lanes_of(jnp.concatenate([elements_of(message[40:48]), elements_of(block[40:48])], axis=0))

    def metrics_of(device, of_right, of_left):
        rows = spread[16 * device : 16 * device + 16]
        return [jnp.where(right, metric(rows, c, of_right), metric(rows, c, of_left)) for c in range(3)]

    def row_of(ref, at):
        row = ref[pl.ds(at, 1), :]
        return jnp.concatenate([row] * (WIDE // LANES), axis=1)[None]

    near, far, last = metrics_of(0, 0, 1), metrics_of(0, 1, 0), metrics_of(1, 0, 1)
    near_scaled, far_scaled, last_scaled = (scaled_metrics(geo, c) for c in (near, far, last))
    mine = [split(factors[c, side]) for c in range(3)]
    for c in range(3):
        near_factors[c] = solid(near_scaled[c])
    half, value = split(halves[side]), split(remainder[15 * side])
    start_face[...] = solid(own(half + near_half))
    stiff = wide_diagonals(diagonals, 0)
    parts = [half, near_half, far_half, last_half]
    along_z = contract_z(jnp.concatenate([solid(v) for v in parts], axis=0), upper, lower, 0)
    here, there = row_of(stiffness, 63 * side), row_of(stiffness, 63 * other)

    def face_row(c, corner, k):
        term = c[1] * contract_y(parts[k], stiff) + c[2] * split(along_z[k * 16 : k * 16 + 16])
        return corner * (c[0] * parts[k]) + WEIGHTS[0] * term

    taken = face_row(mine, here, 1) + face_row(near_scaled, there, 0)
    taken_far = face_row(far_scaled, here, 3) + face_row(last_scaled, there, 2)
    made = [
        geo.assemble(v)
        for v in (
            near_value - taken, mine[0] * near_half, value - taken, near_scaled[0] * half,
            last_value - taken_far, far_scaled[0] * last_half,
        )
    ]
    for k in range(2):
        additions[k] = solid(own(made[k]))
    forward = wide_diagonals(diagonals, 1)
    flat = jnp.concatenate([solid(contract_y(v, forward)) for v in made], axis=0)
    flat = contract_z(flat, upper, lower, 1, True)
    fields[0], fields[1] = flat[0:16], flat[16:32]
    near_total, near_field, far_total, far_field = (split(flat[k * 16 : k * 16 + 16]) for k in range(2, 6))

    cross = line_of(stiffness, 7, WIDE)
    ends = [[row_of(vectors, 56 * at + i) for i in range(8)] for at in (other, side)]
    bends = [[row_of(bend, 8 * at + i) for i in range(8)] for at in (other, side)]
    result, partial = (split(v) for v in read_second(message[FIRST_ROWS + FAR_ROWS :]))
    crossed, divisors = cross * far_field, divisors_of(near, lam)
    close = [
        (ends[0][i] * near_total - bends[0][i] * near_field - ends[1][i] * crossed) * divisors[i] for i in range(8)
    ]
    crossed, divisors = cross * near_field, divisors_of(far, lam)
    distant = [
        (ends[1][i] * far_total - bends[1][i] * far_field - ends[0][i] * crossed) * divisors[i] for i in range(8)
    ]
    result = result + weighted(ends[0], close)
    partial = partial + weighted(bends[0], close) + cross * weighted(ends[0], distant)
    answers[0], answers[1] = solid(result), solid(partial)


def solve_kernel(
    known, spectrum, inverse, sides, stiffness, vectors, bend, upper, lower, diagonals,
    start_faces, residual, local, beside, face_factors, sums,
):
    even = even_index("gx")
    geo = Geometry(WIDE)

    def both(which, *at):
        one, two = sides[0][which][at], sides[1][which][at]
        return jnp.where(even, two, one), jnp.where(even, one, two)

    start_faces[0], start_faces[1] = both(0)
    for c in range(3):
        face_factors[0, c], face_factors[1, c] = both(4, c)
    totals, moved = both(1, 0), both(1, 1)

    rows = [split(known[x]) for x in range(ROWS)]
    rows[0], rows[15] = rows[0] + split(totals[0]), rows[15] + split(totals[1])
    for side, face in ((0, 0), (1, 7)):
        for i in range(8):
            if i != face:
                change = line_of(stiffness, i * 8 + face, LANES) * split(moved[side])
                x = side * 8 + i
                rows[x] = rows[x] - change
                if x in (7, 8):
                    rows[15 - x] = rows[15 - x] - change
    parts = [None, None]
    for x in range(ROWS):
        residual[x] = solid(rows[x])
        for a in range(2):
            if GROUP_X[a][x] * INVERSE_X[x] != 0.0:
                term = (GROUP_X[a][x] * INVERSE_X[x]) * rows[x]
                parts[a] = term if parts[a] is None else parts[a] + term
    weight = own(geo.inverse_y * geo.inverse_z)
    for a in range(2):
        sums[a : a + 1] = down(parts[a] * weight)

    backward = wide_diagonals(diagonals, 2)
    totals, moved = [split(v) for v in both(2, 0)], [split(v) for v in both(2, 1)]

    total, close = join_pair(*totals), join_pair(*moved)
    crossed = line_of(stiffness, 7, BOTH) * join_pair(moved[1], moved[0])
    ready = []
    for i in range(8):
        change = pair_line(vectors, i, 56 + i) * total - pair_line(bend, i, 8 + i) * close
        change = change - pair_line(vectors, 56 + i, i) * crossed
        ready.append(solid((split(spectrum[i]) + change) * split(inverse[i])))
    answers = [both(3, k) for k in range(2)]
    answers = jnp.concatenate([answers[k][side] for side in range(2) for k in range(2)], axis=0)
    back = contract_z(jnp.concatenate(ready, axis=0), upper, lower, 2, True)
    answers = contract_z(answers, upper, lower, 2, True)
    wide_backward = wide_diagonals(diagonals, 2, BOTH)
    back = [contract_y(split(back[k * 16 : k * 16 + 16]), wide_backward) for k in range(8)]
    answers = [contract_y(split(answers[k * 16 : k * 16 + 16]), backward) for k in range(4)]
    solved = part_pairs([contract_x(back, vectors, i) for i in range(8)])
    total = None
    for x in range(ROWS):
        term = own(solved[x]) * rows[x]
        total = term if total is None else total + term
    sums[2:3] = down(total)
    sums[3:8] = jnp.zeros((5, LANES), jnp.float32)
    solved = join_middle(solved)
    solved[0], solved[15] = solved[0] + answers[0], solved[15] + answers[2]
    for x in range(ROWS):
        local[x] = solid(geo.assemble(solved[x]))
    for side in range(2):
        beside[side] = solid(geo.assemble(answers[1 + 2 * side]))


def image_kernel(
    local, factors, face_factors, beside, sums, fixed, stiffness, lines, upper, lower, diagonals,
    image, payload,
):
    geo = Geometry(WIDE)
    rows = [split(local[x]) for x in range(ROWS)]
    stiff = wide_diagonals(diagonals, 0)
    applied, along_z = apply_pairs(
        join_pairs(rows), [split(factors[c]) for c in range(3)], stiffness, upper, lower,
        wide_diagonals(diagonals, 0, BOTH), True,
    )
    applied = part_pairs(applied)
    along_z = (part_pair(along_z[0])[0], part_pair(along_z[7])[1])
    total, parts = None, [None, None]
    for x in range(ROWS):
        term = own(applied[x]) * own(rows[x])
        total = term if total is None else total + term
        for a in range(2):
            if GROUP_X[a][x] != 0.0:
                term = GROUP_X[a][x] * own(applied[x])
                parts[a] = term if parts[a] is None else parts[a] + term
    extra = [down(value * own(geo.keep)) for value in parts + [total]]
    for side, x, across in ((0, 0, 63), (1, 15, 0)):
        there = [split(face_factors[side, c]) for c in range(3)]
        other = there[0] * (split(beside[side]) + line_of(stiffness, across, WIDE) * rows[x])
        other = other + WEIGHTS[0] * (there[1] * contract_y(rows[x], stiff) + there[2] * along_z[side])
        applied[x] = applied[x] + other
    applied = join_middle(applied)
    for x in range(ROWS):
        image[x] = solid(own(geo.assemble(applied[x])))
    zero = jnp.zeros((1, LANES), jnp.float32)
    table = jnp.concatenate(
        [sums[0:2], extra[0], extra[1], fixed[0:9], sums[2:3], extra[2], zero], axis=0
    )
    reduced = contract_z(table, upper, lower, 3)
    mine = (iota((16, LANES), 1) >> 3) == iota((16, LANES), 0)
    row = jnp.sum(jnp.where(mine, reduced, 0.0), axis=0, keepdims=True) + fixed[16:17]
    block = jnp.concatenate([row, fixed[17:18]] * 4, axis=0)
    copies = payload.shape[0] // 8
    payload[...] = jnp.broadcast_to(block[None], (copies, 8, LANES)).reshape(copies * 8, LANES)


def middle_kernel(
    known, pair_factors, spectrum, inverse, _, stiffness, vectors, bend, upper, lower, diagonals, fixed, lines,
    halves, remainder, factors, got, beyond, lam, *refs
):
    one, refs = refs[:5], refs[5:]
    (start_faces, residual, local, face_factors, image, payload, beside, sums), two = refs[:8], refs[8:]
    side_kernel(
        False, halves, remainder, factors, got, beyond, stiffness, vectors, bend, lam, upper, lower, diagonals, *two
    )
    solve_kernel(
        known, spectrum, inverse, (one, two), stiffness, vectors, bend, upper, lower, diagonals,
        start_faces, residual, local, beside, face_factors, sums,
    )
    image_kernel(
        local, pair_factors, face_factors, beside, sums, fixed, stiffness, lines, upper, lower, diagonals, image, payload
    )


def lane_tables():
    one = np.zeros((8, LANES), np.float32)
    two = np.zeros((8, LANES), np.float32)
    top = np.zeros((8, LANES), np.float32)
    for a in range(2):
        for b in range(3):
            one[6, 8 * a + b], two[3 * a + b, 8 * a + b], top[0, 8 * a + b] = 1.0, 1.0, 1.0
            one[6, 8 * (2 + a) + b], two[3 * a + b, 8 * (2 + a) + b] = 2.0, 1.0
            top[1, 8 * (2 + a) + b] = 1.0
    for p, (a, other) in enumerate(PAIRS):
        for b in range(3):
            for c in range(3):
                at = 8 * (4 + 3 * p + b) + c
                one[3 * a + b, at] = 1.0 if a == other else 2.0
                two[3 * other + c, at] = 1.0
                top[1, at] = 1.0
    one[6, 8 * 13 + 3], two[6, 8 * 13 + 3], top[0, 8 * 13 + 3] = 1.0, 1.0, 1.0
    one[6, 8 * 14 + 3], two[6, 8 * 14 + 3], top[1, 8 * 14 + 3] = 1.0, 1.0, 1.0
    return np.stack([one, two, top])


def final_kernel(
    devices, spans, count, per,
    start, start_faces, residual, local, image, pieces, face_factors, waves, stiff_keep, lines, tables,
    gathered, given, new_solution, new_residual, values,
):
    rows = gathered[pl.ds(0, devices, stride=2), :]
    if given is None:
        spot = iota((devices, count), 1)
        hits = []
        rhs = [jnp.zeros((1, devices), jnp.float32) for _ in range(per)]
        owner = iota((devices, devices), 1)
        for k in range(6):
            label = rows[:, 8 * k + 4 : 8 * k + 5].astype(jnp.int32)
            at = 8 * (k // 3) + k % 3
            value = rows[:, at : at + 1]
            hits.append(spot == label)
            for q in range(per):
                chosen = jnp.where(owner * per + q == label, value, 0.0)
                rhs[q] = rhs[q] + jnp.sum(chosen, axis=0, keepdims=True)
        inverse = gathered[pl.ds(1, devices, stride=2), :]
        coarse = None
        for q in range(per):
            term = jnp.dot(
                rhs[q], inverse[:, q * count : q * count + count], precision=EXACT,
                preferred_element_type=jnp.float32,
            )
            coarse = term if coarse is None else coarse + term
        columns = [jnp.sum(jnp.where(hit, coarse, 0.0), axis=1, keepdims=True) for hit in hits]
        kept = jnp.zeros((devices, LANES), jnp.float32)
        for k in range(6):
            kept = jnp.where(iota((devices, LANES), 1) == k, columns[k], kept)
        values[...] = kept
    else:
        columns = [given[:, k : k + 1] for k in range(6)]
        values[...] = given[...]
    one, two = tables[0, 6:7, :], tables[1, 6:7, :]
    for k in range(6):
        one = one + columns[k] * tables[0, k : k + 1, :]
        two = two + columns[k] * tables[1, k : k + 1, :]
    product = jnp.sum(rows * one * two, axis=0, keepdims=True)
    numerator = jnp.sum(product * tables[2, 0:1, :], axis=1, keepdims=True)
    denominator = jnp.sum(product * tables[2, 1:2, :], axis=1, keepdims=True)
    alpha = numerator / denominator

    gx, gz = lax.axis_index("gx"), lax.axis_index("gz")
    before_x = lax.rem(gx + devices // spans - 1, devices // spans)
    before_z = lax.rem(gz + spans - 1, spans)
    here = values[pl.ds(gx * spans + gz, 1), :]
    behind = values[pl.ds(gx * spans + before_z, 1), :]
    aside = values[pl.ds(before_x * spans + gz, 1), :]
    corner = values[pl.ds(before_x * spans + before_z, 1), :]

    def four(line, back, a):
        return [back[:, 3 * a + 1 : 3 * a + 2]] + [line[:, 3 * a + b : 3 * a + b + 1] for b in range(3)]

    def mix(numbers, ref):
        total = numbers[0] * ref[0]
        for b in range(1, 4):
            total = total + numbers[b] * ref[b]
        return total

    near, right, left = four(here, behind, 0), four(here, behind, 1), four(aside, corner, 0)
    whole = [mix(near, pieces.at[0, k]) for k in range(2)]
    low = [mix(near, pieces.at[1, k]) for k in range(2)]
    high = [mix(right, pieces.at[1, k]) for k in range(2)]

    def stiff(line, i):
        return lines[line, i : i + 1, :]

    extra = [stiff(0, i) * whole[0] + WEIGHTS[i] * whole[1] for i in range(8)]
    for i in range(8):
        extra.append(
            stiff(1, i) * low[0] + stiff(2, i) * high[0] + WEIGHTS[i] * (LOW[i] * low[1] + HIGH[i] * high[1])
        )
    extra = join_middle(extra)
    geo = Geometry(WIDE)

    def line(numbers, at):
        total = numbers[0] * waves[at : at + 1, :]
        for b in range(1, 4):
            total = total + numbers[b] * waves[at + b : at + b + 1, :]
        return total

    def wide_stiff(k, i):
        return jnp.concatenate([stiff(k, i)] * (WIDE // LANES), axis=1)

    def beyond(side, stiff_x, plain, turned):
        fx, fy, fz = (split(face_factors[side, c]) for c in range(3))
        value = fx * geo.keep * stiff_x[None]
        value = value + WEIGHTS[0] * (fy * split(stiff_keep[...]) * plain[None] + fz * geo.keep * turned[None])
        return solid(own(geo.assemble(value)))

    wave_near, wave_right = line(near, 0), line(right, 0)
    across = wide_stiff(1, 7) * line(left, 0) + wide_stiff(2, 7) * wave_near
    extra[0] = extra[0] + beyond(0, across, wave_near, line(near, 4))
    extra[15] = extra[15] + beyond(1, wide_stiff(0, 0) * wave_right, wave_right, line(right, 4))
    keep = solid(own(geo.keep))
    line_near, line_right = wave_near[:, :LANES], wave_right[:, :LANES]
    for x in range(ROWS):
        begin = start_faces[x // 15] if x in (0, 15) else start[x]
        mine = local[x, :, :LANES]
        new_residual[x] = residual[x] - alpha * (image[x] + extra[x])
        coarse_line = GROUP_X[0][x] * line_near
        if GROUP_X[1][x] != 0.0:
            coarse_line = coarse_line + GROUP_X[1][x] * line_right
        new_solution[x] = begin + alpha * (mine + keep * coarse_line)


VMEM = pl.BlockSpec(memory_space=pltpu.VMEM)
SMEM = pl.BlockSpec(memory_space=pltpu.SMEM)
FAR = pl.BlockSpec(memory_space=pltpu.HBM)


def call(kernel, shapes, specs, name, scratch=(), cost=None):
    def leaf(shape):
        kind = jnp.float32
        if shape[0] == "half":
            shape, kind = shape[1:], jnp.bfloat16
        return jax.ShapeDtypeStruct(shape, kind)

    return pl.pallas_call(
        kernel,
        out_shape=[leaf(shape) for shape in shapes],
        in_specs=specs,
        out_specs=[VMEM] * len(shapes),
        scratch_shapes=list(scratch),
        compiler_params=pltpu.CompilerParams(vmem_limit_bytes=16 * 1024 * 1024),
        name=name,
        cost_estimate=cost,
    )


def swap(first, second, axis):
    size = lax.axis_size(axis)
    odd = [(i, (i + 1) % size) for i in range(1, size, 2)]
    one = lax.ppermute(first, axis, [(i, i ^ 1) for i in range(size)])
    two = lax.ppermute(second, axis, odd + [(b, a) for a, b in odd])
    return one, two


def second_neighbours(common, axis):
    size = lax.axis_size(axis)
    if size == 4:
        return lax.ppermute(common, axis, [(i, i ^ 2) for i in range(size)])
    left = lax.ppermute(common[:FIRST_ROWS], axis, [(i, (i - 2) % size) for i in range(size)])
    right = lax.ppermute(common[FIRST_ROWS:], axis, [(i, (i + 2) % size) for i in range(size)])
    return jnp.concatenate([left, right], axis=0)


def body(
    source, previous, coefficients, stiffness, fdm_vectors, fdm_values, coarse_inverse, vertex_map
):
    assert source.shape == (ROWS, ROWS, LANES)
    spans = lax.axis_size("gz")
    devices = lax.axis_size("gx") * spans
    per, count = coarse_inverse.shape
    small = per * count <= LANES
    block, wide, face = (ROWS, ROWS, LANES), (ROWS, ROWS, WIDE), (ROWS, LANES)
    halo = (11, 8, LANES)

    coarse = coarse_inverse if small else coarse_inverse[:, :LANES]
    operands = (source, previous, coefficients, fdm_values.reshape(1, 8), coarse)
    first, second, elements, source, previous, eigen, coarse = call(
        pack_kernel,
        [halo, halo, face, block, block, (1, 8), coarse.shape],
        [FAR] * 5,
        "pack",
        [pltpu.VMEM(coefficients.shape, jnp.float32), pltpu.SemaphoreType.DMA((5,))],
    )(*(pltpu.with_memory_space_constraint(v, pltpu.HBM) for v in operands))
    first, second = swap(first, second, "gz")
    upper, lower, diagonals, stiff, vectors, bend, lam, lines, fixed, tables = call(
        functools.partial(prepare_kernel, small),
        [
            ("half", 4, WIDE, WIDE), ("half", 4, WIDE, LANES), (3, 8, 8, LANES),
            (64, LANES), (64, LANES), (16, LANES), (2, 8, LANES), (3, 8, LANES), (24, LANES), (3, 8, LANES),
        ],
        [VMEM] * 7,
        "prepare",
    )(elements, stiffness, fdm_vectors, eigen, vertex_map, coarse, jnp.asarray(lane_tables()))

    message = (FIRST_ROWS + FAR_ROWS + SECOND_ROWS, LANES)
    start, remainder, factors, pair_factors, halves, common, part, metrics = call(
        start_kernel,
        [
            block, wide, (3, 2, ROWS, WIDE), (3, ROWS, BOTH), (2, ROWS, WIDE), (2 * FIRST_ROWS + 16, LANES),
            (2, FIRST_ROWS + FAR_ROWS, LANES), (16, WIDE),
        ],
        [VMEM] * 9,
        "start",
    )(source, previous, elements, first, second, stiff, upper, lower, diagonals)
    beyond = second_neighbours(common, "gx")
    known, spectrum, inverse, side_a, side_b = call(
        guess_kernel, [block, (8, ROWS, BOTH), (8, ROWS, BOTH), message, message], [VMEM] * 10, "guess",
        cost=pl.CostEstimate(flops=4000000000, bytes_accessed=4000000, transcendentals=0),
    )(remainder, metrics, part, stiff, vectors, bend, lam, upper, lower, diagonals)
    side_a, side_b = swap(side_a, side_b, "gx")
    pieces, waves, stiff_keep = call(
        ready_kernel, [(2, 2, 4, ROWS, LANES), (8, WIDE), (ROWS, WIDE)], [VMEM] * 5, "ready"
    )(factors, stiff, lines, upper, lower)

    shapes = [face, (2, ROWS, LANES), (2, ROWS, WIDE), (2, ROWS, WIDE), (3, ROWS, WIDE)]
    one = call(functools.partial(side_kernel, True), shapes, [VMEM] * 12, "side")(
        halves, remainder, factors, side_a, beyond, stiff, vectors, bend, lam, upper, lower, diagonals
    )
    start_faces, residual, local, face_factors, image, payload = call(
        middle_kernel,
        [(2, ROWS, LANES), block, wide, (2, 3, ROWS, WIDE), block, (2 * devices, LANES)],
        [VMEM] * 24,
        "middle",
        [pltpu.VMEM(shape, jnp.float32) for shape in [(2, ROWS, WIDE), (8, LANES)] + shapes],
    )(
        known, pair_factors, spectrum, inverse, waves, stiff, vectors, bend, upper, lower, diagonals, fixed, lines,
        halves, remainder, factors, side_b, beyond, lam, *one,
    )
    gathered = lax.all_to_all(payload.reshape(devices, 2, LANES), ("gx", "gz"), 0, 0)
    gathered = gathered.reshape(2 * devices, LANES)

    operands = [
        start, start_faces, residual, local, image, pieces, face_factors, waves, stiff_keep, lines,
        tables, gathered,
    ]
    finish = functools.partial(final_kernel, devices, spans, count, per)
    if small:

        def kernel(*refs):
            finish(*refs[:12], None, *refs[12:])

    else:
        kernel = finish
        rows = gathered[0::2]
        labels = rows[:, jnp.array([8 * k + 4 for k in range(6)])].astype(jnp.int32)
        parts = rows[:, jnp.array([8 * (k // 3) + k % 3 for k in range(6)])]
        rhs = jnp.zeros((count,), jnp.float32).at[labels.reshape(-1)].add(parts.reshape(-1))
        mine = jnp.dot(coarse_inverse, rhs, precision=EXACT)
        coarse = lax.all_gather(mine, ("gx", "gz"), axis=0, tiled=True)
        operands.append(jnp.pad(coarse[labels], ((0, 0), (0, LANES - 6))))
    return tuple(
        call(kernel, [block, block], [VMEM] * len(operands), "finish", [pltpu.VMEM((devices, LANES), jnp.float32)])(
            *operands
        )
    )


def solution(mesh):
    placed = (
        P("gx", None, "gz"),
        P("gx", None, "gz"),
        P(None, "gx", None, "gz"),
        P(),
        P(),
        P(),
        P(("gx", "gz"), None),
        P(None, "gx", None, "gz"),
    )
    return jax.shard_map(
        body,
        mesh=mesh,
        in_specs=placed,
        out_specs=(P("gx", None, "gz"), P("gx", None, "gz")),
        check_vma=False,
    )
```

```python
import functools

import jax
import jax.numpy as jnp
import numpy as np
from jax import lax
from jax.experimental import pallas as pl
from jax.experimental.pallas import tpu as pltpu
from jax.sharding import PartitionSpec as P

POINTS = [
    -1.0,
    -0.8717401485096066,
    -0.5917001814331423,
    -0.2092992179024789,
    0.2092992179024789,
    0.5917001814331423,
    0.8717401485096066,
    1.0,
]
WEIGHTS = [
    0.03571428571428571,
    0.21070422714350603,
    0.34112269248350435,
    0.4124587946587038,
    0.4124587946587038,
    0.34112269248350435,
    0.21070422714350603,
    0.03571428571428571,
]
ONES = [1.0] * 8
LOW = [(1.0 - s) / 2.0 for s in POINTS]
HIGH = [(1.0 + s) / 2.0 for s in POINTS]
EXACT = lax.Precision.HIGHEST

ROWS = 16
LANES = 128
WIDE = 256
BOTH = 384
HALO = 32
ELEMENTS = 22
CORNERS = (58, 80)
SPARE = (84, 100)
DEEP, SHALLOW = 25, 17
SLOT = DEEP + SHALLOW
FIRST_FIELDS = ((0, 24), (41, 17))
SECOND_FIELDS = ((0, 16), (32, 16), (64, 16), (96, 16))
FAR_FIELDS = ((0, 24), (48, 24))
FIRST_ROWS, FAR_ROWS, SECOND_ROWS = 48, 24, 40
PAIRS = ((0, 0), (0, 1), (1, 1))
GROUP_X = (ONES + LOW, [0.0] * 8 + HIGH)
INVERSE_X = [0.5] + [1.0] * 6 + [0.5] + [0.5] + [1.0] * 6 + [0.5]


def iota(shape, dim):
    return lax.broadcasted_iota(jnp.int32, shape, dim)


def pick(index, values):
    result = jnp.full(index.shape, values[0], jnp.float32)
    for i in range(1, 8):
        result = jnp.where(index == i, values[i], result)
    return result


def even_index(axis):
    return lax.rem(lax.axis_index(axis), 2) == 0


class Geometry:
    def __init__(self, lanes):
        shape = (2, 8, lanes)
        self.element_y, self.row, lane = iota(shape, 0), iota(shape, 1), iota(shape, 2)
        self.position = lane & 7
        self.first = self.position == 0
        self.last = self.position == 7
        self.edge = self.first | self.last
        self.weight_y = pick(self.row, WEIGHTS)
        self.weight_z = pick(self.position, WEIGHTS)
        self.inverse_z = jnp.where(self.edge, 0.5, 1.0)
        self.wall = (self.element_y == 1) & (self.row == 7)
        inner = ((self.element_y == 0) & (self.row == 7)) | ((self.element_y == 1) & (self.row == 0))
        self.inverse_y = jnp.where(inner, 0.5, 1.0)
        self.keep = jnp.where(self.wall, 0.0, 1.0)
        self.lanes = lanes

    def pair_y(self, v):
        lower, upper = v[0], v[1]
        row = self.row[0]
        up = jnp.where(row == 7, pltpu.roll(upper, 7, 0), 0.0)
        down = jnp.where(row == 0, pltpu.roll(lower, 1, 0), 0.0)
        return jnp.stack([lower + up, upper + down])

    def pair_z(self, v):
        flat = v.reshape(16, self.lanes)
        after = pltpu.roll(flat, self.lanes - 1, 1).reshape(v.shape)
        before = pltpu.roll(flat, 1, 1).reshape(v.shape)
        return v + jnp.where(self.edge, jnp.where(self.last, after, before), 0.0)

    def pair(self, v):
        return self.pair_z(self.pair_y(v))

    def assemble(self, v):
        return self.pair(v) * self.keep


def solid(v):
    return v.reshape(ROWS, v.shape[-1])


def split(v):
    return v.reshape(2, 8, v.shape[-1])


def own(v):
    return v[..., :LANES]


def down(v):
    return jnp.sum(v.reshape(ROWS, LANES), axis=0, keepdims=True)


def line_of(ref, at, lanes):
    row = ref[at : at + 1, :]
    return jnp.concatenate([row] * (lanes // LANES), axis=1)[None]


def weighted(factors, rows):
    total = None
    for factor, row in zip(factors, rows):
        total = factor * row if total is None else total + factor * row
    return total


def divisors_of(c, lam):
    lanes = c[0].shape[-1]
    lam_y = jnp.concatenate([lam[0]] * (lanes // LANES), axis=1)[None]
    lam_z = jnp.concatenate([lam[1]] * (lanes // LANES), axis=1)[None]
    base = c[1] * lam_y + c[2] * lam_z
    return [1.0 / (c[0] * line_of(lam.at[0], i, lanes) + base) for i in range(8)]


def halo_lanes():
    lane = iota((1, 1, LANES), 2)
    return (lane < HALO) | (lane >= LANES - HALO)


def join_pair(low, high):
    other = pltpu.roll(solid(high[:, :, LANES:]), LANES // 2, 1).reshape(2, 8, LANES)
    return jnp.concatenate([own(low), own(high), jnp.where(halo_lanes(), low[:, :, LANES:], other)], axis=2)


def part_pair(v):
    last = v[:, :, WIDE:]
    other = pltpu.roll(solid(last), LANES // 2, 1).reshape(2, 8, LANES)
    return jnp.concatenate([own(v), last], axis=2), jnp.concatenate([v[:, :, LANES:WIDE], other], axis=2)


def join_pairs(rows):
    return [join_pair(rows[x], rows[x + 8]) for x in range(8)]


def part_pairs(pairs):
    parted = [part_pair(v) for v in pairs]
    return [v[0] for v in parted] + [v[1] for v in parted]


def pair_line(ref, low, high):
    one, two = ref[low : low + 1, :], ref[high : high + 1, :]
    mixed = jnp.where(halo_lanes()[0], one, two)
    return jnp.concatenate([one, two, mixed], axis=1)[None]


def contract_x(rows, table, i, transpose=False):
    total = None
    for p in range(8):
        factor = line_of(table, p * 8 + i if transpose else i * 8 + p, rows[p].shape[-1])
        term = factor * rows[p]
        total = term if total is None else total + term
    return total


def contract_y(v, diagonals):
    def moved(value, rows):
        return jnp.stack([pltpu.roll(value[e], 8 - rows, 0) for e in range(2)])

    shifted = [v] + [moved(v, d) for d in range(1, 4)]
    return weighted(diagonals[:4], shifted) + moved(weighted(diagonals[4:], shifted), 4)


def thirds(v):
    high = v.astype(jnp.bfloat16)
    rest = v - high.astype(jnp.float32)
    middle = rest.astype(jnp.bfloat16)
    return high, middle, (rest - middle.astype(jnp.float32)).astype(jnp.bfloat16)


def contract_z(flat, upper, lower, which, short=False):
    pieces = []
    for at in range(0, flat.shape[1], LANES):
        high, middle, low = thirds(flat[:, at : at + LANES])
        one = jnp.dot(
            jnp.concatenate([high, middle], axis=1), upper[which], preferred_element_type=jnp.float32
        )
        if short:
            pieces.append(one[:, :LANES] + one[:, LANES:])
            continue
        two = jnp.dot(jnp.concatenate([low, high], axis=1), lower[which], preferred_element_type=jnp.float32)
        pieces.append(one[:, :LANES] + (one[:, LANES:] + two))
    return pieces[0] if len(pieces) == 1 else jnp.concatenate(pieces, axis=1)


def wide_diagonals(ref, which, lanes=WIDE):
    return [jnp.concatenate([ref[which, d]] * (lanes // LANES), axis=1)[None] for d in range(8)]


def metric(ref, component, element):
    at = (component * 2 + element) * 2
    return jnp.stack([jnp.broadcast_to(ref[at + e : at + e + 1, :], (8, WIDE)) for e in range(2)])


def scaled_metrics(geo, c):
    return c[0] * geo.weight_y * geo.weight_z, c[1] * geo.weight_z, c[2] * geo.weight_y


def stored_factors(ref, element):
    return [split(ref[c, element]) for c in range(3)]


def apply_pairs(pairs, factors, stiffness, upper, lower, diagonals, short=False):
    factor_x, factor_y, factor_z = factors
    along_z = contract_z(jnp.concatenate([solid(v) for v in pairs], axis=0), upper, lower, 0, short)
    along_z = [split(along_z[x * 16 : x * 16 + 16]) for x in range(8)]
    result = []
    for i in range(8):
        terms = factor_y * contract_y(pairs[i], diagonals) + factor_z * along_z[i]
        result.append(factor_x * contract_x(pairs, stiffness, i) + WEIGHTS[i] * terms)
    return result, along_z


def join_middle(rows):
    middle = rows[7] + rows[8]
    return rows[:7] + [middle, middle] + rows[9:]


def fold(parts, fields):
    lane = iota((8, LANES), 1)
    result = parts[0]
    for part, (offset, half) in list(zip(parts, fields))[1:]:
        taken = ((lane - offset + half) & (LANES - 1)) < 2 * half
        result = jnp.where(taken, pltpu.roll(part, offset, 1), result)
    return result


def unfold(packed, field, fill=0.0):
    offset, half = field
    lane = iota((8, LANES), 1)
    moved = pltpu.roll(packed, LANES - offset, 1) if offset else packed
    return jnp.where(((lane + half) & (LANES - 1)) < 2 * half, moved, fill)


def widen(tile, pieces):
    return jnp.concatenate([tile, jnp.concatenate(pieces, axis=0)], axis=1)


def group_lanes(lanes, group):
    lane = iota((1, lanes), 1)
    signed = jnp.where(lane < lanes // 2 + lanes // 4, lane, lane - lanes) if lanes > LANES else lane
    element, position = signed >> 3, lane & 7
    low, high = pick(position, LOW), pick(position, HIGH)
    here = jnp.where((element >> 3) == group, low, 0.0)
    return here + jnp.where(((element + 1) >> 3) == group, high, 0.0)


def pack_kernel(
    source, previous, coefficients, eigen, coarse,
    first, second, elements, near_source, near_previous, near_eigen, near_coarse, raw, ready,
):
    copies = [
        pltpu.make_async_copy(source, near_source, ready.at[0]),
        pltpu.make_async_copy(previous, near_previous, ready.at[1]),
        pltpu.make_async_copy(coefficients, raw, ready.at[2]),
        pltpu.make_async_copy(eigen, near_eigen, ready.at[3]),
        pltpu.make_async_copy(coarse, near_coarse, ready.at[4]),
    ]
    for copy in copies:
        copy.start()
    even = even_index("gz")
    elements[...] = jnp.zeros_like(elements)
    for copy in copies:
        copy.wait()
    for c in range(3):
        for element in range(2):
            at = (c * 2 + element) * 2
            elements[at : at + 2, 0:16] = raw[c, element]
    slot = iota((8, LANES), 1)
    for to_right, out in ((even, first), (jnp.logical_not(even), second)):
        for tile in range(11):
            packed = None
            for k in range(3):
                n = 3 * tile + k
                if n >= 2 * ROWS:
                    break
                for ref, width, at in ((near_previous, DEEP, SLOT * k), (near_source, SHALLOW, SLOT * k + DEEP)):
                    shift = jnp.where(to_right, (at + width) % LANES, at)
                    moved = pltpu.roll(ref[n // 2, 8 * (n % 2) : 8 * (n % 2) + 8], shift, 1)
                    packed = moved if packed is None else jnp.where(slot >= at, moved, packed)
            if tile == 10:
                for at, rows in zip(SPARE, (elements[:8], elements[8:])):
                    packed = jnp.where(slot >= at, pltpu.roll(rows, at, 1), packed)
            out[tile] = packed


def lanes_of(elements):
    lane = iota((24, WIDE), 1)
    beyond = lane - LANES
    right, left = LANES + 3 * 8, WIDE - 3 * 8
    index = jnp.where(lane < right, lane >> 3, jnp.where(lane >= left, 19 + ((beyond - (left - LANES)) >> 3), ELEMENTS))
    spread = (iota((24, WIDE), 0) == index).astype(jnp.bfloat16)
    high, middle, low = (jnp.dot(v, spread, preferred_element_type=jnp.float32) for v in thirds(elements[:, 0:24]))
    return high + (middle + low)


def elements_of(folded):
    lane = iota((8, LANES), 1)
    rest = jnp.where(lane == ELEMENTS, 1.0, 0.0)
    return jnp.concatenate(
        [jnp.where(lane < ELEMENTS, pltpu.roll(folded, LANES - at, 1), rest) for at in CORNERS], axis=0
    )


def prepare_kernel(
    with_coarse, elements, stiffness, vectors, eigen, labels, coarse, tables,
    upper, lower, diagonals, stiff_table, vector_table, bend, lam, lines, fixed, near_tables,
):
    near_tables[...] = tables[...]
    widen = (iota((16, LANES), 0) == (iota((16, LANES), 1) >> 3)).astype(jnp.float32)
    metrics = jnp.dot(elements[:, 0:16], widen, precision=EXACT, preferred_element_type=jnp.float32)
    repeat = (iota((LANES, 8), 0) & 7 == iota((LANES, 8), 1)).astype(jnp.float32)
    same = (iota((LANES, LANES), 0) >> 3) == (iota((LANES, LANES), 1) >> 3)
    unit = (iota((8, 8), 0) == iota((8, 8), 1)).astype(jnp.float32)
    row, column = iota((8, 8), 0), iota((8, 8), 1)

    def dot(a, b, dims):
        return lax.dot_general(a, b, (dims, ((), ())), precision=EXACT, preferred_element_type=jnp.float32)

    def put_block(at, matrix):
        half = dot(repeat, matrix, ((1,), (0,)))
        put_thirds(at, jnp.where(same, dot(half, repeat, ((1,), (1,))), 0.0))

    def put_thirds(at, block):
        high, middle, low = thirds(block)
        both = jnp.concatenate([high, middle], axis=1)
        upper[at] = jnp.concatenate([both, both], axis=0)
        lower[at] = jnp.concatenate([high, low], axis=0)

    def put_diagonals(at, matrix):
        turned = jnp.concatenate([matrix[4:], matrix[:4]], axis=0)
        for d in range(8):
            chosen = jnp.where(column == ((row + d % 4) & 7), matrix if d < 4 else turned, 0.0)
            diagonals[at, d] = jnp.broadcast_to(jnp.sum(chosen, axis=1, keepdims=True), (8, LANES))

    def put_table(out, matrix):
        tall = (iota((64, 8), 0) >> 3 == iota((64, 8), 1)).astype(jnp.float32)
        chosen = jnp.where(iota((64, 8), 0) & 7 == iota((64, 8), 1), dot(tall, matrix, ((1,), (0,))), 0.0)
        out[...] = jnp.broadcast_to(jnp.sum(chosen, axis=1, keepdims=True), (64, LANES))

    lane = iota((LANES, LANES), 1) & 7
    node = iota((LANES, LANES), 0)
    element, position = node >> 3, node & 7
    low, high = pick(position, LOW), pick(position, HIGH)
    columns = jnp.where(lane == (element >> 3), low, 0.0) + jnp.where(lane == ((element + 1) >> 3), high, 0.0)
    columns = jnp.where(lane == 3, 1.0, jnp.where(lane < 3, columns, 0.0))
    put_thirds(3, columns)
    k, s = stiffness[...], vectors[...]
    k_turned, s_turned = dot(k, unit, ((0,), (0,))), dot(s, unit, ((0,), (0,)))
    for at, matrix in enumerate((k_turned, s, s_turned)):
        put_block(at, matrix)
    for at, matrix in enumerate((k, s_turned, s)):
        put_diagonals(at, matrix)
    put_table(stiff_table, k)
    put_table(vector_table, s)
    for side, near in ((0, 0), (1, 7)):
        chosen = jnp.where(column == near, 0.0, s_turned * k[near : near + 1, :])
        total = jnp.sum(chosen, axis=1, keepdims=True)
        bend[8 * side : 8 * side + 8] = jnp.broadcast_to(total, (8, LANES))
    values = eigen[...]
    total = jnp.sum(jnp.where(row == column, values, 0.0), axis=1, keepdims=True)
    lam[0] = jnp.broadcast_to(total, (8, LANES))
    lam[1] = jnp.broadcast_to(dot(values, repeat, ((1,), (1,))), (8, LANES))
    stiff_lines = []
    for at, line in enumerate((ONES, LOW, HIGH)):
        total = jnp.sum(k * pick(column, line), axis=1, keepdims=True)
        stiff_lines.append(jnp.broadcast_to(total, (8, LANES)))
        lines[at] = stiff_lines[at]

    groups = [group_lanes(LANES, b) for b in range(3)]
    stacked = jnp.concatenate(groups + [jnp.zeros((13, LANES), jnp.float32)], axis=0)
    stiff_z = contract_z(stacked, upper, lower, 0)
    weight_z = pick(iota((1, LANES), 1) & 7, WEIGHTS)
    node = iota((8, LANES), 0)
    mass_y = [sum(WEIGHTS), sum(WEIGHTS[:7])]
    last = jnp.broadcast_to(k[:, 7:8], (8, LANES))
    inner = jnp.where(node == 7, 0.0, stiff_lines[0] - last)
    stiff_y = [jnp.sum(v, axis=0, keepdims=True) for v in (stiff_lines[0], inner)]
    at = 0
    for a, b in PAIRS:
        across, along = jnp.zeros((1, LANES), jnp.float32), jnp.zeros((1, LANES), jnp.float32)
        for element in range(2):
            fa = GROUP_X[a][element * 8 : element * 8 + 8]
            fb = GROUP_X[b][element * 8 : element * 8 + 8]
            if not (any(fa) and any(fb)):
                continue
            mass_x = sum(w * p * q for w, p, q in zip(WEIGHTS, fa, fb))
            applied = stiff_lines[0 if fb == ONES else 1 + b]
            stiff_x = jnp.sum(applied * pick(node, fa), axis=0, keepdims=True)
            for e in range(2):
                cx, cy, cz = (metrics[(c * 2 + element) * 2 + e].reshape(1, LANES) for c in range(3))
                across = across + cx * (stiff_x * mass_y[e]) + cy * (stiff_y[e] * mass_x)
                along = along + cz * (mass_x * mass_y[e])
        across = across * weight_z
        for b in range(3):
            fixed[at : at + 1] = across * groups[b] + along * stiff_z[b : b + 1]
            at += 1
    fixed[9:16] = jnp.zeros((7, LANES), jnp.float32)
    place = iota((1, LANES), 1)
    numbers = jnp.zeros((1, LANES), jnp.float32)
    for a in range(2):
        for b in range(3):
            corner, x, z = 4 * a + (b == 2), a, (0, 8, 15)[b]
            number = labels[corner, x][0:1, z : z + 1].astype(jnp.float32)
            numbers = jnp.where(place == 8 * (3 * a + b) + 4, number, numbers)
    fixed[16:17] = numbers
    below = jnp.zeros((1, LANES), jnp.float32)
    if with_coarse:
        per, count = coarse.shape
        below = [coarse[i : i + 1, :] for i in range(per)]
        if per * count < LANES:
            below.append(jnp.zeros((1, LANES - per * count), jnp.float32))
        below = jnp.concatenate(below, axis=1)
    fixed[17:18] = below
    fixed[18:24] = jnp.zeros((6, LANES), jnp.float32)


def start_kernel(
    source, previous, elements, first, second, stiffness, upper, lower, diagonals,
    start, remainder, factors, pair_factors, halves, common, part, metrics,
):
    even = even_index("gz")
    lane = iota((8, LANES), 1)
    one, two = first[...], second[...]
    from_right, from_left = jnp.where(even, one, two), jnp.where(even, two, one)

    def beyond(n, at, width):
        at = at + SLOT * (n % 3)
        right, left = from_right[n // 3], from_left[n // 3]
        if at:
            right = pltpu.roll(right, LANES - at, 1)
        left = pltpu.roll(left, (LANES - width - at) % LANES, 1)
        return jnp.where(lane < width, right, jnp.where(lane >= LANES - width, left, 0.0))

    def wide(ref, x, at, width):
        return split(widen(ref[x], [beyond(2 * x + e, at, width) for e in range(2)]))

    geo = Geometry(WIDE)
    right, left = (
        jnp.concatenate([pltpu.roll(tiles[10], (LANES + to - at) % LANES, 1) for at in SPARE], axis=0)
        for tiles, to in ((from_right, 16), (from_left, 6))
    )
    place = iota((16, LANES), 1)
    compact = jnp.where(place < 16, elements[...], jnp.where(place < 19, right, jnp.where(place < ELEMENTS, left, 1.0)))
    metrics[...] = lanes_of(compact)
    factor = geo.keep * geo.inverse_y * geo.inverse_z
    rows = [geo.pair(wide(previous, x, 0, DEEP)) * (factor * INVERSE_X[x]) for x in range(ROWS)]
    rows = join_middle(rows)
    faces = (rows[0], rows[15])
    for x in range(ROWS):
        start[x] = solid(own(rows[x]))
    scaled = [scaled_metrics(geo, [metric(metrics, c, e) for c in range(3)]) for e in range(2)]
    joined = [join_pair(scaled[0][c], scaled[1][c]) for c in range(3)]
    for c in range(3):
        pair_factors[c] = solid(joined[c])
        for e in range(2):
            factors[c, e] = solid(scaled[e][c])
    applied, _ = apply_pairs(join_pairs(rows), joined, stiffness, upper, lower, wide_diagonals(diagonals, 0, BOTH))
    applied = part_pairs(applied)
    rest = [wide(source, x, DEEP, SHALLOW) - applied[x] for x in range(ROWS)]
    halves[0], halves[1] = solid(faces[0]), solid(faces[1])
    for x in range(ROWS):
        remainder[x] = solid(rest[x])
    messages, distant = [], []
    for side, x in ((0, 0), (1, 15)):
        half, value = solid(faces[side]), solid(rest[x])
        lower_fold = fold([half[:8, LANES:], value[:8, LANES:]], FIRST_FIELDS)
        upper_fold = fold([half[8:, LANES:], value[8:, LANES:]], FIRST_FIELDS)
        for at, rows in zip(CORNERS, (compact[:8], compact[8:])):
            upper_fold = jnp.where((lane >= at) & (lane < at + ELEMENTS), pltpu.roll(rows, at, 1), upper_fold)
        messages.append(jnp.concatenate([half[:, :LANES], value[:, :LANES], lower_fold, upper_fold], axis=0))
        folded = fold([half[:8, LANES:], half[8:, LANES:]], FAR_FIELDS)
        distant.append(jnp.concatenate([half[:, :LANES], folded], axis=0))
    common[: 2 * FIRST_ROWS] = jnp.concatenate(messages, axis=0)
    common[2 * FIRST_ROWS :] = jnp.zeros((16, LANES), jnp.float32)
    for side in range(2):
        part[side] = jnp.concatenate([messages[side], distant[1 - side]], axis=0)


def guess_kernel(
    remainder, metrics, part, stiffness, vectors, bend, lam, upper, lower, diagonals,
    known, spectrum, inverse, message_a, message_b,
):
    geo = Geometry(WIDE)
    rest = [split(remainder[x]) for x in range(ROWS)]
    rest = [geo.assemble(v) for v in join_middle(rest)]
    for x in range(ROWS):
        known[x] = solid(own(rest[x]))
    pairs = join_pairs(rest)
    forward = wide_diagonals(diagonals, 1, BOTH)
    moved = [solid(contract_y(contract_x(pairs, vectors, i, True), forward)) for i in range(8)]
    transformed = contract_z(jnp.concatenate(moved, axis=0), upper, lower, 1, True)
    divisors = divisors_of([join_pair(metric(metrics, c, 0), metric(metrics, c, 1)) for c in range(3)], lam)
    damped = []
    for i in range(8):
        value = split(transformed[i * 16 : i * 16 + 16])
        spectrum[i], inverse[i] = solid(value), solid(divisors[i])
        damped.append(value * divisors[i])
    ends = [part_pair(contract_x(damped, vectors, near)) for near in (0, 7)]
    messages = []
    for side, near in ((0, 0), (1, 7)):
        value = ends[side][side]
        beside = part_pair(weighted([line_of(bend, side * 8 + i, BOTH) for i in range(8)], damped))[side]
        beside = beside + line_of(stiffness, near * 8 + 7 - near, WIDE) * ends[side][1 - side]
        value, beside = solid(value), solid(beside)
        folded = fold([v[at : at + 8, LANES:] for v in (value, beside) for at in (0, 8)], SECOND_FIELDS)
        messages.append(jnp.concatenate([value[:, :LANES], beside[:, :LANES], folded], axis=0))
    even_x = even_index("gx")
    both = [jnp.concatenate([part[side], messages[side]], axis=0) for side in range(2)]
    message_a[...] = jnp.where(even_x, both[1], both[0])
    message_b[...] = jnp.where(even_x, both[0], both[1])


def read_first(message):
    lower_fold, upper_fold = message[32:40], message[40:48]
    half, value = (
        widen(message[16 * k : 16 * k + 16], [unfold(lower_fold, FIRST_FIELDS[k]), unfold(upper_fold, FIRST_FIELDS[k])])
        for k in range(2)
    )
    return split(half), split(value)


def read_far(message):
    far = message[FIRST_ROWS : FIRST_ROWS + FAR_ROWS]
    return split(widen(far[0:16], [unfold(far[16:24], field) for field in FAR_FIELDS]))


def read_second(message):
    pieces = [unfold(message[32:40], field) for field in SECOND_FIELDS]
    return widen(message[0:16], pieces[:2]), widen(message[16:32], pieces[2:])


def coarse_pieces(geo, factors, stiff_keep, functions, stiff_functions):
    factor_x, factor_y, factor_z = factors
    kept_x, kept_y, kept_z = factor_x * geo.keep, factor_y * stiff_keep, factor_z * geo.keep
    result = []
    for plain, turned in zip(functions, stiff_functions):
        result.append(
            (geo.assemble(kept_x * plain[None]), geo.assemble(kept_y * plain[None] + kept_z * turned[None]))
        )
    return result


def wide_functions(upper, lower):
    functions = [group_lanes(WIDE, b) for b in (-1, 0, 1, 2)]
    stacked = jnp.concatenate(functions + [jnp.zeros((12, WIDE), jnp.float32)], axis=0)
    turned = contract_z(stacked, upper, lower, 0)
    return functions, [turned[b : b + 1] for b in range(4)]


def kept_stiffness(geo, lines, stiffness):
    row = iota((8, LANES), 0)
    last = jnp.zeros((8, LANES), jnp.float32)
    for j in range(8):
        last = jnp.where(row == j, stiffness[j * 8 + 7 : j * 8 + 8, :], last)
    both = jnp.stack([lines[0], lines[0] - last])
    return jnp.concatenate([both] * (WIDE // LANES), axis=2)


def ready_kernel(factors, stiffness, lines, upper, lower, pieces, waves, stiff_keep):
    geo = Geometry(WIDE)
    functions, turned = wide_functions(upper, lower)
    for b in range(4):
        waves[b : b + 1], waves[4 + b : 5 + b] = functions[b], turned[b]
    along_y = kept_stiffness(geo, lines, stiffness)
    stiff_keep[...] = solid(along_y)
    for element in range(2):
        made = coarse_pieces(geo, stored_factors(factors, element), along_y, functions, turned)
        for b in range(4):
            for k in range(2):
                pieces[element, k, b] = solid(own(made[b][k]))


def side_kernel(
    first, halves, remainder, factors, got, beyond, stiffness, vectors, bend, lam, upper, lower, diagonals,
    start_face, additions, fields, answers, near_factors,
):
    right = even_index("gx") if first else jnp.logical_not(even_index("gx"))
    side = jnp.where(right, 1, 0)
    other = 1 - side
    geo = Geometry(WIDE)
    message = got[...]
    near_half, near_value = read_first(message)
    far_half = read_far(message)
    block = beyond[pl.ds(pl.multiple_of(FIRST_ROWS * other, 8), FIRST_ROWS), :]
    last_half, last_value = read_first(block)
    spread = lanes_of(jnp.concatenate([elements_of(message[40:48]), elements_of(block[40:48])], axis=0))

    def metrics_of(device, of_right, of_left):
        rows = spread[16 * device : 16 * device + 16]
        return [jnp.where(right, metric(rows, c, of_right), metric(rows, c, of_left)) for c in range(3)]

    def row_of(ref, at):
        row = ref[pl.ds(at, 1), :]
        return jnp.concatenate([row] * (WIDE // LANES), axis=1)[None]

    near, far, last = metrics_of(0, 0, 1), metrics_of(0, 1, 0), metrics_of(1, 0, 1)
    near_scaled, far_scaled, last_scaled = (scaled_metrics(geo, c) for c in (near, far, last))
    mine = [split(factors[c, side]) for c in range(3)]
    for c in range(3):
        near_factors[c] = solid(near_scaled[c])
    half, value = split(halves[side]), split(remainder[15 * side])
    start_face[...] = solid(own(half + near_half))
    stiff = wide_diagonals(diagonals, 0)
    parts = [half, near_half, far_half, last_half]
    along_z = contract_z(jnp.concatenate([solid(v) for v in parts], axis=0), upper, lower, 0)
    here, there = row_of(stiffness, 63 * side), row_of(stiffness, 63 * other)

    def face_row(c, corner, k):
        term = c[1] * contract_y(parts[k], stiff) + c[2] * split(along_z[k * 16 : k * 16 + 16])
        return corner * (c[0] * parts[k]) + WEIGHTS[0] * term

    taken = face_row(mine, here, 1) + face_row(near_scaled, there, 0)
    taken_far = face_row(far_scaled, here, 3) + face_row(last_scaled, there, 2)
    made = [
        geo.assemble(v)
        for v in (
            near_value - taken, mine[0] * near_half, value - taken, near_scaled[0] * half,
            last_value - taken_far, far_scaled[0] * last_half,
        )
    ]
    for k in range(2):
        additions[k] = solid(own(made[k]))
    forward = wide_diagonals(diagonals, 1)
    flat = jnp.concatenate([solid(contract_y(v, forward)) for v in made], axis=0)
    flat = contract_z(flat, upper, lower, 1, True)
    fields[0], fields[1] = flat[0:16], flat[16:32]
    near_total, near_field, far_total, far_field = (split(flat[k * 16 : k * 16 + 16]) for k in range(2, 6))

    cross = line_of(stiffness, 7, WIDE)
    ends = [[row_of(vectors, 56 * at + i) for i in range(8)] for at in (other, side)]
    bends = [[row_of(bend, 8 * at + i) for i in range(8)] for at in (other, side)]
    result, partial = (split(v) for v in read_second(message[FIRST_ROWS + FAR_ROWS :]))
    crossed, divisors = cross * far_field, divisors_of(near, lam)
    close = [
        (ends[0][i] * near_total - bends[0][i] * near_field - ends[1][i] * crossed) * divisors[i] for i in range(8)
    ]
    crossed, divisors = cross * near_field, divisors_of(far, lam)
    distant = [
        (ends[1][i] * far_total - bends[1][i] * far_field - ends[0][i] * crossed) * divisors[i] for i in range(8)
    ]
    result = result + weighted(ends[0], close)
    partial = partial + weighted(bends[0], close) + cross * weighted(ends[0], distant)
    answers[0], answers[1] = solid(result), solid(partial)


def solve_kernel(
    known, spectrum, inverse, sides, stiffness, vectors, bend, upper, lower, diagonals,
    start_faces, residual, local, beside, face_factors, sums,
):
    even = even_index("gx")
    geo = Geometry(WIDE)

    def both(which, *at):
        one, two = sides[0][which][at], sides[1][which][at]
        return jnp.where(even, two, one), jnp.where(even, one, two)

    start_faces[0], start_faces[1] = both(0)
    for c in range(3):
        face_factors[0, c], face_factors[1, c] = both(4, c)
    totals, moved = both(1, 0), both(1, 1)

    rows = [split(known[x]) for x in range(ROWS)]
    rows[0], rows[15] = rows[0] + split(totals[0]), rows[15] + split(totals[1])
    for side, face in ((0, 0), (1, 7)):
        for i in range(8):
            if i != face:
                change = line_of(stiffness, i * 8 + face, LANES) * split(moved[side])
                x = side * 8 + i
                rows[x] = rows[x] - change
                if x in (7, 8):
                    rows[15 - x] = rows[15 - x] - change
    parts = [None, None]
    for x in range(ROWS):
        residual[x] = solid(rows[x])
        for a in range(2):
            if GROUP_X[a][x] * INVERSE_X[x] != 0.0:
                term = (GROUP_X[a][x] * INVERSE_X[x]) * rows[x]
                parts[a] = term if parts[a] is None else parts[a] + term
    weight = own(geo.inverse_y * geo.inverse_z)
    for a in range(2):
        sums[a : a + 1] = down(parts[a] * weight)

    backward = wide_diagonals(diagonals, 2)
    totals, moved = [split(v) for v in both(2, 0)], [split(v) for v in both(2, 1)]

    total, close = join_pair(*totals), join_pair(*moved)
    crossed = line_of(stiffness, 7, BOTH) * join_pair(moved[1], moved[0])
    ready = []
    for i in range(8):
        change = pair_line(vectors, i, 56 + i) * total - pair_line(bend, i, 8 + i) * close
        change = change - pair_line(vectors, 56 + i, i) * crossed
        ready.append(solid((split(spectrum[i]) + change) * split(inverse[i])))
    answers = [both(3, k) for k in range(2)]
    answers = jnp.concatenate([answers[k][side] for side in range(2) for k in range(2)], axis=0)
    back = contract_z(jnp.concatenate(ready, axis=0), upper, lower, 2, True)
    answers = contract_z(answers, upper, lower, 2, True)
    wide_backward = wide_diagonals(diagonals, 2, BOTH)
    back = [contract_y(split(back[k * 16 : k * 16 + 16]), wide_backward) for k in range(8)]
    answers = [contract_y(split(answers[k * 16 : k * 16 + 16]), backward) for k in range(4)]
    solved = part_pairs([contract_x(back, vectors, i) for i in range(8)])
    total = None
    for x in range(ROWS):
        term = own(solved[x]) * rows[x]
        total = term if total is None else total + term
    sums[2:3] = down(total)
    sums[3:8] = jnp.zeros((5, LANES), jnp.float32)
    solved = join_middle(solved)
    solved[0], solved[15] = solved[0] + answers[0], solved[15] + answers[2]
    for x in range(ROWS):
        local[x] = solid(geo.assemble(solved[x]))
    for side in range(2):
        beside[side] = solid(geo.assemble(answers[1 + 2 * side]))


def image_kernel(
    local, factors, face_factors, beside, sums, fixed, stiffness, lines, upper, lower, diagonals,
    image, payload,
):
    geo = Geometry(WIDE)
    rows = [split(local[x]) for x in range(ROWS)]
    stiff = wide_diagonals(diagonals, 0)
    applied, along_z = apply_pairs(
        join_pairs(rows), [split(factors[c]) for c in range(3)], stiffness, upper, lower,
        wide_diagonals(diagonals, 0, BOTH), True,
    )
    applied = part_pairs(applied)
    along_z = (part_pair(along_z[0])[0], part_pair(along_z[7])[1])
    total, parts = None, [None, None]
    for x in range(ROWS):
        term = own(applied[x]) * own(rows[x])
        total = term if total is None else total + term
        for a in range(2):
            if GROUP_X[a][x] != 0.0:
                term = GROUP_X[a][x] * own(applied[x])
                parts[a] = term if parts[a] is None else parts[a] + term
    extra = [down(value * own(geo.keep)) for value in parts + [total]]
    for side, x, across in ((0, 0, 63), (1, 15, 0)):
        there = [split(face_factors[side, c]) for c in range(3)]
        other = there[0] * (split(beside[side]) + line_of(stiffness, across, WIDE) * rows[x])
        other = other + WEIGHTS[0] * (there[1] * contract_y(rows[x], stiff) + there[2] * along_z[side])
        applied[x] = applied[x] + other
    applied = join_middle(applied)
    for x in range(ROWS):
        image[x] = solid(own(geo.assemble(applied[x])))
    zero = jnp.zeros((1, LANES), jnp.float32)
    table = jnp.concatenate(
        [sums[0:2], extra[0], extra[1], fixed[0:9], sums[2:3], extra[2], zero], axis=0
    )
    reduced = contract_z(table, upper, lower, 3)
    mine = (iota((16, LANES), 1) >> 3) == iota((16, LANES), 0)
    row = jnp.sum(jnp.where(mine, reduced, 0.0), axis=0, keepdims=True) + fixed[16:17]
    block = jnp.concatenate([row, fixed[17:18]] * 4, axis=0)
    copies = payload.shape[0] // 8
    payload[...] = jnp.broadcast_to(block[None], (copies, 8, LANES)).reshape(copies * 8, LANES)


def middle_kernel(
    known, pair_factors, spectrum, inverse, _, stiffness, vectors, bend, upper, lower, diagonals, fixed, lines,
    halves, remainder, factors, got, beyond, lam, *refs
):
    one, refs = refs[:5], refs[5:]
    (start_faces, residual, local, face_factors, image, payload, beside, sums), two = refs[:8], refs[8:]
    side_kernel(
        False, halves, remainder, factors, got, beyond, stiffness, vectors, bend, lam, upper, lower, diagonals, *two
    )
    solve_kernel(
        known, spectrum, inverse, (one, two), stiffness, vectors, bend, upper, lower, diagonals,
        start_faces, residual, local, beside, face_factors, sums,
    )
    image_kernel(
        local, pair_factors, face_factors, beside, sums, fixed, stiffness, lines, upper, lower, diagonals, image, payload
    )


def lane_tables():
    one = np.zeros((8, LANES), np.float32)
    two = np.zeros((8, LANES), np.float32)
    top = np.zeros((8, LANES), np.float32)
    for a in range(2):
        for b in range(3):
            one[6, 8 * a + b], two[3 * a + b, 8 * a + b], top[0, 8 * a + b] = 1.0, 1.0, 1.0
            one[6, 8 * (2 + a) + b], two[3 * a + b, 8 * (2 + a) + b] = 2.0, 1.0
            top[1, 8 * (2 + a) + b] = 1.0
    for p, (a, other) in enumerate(PAIRS):
        for b in range(3):
            for c in range(3):
                at = 8 * (4 + 3 * p + b) + c
                one[3 * a + b, at] = 1.0 if a == other else 2.0
                two[3 * other + c, at] = 1.0
                top[1, at] = 1.0
    one[6, 8 * 13 + 3], two[6, 8 * 13 + 3], top[0, 8 * 13 + 3] = 1.0, 1.0, 1.0
    one[6, 8 * 14 + 3], two[6, 8 * 14 + 3], top[1, 8 * 14 + 3] = 1.0, 1.0, 1.0
    return np.stack([one, two, top])


def final_kernel(
    devices, spans, count, per,
    start, start_faces, residual, local, image, pieces, face_factors, waves, stiff_keep, lines, tables,
    arrived, given, new_solution, new_residual, values, gathered,
):
    gathered[: 2 * devices] = arrived[...]
    rows = gathered[pl.ds(0, devices, stride=2), :]
    if given is None:
        spot = iota((devices, count), 1)
        hits = []
        rhs = [jnp.zeros((1, devices), jnp.float32) for _ in range(per)]
        owner = iota((devices, devices), 1)
        for k in range(6):
            label = rows[:, 8 * k + 4 : 8 * k + 5].astype(jnp.int32)
            at = 8 * (k // 3) + k % 3
            value = rows[:, at : at + 1]
            hits.append(spot == label)
            for q in range(per):
                chosen = jnp.where(owner * per + q == label, value, 0.0)
                rhs[q] = rhs[q] + jnp.sum(chosen, axis=0, keepdims=True)
        inverse = gathered[pl.ds(1, devices, stride=2), :]
        coarse = None
        for q in range(per):
            term = jnp.dot(
                rhs[q], inverse[:, q * count : q * count + count], precision=EXACT,
                preferred_element_type=jnp.float32,
            )
            coarse = term if coarse is None else coarse + term
        columns = [jnp.sum(jnp.where(hit, coarse, 0.0), axis=1, keepdims=True) for hit in hits]
        kept = jnp.zeros((devices, LANES), jnp.float32)
        for k in range(6):
            kept = jnp.where(iota((devices, LANES), 1) == k, columns[k], kept)
        values[...] = kept
    else:
        columns = [given[:, k : k + 1] for k in range(6)]
        values[...] = given[...]
    one, two = tables[0, 6:7, :], tables[1, 6:7, :]
    for k in range(6):
        one = one + columns[k] * tables[0, k : k + 1, :]
        two = two + columns[k] * tables[1, k : k + 1, :]
    product = jnp.sum(rows * one * two, axis=0, keepdims=True)
    numerator = jnp.sum(product * tables[2, 0:1, :], axis=1, keepdims=True)
    denominator = jnp.sum(product * tables[2, 1:2, :], axis=1, keepdims=True)
    alpha = numerator / denominator

    gx, gz = lax.axis_index("gx"), lax.axis_index("gz")
    before_x = lax.rem(gx + devices // spans - 1, devices // spans)
    before_z = lax.rem(gz + spans - 1, spans)
    here = values[pl.ds(gx * spans + gz, 1), :]
    behind = values[pl.ds(gx * spans + before_z, 1), :]
    aside = values[pl.ds(before_x * spans + gz, 1), :]
    corner = values[pl.ds(before_x * spans + before_z, 1), :]

    def four(line, back, a):
        return [back[:, 3 * a + 1 : 3 * a + 2]] + [line[:, 3 * a + b : 3 * a + b + 1] for b in range(3)]

    def mix(numbers, ref):
        total = numbers[0] * ref[0]
        for b in range(1, 4):
            total = total + numbers[b] * ref[b]
        return total

    near, right, left = four(here, behind, 0), four(here, behind, 1), four(aside, corner, 0)
    whole = [mix(near, pieces.at[0, k]) for k in range(2)]
    low = [mix(near, pieces.at[1, k]) for k in range(2)]
    high = [mix(right, pieces.at[1, k]) for k in range(2)]

    def stiff(line, i):
        return lines[line, i : i + 1, :]

    extra = [stiff(0, i) * whole[0] + WEIGHTS[i] * whole[1] for i in range(8)]
    for i in range(8):
        extra.append(
            stiff(1, i) * low[0] + stiff(2, i) * high[0] + WEIGHTS[i] * (LOW[i] * low[1] + HIGH[i] * high[1])
        )
    extra = join_middle(extra)
    geo = Geometry(WIDE)

    def line(numbers, at):
        total = numbers[0] * waves[at : at + 1, :]
        for b in range(1, 4):
            total = total + numbers[b] * waves[at + b : at + b + 1, :]
        return total

    def wide_stiff(k, i):
        return jnp.concatenate([stiff(k, i)] * (WIDE // LANES), axis=1)

    def beyond(side, stiff_x, plain, turned):
        fx, fy, fz = (split(face_factors[side, c]) for c in range(3))
        value = fx * geo.keep * stiff_x[None]
        value = value + WEIGHTS[0] * (fy * split(stiff_keep[...]) * plain[None] + fz * geo.keep * turned[None])
        return solid(own(geo.assemble(value)))

    wave_near, wave_right = line(near, 0), line(right, 0)
    across = wide_stiff(1, 7) * line(left, 0) + wide_stiff(2, 7) * wave_near
    extra[0] = extra[0] + beyond(0, across, wave_near, line(near, 4))
    extra[15] = extra[15] + beyond(1, wide_stiff(0, 0) * wave_right, wave_right, line(right, 4))
    keep = solid(own(geo.keep))
    line_near, line_right = wave_near[:, :LANES], wave_right[:, :LANES]
    for x in range(ROWS):
        begin = start_faces[x // 15] if x in (0, 15) else start[x]
        mine = local[x, :, :LANES]
        new_residual[x] = residual[x] - alpha * (image[x] + extra[x])
        coarse_line = GROUP_X[0][x] * line_near
        if GROUP_X[1][x] != 0.0:
            coarse_line = coarse_line + GROUP_X[1][x] * line_right
        new_solution[x] = begin + alpha * (mine + keep * coarse_line)


VMEM = pl.BlockSpec(memory_space=pltpu.VMEM)
SMEM = pl.BlockSpec(memory_space=pltpu.SMEM)
FAR = pl.BlockSpec(memory_space=pltpu.HBM)


def call(kernel, shapes, specs, name, scratch=(), cost=None):
    def leaf(shape):
        kind = jnp.float32
        if shape[0] == "half":
            shape, kind = shape[1:], jnp.bfloat16
        return jax.ShapeDtypeStruct(shape, kind)

    return pl.pallas_call(
        kernel,
        out_shape=[leaf(shape) for shape in shapes],
        in_specs=specs,
        out_specs=[VMEM] * len(shapes),
        scratch_shapes=list(scratch),
        compiler_params=pltpu.CompilerParams(vmem_limit_bytes=16 * 1024 * 1024),
        name=name,
        cost_estimate=cost,
    )


def swap(first, second, axis):
    size = lax.axis_size(axis)
    odd = [(i, (i + 1) % size) for i in range(1, size, 2)]
    one = lax.ppermute(first, axis, [(i, i ^ 1) for i in range(size)])
    two = lax.ppermute(second, axis, odd + [(b, a) for a, b in odd])
    return one, two


def second_neighbours(common, axis):
    size = lax.axis_size(axis)
    if size == 4:
        return lax.ppermute(common, axis, [(i, i ^ 2) for i in range(size)])
    left = lax.ppermute(common[:FIRST_ROWS], axis, [(i, (i - 2) % size) for i in range(size)])
    right = lax.ppermute(common[FIRST_ROWS:], axis, [(i, (i + 2) % size) for i in range(size)])
    return jnp.concatenate([left, right], axis=0)


def body(
    source, previous, coefficients, stiffness, fdm_vectors, fdm_values, coarse_inverse, vertex_map
):
    assert source.shape == (ROWS, ROWS, LANES)
    spans = lax.axis_size("gz")
    devices = lax.axis_size("gx") * spans
    per, count = coarse_inverse.shape
    small = per * count <= LANES
    block, wide, face = (ROWS, ROWS, LANES), (ROWS, ROWS, WIDE), (ROWS, LANES)
    halo = (11, 8, LANES)

    coarse = coarse_inverse if small else coarse_inverse[:, :LANES]
    operands = (source, previous, coefficients, fdm_values.reshape(1, 8), coarse)
    first, second, elements, source, previous, eigen, coarse = call(
        pack_kernel,
        [halo, halo, face, block, block, (1, 8), coarse.shape],
        [FAR] * 5,
        "pack",
        [pltpu.VMEM(coefficients.shape, jnp.float32), pltpu.SemaphoreType.DMA((5,))],
    )(*(pltpu.with_memory_space_constraint(v, pltpu.HBM) for v in operands))
    first, second = swap(first, second, "gz")
    upper, lower, diagonals, stiff, vectors, bend, lam, lines, fixed, tables = call(
        functools.partial(prepare_kernel, small),
        [
            ("half", 4, WIDE, WIDE), ("half", 4, WIDE, LANES), (3, 8, 8, LANES),
            (64, LANES), (64, LANES), (16, LANES), (2, 8, LANES), (3, 8, LANES), (24, LANES), (3, 8, LANES),
        ],
        [VMEM] * 7,
        "prepare",
    )(elements, stiffness, fdm_vectors, eigen, vertex_map, coarse, jnp.asarray(lane_tables()))

    message = (FIRST_ROWS + FAR_ROWS + SECOND_ROWS, LANES)
    start, remainder, factors, pair_factors, halves, common, part, metrics = call(
        start_kernel,
        [
            block, wide, (3, 2, ROWS, WIDE), (3, ROWS, BOTH), (2, ROWS, WIDE), (2 * FIRST_ROWS + 16, LANES),
            (2, FIRST_ROWS + FAR_ROWS, LANES), (16, WIDE),
        ],
        [VMEM] * 9,
        "start",
    )(source, previous, elements, first, second, stiff, upper, lower, diagonals)
    beyond = second_neighbours(common, "gx")
    known, spectrum, inverse, side_a, side_b = call(
        guess_kernel, [block, (8, ROWS, BOTH), (8, ROWS, BOTH), message, message], [VMEM] * 10, "guess",
        cost=pl.CostEstimate(flops=4000000000, bytes_accessed=4000000, transcendentals=0),
    )(remainder, metrics, part, stiff, vectors, bend, lam, upper, lower, diagonals)
    side_a, side_b = swap(side_a, side_b, "gx")
    pieces, waves, stiff_keep = call(
        ready_kernel, [(2, 2, 4, ROWS, LANES), (8, WIDE), (ROWS, WIDE)], [VMEM] * 5, "ready"
    )(factors, stiff, lines, upper, lower)

    shapes = [face, (2, ROWS, LANES), (2, ROWS, WIDE), (2, ROWS, WIDE), (3, ROWS, WIDE)]
    one = call(functools.partial(side_kernel, True), shapes, [VMEM] * 12, "side")(
        halves, remainder, factors, side_a, beyond, stiff, vectors, bend, lam, upper, lower, diagonals
    )
    start_faces, residual, local, face_factors, image, payload = call(
        middle_kernel,
        [(2, ROWS, LANES), block, wide, (2, 3, ROWS, WIDE), block, (2 * devices, LANES)],
        [VMEM] * 24,
        "middle",
        [pltpu.VMEM(shape, jnp.float32) for shape in [(2, ROWS, WIDE), (8, LANES)] + shapes],
    )(
        known, pair_factors, spectrum, inverse, waves, stiff, vectors, bend, upper, lower, diagonals, fixed, lines,
        halves, remainder, factors, side_b, beyond, lam, *one,
    )
    gathered = lax.all_to_all(payload.reshape(devices, 2, LANES), ("gx", "gz"), 0, 0)
    gathered = gathered.reshape(2 * devices, LANES)

    operands = [
        start, start_faces, residual, local, image, pieces, face_factors, waves, stiff_keep, lines,
        tables, gathered,
    ]
    finish = functools.partial(final_kernel, devices, spans, count, per)
    if small:

        def kernel(*refs):
            finish(*refs[:12], None, *refs[12:])

    else:
        kernel = finish
        rows = gathered[0::2]
        labels = rows[:, jnp.array([8 * k + 4 for k in range(6)])].astype(jnp.int32)
        parts = rows[:, jnp.array([8 * (k // 3) + k % 3 for k in range(6)])]
        rhs = jnp.zeros((count,), jnp.float32).at[labels.reshape(-1)].add(parts.reshape(-1))
        mine = jnp.dot(coarse_inverse, rhs, precision=EXACT)
        coarse = lax.all_gather(mine, ("gx", "gz"), axis=0, tiled=True)
        operands.append(jnp.pad(coarse[labels], ((0, 0), (0, LANES - 6))))
    scratch = [pltpu.VMEM((devices, LANES), jnp.float32), pltpu.VMEM((2 * devices + 8, LANES), jnp.float32)]
    return tuple(
        call(kernel, [block, block], [VMEM] * len(operands), "finish", scratch)(
            *operands
        )
    )


def solution(mesh):
    placed = (
        P("gx", None, "gz"),
        P("gx", None, "gz"),
        P(None, "gx", None, "gz"),
        P(),
        P(),
        P(),
        P(("gx", "gz"), None),
        P(None, "gx", None, "gz"),
    )
    return jax.shard_map(
        body,
        mesh=mesh,
        in_specs=placed,
        out_specs=(P("gx", None, "gz"), P("gx", None, "gz")),
        check_vma=False,
    )
```

```python
import functools

import jax
import jax.numpy as jnp
import numpy as np
from jax import lax
from jax.experimental import pallas as pl
from jax.experimental.pallas import tpu as pltpu
from jax.sharding import PartitionSpec as P

POINTS = [
    -1.0,
    -0.8717401485096066,
    -0.5917001814331423,
    -0.2092992179024789,
    0.2092992179024789,
    0.5917001814331423,
    0.8717401485096066,
    1.0,
]
WEIGHTS = [
    0.03571428571428571,
    0.21070422714350603,
    0.34112269248350435,
    0.4124587946587038,
    0.4124587946587038,
    0.34112269248350435,
    0.21070422714350603,
    0.03571428571428571,
]
ONES = [1.0] * 8
LOW = [(1.0 - s) / 2.0 for s in POINTS]
HIGH = [(1.0 + s) / 2.0 for s in POINTS]
EXACT = lax.Precision.HIGHEST

ROWS = 16
LANES = 128
WIDE = 256
BOTH = 384
HALO = 32
ELEMENTS = 22
CORNERS = (58, 80)
SPARE = (84, 100)
DEEP, SHALLOW = 25, 17
SLOT = DEEP + SHALLOW
FIRST_FIELDS = ((0, 24), (41, 17))
SECOND_FIELDS = ((0, 16), (32, 16), (64, 16), (96, 16))
FAR_FIELDS = ((0, 24), (48, 24))
FIRST_ROWS, FAR_ROWS, SECOND_ROWS = 48, 24, 40
PAIRS = ((0, 0), (0, 1), (1, 1))
GROUP_X = (ONES + LOW, [0.0] * 8 + HIGH)
INVERSE_X = [0.5] + [1.0] * 6 + [0.5] + [0.5] + [1.0] * 6 + [0.5]


def iota(shape, dim):
    return lax.broadcasted_iota(jnp.int32, shape, dim)


def pick(index, values):
    result = jnp.full(index.shape, values[0], jnp.float32)
    for i in range(1, 8):
        result = jnp.where(index == i, values[i], result)
    return result


def even_index(axis):
    return lax.rem(lax.axis_index(axis), 2) == 0


class Geometry:
    def __init__(self, lanes):
        shape = (2, 8, lanes)
        self.element_y, self.row, lane = iota(shape, 0), iota(shape, 1), iota(shape, 2)
        self.position = lane & 7
        self.first = self.position == 0
        self.last = self.position == 7
        self.edge = self.first | self.last
        self.weight_y = pick(self.row, WEIGHTS)
        self.weight_z = pick(self.position, WEIGHTS)
        self.inverse_z = jnp.where(self.edge, 0.5, 1.0)
        self.wall = (self.element_y == 1) & (self.row == 7)
        inner = ((self.element_y == 0) & (self.row == 7)) | ((self.element_y == 1) & (self.row == 0))
        self.inverse_y = jnp.where(inner, 0.5, 1.0)
        self.keep = jnp.where(self.wall, 0.0, 1.0)
        self.lanes = lanes

    def pair_y(self, v):
        lower, upper = v[0], v[1]
        row = self.row[0]
        up = jnp.where(row == 7, pltpu.roll(upper, 7, 0), 0.0)
        down = jnp.where(row == 0, pltpu.roll(lower, 1, 0), 0.0)
        return jnp.stack([lower + up, upper + down])

    def pair_z(self, v):
        flat = v.reshape(16, self.lanes)
        after = pltpu.roll(flat, self.lanes - 1, 1).reshape(v.shape)
        before = pltpu.roll(flat, 1, 1).reshape(v.shape)
        return v + jnp.where(self.edge, jnp.where(self.last, after, before), 0.0)

    def pair(self, v):
        return self.pair_z(self.pair_y(v))

    def assemble(self, v):
        return self.pair(v) * self.keep

    def assemble_own(self, v):
        v = self.pair_y(v)
        mine, halo = v[:, :, :LANES], v[:, :, LANES:]
        lane = iota((1, 1, LANES), 2)
        edge, last, keep = (mask[:, :, :LANES] for mask in (self.edge, self.last, self.keep))

        def turned(mixed, lanes):
            return pltpu.roll(mixed.reshape(16, LANES), lanes, 1).reshape(2, 8, LANES)

        after = turned(jnp.where(lane == 0, halo, mine), LANES - 1)
        before = turned(jnp.where(lane == LANES - 1, halo, mine), 1)
        return (mine + jnp.where(edge, jnp.where(last, after, before), 0.0)) * keep


def solid(v):
    return v.reshape(ROWS, v.shape[-1])


def split(v):
    return v.reshape(2, 8, v.shape[-1])


def own(v):
    return v[..., :LANES]


def down(v):
    return jnp.sum(v.reshape(ROWS, LANES), axis=0, keepdims=True)


def line_of(ref, at, lanes):
    row = ref[at : at + 1, :]
    return jnp.concatenate([row] * (lanes // LANES), axis=1)[None]


def weighted(factors, rows):
    total = None
    for factor, row in zip(factors, rows):
        total = factor * row if total is None else total + factor * row
    return total


def divisors_of(c, lam):
    lanes = c[0].shape[-1]
    lam_y = jnp.concatenate([lam[0]] * (lanes // LANES), axis=1)[None]
    lam_z = jnp.concatenate([lam[1]] * (lanes // LANES), axis=1)[None]
    base = c[1] * lam_y + c[2] * lam_z
    return [1.0 / (c[0] * line_of(lam.at[0], i, lanes) + base) for i in range(8)]


def halo_lanes():
    lane = iota((1, 1, LANES), 2)
    return (lane < HALO) | (lane >= LANES - HALO)


def join_pair(low, high):
    other = pltpu.roll(solid(high[:, :, LANES:]), LANES // 2, 1).reshape(2, 8, LANES)
    return jnp.concatenate([own(low), own(high), jnp.where(halo_lanes(), low[:, :, LANES:], other)], axis=2)


def part_pair(v):
    last = v[:, :, WIDE:]
    other = pltpu.roll(solid(last), LANES // 2, 1).reshape(2, 8, LANES)
    return jnp.concatenate([own(v), last], axis=2), jnp.concatenate([v[:, :, LANES:WIDE], other], axis=2)


def join_pairs(rows):
    return [join_pair(rows[x], rows[x + 8]) for x in range(8)]


def part_pairs(pairs):
    parted = [part_pair(v) for v in pairs]
    return [v[0] for v in parted] + [v[1] for v in parted]


def pair_line(ref, low, high):
    one, two = ref[low : low + 1, :], ref[high : high + 1, :]
    mixed = jnp.where(halo_lanes()[0], one, two)
    return jnp.concatenate([one, two, mixed], axis=1)[None]


def contract_x(rows, table, i, transpose=False):
    total = None
    for p in range(8):
        factor = line_of(table, p * 8 + i if transpose else i * 8 + p, rows[p].shape[-1])
        term = factor * rows[p]
        total = term if total is None else total + term
    return total


def contract_y(v, diagonals):
    def moved(value, rows):
        return jnp.stack([pltpu.roll(value[e], 8 - rows, 0) for e in range(2)])

    shifted = [v] + [moved(v, d) for d in range(1, 4)]
    return weighted(diagonals[:4], shifted) + moved(weighted(diagonals[4:], shifted), 4)


def thirds(v):
    high = v.astype(jnp.bfloat16)
    rest = v - high.astype(jnp.float32)
    middle = rest.astype(jnp.bfloat16)
    return high, middle, (rest - middle.astype(jnp.float32)).astype(jnp.bfloat16)


def contract_z(flat, upper, lower, which, short=False):
    pieces = []
    for at in range(0, flat.shape[1], LANES):
        high, middle, low = thirds(flat[:, at : at + LANES])
        one = jnp.dot(
            jnp.concatenate([high, middle], axis=1), upper[which], preferred_element_type=jnp.float32
        )
        if short:
            pieces.append(one[:, :LANES] + one[:, LANES:])
            continue
        two = jnp.dot(jnp.concatenate([low, high], axis=1), lower[which], preferred_element_type=jnp.float32)
        pieces.append(one[:, :LANES] + (one[:, LANES:] + two))
    return pieces[0] if len(pieces) == 1 else jnp.concatenate(pieces, axis=1)


def wide_diagonals(ref, which, lanes=WIDE):
    return [jnp.concatenate([ref[which, d]] * (lanes // LANES), axis=1)[None] for d in range(8)]


def metric(ref, component, element):
    at = (component * 2 + element) * 2
    return jnp.stack([jnp.broadcast_to(ref[at + e : at + e + 1, :], (8, WIDE)) for e in range(2)])


def scaled_metrics(geo, c):
    return c[0] * geo.weight_y * geo.weight_z, c[1] * geo.weight_z, c[2] * geo.weight_y


def stored_factors(ref, element):
    return [split(ref[c, element]) for c in range(3)]


def apply_pairs(pairs, factors, stiffness, upper, lower, diagonals, short=False):
    factor_x, factor_y, factor_z = factors
    along_z = contract_z(jnp.concatenate([solid(v) for v in pairs], axis=0), upper, lower, 0, short)
    along_z = [split(along_z[x * 16 : x * 16 + 16]) for x in range(8)]
    result = []
    for i in range(8):
        terms = factor_y * contract_y(pairs[i], diagonals) + factor_z * along_z[i]
        result.append(factor_x * contract_x(pairs, stiffness, i) + WEIGHTS[i] * terms)
    return result, along_z


def join_middle(rows):
    middle = rows[7] + rows[8]
    return rows[:7] + [middle, middle] + rows[9:]


def fold(parts, fields):
    lane = iota((8, LANES), 1)
    result = parts[0]
    for part, (offset, half) in list(zip(parts, fields))[1:]:
        taken = ((lane - offset + half) & (LANES - 1)) < 2 * half
        result = jnp.where(taken, pltpu.roll(part, offset, 1), result)
    return result


def unfold(packed, field, fill=0.0):
    offset, half = field
    lane = iota((8, LANES), 1)
    moved = pltpu.roll(packed, LANES - offset, 1) if offset else packed
    return jnp.where(((lane + half) & (LANES - 1)) < 2 * half, moved, fill)


def widen(tile, pieces):
    return jnp.concatenate([tile, jnp.concatenate(pieces, axis=0)], axis=1)


def group_lanes(lanes, group):
    lane = iota((1, lanes), 1)
    signed = jnp.where(lane < lanes // 2 + lanes // 4, lane, lane - lanes) if lanes > LANES else lane
    element, position = signed >> 3, lane & 7
    low, high = pick(position, LOW), pick(position, HIGH)
    here = jnp.where((element >> 3) == group, low, 0.0)
    return here + jnp.where(((element + 1) >> 3) == group, high, 0.0)


def pack_kernel(
    source, previous, coefficients, eigen, coarse,
    first, second, elements, near_source, near_previous, near_eigen, near_coarse, raw, ready,
):
    copies = [
        pltpu.make_async_copy(source, near_source, ready.at[0]),
        pltpu.make_async_copy(previous, near_previous, ready.at[1]),
        pltpu.make_async_copy(coefficients, raw, ready.at[2]),
        pltpu.make_async_copy(eigen, near_eigen, ready.at[3]),
        pltpu.make_async_copy(coarse, near_coarse, ready.at[4]),
    ]
    for copy in copies:
        copy.start()
    even = even_index("gz")
    elements[...] = jnp.zeros_like(elements)
    for copy in copies:
        copy.wait()
    for c in range(3):
        for element in range(2):
            at = (c * 2 + element) * 2
            elements[at : at + 2, 0:16] = raw[c, element]
    slot = iota((8, LANES), 1)
    for to_right, out in ((even, first), (jnp.logical_not(even), second)):
        for tile in range(11):
            packed = None
            for k in range(3):
                n = 3 * tile + k
                if n >= 2 * ROWS:
                    break
                for ref, width, at in ((near_previous, DEEP, SLOT * k), (near_source, SHALLOW, SLOT * k + DEEP)):
                    shift = jnp.where(to_right, (at + width) % LANES, at)
                    moved = pltpu.roll(ref[n // 2, 8 * (n % 2) : 8 * (n % 2) + 8], shift, 1)
                    packed = moved if packed is None else jnp.where(slot >= at, moved, packed)
            if tile == 10:
                for at, rows in zip(SPARE, (elements[:8], elements[8:])):
                    packed = jnp.where(slot >= at, pltpu.roll(rows, at, 1), packed)
            out[tile] = packed


def lanes_of(elements):
    lane = iota((24, WIDE), 1)
    beyond = lane - LANES
    right, left = LANES + 3 * 8, WIDE - 3 * 8
    index = jnp.where(lane < right, lane >> 3, jnp.where(lane >= left, 19 + ((beyond - (left - LANES)) >> 3), ELEMENTS))
    spread = (iota((24, WIDE), 0) == index).astype(jnp.bfloat16)
    high, middle, low = (jnp.dot(v, spread, preferred_element_type=jnp.float32) for v in thirds(elements[:, 0:24]))
    return high + (middle + low)


def elements_of(folded):
    lane = iota((8, LANES), 1)
    rest = jnp.where(lane == ELEMENTS, 1.0, 0.0)
    return jnp.concatenate(
        [jnp.where(lane < ELEMENTS, pltpu.roll(folded, LANES - at, 1), rest) for at in CORNERS], axis=0
    )


def prepare_kernel(
    with_coarse, elements, stiffness, vectors, eigen, labels, coarse, tables,
    upper, lower, diagonals, stiff_table, vector_table, bend, lam, lines, fixed, near_tables,
):
    near_tables[...] = tables[...]
    widen = (iota((16, LANES), 0) == (iota((16, LANES), 1) >> 3)).astype(jnp.float32)
    metrics = jnp.dot(elements[:, 0:16], widen, precision=EXACT, preferred_element_type=jnp.float32)
    repeat = (iota((LANES, 8), 0) & 7 == iota((LANES, 8), 1)).astype(jnp.float32)
    same = (iota((LANES, LANES), 0) >> 3) == (iota((LANES, LANES), 1) >> 3)
    unit = (iota((8, 8), 0) == iota((8, 8), 1)).astype(jnp.float32)
    row, column = iota((8, 8), 0), iota((8, 8), 1)

    def dot(a, b, dims):
        return lax.dot_general(a, b, (dims, ((), ())), precision=EXACT, preferred_element_type=jnp.float32)

    def put_block(at, matrix):
        half = dot(repeat, matrix, ((1,), (0,)))
        put_thirds(at, jnp.where(same, dot(half, repeat, ((1,), (1,))), 0.0))

    def put_thirds(at, block):
        high, middle, low = thirds(block)
        both = jnp.concatenate([high, middle], axis=1)
        upper[at] = jnp.concatenate([both, both], axis=0)
        lower[at] = jnp.concatenate([high, low], axis=0)

    def put_diagonals(at, matrix):
        turned = jnp.concatenate([matrix[4:], matrix[:4]], axis=0)
        for d in range(8):
            chosen = jnp.where(column == ((row + d % 4) & 7), matrix if d < 4 else turned, 0.0)
            diagonals[at, d] = jnp.broadcast_to(jnp.sum(chosen, axis=1, keepdims=True), (8, LANES))

    def put_table(out, matrix):
        tall = (iota((64, 8), 0) >> 3 == iota((64, 8), 1)).astype(jnp.float32)
        chosen = jnp.where(iota((64, 8), 0) & 7 == iota((64, 8), 1), dot(tall, matrix, ((1,), (0,))), 0.0)
        out[...] = jnp.broadcast_to(jnp.sum(chosen, axis=1, keepdims=True), (64, LANES))

    lane = iota((LANES, LANES), 1) & 7
    node = iota((LANES, LANES), 0)
    element, position = node >> 3, node & 7
    low, high = pick(position, LOW), pick(position, HIGH)
    columns = jnp.where(lane == (element >> 3), low, 0.0) + jnp.where(lane == ((element + 1) >> 3), high, 0.0)
    columns = jnp.where(lane == 3, 1.0, jnp.where(lane < 3, columns, 0.0))
    put_thirds(3, columns)
    k, s = stiffness[...], vectors[...]
    k_turned, s_turned = dot(k, unit, ((0,), (0,))), dot(s, unit, ((0,), (0,)))
    for at, matrix in enumerate((k_turned, s, s_turned)):
        put_block(at, matrix)
    for at, matrix in enumerate((k, s_turned, s)):
        put_diagonals(at, matrix)
    put_table(stiff_table, k)
    put_table(vector_table, s)
    for side, near in ((0, 0), (1, 7)):
        chosen = jnp.where(column == near, 0.0, s_turned * k[near : near + 1, :])
        total = jnp.sum(chosen, axis=1, keepdims=True)
        bend[8 * side : 8 * side + 8] = jnp.broadcast_to(total, (8, LANES))
    values = eigen[...]
    total = jnp.sum(jnp.where(row == column, values, 0.0), axis=1, keepdims=True)
    lam[0] = jnp.broadcast_to(total, (8, LANES))
    lam[1] = jnp.broadcast_to(dot(values, repeat, ((1,), (1,))), (8, LANES))
    stiff_lines = []
    for at, line in enumerate((ONES, LOW, HIGH)):
        total = jnp.sum(k * pick(column, line), axis=1, keepdims=True)
        stiff_lines.append(jnp.broadcast_to(total, (8, LANES)))
        lines[at] = stiff_lines[at]

    groups = [group_lanes(LANES, b) for b in range(3)]
    stacked = jnp.concatenate(groups + [jnp.zeros((13, LANES), jnp.float32)], axis=0)
    stiff_z = contract_z(stacked, upper, lower, 0)
    weight_z = pick(iota((1, LANES), 1) & 7, WEIGHTS)
    node = iota((8, LANES), 0)
    mass_y = [sum(WEIGHTS), sum(WEIGHTS[:7])]
    last = jnp.broadcast_to(k[:, 7:8], (8, LANES))
    inner = jnp.where(node == 7, 0.0, stiff_lines[0] - last)
    stiff_y = [jnp.sum(v, axis=0, keepdims=True) for v in (stiff_lines[0], inner)]
    at = 0
    for a, b in PAIRS:
        across, along = jnp.zeros((1, LANES), jnp.float32), jnp.zeros((1, LANES), jnp.float32)
        for element in range(2):
            fa = GROUP_X[a][element * 8 : element * 8 + 8]
            fb = GROUP_X[b][element * 8 : element * 8 + 8]
            if not (any(fa) and any(fb)):
                continue
            mass_x = sum(w * p * q for w, p, q in zip(WEIGHTS, fa, fb))
            applied = stiff_lines[0 if fb == ONES else 1 + b]
            stiff_x = jnp.sum(applied * pick(node, fa), axis=0, keepdims=True)
            for e in range(2):
                cx, cy, cz = (metrics[(c * 2 + element) * 2 + e].reshape(1, LANES) for c in range(3))
                across = across + cx * (stiff_x * mass_y[e]) + cy * (stiff_y[e] * mass_x)
                along = along + cz * (mass_x * mass_y[e])
        across = across * weight_z
        for b in range(3):
            fixed[at : at + 1] = across * groups[b] + along * stiff_z[b : b + 1]
            at += 1
    fixed[9:16] = jnp.zeros((7, LANES), jnp.float32)
    place = iota((1, LANES), 1)
    numbers = jnp.zeros((1, LANES), jnp.float32)
    for a in range(2):
        for b in range(3):
            corner, x, z = 4 * a + (b == 2), a, (0, 8, 15)[b]
            number = labels[corner, x][0:1, z : z + 1].astype(jnp.float32)
            numbers = jnp.where(place == 8 * (3 * a + b) + 4, number, numbers)
    fixed[16:17] = numbers
    below = jnp.zeros((1, LANES), jnp.float32)
    if with_coarse:
        per, count = coarse.shape
        below = [coarse[i : i + 1, :] for i in range(per)]
        if per * count < LANES:
            below.append(jnp.zeros((1, LANES - per * count), jnp.float32))
        below = jnp.concatenate(below, axis=1)
    fixed[17:18] = below
    fixed[18:24] = jnp.zeros((6, LANES), jnp.float32)


def start_kernel(
    source, previous, elements, first, second, stiffness, upper, lower, diagonals,
    start, remainder, factors, pair_factors, halves, common, part, metrics,
):
    even = even_index("gz")
    lane = iota((8, LANES), 1)
    one, two = first[...], second[...]
    from_right, from_left = jnp.where(even, one, two), jnp.where(even, two, one)

    def beyond(n, at, width):
        at = at + SLOT * (n % 3)
        right, left = from_right[n // 3], from_left[n // 3]
        if at:
            right = pltpu.roll(right, LANES - at, 1)
        left = pltpu.roll(left, (LANES - width - at) % LANES, 1)
        return jnp.where(lane < width, right, jnp.where(lane >= LANES - width, left, 0.0))

    def wide(ref, x, at, width):
        return split(widen(ref[x], [beyond(2 * x + e, at, width) for e in range(2)]))

    geo = Geometry(WIDE)
    right, left = (
        jnp.concatenate([pltpu.roll(tiles[10], (LANES + to - at) % LANES, 1) for at in SPARE], axis=0)
        for tiles, to in ((from_right, 16), (from_left, 6))
    )
    place = iota((16, LANES), 1)
    compact = jnp.where(place < 16, elements[...], jnp.where(place < 19, right, jnp.where(place < ELEMENTS, left, 1.0)))
    metrics[...] = lanes_of(compact)
    factor = geo.keep * geo.inverse_y * geo.inverse_z
    rows = [geo.pair(wide(previous, x, 0, DEEP)) * (factor * INVERSE_X[x]) for x in range(ROWS)]
    rows = join_middle(rows)
    faces = (rows[0], rows[15])
    for x in range(ROWS):
        start[x] = solid(own(rows[x]))
    scaled = [scaled_metrics(geo, [metric(metrics, c, e) for c in range(3)]) for e in range(2)]
    joined = [join_pair(scaled[0][c], scaled[1][c]) for c in range(3)]
    for c in range(3):
        pair_factors[c] = solid(joined[c])
        for e in range(2):
            factors[c, e] = solid(scaled[e][c])
    applied, _ = apply_pairs(join_pairs(rows), joined, stiffness, upper, lower, wide_diagonals(diagonals, 0, BOTH))
    applied = part_pairs(applied)
    rest = [wide(source, x, DEEP, SHALLOW) - applied[x] for x in range(ROWS)]
    halves[0], halves[1] = solid(faces[0]), solid(faces[1])
    for x in range(ROWS):
        remainder[x] = solid(rest[x])
    messages, distant = [], []
    for side, x in ((0, 0), (1, 15)):
        half, value = solid(faces[side]), solid(rest[x])
        lower_fold = fold([half[:8, LANES:], value[:8, LANES:]], FIRST_FIELDS)
        upper_fold = fold([half[8:, LANES:], value[8:, LANES:]], FIRST_FIELDS)
        for at, rows in zip(CORNERS, (compact[:8], compact[8:])):
            upper_fold = jnp.where((lane >= at) & (lane < at + ELEMENTS), pltpu.roll(rows, at, 1), upper_fold)
        messages.append(jnp.concatenate([half[:, :LANES], value[:, :LANES], lower_fold, upper_fold], axis=0))
        folded = fold([half[:8, LANES:], half[8:, LANES:]], FAR_FIELDS)
        distant.append(jnp.concatenate([half[:, :LANES], folded], axis=0))
    common[: 2 * FIRST_ROWS] = jnp.concatenate(messages, axis=0)
    common[2 * FIRST_ROWS :] = jnp.zeros((16, LANES), jnp.float32)
    for side in range(2):
        part[side] = jnp.concatenate([messages[side], distant[1 - side]], axis=0)


def guess_kernel(
    remainder, metrics, part, stiffness, vectors, bend, lam, upper, lower, diagonals,
    known, spectrum, inverse, message_a, message_b,
):
    geo = Geometry(WIDE)
    rest = [split(remainder[x]) for x in range(ROWS)]
    rest = [geo.assemble(v) for v in join_middle(rest)]
    for x in range(ROWS):
        known[x] = solid(own(rest[x]))
    pairs = join_pairs(rest)
    forward = wide_diagonals(diagonals, 1, BOTH)
    moved = [solid(contract_y(contract_x(pairs, vectors, i, True), forward)) for i in range(8)]
    transformed = contract_z(jnp.concatenate(moved, axis=0), upper, lower, 1, True)
    divisors = divisors_of([join_pair(metric(metrics, c, 0), metric(metrics, c, 1)) for c in range(3)], lam)
    damped = []
    for i in range(8):
        value = split(transformed[i * 16 : i * 16 + 16])
        spectrum[i], inverse[i] = solid(value), solid(divisors[i])
        damped.append(value * divisors[i])
    ends = [part_pair(contract_x(damped, vectors, near)) for near in (0, 7)]
    messages = []
    for side, near in ((0, 0), (1, 7)):
        value = ends[side][side]
        beside = part_pair(weighted([line_of(bend, side * 8 + i, BOTH) for i in range(8)], damped))[side]
        beside = beside + line_of(stiffness, near * 8 + 7 - near, WIDE) * ends[side][1 - side]
        value, beside = solid(value), solid(beside)
        folded = fold([v[at : at + 8, LANES:] for v in (value, beside) for at in (0, 8)], SECOND_FIELDS)
        messages.append(jnp.concatenate([value[:, :LANES], beside[:, :LANES], folded], axis=0))
    even_x = even_index("gx")
    both = [jnp.concatenate([part[side], messages[side]], axis=0) for side in range(2)]
    message_a[...] = jnp.where(even_x, both[1], both[0])
    message_b[...] = jnp.where(even_x, both[0], both[1])


def read_first(message):
    lower_fold, upper_fold = message[32:40], message[40:48]
    half, value = (
        widen(message[16 * k : 16 * k + 16], [unfold(lower_fold, FIRST_FIELDS[k]), unfold(upper_fold, FIRST_FIELDS[k])])
        for k in range(2)
    )
    return split(half), split(value)


def read_far(message):
    far = message[FIRST_ROWS : FIRST_ROWS + FAR_ROWS]
    return split(widen(far[0:16], [unfold(far[16:24], field) for field in FAR_FIELDS]))


def read_second(message):
    pieces = [unfold(message[32:40], field) for field in SECOND_FIELDS]
    return widen(message[0:16], pieces[:2]), widen(message[16:32], pieces[2:])


def coarse_pieces(geo, factors, stiff_keep, functions, stiff_functions):
    factor_x, factor_y, factor_z = factors
    kept_x, kept_y, kept_z = factor_x * geo.keep, factor_y * stiff_keep, factor_z * geo.keep
    result = []
    for plain, turned in zip(functions, stiff_functions):
        result.append(
            (geo.assemble(kept_x * plain[None]), geo.assemble(kept_y * plain[None] + kept_z * turned[None]))
        )
    return result


def wide_functions(upper, lower):
    functions = [group_lanes(WIDE, b) for b in (-1, 0, 1, 2)]
    stacked = jnp.concatenate(functions + [jnp.zeros((12, WIDE), jnp.float32)], axis=0)
    turned = contract_z(stacked, upper, lower, 0)
    return functions, [turned[b : b + 1] for b in range(4)]


def kept_stiffness(geo, lines, stiffness):
    row = iota((8, LANES), 0)
    last = jnp.zeros((8, LANES), jnp.float32)
    for j in range(8):
        last = jnp.where(row == j, stiffness[j * 8 + 7 : j * 8 + 8, :], last)
    both = jnp.stack([lines[0], lines[0] - last])
    return jnp.concatenate([both] * (WIDE // LANES), axis=2)


def ready_kernel(factors, stiffness, lines, upper, lower, pieces, waves, stiff_keep):
    geo = Geometry(WIDE)
    functions, turned = wide_functions(upper, lower)
    for b in range(4):
        waves[b : b + 1], waves[4 + b : 5 + b] = functions[b], turned[b]
    along_y = kept_stiffness(geo, lines, stiffness)
    stiff_keep[...] = solid(along_y)
    for element in range(2):
        made = coarse_pieces(geo, stored_factors(factors, element), along_y, functions, turned)
        for b in range(4):
            for k in range(2):
                pieces[element, k, b] = solid(own(made[b][k]))


def side_kernel(
    first, halves, remainder, factors, got, beyond, stiffness, vectors, bend, lam, upper, lower, diagonals,
    start_face, additions, fields, answers, near_factors,
):
    right = even_index("gx") if first else jnp.logical_not(even_index("gx"))
    side = jnp.where(right, 1, 0)
    other = 1 - side
    geo = Geometry(WIDE)
    message = got[...]
    near_half, near_value = read_first(message)
    far_half = read_far(message)
    block = beyond[pl.ds(pl.multiple_of(FIRST_ROWS * other, 8), FIRST_ROWS), :]
    last_half, last_value = read_first(block)
    spread = lanes_of(jnp.concatenate([elements_of(message[40:48]), elements_of(block[40:48])], axis=0))

    def metrics_of(device, of_right, of_left):
        rows = spread[16 * device : 16 * device + 16]
        return [jnp.where(right, metric(rows, c, of_right), metric(rows, c, of_left)) for c in range(3)]

    def row_of(ref, at):
        row = ref[pl.ds(at, 1), :]
        return jnp.concatenate([row] * (WIDE // LANES), axis=1)[None]

    near, far, last = metrics_of(0, 0, 1), metrics_of(0, 1, 0), metrics_of(1, 0, 1)
    near_scaled, far_scaled, last_scaled = (scaled_metrics(geo, c) for c in (near, far, last))
    mine = [split(factors[c, side]) for c in range(3)]
    for c in range(3):
        near_factors[c] = solid(near_scaled[c])
    half, value = split(halves[side]), split(remainder[15 * side])
    start_face[...] = solid(own(half + near_half))
    stiff = wide_diagonals(diagonals, 0)
    parts = [half, near_half, far_half, last_half]
    along_z = contract_z(jnp.concatenate([solid(v) for v in parts], axis=0), upper, lower, 0)
    here, there = row_of(stiffness, 63 * side), row_of(stiffness, 63 * other)

    def face_row(c, corner, k):
        term = c[1] * contract_y(parts[k], stiff) + c[2] * split(along_z[k * 16 : k * 16 + 16])
        return corner * (c[0] * parts[k]) + WEIGHTS[0] * term

    taken = face_row(mine, here, 1) + face_row(near_scaled, there, 0)
    taken_far = face_row(far_scaled, here, 3) + face_row(last_scaled, there, 2)
    made = [
        geo.assemble(v)
        for v in (
            near_value - taken, mine[0] * near_half, value - taken, near_scaled[0] * half,
            last_value - taken_far, far_scaled[0] * last_half,
        )
    ]
    for k in range(2):
        additions[k] = solid(own(made[k]))
    forward = wide_diagonals(diagonals, 1)
    flat = jnp.concatenate([solid(contract_y(v, forward)) for v in made], axis=0)
    flat = contract_z(flat, upper, lower, 1, True)
    fields[0], fields[1] = flat[0:16], flat[16:32]
    near_total, near_field, far_total, far_field = (split(flat[k * 16 : k * 16 + 16]) for k in range(2, 6))

    cross = line_of(stiffness, 7, WIDE)
    ends = [[row_of(vectors, 56 * at + i) for i in range(8)] for at in (other, side)]
    bends = [[row_of(bend, 8 * at + i) for i in range(8)] for at in (other, side)]
    result, partial = (split(v) for v in read_second(message[FIRST_ROWS + FAR_ROWS :]))
    crossed, divisors = cross * far_field, divisors_of(near, lam)
    close = [
        (ends[0][i] * near_total - bends[0][i] * near_field - ends[1][i] * crossed) * divisors[i] for i in range(8)
    ]
    crossed, divisors = cross * near_field, divisors_of(far, lam)
    distant = [
        (ends[1][i] * far_total - bends[1][i] * far_field - ends[0][i] * crossed) * divisors[i] for i in range(8)
    ]
    result = result + weighted(ends[0], close)
    partial = partial + weighted(bends[0], close) + cross * weighted(ends[0], distant)
    answers[0], answers[1] = solid(result), solid(partial)


def solve_kernel(
    known, spectrum, inverse, sides, stiffness, vectors, bend, upper, lower, diagonals,
    start_faces, residual, local, beside, face_factors, sums,
):
    even = even_index("gx")
    geo = Geometry(WIDE)

    def both(which, *at):
        one, two = sides[0][which][at], sides[1][which][at]
        return jnp.where(even, two, one), jnp.where(even, one, two)

    start_faces[0], start_faces[1] = both(0)
    for c in range(3):
        face_factors[0, c], face_factors[1, c] = both(4, c)
    totals, moved = both(1, 0), both(1, 1)

    rows = [split(known[x]) for x in range(ROWS)]
    rows[0], rows[15] = rows[0] + split(totals[0]), rows[15] + split(totals[1])
    for side, face in ((0, 0), (1, 7)):
        for i in range(8):
            if i != face:
                change = line_of(stiffness, i * 8 + face, LANES) * split(moved[side])
                x = side * 8 + i
                rows[x] = rows[x] - change
                if x in (7, 8):
                    rows[15 - x] = rows[15 - x] - change
    parts = [None, None]
    for x in range(ROWS):
        residual[x] = solid(rows[x])
        for a in range(2):
            if GROUP_X[a][x] * INVERSE_X[x] != 0.0:
                term = (GROUP_X[a][x] * INVERSE_X[x]) * rows[x]
                parts[a] = term if parts[a] is None else parts[a] + term
    weight = own(geo.inverse_y * geo.inverse_z)
    for a in range(2):
        sums[a : a + 1] = down(parts[a] * weight)

    backward = wide_diagonals(diagonals, 2)
    totals, moved = [split(v) for v in both(2, 0)], [split(v) for v in both(2, 1)]

    total, close = join_pair(*totals), join_pair(*moved)
    crossed = line_of(stiffness, 7, BOTH) * join_pair(moved[1], moved[0])
    ready = []
    for i in range(8):
        change = pair_line(vectors, i, 56 + i) * total - pair_line(bend, i, 8 + i) * close
        change = change - pair_line(vectors, 56 + i, i) * crossed
        ready.append(solid((split(spectrum[i]) + change) * split(inverse[i])))
    answers = [both(3, k) for k in range(2)]
    answers = jnp.concatenate([answers[k][side] for side in range(2) for k in range(2)], axis=0)
    back = contract_z(jnp.concatenate(ready, axis=0), upper, lower, 2, True)
    answers = contract_z(answers, upper, lower, 2, True)
    wide_backward = wide_diagonals(diagonals, 2, BOTH)
    back = [contract_y(split(back[k * 16 : k * 16 + 16]), wide_backward) for k in range(8)]
    answers = [contract_y(split(answers[k * 16 : k * 16 + 16]), backward) for k in range(4)]
    solved = part_pairs([contract_x(back, vectors, i) for i in range(8)])
    total = None
    for x in range(ROWS):
        term = own(solved[x]) * rows[x]
        total = term if total is None else total + term
    sums[2:3] = down(total)
    sums[3:8] = jnp.zeros((5, LANES), jnp.float32)
    solved = join_middle(solved)
    solved[0], solved[15] = solved[0] + answers[0], solved[15] + answers[2]
    for x in range(ROWS):
        local[x] = solid(geo.assemble(solved[x]))
    for side in range(2):
        beside[side] = solid(geo.assemble(answers[1 + 2 * side]))


def image_kernel(
    local, factors, face_factors, beside, sums, fixed, stiffness, lines, upper, lower, diagonals,
    image, payload,
):
    geo = Geometry(WIDE)
    rows = [split(local[x]) for x in range(ROWS)]
    stiff = wide_diagonals(diagonals, 0)
    applied, along_z = apply_pairs(
        join_pairs(rows), [split(factors[c]) for c in range(3)], stiffness, upper, lower,
        wide_diagonals(diagonals, 0, BOTH), True,
    )
    applied = part_pairs(applied)
    along_z = (part_pair(along_z[0])[0], part_pair(along_z[7])[1])
    total, parts = None, [None, None]
    for x in range(ROWS):
        term = own(applied[x]) * own(rows[x])
        total = term if total is None else total + term
        for a in range(2):
            if GROUP_X[a][x] != 0.0:
                term = GROUP_X[a][x] * own(applied[x])
                parts[a] = term if parts[a] is None else parts[a] + term
    extra = [down(value * own(geo.keep)) for value in parts + [total]]
    for side, x, across in ((0, 0, 63), (1, 15, 0)):
        there = [split(face_factors[side, c]) for c in range(3)]
        other = there[0] * (split(beside[side]) + line_of(stiffness, across, WIDE) * rows[x])
        other = other + WEIGHTS[0] * (there[1] * contract_y(rows[x], stiff) + there[2] * along_z[side])
        applied[x] = applied[x] + other
    applied = join_middle(applied)
    for x in range(ROWS):
        image[x] = solid(geo.assemble_own(applied[x]))
    zero = jnp.zeros((1, LANES), jnp.float32)
    table = jnp.concatenate(
        [sums[0:2], extra[0], extra[1], fixed[0:9], sums[2:3], extra[2], zero], axis=0
    )
    reduced = contract_z(table, upper, lower, 3)
    mine = (iota((16, LANES), 1) >> 3) == iota((16, LANES), 0)
    row = jnp.sum(jnp.where(mine, reduced, 0.0), axis=0, keepdims=True) + fixed[16:17]
    block = jnp.concatenate([row, fixed[17:18]] * 4, axis=0)
    copies = payload.shape[0] // 8
    payload[...] = jnp.broadcast_to(block[None], (copies, 8, LANES)).reshape(copies * 8, LANES)


def middle_kernel(
    known, pair_factors, spectrum, inverse, _, stiffness, vectors, bend, upper, lower, diagonals, fixed, lines,
    halves, remainder, factors, got, beyond, lam, *refs
):
    one, refs = refs[:5], refs[5:]
    (start_faces, residual, local, face_factors, image, payload, beside, sums), two = refs[:8], refs[8:]
    side_kernel(
        False, halves, remainder, factors, got, beyond, stiffness, vectors, bend, lam, upper, lower, diagonals, *two
    )
    solve_kernel(
        known, spectrum, inverse, (one, two), stiffness, vectors, bend, upper, lower, diagonals,
        start_faces, residual, local, beside, face_factors, sums,
    )
    image_kernel(
        local, pair_factors, face_factors, beside, sums, fixed, stiffness, lines, upper, lower, diagonals, image, payload
    )


def lane_tables():
    one = np.zeros((8, LANES), np.float32)
    two = np.zeros((8, LANES), np.float32)
    top = np.zeros((8, LANES), np.float32)
    for a in range(2):
        for b in range(3):
            one[6, 8 * a + b], two[3 * a + b, 8 * a + b], top[0, 8 * a + b] = 1.0, 1.0, 1.0
            one[6, 8 * (2 + a) + b], two[3 * a + b, 8 * (2 + a) + b] = 2.0, 1.0
            top[1, 8 * (2 + a) + b] = 1.0
    for p, (a, other) in enumerate(PAIRS):
        for b in range(3):
            for c in range(3):
                at = 8 * (4 + 3 * p + b) + c
                one[3 * a + b, at] = 1.0 if a == other else 2.0
                two[3 * other + c, at] = 1.0
                top[1, at] = 1.0
    one[6, 8 * 13 + 3], two[6, 8 * 13 + 3], top[0, 8 * 13 + 3] = 1.0, 1.0, 1.0
    one[6, 8 * 14 + 3], two[6, 8 * 14 + 3], top[1, 8 * 14 + 3] = 1.0, 1.0, 1.0
    return np.stack([one, two, top])


def final_kernel(
    devices, spans, count, per,
    start, start_faces, residual, local, image, pieces, face_factors, waves, stiff_keep, lines, tables,
    arrived, given, new_solution, new_residual, values, gathered,
):
    gathered[: 2 * devices] = arrived[...]
    rows = gathered[pl.ds(0, devices, stride=2), :]
    if given is None:
        spot = iota((devices, count), 1)
        hits = []
        rhs = [jnp.zeros((1, devices), jnp.float32) for _ in range(per)]
        owner = iota((devices, devices), 1)
        for k in range(6):
            label = rows[:, 8 * k + 4 : 8 * k + 5].astype(jnp.int32)
            at = 8 * (k // 3) + k % 3
            value = rows[:, at : at + 1]
            hits.append(spot == label)
            for q in range(per):
                chosen = jnp.where(owner * per + q == label, value, 0.0)
                rhs[q] = rhs[q] + jnp.sum(chosen, axis=0, keepdims=True)
        inverse = gathered[pl.ds(1, devices, stride=2), :]
        coarse = None
        for q in range(per):
            term = jnp.dot(
                rhs[q], inverse[:, q * count : q * count + count], precision=EXACT,
                preferred_element_type=jnp.float32,
            )
            coarse = term if coarse is None else coarse + term
        columns = [jnp.sum(jnp.where(hit, coarse, 0.0), axis=1, keepdims=True) for hit in hits]
        kept = jnp.zeros((devices, LANES), jnp.float32)
        for k in range(6):
            kept = jnp.where(iota((devices, LANES), 1) == k, columns[k], kept)
        values[...] = kept
    else:
        columns = [given[:, k : k + 1] for k in range(6)]
        values[...] = given[...]
    one, two = tables[0, 6:7, :], tables[1, 6:7, :]
    for k in range(6):
        one = one + columns[k] * tables[0, k : k + 1, :]
        two = two + columns[k] * tables[1, k : k + 1, :]
    product = jnp.sum(rows * one * two, axis=0, keepdims=True)
    numerator = jnp.sum(product * tables[2, 0:1, :], axis=1, keepdims=True)
    denominator = jnp.sum(product * tables[2, 1:2, :], axis=1, keepdims=True)
    alpha = numerator / denominator

    gx, gz = lax.axis_index("gx"), lax.axis_index("gz")
    before_x = lax.rem(gx + devices // spans - 1, devices // spans)
    before_z = lax.rem(gz + spans - 1, spans)
    here = values[pl.ds(gx * spans + gz, 1), :]
    behind = values[pl.ds(gx * spans + before_z, 1), :]
    aside = values[pl.ds(before_x * spans + gz, 1), :]
    corner = values[pl.ds(before_x * spans + before_z, 1), :]

    def four(line, back, a):
        return [back[:, 3 * a + 1 : 3 * a + 2]] + [line[:, 3 * a + b : 3 * a + b + 1] for b in range(3)]

    def mix(numbers, ref):
        total = numbers[0] * ref[0]
        for b in range(1, 4):
            total = total + numbers[b] * ref[b]
        return total

    near, right, left = four(here, behind, 0), four(here, behind, 1), four(aside, corner, 0)
    whole = [mix(near, pieces.at[0, k]) for k in range(2)]
    low = [mix(near, pieces.at[1, k]) for k in range(2)]
    high = [mix(right, pieces.at[1, k]) for k in range(2)]

    def stiff(line, i):
        return lines[line, i : i + 1, :]

    extra = [stiff(0, i) * whole[0] + WEIGHTS[i] * whole[1] for i in range(8)]
    for i in range(8):
        extra.append(
            stiff(1, i) * low[0] + stiff(2, i) * high[0] + WEIGHTS[i] * (LOW[i] * low[1] + HIGH[i] * high[1])
        )
    extra = join_middle(extra)
    geo = Geometry(WIDE)

    def line(numbers, at):
        total = numbers[0] * waves[at : at + 1, :]
        for b in range(1, 4):
            total = total + numbers[b] * waves[at + b : at + b + 1, :]
        return total

    def wide_stiff(k, i):
        return jnp.concatenate([stiff(k, i)] * (WIDE // LANES), axis=1)

    def beyond(side, stiff_x, plain, turned):
        fx, fy, fz = (split(face_factors[side, c]) for c in range(3))
        value = fx * geo.keep * stiff_x[None]
        value = value + WEIGHTS[0] * (fy * split(stiff_keep[...]) * plain[None] + fz * geo.keep * turned[None])
        return solid(geo.assemble_own(value))

    wave_near, wave_right = line(near, 0), line(right, 0)
    across = wide_stiff(1, 7) * line(left, 0) + wide_stiff(2, 7) * wave_near
    extra[0] = extra[0] + beyond(0, across, wave_near, line(near, 4))
    extra[15] = extra[15] + beyond(1, wide_stiff(0, 0) * wave_right, wave_right, line(right, 4))
    keep = solid(own(geo.keep))
    line_near, line_right = wave_near[:, :LANES], wave_right[:, :LANES]
    for x in range(ROWS):
        begin = start_faces[x // 15] if x in (0, 15) else start[x]
        mine = local[x, :, :LANES]
        new_residual[x] = residual[x] - alpha * (image[x] + extra[x])
        coarse_line = GROUP_X[0][x] * line_near
        if GROUP_X[1][x] != 0.0:
            coarse_line = coarse_line + GROUP_X[1][x] * line_right
        new_solution[x] = begin + alpha * (mine + keep * coarse_line)


VMEM = pl.BlockSpec(memory_space=pltpu.VMEM)
SMEM = pl.BlockSpec(memory_space=pltpu.SMEM)
FAR = pl.BlockSpec(memory_space=pltpu.HBM)


def call(kernel, shapes, specs, name, scratch=(), cost=None):
    def leaf(shape):
        kind = jnp.float32
        if shape[0] == "half":
            shape, kind = shape[1:], jnp.bfloat16
        return jax.ShapeDtypeStruct(shape, kind)

    return pl.pallas_call(
        kernel,
        out_shape=[leaf(shape) for shape in shapes],
        in_specs=specs,
        out_specs=[VMEM] * len(shapes),
        scratch_shapes=list(scratch),
        compiler_params=pltpu.CompilerParams(vmem_limit_bytes=16 * 1024 * 1024),
        name=name,
        cost_estimate=cost,
    )


def swap(first, second, axis):
    size = lax.axis_size(axis)
    odd = [(i, (i + 1) % size) for i in range(1, size, 2)]
    one = lax.ppermute(first, axis, [(i, i ^ 1) for i in range(size)])
    two = lax.ppermute(second, axis, odd + [(b, a) for a, b in odd])
    return one, two


def second_neighbours(common, axis):
    size = lax.axis_size(axis)
    if size == 4:
        return lax.ppermute(common, axis, [(i, i ^ 2) for i in range(size)])
    left = lax.ppermute(common[:FIRST_ROWS], axis, [(i, (i - 2) % size) for i in range(size)])
    right = lax.ppermute(common[FIRST_ROWS:], axis, [(i, (i + 2) % size) for i in range(size)])
    return jnp.concatenate([left, right], axis=0)


def body(
    source, previous, coefficients, stiffness, fdm_vectors, fdm_values, coarse_inverse, vertex_map
):
    assert source.shape == (ROWS, ROWS, LANES)
    spans = lax.axis_size("gz")
    devices = lax.axis_size("gx") * spans
    per, count = coarse_inverse.shape
    small = per * count <= LANES
    block, wide, face = (ROWS, ROWS, LANES), (ROWS, ROWS, WIDE), (ROWS, LANES)
    halo = (11, 8, LANES)

    coarse = coarse_inverse if small else coarse_inverse[:, :LANES]
    operands = (source, previous, coefficients, fdm_values.reshape(1, 8), coarse)
    first, second, elements, source, previous, eigen, coarse = call(
        pack_kernel,
        [halo, halo, face, block, block, (1, 8), coarse.shape],
        [FAR] * 5,
        "pack",
        [pltpu.VMEM(coefficients.shape, jnp.float32), pltpu.SemaphoreType.DMA((5,))],
    )(*(pltpu.with_memory_space_constraint(v, pltpu.HBM) for v in operands))
    first, second = swap(first, second, "gz")
    upper, lower, diagonals, stiff, vectors, bend, lam, lines, fixed, tables = call(
        functools.partial(prepare_kernel, small),
        [
            ("half", 4, WIDE, WIDE), ("half", 4, WIDE, LANES), (3, 8, 8, LANES),
            (64, LANES), (64, LANES), (16, LANES), (2, 8, LANES), (3, 8, LANES), (24, LANES), (3, 8, LANES),
        ],
        [VMEM] * 7,
        "prepare",
    )(elements, stiffness, fdm_vectors, eigen, vertex_map, coarse, jnp.asarray(lane_tables()))

    message = (FIRST_ROWS + FAR_ROWS + SECOND_ROWS, LANES)
    start, remainder, factors, pair_factors, halves, common, part, metrics = call(
        start_kernel,
        [
            block, wide, (3, 2, ROWS, WIDE), (3, ROWS, BOTH), (2, ROWS, WIDE), (2 * FIRST_ROWS + 16, LANES),
            (2, FIRST_ROWS + FAR_ROWS, LANES), (16, WIDE),
        ],
        [VMEM] * 9,
        "start",
    )(source, previous, elements, first, second, stiff, upper, lower, diagonals)
    beyond = second_neighbours(common, "gx")
    known, spectrum, inverse, side_a, side_b = call(
        guess_kernel, [block, (8, ROWS, BOTH), (8, ROWS, BOTH), message, message], [VMEM] * 10, "guess",
        cost=pl.CostEstimate(flops=4000000000, bytes_accessed=4000000, transcendentals=0),
    )(remainder, metrics, part, stiff, vectors, bend, lam, upper, lower, diagonals)
    side_a, side_b = swap(side_a, side_b, "gx")
    pieces, waves, stiff_keep = call(
        ready_kernel, [(2, 2, 4, ROWS, LANES), (8, WIDE), (ROWS, WIDE)], [VMEM] * 5, "ready"
    )(factors, stiff, lines, upper, lower)

    shapes = [face, (2, ROWS, LANES), (2, ROWS, WIDE), (2, ROWS, WIDE), (3, ROWS, WIDE)]
    one = call(functools.partial(side_kernel, True), shapes, [VMEM] * 12, "side")(
        halves, remainder, factors, side_a, beyond, stiff, vectors, bend, lam, upper, lower, diagonals
    )
    start_faces, residual, local, face_factors, image, payload = call(
        middle_kernel,
        [(2, ROWS, LANES), block, wide, (2, 3, ROWS, WIDE), block, (2 * devices, LANES)],
        [VMEM] * 24,
        "middle",
        [pltpu.VMEM(shape, jnp.float32) for shape in [(2, ROWS, WIDE), (8, LANES)] + shapes],
    )(
        known, pair_factors, spectrum, inverse, waves, stiff, vectors, bend, upper, lower, diagonals, fixed, lines,
        halves, remainder, factors, side_b, beyond, lam, *one,
    )
    gathered = lax.all_to_all(payload.reshape(devices, 2, LANES), ("gx", "gz"), 0, 0)
    gathered = gathered.reshape(2 * devices, LANES)

    operands = [
        start, start_faces, residual, local, image, pieces, face_factors, waves, stiff_keep, lines,
        tables, gathered,
    ]
    finish = functools.partial(final_kernel, devices, spans, count, per)
    if small:

        def kernel(*refs):
            finish(*refs[:12], None, *refs[12:])

    else:
        kernel = finish
        rows = gathered[0::2]
        labels = rows[:, jnp.array([8 * k + 4 for k in range(6)])].astype(jnp.int32)
        parts = rows[:, jnp.array([8 * (k // 3) + k % 3 for k in range(6)])]
        rhs = jnp.zeros((count,), jnp.float32).at[labels.reshape(-1)].add(parts.reshape(-1))
        mine = jnp.dot(coarse_inverse, rhs, precision=EXACT)
        coarse = lax.all_gather(mine, ("gx", "gz"), axis=0, tiled=True)
        operands.append(jnp.pad(coarse[labels], ((0, 0), (0, LANES - 6))))
    scratch = [pltpu.VMEM((devices, LANES), jnp.float32), pltpu.VMEM((2 * devices + 8, LANES), jnp.float32)]
    return tuple(
        call(kernel, [block, block], [VMEM] * len(operands), "finish", scratch)(
            *operands
        )
    )


def solution(mesh):
    placed = (
        P("gx", None, "gz"),
        P("gx", None, "gz"),
        P(None, "gx", None, "gz"),
        P(),
        P(),
        P(),
        P(("gx", "gz"), None),
        P(None, "gx", None, "gz"),
    )
    return jax.shard_map(
        body,
        mesh=mesh,
        in_specs=placed,
        out_specs=(P("gx", None, "gz"), P("gx", None, "gz")),
        check_vma=False,
    )
```

```python
import functools

import jax
import jax.numpy as jnp
import numpy as np
from jax import lax
from jax.experimental import pallas as pl
from jax.experimental.pallas import tpu as pltpu
from jax.sharding import PartitionSpec as P

POINTS = [
    -1.0,
    -0.8717401485096066,
    -0.5917001814331423,
    -0.2092992179024789,
    0.2092992179024789,
    0.5917001814331423,
    0.8717401485096066,
    1.0,
]
WEIGHTS = [
    0.03571428571428571,
    0.21070422714350603,
    0.34112269248350435,
    0.4124587946587038,
    0.4124587946587038,
    0.34112269248350435,
    0.21070422714350603,
    0.03571428571428571,
]
ONES = [1.0] * 8
LOW = [(1.0 - s) / 2.0 for s in POINTS]
HIGH = [(1.0 + s) / 2.0 for s in POINTS]
EXACT = lax.Precision.HIGHEST

ROWS = 16
LANES = 128
WIDE = 256
BOTH = 384
HALO = 32
ELEMENTS = 22
CORNERS = (58, 80)
SPARE = (84, 100)
DEEP, SHALLOW = 25, 17
SLOT = DEEP + SHALLOW
FIRST_FIELDS = ((0, 24), (41, 17))
SECOND_FIELDS = ((0, 16), (32, 16), (64, 16), (96, 16))
FAR_FIELDS = ((0, 24), (48, 24))
FIRST_ROWS, FAR_ROWS, SECOND_ROWS = 48, 24, 40
PAIRS = ((0, 0), (0, 1), (1, 1))
GROUP_X = (ONES + LOW, [0.0] * 8 + HIGH)
INVERSE_X = [0.5] + [1.0] * 6 + [0.5] + [0.5] + [1.0] * 6 + [0.5]


def iota(shape, dim):
    return lax.broadcasted_iota(jnp.int32, shape, dim)


def pick(index, values):
    result = jnp.full(index.shape, values[0], jnp.float32)
    for i in range(1, 8):
        result = jnp.where(index == i, values[i], result)
    return result


def even_index(axis):
    return lax.rem(lax.axis_index(axis), 2) == 0


class Geometry:
    def __init__(self, lanes):
        shape = (2, 8, lanes)
        self.element_y, self.row, lane = iota(shape, 0), iota(shape, 1), iota(shape, 2)
        self.position = lane & 7
        self.first = self.position == 0
        self.last = self.position == 7
        self.edge = self.first | self.last
        self.weight_y = pick(self.row, WEIGHTS)
        self.weight_z = pick(self.position, WEIGHTS)
        self.inverse_z = jnp.where(self.edge, 0.5, 1.0)
        self.wall = (self.element_y == 1) & (self.row == 7)
        inner = ((self.element_y == 0) & (self.row == 7)) | ((self.element_y == 1) & (self.row == 0))
        self.inverse_y = jnp.where(inner, 0.5, 1.0)
        self.keep = jnp.where(self.wall, 0.0, 1.0)
        self.lanes = lanes

    def pair_y(self, v):
        lower, upper = v[0], v[1]
        row = self.row[0]
        up = jnp.where(row == 7, pltpu.roll(upper, 7, 0), 0.0)
        down = jnp.where(row == 0, pltpu.roll(lower, 1, 0), 0.0)
        return jnp.stack([lower + up, upper + down])

    def pair_z(self, v):
        flat = v.reshape(16, self.lanes)
        after = pltpu.roll(flat, self.lanes - 1, 1).reshape(v.shape)
        before = pltpu.roll(flat, 1, 1).reshape(v.shape)
        return v + jnp.where(self.edge, jnp.where(self.last, after, before), 0.0)

    def pair(self, v):
        return self.pair_z(self.pair_y(v))

    def assemble(self, v):
        return self.pair(v) * self.keep

    def assemble_own(self, v):
        v = self.pair_y(v)
        mine, halo = v[:, :, :LANES], v[:, :, LANES:]
        lane = iota((1, 1, LANES), 2)
        edge, last, keep = (mask[:, :, :LANES] for mask in (self.edge, self.last, self.keep))

        def turned(mixed, lanes):
            return pltpu.roll(mixed.reshape(16, LANES), lanes, 1).reshape(2, 8, LANES)

        after = turned(jnp.where(lane == 0, halo, mine), LANES - 1)
        before = turned(jnp.where(lane == LANES - 1, halo, mine), 1)
        return (mine + jnp.where(edge, jnp.where(last, after, before), 0.0)) * keep


def solid(v):
    return v.reshape(ROWS, v.shape[-1])


def split(v):
    return v.reshape(2, 8, v.shape[-1])


def own(v):
    return v[..., :LANES]


def down(v):
    return jnp.sum(v.reshape(ROWS, LANES), axis=0, keepdims=True)


def line_of(ref, at, lanes):
    row = ref[at : at + 1, :]
    return jnp.concatenate([row] * (lanes // LANES), axis=1)[None]


def weighted(factors, rows):
    total = None
    for factor, row in zip(factors, rows):
        total = factor * row if total is None else total + factor * row
    return total


def divisors_of(c, lam):
    lanes = c[0].shape[-1]
    lam_y = jnp.concatenate([lam[0]] * (lanes // LANES), axis=1)[None]
    lam_z = jnp.concatenate([lam[1]] * (lanes // LANES), axis=1)[None]
    base = c[1] * lam_y + c[2] * lam_z
    return [1.0 / (c[0] * line_of(lam.at[0], i, lanes) + base) for i in range(8)]


def halo_lanes():
    lane = iota((1, 1, LANES), 2)
    return (lane < HALO) | (lane >= LANES - HALO)


def join_pair(low, high):
    other = pltpu.roll(solid(high[:, :, LANES:]), LANES // 2, 1).reshape(2, 8, LANES)
    return jnp.concatenate([own(low), own(high), jnp.where(halo_lanes(), low[:, :, LANES:], other)], axis=2)


def part_pair(v):
    last = v[:, :, WIDE:]
    other = pltpu.roll(solid(last), LANES // 2, 1).reshape(2, 8, LANES)
    return jnp.concatenate([own(v), last], axis=2), jnp.concatenate([v[:, :, LANES:WIDE], other], axis=2)


def join_pairs(rows):
    return [join_pair(rows[x], rows[x + 8]) for x in range(8)]


def part_pairs(pairs):
    parted = [part_pair(v) for v in pairs]
    return [v[0] for v in parted] + [v[1] for v in parted]


def pair_line(ref, low, high):
    one, two = ref[low : low + 1, :], ref[high : high + 1, :]
    mixed = jnp.where(halo_lanes()[0], one, two)
    return jnp.concatenate([one, two, mixed], axis=1)[None]


def contract_x(rows, table, i, transpose=False):
    total = None
    for p in range(8):
        factor = line_of(table, p * 8 + i if transpose else i * 8 + p, rows[p].shape[-1])
        term = factor * rows[p]
        total = term if total is None else total + term
    return total


def contract_y(v, diagonals):
    def moved(value, rows):
        return jnp.stack([pltpu.roll(value[e], 8 - rows, 0) for e in range(2)])

    shifted = [v] + [moved(v, d) for d in range(1, 4)]
    return weighted(diagonals[:4], shifted) + moved(weighted(diagonals[4:], shifted), 4)


def thirds(v):
    high = v.astype(jnp.bfloat16)
    rest = v - high.astype(jnp.float32)
    middle = rest.astype(jnp.bfloat16)
    return high, middle, (rest - middle.astype(jnp.float32)).astype(jnp.bfloat16)


def contract_z(flat, upper, lower, which, short=False):
    pieces = []
    for at in range(0, flat.shape[1], LANES):
        high, middle, low = thirds(flat[:, at : at + LANES])
        one = jnp.dot(
            jnp.concatenate([high, middle], axis=1), upper[which], preferred_element_type=jnp.float32
        )
        if short:
            pieces.append(one[:, :LANES] + one[:, LANES:])
            continue
        two = jnp.dot(jnp.concatenate([low, high], axis=1), lower[which], preferred_element_type=jnp.float32)
        pieces.append(one[:, :LANES] + (one[:, LANES:] + two))
    return pieces[0] if len(pieces) == 1 else jnp.concatenate(pieces, axis=1)


def wide_diagonals(ref, which, lanes=WIDE):
    return [jnp.concatenate([ref[which, d]] * (lanes // LANES), axis=1)[None] for d in range(8)]


def metric(ref, component, element):
    at = (component * 2 + element) * 2
    return jnp.stack([jnp.broadcast_to(ref[at + e : at + e + 1, :], (8, WIDE)) for e in range(2)])


def scaled_metrics(geo, c):
    return c[0] * geo.weight_y * geo.weight_z, c[1] * geo.weight_z, c[2] * geo.weight_y


def stored_factors(ref, element):
    return [split(ref[c, element]) for c in range(3)]


def apply_pairs(pairs, factors, stiffness, upper, lower, diagonals, short=False):
    factor_x, factor_y, factor_z = factors
    along_z = contract_z(jnp.concatenate([solid(v) for v in pairs], axis=0), upper, lower, 0, short)
    along_z = [split(along_z[x * 16 : x * 16 + 16]) for x in range(8)]
    result = []
    for i in range(8):
        terms = factor_y * contract_y(pairs[i], diagonals) + factor_z * along_z[i]
        result.append(factor_x * contract_x(pairs, stiffness, i) + WEIGHTS[i] * terms)
    return result, along_z


def join_middle(rows):
    middle = rows[7] + rows[8]
    return rows[:7] + [middle, middle] + rows[9:]


def fold(parts, fields):
    lane = iota((8, LANES), 1)
    result = parts[0]
    for part, (offset, half) in list(zip(parts, fields))[1:]:
        taken = ((lane - offset + half) & (LANES - 1)) < 2 * half
        result = jnp.where(taken, pltpu.roll(part, offset, 1), result)
    return result


def unfold(packed, field, fill=0.0):
    offset, half = field
    lane = iota((8, LANES), 1)
    moved = pltpu.roll(packed, LANES - offset, 1) if offset else packed
    return jnp.where(((lane + half) & (LANES - 1)) < 2 * half, moved, fill)


def widen(tile, pieces):
    return jnp.concatenate([tile, jnp.concatenate(pieces, axis=0)], axis=1)


def group_lanes(lanes, group):
    lane = iota((1, lanes), 1)
    signed = jnp.where(lane < lanes // 2 + lanes // 4, lane, lane - lanes) if lanes > LANES else lane
    element, position = signed >> 3, lane & 7
    low, high = pick(position, LOW), pick(position, HIGH)
    here = jnp.where((element >> 3) == group, low, 0.0)
    return here + jnp.where(((element + 1) >> 3) == group, high, 0.0)


def pack_kernel(
    source, previous, coefficients, eigen, coarse,
    first, second, elements, near_source, near_previous, near_eigen, near_coarse, raw, ready,
):
    copies = [
        pltpu.make_async_copy(coefficients, raw, ready.at[2]),
        pltpu.make_async_copy(eigen, near_eigen, ready.at[3]),
        pltpu.make_async_copy(coarse, near_coarse, ready.at[4]),
    ]
    for k in range(4):
        part = pl.ds(4 * k, 4)
        copies.append(pltpu.make_async_copy(source.at[part], near_source.at[part], ready.at[5 + k]))
        copies.append(pltpu.make_async_copy(previous.at[part], near_previous.at[part], ready.at[9 + k]))
    for copy in copies:
        copy.start()
    even = even_index("gz")
    elements[...] = jnp.zeros_like(elements)
    for copy in copies:
        copy.wait()
    for c in range(3):
        for element in range(2):
            at = (c * 2 + element) * 2
            elements[at : at + 2, 0:16] = raw[c, element]
    slot = iota((8, LANES), 1)
    for to_right, out in ((even, first), (jnp.logical_not(even), second)):
        for tile in range(11):
            packed = None
            for k in range(3):
                n = 3 * tile + k
                if n >= 2 * ROWS:
                    break
                for ref, width, at in ((near_previous, DEEP, SLOT * k), (near_source, SHALLOW, SLOT * k + DEEP)):
                    shift = jnp.where(to_right, (at + width) % LANES, at)
                    moved = pltpu.roll(ref[n // 2, 8 * (n % 2) : 8 * (n % 2) + 8], shift, 1)
                    packed = moved if packed is None else jnp.where(slot >= at, moved, packed)
            if tile == 10:
                for at, rows in zip(SPARE, (elements[:8], elements[8:])):
                    packed = jnp.where(slot >= at, pltpu.roll(rows, at, 1), packed)
            out[tile] = packed


def lanes_of(elements):
    lane = iota((24, WIDE), 1)
    beyond = lane - LANES
    right, left = LANES + 3 * 8, WIDE - 3 * 8
    index = jnp.where(lane < right, lane >> 3, jnp.where(lane >= left, 19 + ((beyond - (left - LANES)) >> 3), ELEMENTS))
    spread = (iota((24, WIDE), 0) == index).astype(jnp.bfloat16)
    high, middle, low = (jnp.dot(v, spread, preferred_element_type=jnp.float32) for v in thirds(elements[:, 0:24]))
    return high + (middle + low)


def elements_of(folded):
    lane = iota((8, LANES), 1)
    rest = jnp.where(lane == ELEMENTS, 1.0, 0.0)
    return jnp.concatenate(
        [jnp.where(lane < ELEMENTS, pltpu.roll(folded, LANES - at, 1), rest) for at in CORNERS], axis=0
    )


def prepare_kernel(
    with_coarse, elements, stiffness, vectors, eigen, labels, coarse, tables,
    upper, lower, diagonals, stiff_table, vector_table, bend, lam, lines, fixed, near_tables,
):
    near_tables[...] = tables[...]
    widen = (iota((16, LANES), 0) == (iota((16, LANES), 1) >> 3)).astype(jnp.float32)
    metrics = jnp.dot(elements[:, 0:16], widen, precision=EXACT, preferred_element_type=jnp.float32)
    repeat = (iota((LANES, 8), 0) & 7 == iota((LANES, 8), 1)).astype(jnp.float32)
    same = (iota((LANES, LANES), 0) >> 3) == (iota((LANES, LANES), 1) >> 3)
    unit = (iota((8, 8), 0) == iota((8, 8), 1)).astype(jnp.float32)
    row, column = iota((8, 8), 0), iota((8, 8), 1)

    def dot(a, b, dims):
        return lax.dot_general(a, b, (dims, ((), ())), precision=EXACT, preferred_element_type=jnp.float32)

    def put_block(at, matrix):
        half = dot(repeat, matrix, ((1,), (0,)))
        put_thirds(at, jnp.where(same, dot(half, repeat, ((1,), (1,))), 0.0))

    def put_thirds(at, block):
        high, middle, low = thirds(block)
        both = jnp.concatenate([high, middle], axis=1)
        upper[at] = jnp.concatenate([both, both], axis=0)
        lower[at] = jnp.concatenate([high, low], axis=0)

    def put_diagonals(at, matrix):
        turned = jnp.concatenate([matrix[4:], matrix[:4]], axis=0)
        for d in range(8):
            chosen = jnp.where(column == ((row + d % 4) & 7), matrix if d < 4 else turned, 0.0)
            diagonals[at, d] = jnp.broadcast_to(jnp.sum(chosen, axis=1, keepdims=True), (8, LANES))

    def put_table(out, matrix):
        tall = (iota((64, 8), 0) >> 3 == iota((64, 8), 1)).astype(jnp.float32)
        chosen = jnp.where(iota((64, 8), 0) & 7 == iota((64, 8), 1), dot(tall, matrix, ((1,), (0,))), 0.0)
        out[...] = jnp.broadcast_to(jnp.sum(chosen, axis=1, keepdims=True), (64, LANES))

    lane = iota((LANES, LANES), 1) & 7
    node = iota((LANES, LANES), 0)
    element, position = node >> 3, node & 7
    low, high = pick(position, LOW), pick(position, HIGH)
    columns = jnp.where(lane == (element >> 3), low, 0.0) + jnp.where(lane == ((element + 1) >> 3), high, 0.0)
    columns = jnp.where(lane == 3, 1.0, jnp.where(lane < 3, columns, 0.0))
    put_thirds(3, columns)
    k, s = stiffness[...], vectors[...]
    k_turned, s_turned = dot(k, unit, ((0,), (0,))), dot(s, unit, ((0,), (0,)))
    for at, matrix in enumerate((k_turned, s, s_turned)):
        put_block(at, matrix)
    for at, matrix in enumerate((k, s_turned, s)):
        put_diagonals(at, matrix)
    put_table(stiff_table, k)
    put_table(vector_table, s)
    for side, near in ((0, 0), (1, 7)):
        chosen = jnp.where(column == near, 0.0, s_turned * k[near : near + 1, :])
        total = jnp.sum(chosen, axis=1, keepdims=True)
        bend[8 * side : 8 * side + 8] = jnp.broadcast_to(total, (8, LANES))
    values = eigen[...]
    total = jnp.sum(jnp.where(row == column, values, 0.0), axis=1, keepdims=True)
    lam[0] = jnp.broadcast_to(total, (8, LANES))
    lam[1] = jnp.broadcast_to(dot(values, repeat, ((1,), (1,))), (8, LANES))
    stiff_lines = []
    for at, line in enumerate((ONES, LOW, HIGH)):
        total = jnp.sum(k * pick(column, line), axis=1, keepdims=True)
        stiff_lines.append(jnp.broadcast_to(total, (8, LANES)))
        lines[at] = stiff_lines[at]

    groups = [group_lanes(LANES, b) for b in range(3)]
    stacked = jnp.concatenate(groups + [jnp.zeros((13, LANES), jnp.float32)], axis=0)
    stiff_z = contract_z(stacked, upper, lower, 0)
    weight_z = pick(iota((1, LANES), 1) & 7, WEIGHTS)
    node = iota((8, LANES), 0)
    mass_y = [sum(WEIGHTS), sum(WEIGHTS[:7])]
    last = jnp.broadcast_to(k[:, 7:8], (8, LANES))
    inner = jnp.where(node == 7, 0.0, stiff_lines[0] - last)
    stiff_y = [jnp.sum(v, axis=0, keepdims=True) for v in (stiff_lines[0], inner)]
    at = 0
    for a, b in PAIRS:
        across, along = jnp.zeros((1, LANES), jnp.float32), jnp.zeros((1, LANES), jnp.float32)
        for element in range(2):
            fa = GROUP_X[a][element * 8 : element * 8 + 8]
            fb = GROUP_X[b][element * 8 : element * 8 + 8]
            if not (any(fa) and any(fb)):
                continue
            mass_x = sum(w * p * q for w, p, q in zip(WEIGHTS, fa, fb))
            applied = stiff_lines[0 if fb == ONES else 1 + b]
            stiff_x = jnp.sum(applied * pick(node, fa), axis=0, keepdims=True)
            for e in range(2):
                cx, cy, cz = (metrics[(c * 2 + element) * 2 + e].reshape(1, LANES) for c in range(3))
                across = across + cx * (stiff_x * mass_y[e]) + cy * (stiff_y[e] * mass_x)
                along = along + cz * (mass_x * mass_y[e])
        across = across * weight_z
        for b in range(3):
            fixed[at : at + 1] = across * groups[b] + along * stiff_z[b : b + 1]
            at += 1
    fixed[9:16] = jnp.zeros((7, LANES), jnp.float32)
    place = iota((1, LANES), 1)
    numbers = jnp.zeros((1, LANES), jnp.float32)
    for a in range(2):
        for b in range(3):
            corner, x, z = 4 * a + (b == 2), a, (0, 8, 15)[b]
            number = labels[corner, x][0:1, z : z + 1].astype(jnp.float32)
            numbers = jnp.where(place == 8 * (3 * a + b) + 4, number, numbers)
    fixed[16:17] = numbers
    below = jnp.zeros((1, LANES), jnp.float32)
    if with_coarse:
        per, count = coarse.shape
        below = [coarse[i : i + 1, :] for i in range(per)]
        if per * count < LANES:
            below.append(jnp.zeros((1, LANES - per * count), jnp.float32))
        below = jnp.concatenate(below, axis=1)
    fixed[17:18] = below
    fixed[18:24] = jnp.zeros((6, LANES), jnp.float32)


def start_kernel(
    source, previous, elements, first, second, stiffness, upper, lower, diagonals,
    start, remainder, factors, pair_factors, halves, common, part, metrics,
):
    even = even_index("gz")
    lane = iota((8, LANES), 1)
    one, two = first[...], second[...]
    from_right, from_left = jnp.where(even, one, two), jnp.where(even, two, one)

    def beyond(n, at, width):
        at = at + SLOT * (n % 3)
        right, left = from_right[n // 3], from_left[n // 3]
        if at:
            right = pltpu.roll(right, LANES - at, 1)
        left = pltpu.roll(left, (LANES - width - at) % LANES, 1)
        return jnp.where(lane < width, right, jnp.where(lane >= LANES - width, left, 0.0))

    def wide(ref, x, at, width):
        return split(widen(ref[x], [beyond(2 * x + e, at, width) for e in range(2)]))

    geo = Geometry(WIDE)
    right, left = (
        jnp.concatenate([pltpu.roll(tiles[10], (LANES + to - at) % LANES, 1) for at in SPARE], axis=0)
        for tiles, to in ((from_right, 16), (from_left, 6))
    )
    place = iota((16, LANES), 1)
    compact = jnp.where(place < 16, elements[...], jnp.where(place < 19, right, jnp.where(place < ELEMENTS, left, 1.0)))
    metrics[...] = lanes_of(compact)
    factor = geo.keep * geo.inverse_y * geo.inverse_z
    rows = [geo.pair(wide(previous, x, 0, DEEP)) * (factor * INVERSE_X[x]) for x in range(ROWS)]
    rows = join_middle(rows)
    faces = (rows[0], rows[15])
    for x in range(ROWS):
        start[x] = solid(own(rows[x]))
    scaled = [scaled_metrics(geo, [metric(metrics, c, e) for c in range(3)]) for e in range(2)]
    joined = [join_pair(scaled[0][c], scaled[1][c]) for c in range(3)]
    for c in range(3):
        pair_factors[c] = solid(joined[c])
        for e in range(2):
            factors[c, e] = solid(scaled[e][c])
    applied, _ = apply_pairs(join_pairs(rows), joined, stiffness, upper, lower, wide_diagonals(diagonals, 0, BOTH))
    applied = part_pairs(applied)
    rest = [wide(source, x, DEEP, SHALLOW) - applied[x] for x in range(ROWS)]
    halves[0], halves[1] = solid(faces[0]), solid(faces[1])
    for x in range(ROWS):
        remainder[x] = solid(rest[x])
    messages, distant = [], []
    for side, x in ((0, 0), (1, 15)):
        half, value = solid(faces[side]), solid(rest[x])
        lower_fold = fold([half[:8, LANES:], value[:8, LANES:]], FIRST_FIELDS)
        upper_fold = fold([half[8:, LANES:], value[8:, LANES:]], FIRST_FIELDS)
        for at, rows in zip(CORNERS, (compact[:8], compact[8:])):
            upper_fold = jnp.where((lane >= at) & (lane < at + ELEMENTS), pltpu.roll(rows, at, 1), upper_fold)
        messages.append(jnp.concatenate([half[:, :LANES], value[:, :LANES], lower_fold, upper_fold], axis=0))
        folded = fold([half[:8, LANES:], half[8:, LANES:]], FAR_FIELDS)
        distant.append(jnp.concatenate([half[:, :LANES], folded], axis=0))
    common[: 2 * FIRST_ROWS] = jnp.concatenate(messages, axis=0)
    common[2 * FIRST_ROWS :] = jnp.zeros((16, LANES), jnp.float32)
    for side in range(2):
        part[side] = jnp.concatenate([messages[side], distant[1 - side]], axis=0)


def guess_kernel(
    remainder, metrics, part, stiffness, vectors, bend, lam, upper, lower, diagonals,
    known, spectrum, inverse, message_a, message_b,
):
    geo = Geometry(WIDE)
    rest = [split(remainder[x]) for x in range(ROWS)]
    rest = [geo.assemble(v) for v in join_middle(rest)]
    for x in range(ROWS):
        known[x] = solid(own(rest[x]))
    pairs = join_pairs(rest)
    forward = wide_diagonals(diagonals, 1, BOTH)
    moved = [solid(contract_y(contract_x(pairs, vectors, i, True), forward)) for i in range(8)]
    transformed = contract_z(jnp.concatenate(moved, axis=0), upper, lower, 1, True)
    divisors = divisors_of([join_pair(metric(metrics, c, 0), metric(metrics, c, 1)) for c in range(3)], lam)
    damped = []
    for i in range(8):
        value = split(transformed[i * 16 : i * 16 + 16])
        spectrum[i], inverse[i] = solid(value), solid(divisors[i])
        damped.append(value * divisors[i])
    ends = [part_pair(contract_x(damped, vectors, near)) for near in (0, 7)]
    messages = []
    for side, near in ((0, 0), (1, 7)):
        value = ends[side][side]
        beside = part_pair(weighted([line_of(bend, side * 8 + i, BOTH) for i in range(8)], damped))[side]
        beside = beside + line_of(stiffness, near * 8 + 7 - near, WIDE) * ends[side][1 - side]
        value, beside = solid(value), solid(beside)
        folded = fold([v[at : at + 8, LANES:] for v in (value, beside) for at in (0, 8)], SECOND_FIELDS)
        messages.append(jnp.concatenate([value[:, :LANES], beside[:, :LANES], folded], axis=0))
    even_x = even_index("gx")
    both = [jnp.concatenate([part[side], messages[side]], axis=0) for side in range(2)]
    message_a[...] = jnp.where(even_x, both[1], both[0])
    message_b[...] = jnp.where(even_x, both[0], both[1])


def read_first(message):
    lower_fold, upper_fold = message[32:40], message[40:48]
    half, value = (
        widen(message[16 * k : 16 * k + 16], [unfold(lower_fold, FIRST_FIELDS[k]), unfold(upper_fold, FIRST_FIELDS[k])])
        for k in range(2)
    )
    return split(half), split(value)


def read_far(message):
    far = message[FIRST_ROWS : FIRST_ROWS + FAR_ROWS]
    return split(widen(far[0:16], [unfold(far[16:24], field) for field in FAR_FIELDS]))


def read_second(message):
    pieces = [unfold(message[32:40], field) for field in SECOND_FIELDS]
    return widen(message[0:16], pieces[:2]), widen(message[16:32], pieces[2:])


def coarse_pieces(geo, factors, stiff_keep, functions, stiff_functions):
    factor_x, factor_y, factor_z = factors
    kept_x, kept_y, kept_z = factor_x * geo.keep, factor_y * stiff_keep, factor_z * geo.keep
    result = []
    for plain, turned in zip(functions, stiff_functions):
        result.append(
            (geo.assemble(kept_x * plain[None]), geo.assemble(kept_y * plain[None] + kept_z * turned[None]))
        )
    return result


def wide_functions(upper, lower):
    functions = [group_lanes(WIDE, b) for b in (-1, 0, 1, 2)]
    stacked = jnp.concatenate(functions + [jnp.zeros((12, WIDE), jnp.float32)], axis=0)
    turned = contract_z(stacked, upper, lower, 0)
    return functions, [turned[b : b + 1] for b in range(4)]


def kept_stiffness(geo, lines, stiffness):
    row = iota((8, LANES), 0)
    last = jnp.zeros((8, LANES), jnp.float32)
    for j in range(8):
        last = jnp.where(row == j, stiffness[j * 8 + 7 : j * 8 + 8, :], last)
    both = jnp.stack([lines[0], lines[0] - last])
    return jnp.concatenate([both] * (WIDE // LANES), axis=2)


def ready_kernel(factors, stiffness, lines, upper, lower, pieces, waves, stiff_keep):
    geo = Geometry(WIDE)
    functions, turned = wide_functions(upper, lower)
    for b in range(4):
        waves[b : b + 1], waves[4 + b : 5 + b] = functions[b], turned[b]
    along_y = kept_stiffness(geo, lines, stiffness)
    stiff_keep[...] = solid(along_y)
    for element in range(2):
        made = coarse_pieces(geo, stored_factors(factors, element), along_y, functions, turned)
        for b in range(4):
            for k in range(2):
                pieces[element, k, b] = solid(own(made[b][k]))


def side_kernel(
    first, halves, remainder, factors, got, beyond, stiffness, vectors, bend, lam, upper, lower, diagonals,
    start_face, additions, fields, answers, near_factors,
):
    right = even_index("gx") if first else jnp.logical_not(even_index("gx"))
    side = jnp.where(right, 1, 0)
    other = 1 - side
    geo = Geometry(WIDE)
    message = got[...]
    near_half, near_value = read_first(message)
    far_half = read_far(message)
    block = beyond[pl.ds(pl.multiple_of(FIRST_ROWS * other, 8), FIRST_ROWS), :]
    last_half, last_value = read_first(block)
    spread = lanes_of(jnp.concatenate([elements_of(message[40:48]), elements_of(block[40:48])], axis=0))

    def metrics_of(device, of_right, of_left):
        rows = spread[16 * device : 16 * device + 16]
        return [jnp.where(right, metric(rows, c, of_right), metric(rows, c, of_left)) for c in range(3)]

    def row_of(ref, at):
        row = ref[pl.ds(at, 1), :]
        return jnp.concatenate([row] * (WIDE // LANES), axis=1)[None]

    near, far, last = metrics_of(0, 0, 1), metrics_of(0, 1, 0), metrics_of(1, 0, 1)
    near_scaled, far_scaled, last_scaled = (scaled_metrics(geo, c) for c in (near, far, last))
    mine = [split(factors[c, side]) for c in range(3)]
    for c in range(3):
        near_factors[c] = solid(near_scaled[c])
    half, value = split(halves[side]), split(remainder[15 * side])
    start_face[...] = solid(own(half + near_half))
    stiff = wide_diagonals(diagonals, 0)
    parts = [half, near_half, far_half, last_half]
    along_z = contract_z(jnp.concatenate([solid(v) for v in parts], axis=0), upper, lower, 0)
    here, there = row_of(stiffness, 63 * side), row_of(stiffness, 63 * other)

    def face_row(c, corner, k):
        term = c[1] * contract_y(parts[k], stiff) + c[2] * split(along_z[k * 16 : k * 16 + 16])
        return corner * (c[0] * parts[k]) + WEIGHTS[0] * term

    taken = face_row(mine, here, 1) + face_row(near_scaled, there, 0)
    taken_far = face_row(far_scaled, here, 3) + face_row(last_scaled, there, 2)
    made = [
        geo.assemble(v)
        for v in (
            near_value - taken, mine[0] * near_half, value - taken, near_scaled[0] * half,
            last_value - taken_far, far_scaled[0] * last_half,
        )
    ]
    for k in range(2):
        additions[k] = solid(own(made[k]))
    forward = wide_diagonals(diagonals, 1)
    flat = jnp.concatenate([solid(contract_y(v, forward)) for v in made], axis=0)
    flat = contract_z(flat, upper, lower, 1, True)
    fields[0], fields[1] = flat[0:16], flat[16:32]
    near_total, near_field, far_total, far_field = (split(flat[k * 16 : k * 16 + 16]) for k in range(2, 6))

    cross = line_of(stiffness, 7, WIDE)
    ends = [[row_of(vectors, 56 * at + i) for i in range(8)] for at in (other, side)]
    bends = [[row_of(bend, 8 * at + i) for i in range(8)] for at in (other, side)]
    result, partial = (split(v) for v in read_second(message[FIRST_ROWS + FAR_ROWS :]))
    crossed, divisors = cross * far_field, divisors_of(near, lam)
    close = [
        (ends[0][i] * near_total - bends[0][i] * near_field - ends[1][i] * crossed) * divisors[i] for i in range(8)
    ]
    crossed, divisors = cross * near_field, divisors_of(far, lam)
    distant = [
        (ends[1][i] * far_total - bends[1][i] * far_field - ends[0][i] * crossed) * divisors[i] for i in range(8)
    ]
    result = result + weighted(ends[0], close)
    partial = partial + weighted(bends[0], close) + cross * weighted(ends[0], distant)
    answers[0], answers[1] = solid(result), solid(partial)


def solve_kernel(
    known, spectrum, inverse, sides, stiffness, vectors, bend, upper, lower, diagonals,
    start_faces, residual, local, beside, face_factors, sums,
):
    even = even_index("gx")
    geo = Geometry(WIDE)

    def both(which, *at):
        one, two = sides[0][which][at], sides[1][which][at]
        return jnp.where(even, two, one), jnp.where(even, one, two)

    start_faces[0], start_faces[1] = both(0)
    for c in range(3):
        face_factors[0, c], face_factors[1, c] = both(4, c)
    totals, moved = both(1, 0), both(1, 1)

    rows = [split(known[x]) for x in range(ROWS)]
    rows[0], rows[15] = rows[0] + split(totals[0]), rows[15] + split(totals[1])
    for side, face in ((0, 0), (1, 7)):
        for i in range(8):
            if i != face:
                change = line_of(stiffness, i * 8 + face, LANES) * split(moved[side])
                x = side * 8 + i
                rows[x] = rows[x] - change
                if x in (7, 8):
                    rows[15 - x] = rows[15 - x] - change
    parts = [None, None]
    for x in range(ROWS):
        residual[x] = solid(rows[x])
        for a in range(2):
            if GROUP_X[a][x] * INVERSE_X[x] != 0.0:
                term = (GROUP_X[a][x] * INVERSE_X[x]) * rows[x]
                parts[a] = term if parts[a] is None else parts[a] + term
    weight = own(geo.inverse_y * geo.inverse_z)
    for a in range(2):
        sums[a : a + 1] = down(parts[a] * weight)

    backward = wide_diagonals(diagonals, 2)
    totals, moved = [split(v) for v in both(2, 0)], [split(v) for v in both(2, 1)]

    total, close = join_pair(*totals), join_pair(*moved)
    crossed = line_of(stiffness, 7, BOTH) * join_pair(moved[1], moved[0])
    ready = []
    for i in range(8):
        change = pair_line(vectors, i, 56 + i) * total - pair_line(bend, i, 8 + i) * close
        change = change - pair_line(vectors, 56 + i, i) * crossed
        ready.append(solid((split(spectrum[i]) + change) * split(inverse[i])))
    answers = [both(3, k) for k in range(2)]
    answers = jnp.concatenate([answers[k][side] for side in range(2) for k in range(2)], axis=0)
    back = contract_z(jnp.concatenate(ready, axis=0), upper, lower, 2, True)
    answers = contract_z(answers, upper, lower, 2, True)
    wide_backward = wide_diagonals(diagonals, 2, BOTH)
    back = [contract_y(split(back[k * 16 : k * 16 + 16]), wide_backward) for k in range(8)]
    answers = [contract_y(split(answers[k * 16 : k * 16 + 16]), backward) for k in range(4)]
    solved = part_pairs([contract_x(back, vectors, i) for i in range(8)])
    total = None
    for x in range(ROWS):
        term = own(solved[x]) * rows[x]
        total = term if total is None else total + term
    sums[2:3] = down(total)
    sums[3:8] = jnp.zeros((5, LANES), jnp.float32)
    solved = join_middle(solved)
    solved[0], solved[15] = solved[0] + answers[0], solved[15] + answers[2]
    for x in range(ROWS):
        local[x] = solid(geo.assemble(solved[x]))
    for side in range(2):
        beside[side] = solid(geo.assemble(answers[1 + 2 * side]))


def image_kernel(
    local, factors, face_factors, beside, sums, fixed, stiffness, lines, upper, lower, diagonals,
    image, payload,
):
    geo = Geometry(WIDE)
    rows = [split(local[x]) for x in range(ROWS)]
    stiff = wide_diagonals(diagonals, 0)
    applied, along_z = apply_pairs(
        join_pairs(rows), [split(factors[c]) for c in range(3)], stiffness, upper, lower,
        wide_diagonals(diagonals, 0, BOTH), True,
    )
    applied = part_pairs(applied)
    along_z = (part_pair(along_z[0])[0], part_pair(along_z[7])[1])
    total, parts = None, [None, None]
    for x in range(ROWS):
        term = own(applied[x]) * own(rows[x])
        total = term if total is None else total + term
        for a in range(2):
            if GROUP_X[a][x] != 0.0:
                term = GROUP_X[a][x] * own(applied[x])
                parts[a] = term if parts[a] is None else parts[a] + term
    extra = [down(value * own(geo.keep)) for value in parts + [total]]
    for side, x, across in ((0, 0, 63), (1, 15, 0)):
        there = [split(face_factors[side, c]) for c in range(3)]
        other = there[0] * (split(beside[side]) + line_of(stiffness, across, WIDE) * rows[x])
        other = other + WEIGHTS[0] * (there[1] * contract_y(rows[x], stiff) + there[2] * along_z[side])
        applied[x] = applied[x] + other
    applied = join_middle(applied)
    for x in range(ROWS):
        image[x] = solid(geo.assemble_own(applied[x]))
    zero = jnp.zeros((1, LANES), jnp.float32)
    table = jnp.concatenate(
        [sums[0:2], extra[0], extra[1], fixed[0:9], sums[2:3], extra[2], zero], axis=0
    )
    reduced = contract_z(table, upper, lower, 3)
    mine = (iota((16, LANES), 1) >> 3) == iota((16, LANES), 0)
    row = jnp.sum(jnp.where(mine, reduced, 0.0), axis=0, keepdims=True) + fixed[16:17]
    block = jnp.concatenate([row, fixed[17:18]] * 4, axis=0)
    copies = payload.shape[0] // 8
    payload[...] = jnp.broadcast_to(block[None], (copies, 8, LANES)).reshape(copies * 8, LANES)


def middle_kernel(
    known, pair_factors, spectrum, inverse, _, stiffness, vectors, bend, upper, lower, diagonals, fixed, lines,
    halves, remainder, factors, got, beyond, lam, *refs
):
    one, refs = refs[:5], refs[5:]
    (start_faces, residual, local, face_factors, image, payload, beside, sums), two = refs[:8], refs[8:]
    side_kernel(
        False, halves, remainder, factors, got, beyond, stiffness, vectors, bend, lam, upper, lower, diagonals, *two
    )
    solve_kernel(
        known, spectrum, inverse, (one, two), stiffness, vectors, bend, upper, lower, diagonals,
        start_faces, residual, local, beside, face_factors, sums,
    )
    image_kernel(
        local, pair_factors, face_factors, beside, sums, fixed, stiffness, lines, upper, lower, diagonals, image, payload
    )


def lane_tables():
    one = np.zeros((8, LANES), np.float32)
    two = np.zeros((8, LANES), np.float32)
    top = np.zeros((8, LANES), np.float32)
    for a in range(2):
        for b in range(3):
            one[6, 8 * a + b], two[3 * a + b, 8 * a + b], top[0, 8 * a + b] = 1.0, 1.0, 1.0
            one[6, 8 * (2 + a) + b], two[3 * a + b, 8 * (2 + a) + b] = 2.0, 1.0
            top[1, 8 * (2 + a) + b] = 1.0
    for p, (a, other) in enumerate(PAIRS):
        for b in range(3):
            for c in range(3):
                at = 8 * (4 + 3 * p + b) + c
                one[3 * a + b, at] = 1.0 if a == other else 2.0
                two[3 * other + c, at] = 1.0
                top[1, at] = 1.0
    one[6, 8 * 13 + 3], two[6, 8 * 13 + 3], top[0, 8 * 13 + 3] = 1.0, 1.0, 1.0
    one[6, 8 * 14 + 3], two[6, 8 * 14 + 3], top[1, 8 * 14 + 3] = 1.0, 1.0, 1.0
    return np.stack([one, two, top])


def final_kernel(
    devices, spans, count, per,
    start, start_faces, residual, local, image, pieces, face_factors, waves, stiff_keep, lines, tables,
    arrived, given, new_solution, new_residual, values, gathered,
):
    gathered[: 2 * devices] = arrived[...]
    rows = gathered[pl.ds(0, devices, stride=2), :]
    if given is None:
        spot = iota((devices, count), 1)
        hits = []
        rhs = [jnp.zeros((1, devices), jnp.float32) for _ in range(per)]
        owner = iota((devices, devices), 1)
        for k in range(6):
            label = rows[:, 8 * k + 4 : 8 * k + 5].astype(jnp.int32)
            at = 8 * (k // 3) + k % 3
            value = rows[:, at : at + 1]
            hits.append(spot == label)
            for q in range(per):
                chosen = jnp.where(owner * per + q == label, value, 0.0)
                rhs[q] = rhs[q] + jnp.sum(chosen, axis=0, keepdims=True)
        inverse = gathered[pl.ds(1, devices, stride=2), :]
        coarse = None
        for q in range(per):
            term = jnp.dot(
                rhs[q], inverse[:, q * count : q * count + count], precision=EXACT,
                preferred_element_type=jnp.float32,
            )
            coarse = term if coarse is None else coarse + term
        columns = [jnp.sum(jnp.where(hit, coarse, 0.0), axis=1, keepdims=True) for hit in hits]
        kept = jnp.zeros((devices, LANES), jnp.float32)
        for k in range(6):
            kept = jnp.where(iota((devices, LANES), 1) == k, columns[k], kept)
        values[...] = kept
    else:
        columns = [given[:, k : k + 1] for k in range(6)]
        values[...] = given[...]
    one, two = tables[0, 6:7, :], tables[1, 6:7, :]
    for k in range(6):
        one = one + columns[k] * tables[0, k : k + 1, :]
        two = two + columns[k] * tables[1, k : k + 1, :]
    product = jnp.sum(rows * one * two, axis=0, keepdims=True)
    numerator = jnp.sum(product * tables[2, 0:1, :], axis=1, keepdims=True)
    denominator = jnp.sum(product * tables[2, 1:2, :], axis=1, keepdims=True)
    alpha = numerator / denominator

    gx, gz = lax.axis_index("gx"), lax.axis_index("gz")
    before_x = lax.rem(gx + devices // spans - 1, devices // spans)
    before_z = lax.rem(gz + spans - 1, spans)
    here = values[pl.ds(gx * spans + gz, 1), :]
    behind = values[pl.ds(gx * spans + before_z, 1), :]
    aside = values[pl.ds(before_x * spans + gz, 1), :]
    corner = values[pl.ds(before_x * spans + before_z, 1), :]

    def four(line, back, a):
        return [back[:, 3 * a + 1 : 3 * a + 2]] + [line[:, 3 * a + b : 3 * a + b + 1] for b in range(3)]

    def mix(numbers, ref):
        total = numbers[0] * ref[0]
        for b in range(1, 4):
            total = total + numbers[b] * ref[b]
        return total

    near, right, left = four(here, behind, 0), four(here, behind, 1), four(aside, corner, 0)
    whole = [mix(near, pieces.at[0, k]) for k in range(2)]
    low = [mix(near, pieces.at[1, k]) for k in range(2)]
    high = [mix(right, pieces.at[1, k]) for k in range(2)]

    def stiff(line, i):
        return lines[line, i : i + 1, :]

    extra = [stiff(0, i) * whole[0] + WEIGHTS[i] * whole[1] for i in range(8)]
    for i in range(8):
        extra.append(
            stiff(1, i) * low[0] + stiff(2, i) * high[0] + WEIGHTS[i] * (LOW[i] * low[1] + HIGH[i] * high[1])
        )
    extra = join_middle(extra)
    geo = Geometry(WIDE)

    def line(numbers, at):
        total = numbers[0] * waves[at : at + 1, :]
        for b in range(1, 4):
            total = total + numbers[b] * waves[at + b : at + b + 1, :]
        return total

    def wide_stiff(k, i):
        return jnp.concatenate([stiff(k, i)] * (WIDE // LANES), axis=1)

    def beyond(side, stiff_x, plain, turned):
        fx, fy, fz = (split(face_factors[side, c]) for c in range(3))
        value = fx * geo.keep * stiff_x[None]
        value = value + WEIGHTS[0] * (fy * split(stiff_keep[...]) * plain[None] + fz * geo.keep * turned[None])
        return solid(geo.assemble_own(value))

    wave_near, wave_right = line(near, 0), line(right, 0)
    across = wide_stiff(1, 7) * line(left, 0) + wide_stiff(2, 7) * wave_near
    extra[0] = extra[0] + beyond(0, across, wave_near, line(near, 4))
    extra[15] = extra[15] + beyond(1, wide_stiff(0, 0) * wave_right, wave_right, line(right, 4))
    keep = solid(own(geo.keep))
    line_near, line_right = wave_near[:, :LANES], wave_right[:, :LANES]
    for x in range(ROWS):
        begin = start_faces[x // 15] if x in (0, 15) else start[x]
        mine = local[x, :, :LANES]
        new_residual[x] = residual[x] - alpha * (image[x] + extra[x])
        coarse_line = GROUP_X[0][x] * line_near
        if GROUP_X[1][x] != 0.0:
            coarse_line = coarse_line + GROUP_X[1][x] * line_right
        new_solution[x] = begin + alpha * (mine + keep * coarse_line)


VMEM = pl.BlockSpec(memory_space=pltpu.VMEM)
SMEM = pl.BlockSpec(memory_space=pltpu.SMEM)
FAR = pl.BlockSpec(memory_space=pltpu.HBM)


def call(kernel, shapes, specs, name, scratch=(), cost=None):
    def leaf(shape):
        kind = jnp.float32
        if shape[0] == "half":
            shape, kind = shape[1:], jnp.bfloat16
        return jax.ShapeDtypeStruct(shape, kind)

    return pl.pallas_call(
        kernel,
        out_shape=[leaf(shape) for shape in shapes],
        in_specs=specs,
        out_specs=[VMEM] * len(shapes),
        scratch_shapes=list(scratch),
        compiler_params=pltpu.CompilerParams(vmem_limit_bytes=16 * 1024 * 1024),
        name=name,
        cost_estimate=cost,
    )


def swap(first, second, axis):
    size = lax.axis_size(axis)
    odd = [(i, (i + 1) % size) for i in range(1, size, 2)]
    one = lax.ppermute(first, axis, [(i, i ^ 1) for i in range(size)])
    two = lax.ppermute(second, axis, odd + [(b, a) for a, b in odd])
    return one, two


def second_neighbours(common, axis):
    size = lax.axis_size(axis)
    if size == 4:
        return lax.ppermute(common, axis, [(i, i ^ 2) for i in range(size)])
    left = lax.ppermute(common[:FIRST_ROWS], axis, [(i, (i - 2) % size) for i in range(size)])
    right = lax.ppermute(common[FIRST_ROWS:], axis, [(i, (i + 2) % size) for i in range(size)])
    return jnp.concatenate([left, right], axis=0)


def body(
    source, previous, coefficients, stiffness, fdm_vectors, fdm_values, coarse_inverse, vertex_map
):
    assert source.shape == (ROWS, ROWS, LANES)
    spans = lax.axis_size("gz")
    devices = lax.axis_size("gx") * spans
    per, count = coarse_inverse.shape
    small = per * count <= LANES
    block, wide, face = (ROWS, ROWS, LANES), (ROWS, ROWS, WIDE), (ROWS, LANES)
    halo = (11, 8, LANES)

    coarse = coarse_inverse if small else coarse_inverse[:, :LANES]
    operands = (source, previous, coefficients, fdm_values.reshape(1, 8), coarse)
    first, second, elements, source, previous, eigen, coarse = call(
        pack_kernel,
        [halo, halo, face, block, block, (1, 8), coarse.shape],
        [FAR] * 5,
        "pack",
        [pltpu.VMEM(coefficients.shape, jnp.float32), pltpu.SemaphoreType.DMA((13,))],
    )(*(pltpu.with_memory_space_constraint(v, pltpu.HBM) for v in operands))
    first, second = swap(first, second, "gz")
    upper, lower, diagonals, stiff, vectors, bend, lam, lines, fixed, tables = call(
        functools.partial(prepare_kernel, small),
        [
            ("half", 4, WIDE, WIDE), ("half", 4, WIDE, LANES), (3, 8, 8, LANES),
            (64, LANES), (64, LANES), (16, LANES), (2, 8, LANES), (3, 8, LANES), (24, LANES), (3, 8, LANES),
        ],
        [VMEM] * 7,
        "prepare",
    )(elements, stiffness, fdm_vectors, eigen, vertex_map, coarse, jnp.asarray(lane_tables()))

    message = (FIRST_ROWS + FAR_ROWS + SECOND_ROWS, LANES)
    start, remainder, factors, pair_factors, halves, common, part, metrics = call(
        start_kernel,
        [
            block, wide, (3, 2, ROWS, WIDE), (3, ROWS, BOTH), (2, ROWS, WIDE), (2 * FIRST_ROWS + 16, LANES),
            (2, FIRST_ROWS + FAR_ROWS, LANES), (16, WIDE),
        ],
        [VMEM] * 9,
        "start",
    )(source, previous, elements, first, second, stiff, upper, lower, diagonals)
    beyond = second_neighbours(common, "gx")
    known, spectrum, inverse, side_a, side_b = call(
        guess_kernel, [block, (8, ROWS, BOTH), (8, ROWS, BOTH), message, message], [VMEM] * 10, "guess",
        cost=pl.CostEstimate(flops=4000000000, bytes_accessed=4000000, transcendentals=0),
    )(remainder, metrics, part, stiff, vectors, bend, lam, upper, lower, diagonals)
    side_a, side_b = swap(side_a, side_b, "gx")
    pieces, waves, stiff_keep = call(
        ready_kernel, [(2, 2, 4, ROWS, LANES), (8, WIDE), (ROWS, WIDE)], [VMEM] * 5, "ready"
    )(factors, stiff, lines, upper, lower)

    shapes = [face, (2, ROWS, LANES), (2, ROWS, WIDE), (2, ROWS, WIDE), (3, ROWS, WIDE)]
    one = call(functools.partial(side_kernel, True), shapes, [VMEM] * 12, "side")(
        halves, remainder, factors, side_a, beyond, stiff, vectors, bend, lam, upper, lower, diagonals
    )
    start_faces, residual, local, face_factors, image, payload = call(
        middle_kernel,
        [(2, ROWS, LANES), block, wide, (2, 3, ROWS, WIDE), block, (2 * devices, LANES)],
        [VMEM] * 24,
        "middle",
        [pltpu.VMEM(shape, jnp.float32) for shape in [(2, ROWS, WIDE), (8, LANES)] + shapes],
    )(
        known, pair_factors, spectrum, inverse, waves, stiff, vectors, bend, upper, lower, diagonals, fixed, lines,
        halves, remainder, factors, side_b, beyond, lam, *one,
    )
    gathered = lax.all_to_all(payload.reshape(devices, 2, LANES), ("gx", "gz"), 0, 0)
    gathered = gathered.reshape(2 * devices, LANES)

    operands = [
        start, start_faces, residual, local, image, pieces, face_factors, waves, stiff_keep, lines,
        tables, gathered,
    ]
    finish = functools.partial(final_kernel, devices, spans, count, per)
    if small:

        def kernel(*refs):
            finish(*refs[:12], None, *refs[12:])

    else:
        kernel = finish
        rows = gathered[0::2]
        labels = rows[:, jnp.array([8 * k + 4 for k in range(6)])].astype(jnp.int32)
        parts = rows[:, jnp.array([8 * (k // 3) + k % 3 for k in range(6)])]
        rhs = jnp.zeros((count,), jnp.float32).at[labels.reshape(-1)].add(parts.reshape(-1))
        mine = jnp.dot(coarse_inverse, rhs, precision=EXACT)
        coarse = lax.all_gather(mine, ("gx", "gz"), axis=0, tiled=True)
        operands.append(jnp.pad(coarse[labels], ((0, 0), (0, LANES - 6))))
    scratch = [pltpu.VMEM((devices, LANES), jnp.float32), pltpu.VMEM((2 * devices + 8, LANES), jnp.float32)]
    return tuple(
        call(kernel, [block, block], [VMEM] * len(operands), "finish", scratch)(
            *operands
        )
    )


def solution(mesh):
    placed = (
        P("gx", None, "gz"),
        P("gx", None, "gz"),
        P(None, "gx", None, "gz"),
        P(),
        P(),
        P(),
        P(("gx", "gz"), None),
        P(None, "gx", None, "gz"),
    )
    return jax.shard_map(
        body,
        mesh=mesh,
        in_specs=placed,
        out_specs=(P("gx", None, "gz"), P("gx", None, "gz")),
        check_vma=False,
    )
```
